32 devices in a mesh: seq: 8 (over z, y), chan: 4 (over x, core).
Axes of the slice: x: 2, y: 2, z: 4, core: 2. Of those that a mesh axis runs over, the one named last changes fastest.
Arguments:
- query_proj: bfloat16 [2048, 4096], P('seq', 'chan'), may hold values from -6 to 6
- key_proj: bfloat16 [2048, 4096], P('seq', 'chan'), may hold values from -6 to 6
- value_proj: bfloat16 [2048, 4096], P('seq', 'chan'), may hold values from -6 to 6
- out_grad: bfloat16 [2048, 4096], P('seq', 'chan'), may hold values from -6 to 6
- residues: float32 [256, 16], replicated, may hold values from -2.1 to 2.1
- decay_rate: float32 [256, 16], replicated, as said below
- skip_gain: float32 [4096], P('chan'), may hold values from -3 to 3
Outputs:
- layer_out: bfloat16 [2048, 4096], P('seq', 'chan')
- key_grad: bfloat16 [2048, 4096], P('seq', 'chan')
- value_grad: bfloat16 [2048, 4096], P('seq', 'chan')
- filter_grad: float32 [2048, 256], P('seq', 'chan')
The draws below stay inside these ranges and needn't reach their ends.
Inputs may be any that keep to these rules, and one draw needn't show every extreme that they name: `decay_rate`: every rate is positive.
All inputs are finite; a program needn't handle non-finite values.
Results may differ from the reference program's by a relative error of at most 0.022.
Values may be sent and summed in bfloat16 or wider, within the bound.
No kernel may reach another device: no remote copies, remote signals or barrier semaphores. Data moves between devices by JAX's collectives and lax.ppermute only.
A program may use at most 192 MiB of HBM per device.

```python
import math
import jax
import jax.numpy as jnp
from jax import lax

CHANNELS = 4096
FILTERS = 256
MODES = 16
SEQ_LEN = 2048


def draw_decay_rate(key, part):
    pick_key, slow_key, fast_key = jax.random.split(key, 3)
    slow_share = 0.5
    slow_low = 0.25 / SEQ_LEN
    slow_high = 2.0 / SEQ_LEN
    grid_shape = (FILTERS, MODES)
    slow_pick = jax.random.bernoulli(pick_key, slow_share, grid_shape)
    slow_rates = jnp.exp(jax.random.uniform(slow_key, grid_shape, jnp.float32, math.log(slow_low), math.log(slow_high)))
    fast_rates = jnp.exp(jax.random.uniform(fast_key, grid_shape, jnp.float32, math.log(1.0 / 50.0), math.log(1.0 / 20.0)))
    return jnp.where(slow_pick, slow_rates, fast_rates).astype(jnp.float32)


def steps_of(stream_key, dims, cuts, smallest, top_value):
    level = 1.0
    for axis_at, blocks in cuts:
        heights = jax.random.uniform(jax.random.fold_in(jax.random.fold_in(stream_key, 6), axis_at), (blocks,), jnp.float32, smallest / len(cuts), top_value / len(cuts))
        level = level * jnp.repeat(jnp.exp(heights), dims[axis_at] // blocks).reshape((-1,) + (1,) * (len(dims) - 1 - axis_at))
    return level


def centred(own_key, extent, width, reach, cuts=(), kind=jnp.bfloat16):
    entries = width * jax.random.normal(own_key, extent, jnp.float32)
    if cuts:
        entries = entries * steps_of(own_key, extent, cuts, -0.22, 0.18)
    return jnp.clip(entries, -reach, reach).astype(kind)


def setup_inputs(seed: int = 0) -> dict:
    streams_of = jax.random.split(jax.random.key(seed), 8)
    return {
        "query_proj": centred(streams_of[0], (SEQ_LEN, CHANNELS), 1.0, 6.0, ((0, 8), (1, 4))),
        "key_proj": centred(streams_of[1], (SEQ_LEN, CHANNELS), 1.0, 6.0, ((0, 8), (1, 4))),
        "value_proj": centred(streams_of[2], (SEQ_LEN, CHANNELS), 1.0, 6.0, ((0, 8), (1, 4))),
        "out_grad": centred(streams_of[3], (SEQ_LEN, CHANNELS), 1.0, 6.0, ((0, 8), (1, 4))),
        "residues": centred(streams_of[4], (FILTERS, MODES), 0.35, 2.1, (), jnp.float32),
        "decay_rate": draw_decay_rate(jax.random.fold_in(streams_of[7], 71), 0),
        "skip_gain": centred(streams_of[6], (CHANNELS,), 0.5, 3.0, ((0, 4),), jnp.float32),
    }


def filter_taps(residues, decay_rate, positions):
    weight = residues * jnp.sqrt(decay_rate)

    def one_filter(row_pair):
        weight_row, rate_row = row_pair
        return lax.optimization_barrier(jnp.sum(weight_row[:, None] * jnp.exp(-(rate_row[:, None] * positions[None, :])), axis=0))
    return lax.map(one_filter, (weight, decay_rate))

def reference(query_proj, key_proj, value_proj, out_grad, residues, decay_rate, skip_gain):
    length = SEQ_LEN
    fft_size = 2 * length
    blocks = CHANNELS // FILTERS
    conv_in = (key_proj.astype(jnp.float32) * value_proj.astype(jnp.float32)).astype(jnp.bfloat16)
    mid_grad = (out_grad.astype(jnp.float32) * query_proj.astype(jnp.float32)).astype(jnp.bfloat16)
    positions = jnp.arange(length, dtype=jnp.int32).astype(jnp.float32)
    taps = filter_taps(residues, decay_rate, positions)
    spectrum = jnp.fft.fft(taps, n=fft_size, axis=1).T

    def block_step(totals, block_id):
        first_col = (block_id * FILTERS).astype(jnp.int32)

        def columns(source):
            return lax.dynamic_slice_in_dim(source, first_col, FILTERS, 1).astype(jnp.float32)
        conv_block = columns(conv_in)
        grad_block = columns(mid_grad)
        query_block = columns(query_proj)
        key_block = columns(key_proj)
        value_block = columns(value_proj)
        gain_block = lax.dynamic_slice_in_dim(skip_gain, first_col, FILTERS, 0)[None, :]
        conv_spec = jnp.fft.fft(conv_block, n=fft_size, axis=0)
        grad_spec = jnp.fft.fft(grad_block, n=fft_size, axis=0)
        long_conv = jnp.fft.ifft(spectrum * conv_spec, axis=0)[:length].real
        corr_part = jnp.fft.ifft(jnp.conj(spectrum) * grad_spec, axis=0)[:length].real
        product = jnp.conj(conv_spec) * grad_spec
        totals = (totals[0] + product.real, totals[1] + product.imag)
        layer_block = (query_block * (long_conv + gain_block * conv_block)).astype(jnp.bfloat16)
        total_grad = corr_part + gain_block * grad_block
        key_block_grad = (total_grad * value_block).astype(jnp.bfloat16)
        value_block_grad = (total_grad * key_block).astype(jnp.bfloat16)
        return (totals, (layer_block, key_block_grad, value_block_grad))
    zero_sum = jnp.zeros((fft_size, FILTERS), jnp.float32)
    totals, outputs = lax.scan(block_step, (zero_sum, zero_sum), jnp.arange(blocks, dtype=jnp.int32))

    def assemble(stacked):
        return jnp.transpose(stacked, (1, 0, 2)).reshape(length, CHANNELS)
    scale = 1.0 / math.sqrt(SEQ_LEN * (CHANNELS // FILTERS))
    filter_grad = (jnp.fft.ifft(totals[0] + 1j * totals[1], axis=0)[:length].real * scale).astype(jnp.float32)
    return (assemble(outputs[0]), assemble(outputs[1]), assemble(outputs[2]), filter_grad)
```

```python
import functools
import math

import jax
import jax.numpy as jnp
from jax import lax
from jax.experimental import pallas as pl
from jax.experimental.pallas import tpu as pltpu
from jax.sharding import PartitionSpec as P

CHANNELS = 4096
FILTERS = 256
LANES = 128
SUBLANES = 8
VMEM_BYTES = 48 * 1024 * 1024
F32 = jnp.float32
BF16 = jnp.bfloat16


def product(first, second):
    return (first.astype(F32) * second.astype(F32)).astype(BF16)


def one_hot(rows, cols, column_of):
    row = lax.broadcasted_iota(jnp.int32, (rows, cols), 0)
    col = lax.broadcasted_iota(jnp.int32, (rows, cols), 1)
    return (col == column_of(row)).astype(F32).astype(BF16)


def pack_kernel(shards, chans, owned, q_ref, k_ref, v_ref, o_ref, send_ref):
    per_chan = FILTERS // chans

    def owned_filter(row):
        seq = row // (chans * owned)
        chan = row // owned % chans
        return chan * per_chan + seq * owned + row % owned

    order = one_hot(FILTERS, FILTERS, owned_filter)
    width = k_ref.shape[1]
    groups = width // FILTERS
    for which, (a_ref, b_ref) in enumerate(((k_ref, v_ref), (o_ref, q_ref))):
        signal = product(a_ref[...], b_ref[...])
        parts = []
        for group in range(groups):
            part = lax.dot_general(
                order,
                signal[:, group * FILTERS : (group + 1) * FILTERS],
                (((1,), (1,)), ((), ())),
                preferred_element_type=F32,
            )
            if owned % SUBLANES:
                send_ref[which, group] = part.astype(BF16)
            else:
                parts.append(part.reshape(shards * chans, owned, part.shape[1]))
        if parts:
            rows = groups * owned
            send_ref[:, which * rows : (which + 1) * rows, :] = jnp.concatenate(
                parts, axis=1
            ).astype(BF16)


def pack_signals(shards, chans, owned, query_proj, key_proj, value_proj, out_grad):
    tok_rows, width = key_proj.shape
    groups = width // FILTERS
    dests = shards * chans
    steps = tok_rows // LANES
    block = pl.BlockSpec((LANES, width), lambda i: (i, 0))
    if owned % SUBLANES:
        shape = (2, groups, FILTERS, tok_rows)
        out_spec = pl.BlockSpec((2, groups, FILTERS, LANES), lambda i: (0, 0, 0, i))
    else:
        shape = (dests, 2 * groups * owned, tok_rows)
        out_spec = pl.BlockSpec((dests, 2 * groups * owned, LANES), lambda i: (0, 0, i))
    send = pl.pallas_call(
        functools.partial(pack_kernel, shards, chans, owned),
        grid=(steps,),
        in_specs=[block] * 4,
        out_specs=out_spec,
        out_shape=jax.ShapeDtypeStruct(shape, BF16),
        compiler_params=pltpu.CompilerParams(vmem_limit_bytes=VMEM_BYTES),
        name="pack_signals",
    )(query_proj, key_proj, value_proj, out_grad)
    if owned % SUBLANES:
        send = send.reshape(2, groups, dests, owned, tok_rows)
        send = send.transpose(2, 0, 1, 3, 4).reshape(dests, 2 * groups * owned, tok_rows)
    return send


def state_kernel(q_ref, k_ref, v_ref, o_ref, coef_ref, state_ref, x_ref, g_ref):
    tok_rows, width = k_ref.shape
    tiles = width // LANES
    modes = coef_ref.shape[1]
    spread_tokens(k_ref, v_ref, x_ref)
    spread_tokens(o_ref, q_ref, g_ref)

    def step(t, carry):
        x = x_ref[pl.ds(t, tiles, stride=tok_rows), :]
        g = g_ref[pl.ds(tok_rows - 1 - t, tiles, stride=tok_rows), :]
        ahead = tuple(coef_ref[0, m] * carry[0][m] + x for m in range(modes))
        behind = tuple(coef_ref[0, m] * carry[1][m] + g for m in range(modes))
        return (ahead, behind)

    zero = tuple(jnp.zeros((tiles, LANES), F32) for _ in range(modes))
    ahead, behind = lax.fori_loop(0, tok_rows, step, (zero, zero), unroll=8)
    for m in range(modes):
        state_ref[0, m] = ahead[m]
        state_ref[1, m] = behind[m]


def spread_tokens(a_ref, b_ref, x_ref):
    tok_rows, width = a_ref.shape
    for tile in range(width // LANES):
        cols = slice(tile * LANES, (tile + 1) * LANES)
        x_ref[tile * tok_rows : (tile + 1) * tok_rows, :] = product(
            a_ref[:, cols], b_ref[:, cols]
        ).astype(F32)


def block_states(query_proj, key_proj, value_proj, out_grad, coefs):
    tok_rows, width = key_proj.shape
    tiles = width // LANES
    modes = coefs.shape[1]
    return pl.pallas_call(
        state_kernel,
        out_shape=jax.ShapeDtypeStruct((2, modes, tiles, LANES), F32),
        scratch_shapes=[pltpu.VMEM((tok_rows * tiles, LANES), F32)] * 2,
        compiler_params=pltpu.CompilerParams(vmem_limit_bytes=VMEM_BYTES),
        cost_estimate=pl.CostEstimate(
            flops=4 * modes * tok_rows * width, bytes_accessed=8 * tok_rows * width, transcendentals=0
        ),
        name="block_states",
    )(query_proj, key_proj, value_proj, out_grad, coefs)


def output_kernel(
    seq_ref, q_ref, k_ref, v_ref, o_ref, coef_ref, gain_ref, all_ref,
    layer_ref, key_ref, value_ref, x_ref, g_ref,
):
    tok_rows, width = k_ref.shape
    tiles = width // LANES
    modes = coef_ref.shape[1]
    shards = all_ref.shape[0]
    seq = seq_ref[0]
    spread_tokens(k_ref, v_ref, x_ref)
    spread_tokens(o_ref, q_ref, g_ref)
    zero = tuple(jnp.zeros((tiles, LANES), F32) for _ in range(modes))

    def join_ahead(s, held):
        return tuple(coef_ref[1, m] * held[m] + all_ref[s, 0, m] for m in range(modes))

    def join_behind(i, held):
        s = shards - 1 - i
        return tuple(coef_ref[1, m] * held[m] + all_ref[s, 1, m] for m in range(modes))

    def total(held):
        terms = [coef_ref[2, m] * held[m] for m in range(modes)]
        while len(terms) > 1:
            terms = [sum(terms[i : i + 2][1:], terms[i]) for i in range(0, len(terms), 2)]
        return terms[0]

    def walk(ref, start, move):
        def step(t, held):
            rows = pl.ds(start + move * t, tiles, stride=tok_rows)
            x = ref[rows, :]
            held = tuple(coef_ref[0, m] * held[m] + x for m in range(modes))
            ref[rows, :] = total(held)
            return held

        return step

    held = lax.fori_loop(0, seq, join_ahead, zero)
    lax.fori_loop(0, tok_rows, walk(x_ref, 0, 1), held, unroll=8)
    held = lax.fori_loop(0, shards - 1 - seq, join_behind, zero)
    lax.fori_loop(0, tok_rows, walk(g_ref, tok_rows - 1, -1), held, unroll=8)
    for tile in range(tiles):
        cols = slice(tile * LANES, (tile + 1) * LANES)
        rows = slice(tile * tok_rows, (tile + 1) * tok_rows)
        q = q_ref[:, cols].astype(F32)
        k = k_ref[:, cols].astype(F32)
        v = v_ref[:, cols].astype(F32)
        gain = gain_ref[:, cols]
        conv_in = (k * v).astype(BF16).astype(F32)
        mid_grad = (o_ref[:, cols].astype(F32) * q).astype(BF16).astype(F32)
        layer_ref[:, cols] = (q * (x_ref[rows, :] + gain * conv_in)).astype(BF16)
        conv_grad = g_ref[rows, :] + gain * mid_grad
        key_ref[:, cols] = (conv_grad * v).astype(BF16)
        value_ref[:, cols] = (conv_grad * k).astype(BF16)


def local_outputs(seq_index, query_proj, key_proj, value_proj, out_grad, coefs, gain, states):
    tok_rows, width = key_proj.shape
    tiles = width // LANES
    modes = coefs.shape[1]
    whole = pl.BlockSpec(memory_space=pltpu.VMEM)
    return pl.pallas_call(
        output_kernel,
        in_specs=[pl.BlockSpec(memory_space=pltpu.SMEM)] + [whole] * 7,
        out_specs=[whole] * 3,
        out_shape=[jax.ShapeDtypeStruct((tok_rows, width), BF16)] * 3,
        scratch_shapes=[pltpu.VMEM((tok_rows * tiles, LANES), F32)] * 2,
        compiler_params=pltpu.CompilerParams(vmem_limit_bytes=VMEM_BYTES),
        cost_estimate=pl.CostEstimate(
            flops=8 * modes * tok_rows * width, bytes_accessed=14 * tok_rows * width, transcendentals=0
        ),
        name="local_outputs",
    )(seq_index.reshape(1), query_proj, key_proj, value_proj, out_grad, coefs, gain, states)


def lag_kernel(shards, chans, groups, owned, scale, *refs):
    in_refs, out_ref, u_all, g_all = refs[:-3], refs[-3], refs[-2], refs[-1]
    tok_rows = out_ref.shape[2]
    halves = tok_rows // LANES
    blocks = shards * halves
    depth = chans * groups
    full = blocks * depth
    if len(in_refs) == 1:
        take = chans * groups * owned

        def by_filter(row):
            return row % depth * owned + row // depth

        order = one_hot(take, take, by_filter)
        for which, kept in enumerate((u_all, g_all)):
            rows = slice(which * groups * owned, (which + 1) * groups * owned)
            for s in range(shards):
                piece = in_refs[0][s * chans : (s + 1) * chans, rows, :].reshape(take, tok_rows)
                piece = jnp.dot(order, piece, preferred_element_type=F32).astype(BF16)
                piece = piece.reshape(owned, depth, tok_rows)
                for h in range(halves):
                    first = (s * halves + h) * depth
                    kept[:, first : first + depth, :] = piece[:, :, h * LANES : (h + 1) * LANES]
    else:
        u_all[...] = in_refs[0][...]
        g_all[:, :full, :] = in_refs[1][...]
    g_all[:, full:, :] = jnp.zeros((owned, g_all.shape[1] - full, LANES), BF16)
    mirror = one_hot(LANES, LANES, lambda row: LANES - 1 - row)
    row = lax.broadcasted_iota(jnp.int32, (LANES, LANES), 0)
    col = lax.broadcasted_iota(jnp.int32, (LANES, LANES), 1)
    same_block = row + col >= LANES - 1
    filter_row = lax.broadcasted_iota(jnp.int32, (owned, LANES), 0)
    batch = min(blocks, 16)

    def one_filter(f, _):
        turned = lax.dot_general(
            mirror, u_all[f], (((1,), (1,)), ((), ())), preferred_element_type=F32
        ).astype(BF16)

        def some_lags(first):
            tables = []
            for d in range(0, batch, 2):
                pair = jnp.concatenate(
                    [
                        g_all[f, pl.ds(pl.multiple_of((first + d + e) * depth, depth), full), :]
                        for e in range(2)
                    ],
                    axis=1,
                )
                table = jnp.dot(turned, pair, preferred_element_type=F32)
                tables += [table[:, :LANES], table[:, LANES:]]
            last = g_all[f, pl.ds(pl.multiple_of((first + batch) * depth, depth), full), :]
            if batch < blocks:
                tables.append(jnp.dot(turned, last, preferred_element_type=F32))
            else:
                tables.append(jnp.zeros((LANES, LANES), F32))
            for d in range(batch):
                joined = jnp.where(same_block, tables[d], tables[d + 1])
                skewed = pltpu.roll(joined, 1, 1, stride=1, stride_axis=0)
                sums = jnp.sum(skewed, axis=0, keepdims=True) * scale
                lane = d % halves * LANES
                place = ((first + d) // halves, slice(None), slice(lane, lane + LANES))
                out_ref[place] = jnp.where(filter_row == f, sums, out_ref[place])

        if batch == blocks:
            some_lags(0)
        else:
            lax.fori_loop(0, blocks // batch, lambda i, c: (some_lags(i * batch), c)[1], 0)
        return 0

    lax.fori_loop(0, owned, one_filter, 0)


def filter_lags(received, shards, chans, owned, scale):
    tok_rows = received.shape[2]
    groups = received.shape[1] // (2 * owned)
    halves = tok_rows // LANES
    depth = chans * groups
    full = shards * halves * depth
    args = (received,)
    if owned % SUBLANES:
        split = received.reshape(shards, chans, 2, groups, owned, halves, LANES)
        split = split.transpose(2, 4, 0, 5, 1, 3, 6).reshape(2, owned, full, LANES)
        args = (split[0], split[1])
    return pl.pallas_call(
        functools.partial(lag_kernel, shards, chans, groups, owned, scale),
        out_shape=jax.ShapeDtypeStruct((shards, owned, tok_rows), F32),
        scratch_shapes=[
            pltpu.VMEM((owned, full, LANES), BF16),
            pltpu.VMEM((owned, 2 * full + depth, LANES), BF16),
        ],
        compiler_params=pltpu.CompilerParams(vmem_limit_bytes=VMEM_BYTES),
        name="filter_lags",
    )(*args)


def per_device(query_proj, key_proj, value_proj, out_grad, residues, decay_rate, skip_gain):
    tok_rows, width = key_proj.shape
    shards = lax.axis_size("seq")
    chans = lax.axis_size("chan")
    seq_index = lax.axis_index("seq")
    length = shards * tok_rows
    owned = FILTERS // (shards * chans)
    modes = residues.shape[1]
    signals = (query_proj, key_proj, value_proj, out_grad)

    send = pack_signals(shards, chans, owned, *signals)
    received = lax.all_to_all(send, ("seq", "chan"), split_axis=0, concat_axis=0, tiled=True)

    coefs = jnp.stack(
        [
            jnp.exp(-decay_rate),
            jnp.exp(-(decay_rate * float(tok_rows))),
            residues * jnp.sqrt(decay_rate),
        ]
    )
    coefs = coefs.transpose(0, 2, 1).reshape(3, modes, 1, FILTERS // LANES, LANES)
    coefs = jnp.broadcast_to(coefs, (3, modes, width // FILTERS, FILTERS // LANES, LANES))
    coefs = coefs.reshape(3, modes, width // LANES, LANES)
    states = block_states(*signals, coefs)
    states = lax.all_gather(states, "seq", axis=0)
    layer_out, key_grad, value_grad = local_outputs(
        seq_index, *signals, coefs, skip_gain[None, :], states
    )

    scale = 1.0 / math.sqrt(length * (CHANNELS // FILTERS))
    lags = filter_lags(received, shards, chans, owned, scale)
    lags = lax.all_to_all(lags, "seq", split_axis=0, concat_axis=0, tiled=True)
    filter_grad = lags.reshape(shards * owned, tok_rows).T
    return (layer_out, key_grad, value_grad, filter_grad)


def solution(mesh):
    split = P("seq", "chan")
    return jax.shard_map(
        per_device,
        mesh=mesh,
        in_specs=(split, split, split, split, P(), P(), P("chan")),
        out_specs=(split, split, split, split),
        check_vma=False,
    )
```

```python
import functools
import math

import jax
import jax.numpy as jnp
from jax import lax
from jax.experimental import pallas as pl
from jax.experimental.pallas import tpu as pltpu
from jax.sharding import PartitionSpec as P

CHANNELS = 4096
FILTERS = 256
LANES = 128
SUBLANES = 8
VMEM_BYTES = 48 * 1024 * 1024
PACK_VMEM_BYTES = 62 * 1024 * 1024
F32 = jnp.float32
BF16 = jnp.bfloat16


def product(first, second):
    return (first.astype(F32) * second.astype(F32)).astype(BF16)


def one_hot(rows, cols, column_of):
    row = lax.broadcasted_iota(jnp.int32, (rows, cols), 0)
    col = lax.broadcasted_iota(jnp.int32, (rows, cols), 1)
    return (col == column_of(row)).astype(F32).astype(BF16)


def pack_kernel(shards, chans, owned, q_ref, k_ref, v_ref, o_ref, send_ref):
    per_chan = FILTERS // chans

    def owned_filter(row):
        seq = row // (chans * owned)
        chan = row // owned % chans
        return chan * per_chan + seq * owned + row % owned

    order = one_hot(FILTERS, FILTERS, owned_filter)
    width = k_ref.shape[1]
    groups = width // FILTERS
    for which, (a_ref, b_ref) in enumerate(((k_ref, v_ref), (o_ref, q_ref))):
        signal = product(a_ref[...], b_ref[...])
        parts = []
        for group in range(groups):
            part = lax.dot_general(
                order,
                signal[:, group * FILTERS : (group + 1) * FILTERS],
                (((1,), (1,)), ((), ())),
                preferred_element_type=F32,
            )
            if owned % SUBLANES:
                send_ref[which, group] = part.astype(BF16)
            else:
                parts.append(part.reshape(shards * chans, owned, part.shape[1]))
        if parts:
            rows = groups * owned
            send_ref[:, which * rows : (which + 1) * rows, :] = jnp.concatenate(
                parts, axis=1
            ).astype(BF16)


def pack_signals(shards, chans, owned, query_proj, key_proj, value_proj, out_grad):
    tok_rows, width = key_proj.shape
    groups = width // FILTERS
    dests = shards * chans
    steps = tok_rows // LANES
    block = pl.BlockSpec((LANES, width), lambda i: (i, 0))
    if owned % SUBLANES:
        shape = (2, groups, FILTERS, tok_rows)
        out_spec = pl.BlockSpec((2, groups, FILTERS, LANES), lambda i: (0, 0, 0, i))
    else:
        shape = (dests, 2 * groups * owned, tok_rows)
        out_spec = pl.BlockSpec((dests, 2 * groups * owned, LANES), lambda i: (0, 0, i))
    send = pl.pallas_call(
        functools.partial(pack_kernel, shards, chans, owned),
        grid=(steps,),
        in_specs=[block] * 4,
        out_specs=out_spec,
        out_shape=jax.ShapeDtypeStruct(shape, BF16),
        compiler_params=pltpu.CompilerParams(vmem_limit_bytes=PACK_VMEM_BYTES),
        name="pack_signals",
    )(query_proj, key_proj, value_proj, out_grad)
    if owned % SUBLANES:
        send = send.reshape(2, groups, dests, owned, tok_rows)
        send = send.transpose(2, 0, 1, 3, 4).reshape(dests, 2 * groups * owned, tok_rows)
    return send


def state_kernel(seq_ref, q_ref, k_ref, v_ref, o_ref, coef_ref, state_ref, x_ref, g_ref):
    tok_rows, width = k_ref.shape
    tiles = width // LANES
    modes = coef_ref.shape[1]
    spread_tokens(k_ref, v_ref, x_ref)
    spread_tokens(o_ref, q_ref, g_ref)
    decay = [coef_ref[0, m] for m in range(modes)]

    def step(t, carry):
        x = x_ref[pl.ds(t, tiles, stride=tok_rows), :]
        g = g_ref[pl.ds(tok_rows - 1 - t, tiles, stride=tok_rows), :]
        ahead = tuple(decay[m] * carry[0][m] + x for m in range(modes))
        behind = tuple(decay[m] * carry[1][m] + g for m in range(modes))
        return (ahead, behind)

    zero = tuple(jnp.zeros((tiles, LANES), F32) for _ in range(modes))
    ahead, behind = lax.fori_loop(0, tok_rows, step, (zero, zero), unroll=8)
    ahead = jnp.concatenate(ahead, axis=0).astype(BF16)
    behind = jnp.concatenate(behind, axis=0).astype(BF16)

    def fill(s, _):
        @pl.when(s > seq_ref[0])
        def _():
            state_ref[s] = ahead

        @pl.when(s <= seq_ref[0])
        def _():
            state_ref[s] = behind

        return 0

    lax.fori_loop(0, state_ref.shape[0], fill, 0)


def spread_tokens(a_ref, b_ref, x_ref):
    tok_rows, width = a_ref.shape
    for tile in range(width // LANES):
        cols = slice(tile * LANES, (tile + 1) * LANES)
        x_ref[tile * tok_rows : (tile + 1) * tok_rows, :] = product(
            a_ref[:, cols], b_ref[:, cols]
        ).astype(F32)


def block_states(seq_index, shards, query_proj, key_proj, value_proj, out_grad, coefs):
    tok_rows, width = key_proj.shape
    tiles = width // LANES
    modes = coefs.shape[1]
    whole = pl.BlockSpec(memory_space=pltpu.VMEM)
    return pl.pallas_call(
        state_kernel,
        in_specs=[pl.BlockSpec(memory_space=pltpu.SMEM)] + [whole] * 5,
        out_specs=whole,
        out_shape=jax.ShapeDtypeStruct((shards, modes * tiles, LANES), BF16),
        scratch_shapes=[pltpu.VMEM((tok_rows * tiles, LANES), F32)] * 2,
        compiler_params=pltpu.CompilerParams(vmem_limit_bytes=VMEM_BYTES),
        cost_estimate=pl.CostEstimate(
            flops=4 * modes * tok_rows * width, bytes_accessed=8 * tok_rows * width, transcendentals=0
        ),
        name="block_states",
    )(seq_index, query_proj, key_proj, value_proj, out_grad, coefs)


def output_kernel(
    seq_ref, q_ref, k_ref, v_ref, o_ref, coef_ref, gain_ref, all_ref,
    layer_ref, key_ref, value_ref, x_ref, g_ref,
):
    tok_rows, width = k_ref.shape
    tiles = width // LANES
    modes = coef_ref.shape[1]
    shards = all_ref.shape[0]
    seq = seq_ref[0]
    spread_tokens(k_ref, v_ref, x_ref)
    spread_tokens(o_ref, q_ref, g_ref)
    zero = tuple(jnp.zeros((tiles, LANES), F32) for _ in range(modes))

    def join(s, held):
        block = all_ref[s].astype(F32)
        return tuple(
            coef_ref[1, m] * held[m] + block[m * tiles : (m + 1) * tiles] for m in range(modes)
        )

    def total(held):
        terms = [weight[m] * held[m] for m in range(modes)]
        while len(terms) > 1:
            terms = [sum(terms[i : i + 2][1:], terms[i]) for i in range(0, len(terms), 2)]
        return terms[0]

    def walk(ref, start, move):
        def step(t, held):
            rows = pl.ds(start + move * t, tiles, stride=tok_rows)
            x = ref[rows, :]
            held = tuple(decay[m] * held[m] + x for m in range(modes))
            ref[rows, :] = total(held)
            return held

        return step

    before = lax.fori_loop(0, seq, join, zero)
    after = lax.fori_loop(0, shards - 1 - seq, lambda i, held: join(shards - 1 - i, held), zero)
    decay = [coef_ref[0, m] for m in range(modes)]
    weight = [coef_ref[2, m] for m in range(modes)]
    lax.fori_loop(0, tok_rows, walk(x_ref, 0, 1), before, unroll=8)
    lax.fori_loop(0, tok_rows, walk(g_ref, tok_rows - 1, -1), after, unroll=8)
    for tile in range(tiles):
        cols = slice(tile * LANES, (tile + 1) * LANES)
        rows = slice(tile * tok_rows, (tile + 1) * tok_rows)
        q = q_ref[:, cols].astype(F32)
        k = k_ref[:, cols].astype(F32)
        v = v_ref[:, cols].astype(F32)
        gain = gain_ref[:, cols]
        conv_in = (k * v).astype(BF16).astype(F32)
        mid_grad = (o_ref[:, cols].astype(F32) * q).astype(BF16).astype(F32)
        layer_ref[:, cols] = (q * (x_ref[rows, :] + gain * conv_in)).astype(BF16)
        conv_grad = g_ref[rows, :] + gain * mid_grad
        key_ref[:, cols] = (conv_grad * v).astype(BF16)
        value_ref[:, cols] = (conv_grad * k).astype(BF16)


def local_outputs(seq_index, query_proj, key_proj, value_proj, out_grad, coefs, gain, states):
    tok_rows, width = key_proj.shape
    tiles = width // LANES
    modes = coefs.shape[1]
    whole = pl.BlockSpec(memory_space=pltpu.VMEM)
    return pl.pallas_call(
        output_kernel,
        in_specs=[pl.BlockSpec(memory_space=pltpu.SMEM)] + [whole] * 7,
        out_specs=[whole] * 3,
        out_shape=[jax.ShapeDtypeStruct((tok_rows, width), BF16)] * 3,
        scratch_shapes=[pltpu.VMEM((tok_rows * tiles, LANES), F32)] * 2,
        compiler_params=pltpu.CompilerParams(vmem_limit_bytes=VMEM_BYTES),
        cost_estimate=pl.CostEstimate(
            flops=8 * modes * tok_rows * width, bytes_accessed=14 * tok_rows * width, transcendentals=0
        ),
        name="local_outputs",
    )(seq_index, query_proj, key_proj, value_proj, out_grad, coefs, gain, states)


def lag_kernel(shards, chans, groups, owned, scale, *refs):
    in_refs, out_ref, u_all, g_all = refs[:-3], refs[-3], refs[-2], refs[-1]
    tok_rows = out_ref.shape[2]
    halves = tok_rows // LANES
    blocks = shards * halves
    depth = chans * groups
    full = blocks * depth
    if len(in_refs) == 1:
        take = chans * groups * owned

        def by_filter(row):
            return row % depth * owned + row // depth

        order = one_hot(take, take, by_filter)
        for which, kept in enumerate((u_all, g_all)):
            rows = slice(which * groups * owned, (which + 1) * groups * owned)
            for s in range(shards):
                piece = in_refs[0][s * chans : (s + 1) * chans, rows, :].reshape(take, tok_rows)
                piece = jnp.dot(order, piece, preferred_element_type=F32).astype(BF16)
                piece = piece.reshape(owned, depth, tok_rows)
                for h in range(halves):
                    first = (s * halves + h) * depth
                    kept[:, first : first + depth, :] = piece[:, :, h * LANES : (h + 1) * LANES]
    else:
        u_all[...] = in_refs[0][...]
        g_all[:, :full, :] = in_refs[1][...]
    g_all[:, full:, :] = jnp.zeros((owned, g_all.shape[1] - full, LANES), BF16)
    mirror = one_hot(LANES, LANES, lambda row: LANES - 1 - row)
    row = lax.broadcasted_iota(jnp.int32, (LANES, LANES), 0)
    col = lax.broadcasted_iota(jnp.int32, (LANES, LANES), 1)
    same_block = row + col >= LANES - 1
    filter_row = lax.broadcasted_iota(jnp.int32, (owned, LANES), 0)
    batch = min(blocks, 16)

    def one_filter(f, _):
        turned = lax.dot_general(
            mirror, u_all[f], (((1,), (1,)), ((), ())), preferred_element_type=F32
        ).astype(BF16)

        def some_lags(first):
            tables = []
            for d in range(0, batch, 2):
                pair = jnp.concatenate(
                    [
                        g_all[f, pl.ds(pl.multiple_of((first + d + e) * depth, depth), full), :]
                        for e in range(2)
                    ],
                    axis=1,
                )
                table = jnp.dot(turned, pair, preferred_element_type=F32)
                tables += [table[:, :LANES], table[:, LANES:]]
            last = g_all[f, pl.ds(pl.multiple_of((first + batch) * depth, depth), full), :]
            if batch < blocks:
                tables.append(jnp.dot(turned, last, preferred_element_type=F32))
            else:
                tables.append(jnp.zeros((LANES, LANES), F32))
            for d in range(batch):
                joined = jnp.where(same_block, tables[d], tables[d + 1])
                skewed = pltpu.roll(joined, 1, 1, stride=1, stride_axis=0)
                sums = jnp.sum(skewed, axis=0, keepdims=True) * scale
                lane = d % halves * LANES
                place = ((first + d) // halves, slice(None), slice(lane, lane + LANES))
                out_ref[place] = jnp.where(filter_row == f, sums, out_ref[place])

        if batch == blocks:
            some_lags(0)
        else:
            lax.fori_loop(0, blocks // batch, lambda i, c: (some_lags(i * batch), c)[1], 0)
        return 0

    lax.fori_loop(0, owned, one_filter, 0)


def filter_lags(received, shards, chans, owned, scale):
    tok_rows = received.shape[2]
    groups = received.shape[1] // (2 * owned)
    halves = tok_rows // LANES
    depth = chans * groups
    full = shards * halves * depth
    args = (received,)
    if owned % SUBLANES:
        split = received.reshape(shards, chans, 2, groups, owned, halves, LANES)
        split = split.transpose(2, 4, 0, 5, 1, 3, 6).reshape(2, owned, full, LANES)
        args = (split[0], split[1])
    return pl.pallas_call(
        functools.partial(lag_kernel, shards, chans, groups, owned, scale),
        out_shape=jax.ShapeDtypeStruct((shards, owned, tok_rows), F32),
        scratch_shapes=[
            pltpu.VMEM((owned, full, LANES), BF16),
            pltpu.VMEM((owned, 2 * full + depth, LANES), BF16),
        ],
        compiler_params=pltpu.CompilerParams(vmem_limit_bytes=VMEM_BYTES),
        name="filter_lags",
    )(*args)


def per_device(query_proj, key_proj, value_proj, out_grad, residues, decay_rate, skip_gain):
    tok_rows, width = key_proj.shape
    shards = lax.axis_size("seq")
    chans = lax.axis_size("chan")
    seq_index = lax.axis_index("seq").reshape(1)
    length = shards * tok_rows
    owned = FILTERS // (shards * chans)
    modes = residues.shape[1]
    signals = (query_proj, key_proj, value_proj, out_grad)

    send = pack_signals(shards, chans, owned, *signals)
    send, *signals = lax.optimization_barrier((send, *signals))
    received = lax.all_to_all(send, ("seq", "chan"), split_axis=0, concat_axis=0, tiled=True)

    coefs = jnp.stack(
        [
            jnp.exp(-decay_rate),
            jnp.exp(-(decay_rate * float(tok_rows))),
            residues * jnp.sqrt(decay_rate),
        ]
    )
    coefs = coefs.transpose(0, 2, 1).reshape(3, modes, 1, FILTERS // LANES, LANES)
    coefs = jnp.broadcast_to(coefs, (3, modes, width // FILTERS, FILTERS // LANES, LANES))
    coefs = coefs.reshape(3, modes, width // LANES, LANES)
    states = block_states(seq_index, shards, *signals, coefs)
    states = lax.all_to_all(states, "seq", split_axis=0, concat_axis=0, tiled=True)
    local = local_outputs(seq_index, *signals, coefs, skip_gain[None, :], states)
    received, layer_out, key_grad, value_grad = lax.optimization_barrier((received, *local))

    scale = 1.0 / math.sqrt(length * (CHANNELS // FILTERS))
    lags = filter_lags(received, shards, chans, owned, scale)
    lags = lax.all_to_all(lags, "seq", split_axis=0, concat_axis=0, tiled=True)
    filter_grad = lags.reshape(shards * owned, tok_rows).T
    return (layer_out, key_grad, value_grad, filter_grad)


def solution(mesh):
    split = P("seq", "chan")
    return jax.shard_map(
        per_device,
        mesh=mesh,
        in_specs=(split, split, split, split, P(), P(), P("chan")),
        out_specs=(split, split, split, split),
        check_vma=False,
    )
```

```python
import functools
import math

import jax
import jax.numpy as jnp
from jax import lax
from jax.experimental import pallas as pl
from jax.experimental.pallas import tpu as pltpu
from jax.sharding import PartitionSpec as P

CHANNELS = 4096
FILTERS = 256
LANES = 128
SUBLANES = 8
VMEM_BYTES = 48 * 1024 * 1024
PACK_VMEM_BYTES = 24 * 1024 * 1024
F32 = jnp.float32
BF16 = jnp.bfloat16
LINK = jnp.bfloat16


def product(first, second):
    return (first.astype(F32) * second.astype(F32)).astype(BF16)


def one_hot(rows, cols, column_of):
    row = lax.broadcasted_iota(jnp.int32, (rows, cols), 0)
    col = lax.broadcasted_iota(jnp.int32, (rows, cols), 1)
    return (col == column_of(row)).astype(F32).astype(BF16)


def pack_kernel(shards, chans, owned, *refs):
    hbm_refs, send_ref, held, sems = refs[:4], refs[4], refs[5], refs[6]
    tok_rows, width = held.shape[1:]
    groups = width // FILTERS
    per_chan = FILTERS // chans
    copies = [
        pltpu.make_async_copy(hbm_refs[i], held.at[i], sems.at[i]) for i in range(len(hbm_refs))
    ]
    for copy in copies:
        copy.start()

    def owned_filter(row):
        seq = row // (chans * owned)
        chan = row // owned % chans
        return chan * per_chan + seq * owned + row % owned

    order = one_hot(FILTERS, FILTERS, owned_filter)
    for which in range(2):
        copies[2 * which].wait()
        copies[2 * which + 1].wait()
        signal = product(held[2 * which], held[2 * which + 1])
        parts = []
        for group in range(groups):
            part = lax.dot_general(
                order,
                signal[:, group * FILTERS : (group + 1) * FILTERS],
                (((1,), (1,)), ((), ())),
                preferred_element_type=F32,
            )
            if owned % SUBLANES:
                send_ref[which, group] = part.astype(BF16)
            else:
                parts.append(part.reshape(shards * chans, owned, tok_rows))
        if parts:
            rows = groups * owned
            send_ref[:, which * rows : (which + 1) * rows, :] = jnp.concatenate(
                parts, axis=1
            ).astype(BF16)


def pack_signals(shards, chans, owned, query_proj, key_proj, value_proj, out_grad):
    tok_rows, width = key_proj.shape
    groups = width // FILTERS
    dests = shards * chans
    if owned % SUBLANES:
        shape = (2, groups, FILTERS, tok_rows)
    else:
        shape = (dests, 2 * groups * owned, tok_rows)
    send = pl.pallas_call(
        functools.partial(pack_kernel, shards, chans, owned),
        in_specs=[pl.BlockSpec(memory_space=pltpu.HBM)] * 4,
        out_specs=pl.BlockSpec(memory_space=pltpu.VMEM),
        out_shape=jax.ShapeDtypeStruct(shape, BF16),
        scratch_shapes=[
            pltpu.VMEM((4, tok_rows, width), BF16),
            pltpu.SemaphoreType.DMA((4,)),
        ],
        compiler_params=pltpu.CompilerParams(vmem_limit_bytes=PACK_VMEM_BYTES),
        name="pack_signals",
    )(key_proj, value_proj, out_grad, query_proj)
    if owned % SUBLANES:
        send = send.reshape(2, groups, dests, owned, tok_rows)
        send = send.transpose(2, 0, 1, 3, 4).reshape(dests, 2 * groups * owned, tok_rows)
    return send


def state_kernel(q_ref, k_ref, v_ref, o_ref, coef_ref, ahead_ref, behind_ref, x_ref, g_ref):
    tok_rows, width = k_ref.shape
    tiles = width // LANES
    modes = coef_ref.shape[1]
    spread_tokens(k_ref, v_ref, x_ref)
    spread_tokens(o_ref, q_ref, g_ref)
    decay = [coef_ref[0, m] for m in range(modes)]

    def step(t, carry):
        x = x_ref[pl.ds(t, tiles, stride=tok_rows), :]
        g = g_ref[pl.ds(tok_rows - 1 - t, tiles, stride=tok_rows), :]
        ahead = tuple(decay[m] * carry[0][m] + x for m in range(modes))
        behind = tuple(decay[m] * carry[1][m] + g for m in range(modes))
        return (ahead, behind)

    zero = tuple(jnp.zeros((tiles, LANES), F32) for _ in range(modes))
    ahead, behind = lax.fori_loop(0, tok_rows, step, (zero, zero), unroll=8)
    for m in range(modes):
        ahead_ref[m] = ahead[m].astype(ahead_ref.dtype)
        behind_ref[m] = behind[m].astype(behind_ref.dtype)


def spread_tokens(a_ref, b_ref, x_ref):
    tok_rows, width = a_ref.shape
    for tile in range(width // LANES):
        cols = slice(tile * LANES, (tile + 1) * LANES)
        x_ref[tile * tok_rows : (tile + 1) * tok_rows, :] = product(
            a_ref[:, cols], b_ref[:, cols]
        ).astype(F32)


def block_states(query_proj, key_proj, value_proj, out_grad, coefs):
    tok_rows, width = key_proj.shape
    tiles = width // LANES
    modes = coefs.shape[1]
    return pl.pallas_call(
        state_kernel,
        out_shape=[jax.ShapeDtypeStruct((modes, tiles, LANES), F32)] * 2,
        scratch_shapes=[pltpu.VMEM((tok_rows * tiles, LANES), F32)] * 2,
        compiler_params=pltpu.CompilerParams(vmem_limit_bytes=VMEM_BYTES),
        cost_estimate=pl.CostEstimate(
            flops=4 * modes * tok_rows * width, bytes_accessed=8 * tok_rows * width, transcendentals=0
        ),
        name="block_states",
    )(query_proj, key_proj, value_proj, out_grad, coefs)


def blocks_before(state, block_decay, move):
    shards = lax.axis_size("seq")

    def shift(value, count):
        route = [
            (i, i + move * count) for i in range(shards) if 0 <= i + move * count < shards
        ]
        if not route:
            return jnp.zeros_like(value)
        return lax.ppermute(value, "seq", route)

    sent = state.astype(LINK)
    total = shift(sent, 1).astype(F32) + block_decay * shift(sent, 2).astype(F32)
    span = 2
    while span < shards - 1:
        block_decay = block_decay * block_decay
        total = total + block_decay * shift(total.astype(LINK), span).astype(F32)
        span *= 2
    return total


def walk_tokens(ref, held, coef_ref, tok_rows, tiles, start, move):
    modes = coef_ref.shape[1]
    decay = [coef_ref[0, m] for m in range(modes)]
    weight = [coef_ref[2, m] for m in range(modes)]

    def step(t, held):
        rows = pl.ds(start + move * t, tiles, stride=tok_rows)
        x = ref[rows, :]
        held = tuple(decay[m] * held[m] + x for m in range(modes))
        terms = [weight[m] * held[m] for m in range(modes)]
        while len(terms) > 1:
            terms = [sum(terms[i : i + 2][1:], terms[i]) for i in range(0, len(terms), 2)]
        ref[rows, :] = terms[0]
        return held

    lax.fori_loop(0, tok_rows, step, tuple(held[m] for m in range(modes)), unroll=8)


def conv_kernel(q_ref, k_ref, v_ref, coef_ref, gain_ref, before_ref, layer_ref, x_ref):
    tok_rows, width = k_ref.shape
    tiles = width // LANES
    spread_tokens(k_ref, v_ref, x_ref)
    walk_tokens(x_ref, before_ref, coef_ref, tok_rows, tiles, 0, 1)
    for tile in range(tiles):
        cols = slice(tile * LANES, (tile + 1) * LANES)
        rows = slice(tile * tok_rows, (tile + 1) * tok_rows)
        conv_in = product(k_ref[:, cols], v_ref[:, cols]).astype(F32)
        long_conv = x_ref[rows, :] + gain_ref[:, cols] * conv_in
        layer_ref[:, cols] = (q_ref[:, cols].astype(F32) * long_conv).astype(BF16)


def grad_kernel(
    q_ref, k_ref, v_ref, o_ref, coef_ref, gain_ref, after_ref, key_ref, value_ref, g_ref
):
    tok_rows, width = k_ref.shape
    tiles = width // LANES
    spread_tokens(o_ref, q_ref, g_ref)
    walk_tokens(g_ref, after_ref, coef_ref, tok_rows, tiles, tok_rows - 1, -1)
    for tile in range(tiles):
        cols = slice(tile * LANES, (tile + 1) * LANES)
        rows = slice(tile * tok_rows, (tile + 1) * tok_rows)
        mid_grad = product(o_ref[:, cols], q_ref[:, cols]).astype(F32)
        conv_grad = g_ref[rows, :] + gain_ref[:, cols] * mid_grad
        key_ref[:, cols] = (conv_grad * v_ref[:, cols].astype(F32)).astype(BF16)
        value_ref[:, cols] = (conv_grad * k_ref[:, cols].astype(F32)).astype(BF16)


def local_outputs(kernel, count, name, *args):
    tok_rows, width = args[0].shape
    modes, tiles = args[-1].shape[:2]
    return pl.pallas_call(
        kernel,
        out_shape=[jax.ShapeDtypeStruct((tok_rows, width), BF16)] * count,
        scratch_shapes=[pltpu.VMEM((tok_rows * tiles, LANES), F32)],
        compiler_params=pltpu.CompilerParams(vmem_limit_bytes=VMEM_BYTES),
        cost_estimate=pl.CostEstimate(
            flops=4 * modes * tok_rows * width, bytes_accessed=8 * tok_rows * width, transcendentals=0
        ),
        name=name,
    )(*args)


def lag_kernel(shards, chans, groups, owned, scale, *refs):
    in_refs, out_ref, u_all, g_all = refs[:-3], refs[-3], refs[-2], refs[-1]
    tok_rows = out_ref.shape[2]
    halves = tok_rows // LANES
    blocks = shards * halves
    depth = chans * groups
    full = blocks * depth
    if len(in_refs) == 1:
        take = chans * groups * owned

        def by_filter(row):
            return row % depth * owned + row // depth

        order = one_hot(take, take, by_filter)
        for which, kept in enumerate((u_all, g_all)):
            rows = slice(which * groups * owned, (which + 1) * groups * owned)
            for s in range(shards):
                piece = in_refs[0][s * chans : (s + 1) * chans, rows, :].reshape(take, tok_rows)
                piece = jnp.dot(order, piece, preferred_element_type=F32).astype(BF16)
                piece = piece.reshape(owned, depth, tok_rows)
                for h in range(halves):
                    first = (s * halves + h) * depth
                    kept[:, first : first + depth, :] = piece[:, :, h * LANES : (h + 1) * LANES]
    else:
        u_all[...] = in_refs[0][...]
        g_all[:, :full, :] = in_refs[1][...]
    g_all[:, full:, :] = jnp.zeros((owned, g_all.shape[1] - full, LANES), BF16)
    mirror = one_hot(LANES, LANES, lambda row: LANES - 1 - row)
    row = lax.broadcasted_iota(jnp.int32, (LANES, LANES), 0)
    col = lax.broadcasted_iota(jnp.int32, (LANES, LANES), 1)
    same_block = row + col >= LANES - 1
    filter_row = lax.broadcasted_iota(jnp.int32, (owned, LANES), 0)
    batch = min(blocks, 16)

    def one_filter(f, _):
        turned = lax.dot_general(
            mirror, u_all[f], (((1,), (1,)), ((), ())), preferred_element_type=F32
        ).astype(BF16)

        def some_lags(first):
            tables = []
            for d in range(0, batch, 2):
                pair = jnp.concatenate(
                    [
                        g_all[f, pl.ds(pl.multiple_of((first + d + e) * depth, depth), full), :]
                        for e in range(2)
                    ],
                    axis=1,
                )
                table = jnp.dot(turned, pair, preferred_element_type=F32)
                tables += [table[:, :LANES], table[:, LANES:]]
            last = g_all[f, pl.ds(pl.multiple_of((first + batch) * depth, depth), full), :]
            if batch < blocks:
                tables.append(jnp.dot(turned, last, preferred_element_type=F32))
            else:
                tables.append(jnp.zeros((LANES, LANES), F32))
            for d in range(batch):
                joined = jnp.where(same_block, tables[d], tables[d + 1])
                skewed = pltpu.roll(joined, 1, 1, stride=1, stride_axis=0)
                sums = jnp.sum(skewed, axis=0, keepdims=True) * scale
                lane = d % halves * LANES
                place = ((first + d) // halves, slice(None), slice(lane, lane + LANES))
                out_ref[place] = jnp.where(filter_row == f, sums, out_ref[place])

        if batch == blocks:
            some_lags(0)
        else:
            lax.fori_loop(0, blocks // batch, lambda i, c: (some_lags(i * batch), c)[1], 0)
        return 0

    lax.fori_loop(0, owned, one_filter, 0)


def filter_lags(received, shards, chans, owned, scale):
    tok_rows = received.shape[2]
    groups = received.shape[1] // (2 * owned)
    halves = tok_rows // LANES
    depth = chans * groups
    full = shards * halves * depth
    args = (received,)
    if owned % SUBLANES:
        split = received.reshape(shards, chans, 2, groups, owned, halves, LANES)
        split = split.transpose(2, 4, 0, 5, 1, 3, 6).reshape(2, owned, full, LANES)
        args = (split[0], split[1])
    return pl.pallas_call(
        functools.partial(lag_kernel, shards, chans, groups, owned, scale),
        out_shape=jax.ShapeDtypeStruct((shards, owned, tok_rows), F32),
        scratch_shapes=[
            pltpu.VMEM((owned, full, LANES), BF16),
            pltpu.VMEM((owned, 2 * full + depth, LANES), BF16),
        ],
        compiler_params=pltpu.CompilerParams(vmem_limit_bytes=VMEM_BYTES),
        name="filter_lags",
    )(*args)


def per_device(query_proj, key_proj, value_proj, out_grad, residues, decay_rate, skip_gain):
    tok_rows, width = key_proj.shape
    shards = lax.axis_size("seq")
    chans = lax.axis_size("chan")
    length = shards * tok_rows
    owned = FILTERS // (shards * chans)
    modes = residues.shape[1]
    signals = (query_proj, key_proj, value_proj, out_grad)

    send = pack_signals(shards, chans, owned, *signals)
    send, *signals, residues, decay_rate = lax.optimization_barrier(
        (send, *signals, residues, decay_rate)
    )
    received = lax.all_to_all(send, ("seq", "chan"), split_axis=0, concat_axis=0, tiled=True)

    coefs = jnp.stack(
        [
            jnp.exp(-decay_rate),
            jnp.exp(-(decay_rate * float(tok_rows))),
            residues * jnp.sqrt(decay_rate),
        ]
    )
    coefs = coefs.transpose(0, 2, 1).reshape(3, modes, 1, FILTERS // LANES, LANES)
    coefs = jnp.broadcast_to(coefs, (3, modes, width // FILTERS, FILTERS // LANES, LANES))
    coefs = coefs.reshape(3, modes, width // LANES, LANES)
    ahead, behind = block_states(*signals, coefs)
    before = blocks_before(ahead, coefs[1], 1)
    after = blocks_before(behind, coefs[1], -1)
    query_proj, key_proj, value_proj, out_grad = signals
    gain = skip_gain[None, :]
    (layer_out,) = local_outputs(
        conv_kernel, 1, "conv_outputs", query_proj, key_proj, value_proj, coefs, gain, before
    )
    received, layer_out = lax.optimization_barrier((received, layer_out))
    key_grad, value_grad = local_outputs(
        grad_kernel, 2, "grad_outputs", *signals, coefs, gain, after
    )

    scale = 1.0 / math.sqrt(length * (CHANNELS // FILTERS))
    lags = filter_lags(received, shards, chans, owned, scale)
    lags = lax.all_to_all(lags, "seq", split_axis=0, concat_axis=0, tiled=True)
    filter_grad = lags.reshape(shards * owned, tok_rows).T
    return (layer_out, key_grad, value_grad, filter_grad)


def solution(mesh):
    split = P("seq", "chan")
    return jax.shard_map(
        per_device,
        mesh=mesh,
        in_specs=(split, split, split, split, P(), P(), P("chan")),
        out_specs=(split, split, split, split),
        check_vma=False,
    )
```

```python
import functools
import math

import jax
import jax.numpy as jnp
from jax import lax
from jax.experimental import pallas as pl
from jax.experimental.pallas import tpu as pltpu
from jax.sharding import PartitionSpec as P

CHANNELS = 4096
FILTERS = 256
LANES = 128
SUBLANES = 8
VMEM_BYTES = 48 * 1024 * 1024
PACK_VMEM_BYTES = 62 * 1024 * 1024
F32 = jnp.float32
BF16 = jnp.bfloat16
LINK = jnp.bfloat16


def product(first, second):
    return (first.astype(F32) * second.astype(F32)).astype(BF16)


def one_hot(rows, cols, column_of):
    row = lax.broadcasted_iota(jnp.int32, (rows, cols), 0)
    col = lax.broadcasted_iota(jnp.int32, (rows, cols), 1)
    return (col == column_of(row)).astype(F32).astype(BF16)


def pack_kernel(shards, chans, owned, *refs):
    hbm_refs, send_ref, held, packed, in_sems, out_sems = refs[:4], *refs[4:]
    tok_rows, width = held.shape[1:]
    groups = width // FILTERS
    per_chan = FILTERS // chans
    parts = tok_rows // LANES
    rows = groups * owned

    def arrival(i, part):
        place = pl.ds(part * LANES, LANES)
        return pltpu.make_async_copy(
            hbm_refs[i].at[place, :], held.at[i, place, :], in_sems.at[i, part]
        )

    def departure(which, part):
        lanes = pl.ds(part * LANES, LANES)
        if owned % SUBLANES:
            place = (which, slice(None), slice(None), lanes)
        else:
            place = (slice(None), pl.ds(which * rows, rows), lanes)
        return pltpu.make_async_copy(
            packed.at[place], send_ref.at[place], out_sems.at[which, part]
        )

    units = [(which, part) for which in range(2) for part in range(parts)]
    for which, part in units:
        for i in (2 * which, 2 * which + 1):
            arrival(i, part).start()

    def owned_filter(row):
        seq = row // (chans * owned)
        chan = row // owned % chans
        return chan * per_chan + seq * owned + row % owned

    order = one_hot(FILTERS, FILTERS, owned_filter)
    for which, part in units:
        for i in (2 * which, 2 * which + 1):
            arrival(i, part).wait()
        place = slice(part * LANES, (part + 1) * LANES)
        signal = product(held[2 * which, place, :], held[2 * which + 1, place, :])
        pieces = []
        for group in range(groups):
            piece = lax.dot_general(
                order,
                signal[:, group * FILTERS : (group + 1) * FILTERS],
                (((1,), (1,)), ((), ())),
                preferred_element_type=F32,
            )
            if owned % SUBLANES:
                packed[which, group, :, place] = piece.astype(BF16)
            else:
                pieces.append(piece.reshape(shards * chans, owned, LANES))
        if pieces:
            packed[:, which * rows : (which + 1) * rows, place] = jnp.concatenate(
                pieces, axis=1
            ).astype(BF16)
        departure(which, part).start()
    for which, part in units:
        departure(which, part).wait()


def pack_signals(shards, chans, owned, query_proj, key_proj, value_proj, out_grad):
    tok_rows, width = key_proj.shape
    groups = width // FILTERS
    dests = shards * chans
    parts = tok_rows // LANES
    if owned % SUBLANES:
        shape = (2, groups, FILTERS, tok_rows)
    else:
        shape = (dests, 2 * groups * owned, tok_rows)
    send = pl.pallas_call(
        functools.partial(pack_kernel, shards, chans, owned),
        in_specs=[pl.BlockSpec(memory_space=pl.ANY)] * 4,
        out_specs=pl.BlockSpec(memory_space=pl.ANY),
        out_shape=jax.ShapeDtypeStruct(shape, BF16),
        scratch_shapes=[
            pltpu.VMEM((4, tok_rows, width), BF16),
            pltpu.VMEM(shape, BF16),
            pltpu.SemaphoreType.DMA((4, parts)),
            pltpu.SemaphoreType.DMA((2, parts)),
        ],
        compiler_params=pltpu.CompilerParams(vmem_limit_bytes=PACK_VMEM_BYTES),
        name="pack_signals",
    )(key_proj, value_proj, out_grad, query_proj)
    if owned % SUBLANES:
        send = send.reshape(2, groups, dests, owned, tok_rows)
        send = send.transpose(2, 0, 1, 3, 4).reshape(dests, 2 * groups * owned, tok_rows)
    return send


def state_kernel(seq_ref, q_ref, k_ref, v_ref, o_ref, coef_ref, *refs):
    state_refs, x_ref, g_ref = refs[:-2], refs[-2], refs[-1]
    tok_rows, width = k_ref.shape
    tiles = width // LANES
    modes = coef_ref.shape[1]
    shards = len(state_refs) + 1
    spread_tokens(k_ref, v_ref, x_ref)
    spread_tokens(o_ref, q_ref, g_ref)
    decay = [coef_ref[0, m] for m in range(modes)]

    def step(t, carry):
        x = x_ref[pl.ds(t, tiles, stride=tok_rows), :]
        g = g_ref[pl.ds(tok_rows - 1 - t, tiles, stride=tok_rows), :]
        ahead = tuple(decay[m] * carry[0][m] + x for m in range(modes))
        behind = tuple(decay[m] * carry[1][m] + g for m in range(modes))
        return (ahead, behind)

    zero = tuple(jnp.zeros((tiles, LANES), F32) for _ in range(modes))
    ahead, behind = lax.fori_loop(0, tok_rows, step, (zero, zero), unroll=8)
    ahead = jnp.concatenate(ahead, axis=0).astype(LINK)
    behind = jnp.concatenate(behind, axis=0).astype(LINK)
    for k in range(1, shards):
        stays = seq_ref[0] + k < shards

        @pl.when(stays)
        def _():
            state_refs[k - 1][...] = ahead

        @pl.when(jnp.logical_not(stays))
        def _():
            state_refs[k - 1][...] = behind


def spread_tokens(a_ref, b_ref, x_ref):
    tok_rows, width = a_ref.shape
    for tile in range(width // LANES):
        cols = slice(tile * LANES, (tile + 1) * LANES)
        x_ref[tile * tok_rows : (tile + 1) * tok_rows, :] = product(
            a_ref[:, cols], b_ref[:, cols]
        ).astype(F32)


def block_states(seq_index, shards, query_proj, key_proj, value_proj, out_grad, coefs):
    tok_rows, width = key_proj.shape
    tiles = width // LANES
    modes = coefs.shape[1]
    whole = pl.BlockSpec(memory_space=pltpu.VMEM)
    return pl.pallas_call(
        state_kernel,
        in_specs=[pl.BlockSpec(memory_space=pltpu.SMEM)] + [whole] * 5,
        out_specs=[whole] * (shards - 1),
        out_shape=[jax.ShapeDtypeStruct((modes * tiles, LANES), LINK)] * (shards - 1),
        scratch_shapes=[pltpu.VMEM((tok_rows * tiles, LANES), F32)] * 2,
        compiler_params=pltpu.CompilerParams(vmem_limit_bytes=VMEM_BYTES),
        cost_estimate=pl.CostEstimate(
            flops=4 * modes * tok_rows * width, bytes_accessed=8 * tok_rows * width, transcendentals=0
        ),
        name="block_states",
    )(seq_index, query_proj, key_proj, value_proj, out_grad, coefs)


def exchange_states(states):
    shards = len(states) + 1
    return [
        lax.ppermute(states[k - 1], "seq", [(i, (i + k) % shards) for i in range(shards)])
        for k in range(1, shards)
    ]


def edge_states(seq, state_refs, coef_ref, later):
    shards = len(state_refs) + 1
    modes, tiles = coef_ref.shape[1:3]
    held = [jnp.zeros((tiles, LANES), F32) for _ in range(modes)]
    count = shards - 1 - seq if later else seq
    for k in range(shards - 1, 0, -1):
        ref = state_refs[shards - k - 1 if later else k - 1]
        block = jnp.where(k <= count, ref[...].astype(F32), 0.0)
        held = [
            coef_ref[1, m] * held[m] + block[m * tiles : (m + 1) * tiles] for m in range(modes)
        ]
    return held


def walk_tokens(ref, held, coef_ref, tok_rows, tiles, start, move):
    modes = coef_ref.shape[1]
    decay = [coef_ref[0, m] for m in range(modes)]
    weight = [coef_ref[2, m] for m in range(modes)]

    def step(t, held):
        rows = pl.ds(start + move * t, tiles, stride=tok_rows)
        x = ref[rows, :]
        held = tuple(decay[m] * held[m] + x for m in range(modes))
        terms = [weight[m] * held[m] for m in range(modes)]
        while len(terms) > 1:
            terms = [sum(terms[i : i + 2][1:], terms[i]) for i in range(0, len(terms), 2)]
        ref[rows, :] = terms[0]
        return held

    lax.fori_loop(0, tok_rows, step, tuple(held), unroll=8)


def conv_kernel(seq_ref, q_ref, k_ref, v_ref, coef_ref, gain_ref, *refs):
    state_refs, layer_ref, x_ref = refs[:-2], refs[-2], refs[-1]
    tok_rows, width = k_ref.shape
    tiles = width // LANES
    spread_tokens(k_ref, v_ref, x_ref)
    held = edge_states(seq_ref[0], state_refs, coef_ref, False)
    walk_tokens(x_ref, held, coef_ref, tok_rows, tiles, 0, 1)
    for tile in range(tiles):
        cols = slice(tile * LANES, (tile + 1) * LANES)
        rows = slice(tile * tok_rows, (tile + 1) * tok_rows)
        conv_in = product(k_ref[:, cols], v_ref[:, cols]).astype(F32)
        long_conv = x_ref[rows, :] + gain_ref[:, cols] * conv_in
        layer_ref[:, cols] = (q_ref[:, cols].astype(F32) * long_conv).astype(BF16)


def grad_kernel(seq_ref, q_ref, k_ref, v_ref, o_ref, coef_ref, gain_ref, *refs):
    state_refs, key_ref, value_ref, g_ref = refs[:-3], *refs[-3:]
    tok_rows, width = k_ref.shape
    tiles = width // LANES
    spread_tokens(o_ref, q_ref, g_ref)
    held = edge_states(seq_ref[0], state_refs, coef_ref, True)
    walk_tokens(g_ref, held, coef_ref, tok_rows, tiles, tok_rows - 1, -1)
    for tile in range(tiles):
        cols = slice(tile * LANES, (tile + 1) * LANES)
        rows = slice(tile * tok_rows, (tile + 1) * tok_rows)
        mid_grad = product(o_ref[:, cols], q_ref[:, cols]).astype(F32)
        conv_grad = g_ref[rows, :] + gain_ref[:, cols] * mid_grad
        key_ref[:, cols] = (conv_grad * v_ref[:, cols].astype(F32)).astype(BF16)
        value_ref[:, cols] = (conv_grad * k_ref[:, cols].astype(F32)).astype(BF16)


def local_outputs(kernel, count, name, seq_index, signals, coefs, gain, states):
    tok_rows, width = signals[0].shape
    modes, tiles = coefs.shape[1:3]
    args = (*signals, coefs, gain, *states)
    whole = pl.BlockSpec(memory_space=pltpu.VMEM)
    return pl.pallas_call(
        kernel,
        in_specs=[pl.BlockSpec(memory_space=pltpu.SMEM)] + [whole] * len(args),
        out_specs=[whole] * count,
        out_shape=[jax.ShapeDtypeStruct((tok_rows, width), BF16)] * count,
        scratch_shapes=[pltpu.VMEM((tok_rows * tiles, LANES), F32)],
        compiler_params=pltpu.CompilerParams(vmem_limit_bytes=VMEM_BYTES),
        cost_estimate=pl.CostEstimate(
            flops=4 * modes * tok_rows * width, bytes_accessed=8 * tok_rows * width, transcendentals=0
        ),
        name=name,
    )(seq_index, *args)


def lag_kernel(shards, chans, groups, owned, scale, *refs):
    in_refs, out_ref, u_all, g_all, turned_all = refs[:-4], *refs[-4:]
    tok_rows = out_ref.shape[2]
    halves = tok_rows // LANES
    blocks = shards * halves
    depth = chans * groups
    full = blocks * depth
    if len(in_refs) == 1:
        take = chans * groups * owned

        def by_filter(row):
            return row % depth * owned + row // depth

        order = one_hot(take, take, by_filter)
        for which, kept in enumerate((u_all, g_all)):
            rows = slice(which * groups * owned, (which + 1) * groups * owned)
            for s in range(shards):
                piece = in_refs[0][s * chans : (s + 1) * chans, rows, :].reshape(take, tok_rows)
                piece = jnp.dot(order, piece, preferred_element_type=F32).astype(BF16)
                piece = piece.reshape(owned, depth, tok_rows)
                for h in range(halves):
                    first = (s * halves + h) * depth
                    kept[:, first : first + depth, :] = piece[:, :, h * LANES : (h + 1) * LANES]
    else:
        u_all[...] = in_refs[0][...]
        g_all[:, :full, :] = in_refs[1][...]
    g_all[:, full:, :] = jnp.zeros((owned, g_all.shape[1] - full, LANES), BF16)
    mirror = one_hot(LANES, LANES, lambda row: LANES - 1 - row)
    row = lax.broadcasted_iota(jnp.int32, (LANES, LANES), 0)
    col = lax.broadcasted_iota(jnp.int32, (LANES, LANES), 1)
    same_block = row + col >= LANES - 1
    filter_row = lax.broadcasted_iota(jnp.int32, (owned, LANES), 0)
    batch = min(blocks, 16)

    def one_filter(f, _):
        turned = turned_all[f]

        def some_lags(first):
            tables = []
            for d in range(0, batch, 2):
                live = full
                if batch == blocks:
                    live = min(full, -(-(blocks - d) * depth // LANES) * LANES)
                pair = jnp.concatenate(
                    [
                        g_all[f, pl.ds(pl.multiple_of((first + d + e) * depth, depth), live), :]
                        for e in range(2)
                    ],
                    axis=1,
                )
                table = jnp.dot(turned[:, :live], pair, preferred_element_type=F32)
                tables += [table[:, :LANES], table[:, LANES:]]
            last = g_all[f, pl.ds(pl.multiple_of((first + batch) * depth, depth), full), :]
            if batch < blocks:
                tables.append(jnp.dot(turned, last, preferred_element_type=F32))
            else:
                tables.append(jnp.zeros((LANES, LANES), F32))
            for d in range(batch):
                joined = jnp.where(same_block, tables[d], tables[d + 1])
                skewed = pltpu.roll(joined, 1, 1, stride=1, stride_axis=0)
                sums = jnp.sum(skewed, axis=0, keepdims=True) * scale
                lane = d % halves * LANES
                place = ((first + d) // halves, slice(None), slice(lane, lane + LANES))
                out_ref[place] = jnp.where(filter_row == f, sums, out_ref[place])

        if batch == blocks:
            some_lags(0)
        else:
            lax.fori_loop(0, blocks // batch, lambda i, c: (some_lags(i * batch), c)[1], 0)
        return 0

    for f in range(owned):
        turned_all[f] = lax.dot_general(
            mirror, u_all[f], (((1,), (1,)), ((), ())), preferred_element_type=F32
        ).astype(BF16)
    lax.fori_loop(0, owned, one_filter, 0, unroll=min(owned, 2))


def filter_lags(received, shards, chans, owned, scale):
    tok_rows = received.shape[2]
    groups = received.shape[1] // (2 * owned)
    halves = tok_rows // LANES
    depth = chans * groups
    full = shards * halves * depth
    args = (received,)
    if owned % SUBLANES:
        split = received.reshape(shards, chans, 2, groups, owned, halves, LANES)
        split = split.transpose(2, 4, 0, 5, 1, 3, 6).reshape(2, owned, full, LANES)
        args = (split[0], split[1])
    return pl.pallas_call(
        functools.partial(lag_kernel, shards, chans, groups, owned, scale),
        out_shape=jax.ShapeDtypeStruct((shards, owned, tok_rows), F32),
        scratch_shapes=[
            pltpu.VMEM((owned, full, LANES), BF16),
            pltpu.VMEM((owned, 2 * full + depth, LANES), BF16),
            pltpu.VMEM((owned, LANES, full), BF16),
        ],
        compiler_params=pltpu.CompilerParams(vmem_limit_bytes=VMEM_BYTES),
        name="filter_lags",
    )(*args)


def per_device(query_proj, key_proj, value_proj, out_grad, residues, decay_rate, skip_gain):
    tok_rows, width = key_proj.shape
    shards = lax.axis_size("seq")
    chans = lax.axis_size("chan")
    length = shards * tok_rows
    owned = FILTERS // (shards * chans)
    modes = residues.shape[1]
    signals = (query_proj, key_proj, value_proj, out_grad)

    send = pack_signals(shards, chans, owned, *signals)
    send, *signals, residues, decay_rate = lax.optimization_barrier(
        (send, *signals, residues, decay_rate)
    )
    received = lax.all_to_all(send, ("seq", "chan"), split_axis=0, concat_axis=0, tiled=True)

    coefs = jnp.stack(
        [
            jnp.exp(-decay_rate),
            jnp.exp(-(decay_rate * float(tok_rows))),
            residues * jnp.sqrt(decay_rate),
        ]
    )
    coefs = coefs.transpose(0, 2, 1).reshape(3, modes, 1, FILTERS // LANES, LANES)
    coefs = jnp.broadcast_to(coefs, (3, modes, width // FILTERS, FILTERS // LANES, LANES))
    coefs = coefs.reshape(3, modes, width // LANES, LANES)
    seq_index = lax.axis_index("seq").reshape(1)
    states = exchange_states(block_states(seq_index, shards, *signals, coefs))
    gain = skip_gain[None, :]
    (layer_out,) = local_outputs(
        conv_kernel, 1, "conv_outputs", seq_index, signals[:3], coefs, gain, states
    )
    received, layer_out = lax.optimization_barrier((received, layer_out))
    key_grad, value_grad = local_outputs(
        grad_kernel, 2, "grad_outputs", seq_index, signals, coefs, gain, states
    )

    scale = 1.0 / math.sqrt(length * (CHANNELS // FILTERS))
    lags = filter_lags(received, shards, chans, owned, scale)
    lags = lax.all_to_all(lags, "seq", split_axis=0, concat_axis=0, tiled=True)
    filter_grad = lags.reshape(shards * owned, tok_rows).T
    return (layer_out, key_grad, value_grad, filter_grad)


def solution(mesh):
    split = P("seq", "chan")
    return jax.shard_map(
        per_device,
        mesh=mesh,
        in_specs=(split, split, split, split, P(), P(), P("chan")),
        out_specs=(split, split, split, split),
        check_vma=False,
    )
```

```python
import functools
import math

import jax
import jax.numpy as jnp
from jax import lax
from jax.experimental import pallas as pl
from jax.experimental.pallas import tpu as pltpu
from jax.sharding import PartitionSpec as P

CHANNELS = 4096
FILTERS = 256
LANES = 128
SUBLANES = 8
VMEM_BYTES = 48 * 1024 * 1024
PACK_VMEM_BYTES = 62 * 1024 * 1024
F32 = jnp.float32
BF16 = jnp.bfloat16
LINK = jnp.bfloat16


def product(first, second):
    return (first.astype(F32) * second.astype(F32)).astype(BF16)


def one_hot(rows, cols, column_of):
    row = lax.broadcasted_iota(jnp.int32, (rows, cols), 0)
    col = lax.broadcasted_iota(jnp.int32, (rows, cols), 1)
    return (col == column_of(row)).astype(F32).astype(BF16)


def pack_kernel(shards, chans, owned, *refs):
    hbm_refs, send_ref, held, packed, in_sems, out_sems = refs[:4], *refs[4:]
    tok_rows, width = held.shape[1:]
    groups = width // FILTERS
    per_chan = FILTERS // chans
    parts = tok_rows // LANES
    rows = groups * owned

    def arrival(i, part):
        place = pl.ds(part * LANES, LANES)
        return pltpu.make_async_copy(
            hbm_refs[i].at[place, :], held.at[i, place, :], in_sems.at[i, part]
        )

    def departure(which, part):
        lanes = pl.ds(part * LANES, LANES)
        if owned % SUBLANES:
            place = (which, slice(None), slice(None), lanes)
        else:
            place = (slice(None), pl.ds(which * rows, rows), lanes)
        return pltpu.make_async_copy(
            packed.at[place], send_ref.at[place], out_sems.at[which, part]
        )

    units = [(which, part) for which in range(2) for part in range(parts)]
    for which, part in units:
        for i in (2 * which, 2 * which + 1):
            arrival(i, part).start()

    def owned_filter(row):
        seq = row // (chans * owned)
        chan = row // owned % chans
        return chan * per_chan + seq * owned + row % owned

    order = one_hot(FILTERS, FILTERS, owned_filter)
    for which, part in units:
        for i in (2 * which, 2 * which + 1):
            arrival(i, part).wait()
        place = slice(part * LANES, (part + 1) * LANES)
        signal = product(held[2 * which, place, :], held[2 * which + 1, place, :])
        pieces = []
        for group in range(groups):
            piece = lax.dot_general(
                order,
                signal[:, group * FILTERS : (group + 1) * FILTERS],
                (((1,), (1,)), ((), ())),
                preferred_element_type=F32,
            )
            if owned % SUBLANES:
                packed[which, group, :, place] = piece.astype(BF16)
            else:
                pieces.append(piece.reshape(shards * chans, owned, LANES))
        if pieces:
            packed[:, which * rows : (which + 1) * rows, place] = jnp.concatenate(
                pieces, axis=1
            ).astype(BF16)
        departure(which, part).start()
    for which, part in units:
        departure(which, part).wait()


def pack_signals(shards, chans, owned, query_proj, key_proj, value_proj, out_grad):
    tok_rows, width = key_proj.shape
    groups = width // FILTERS
    dests = shards * chans
    parts = tok_rows // LANES
    if owned % SUBLANES:
        shape = (2, groups, FILTERS, tok_rows)
    else:
        shape = (dests, 2 * groups * owned, tok_rows)
    send = pl.pallas_call(
        functools.partial(pack_kernel, shards, chans, owned),
        in_specs=[pl.BlockSpec(memory_space=pl.ANY)] * 4,
        out_specs=pl.BlockSpec(memory_space=pl.ANY),
        out_shape=jax.ShapeDtypeStruct(shape, BF16),
        scratch_shapes=[
            pltpu.VMEM((4, tok_rows, width), BF16),
            pltpu.VMEM(shape, BF16),
            pltpu.SemaphoreType.DMA((4, parts)),
            pltpu.SemaphoreType.DMA((2, parts)),
        ],
        compiler_params=pltpu.CompilerParams(vmem_limit_bytes=PACK_VMEM_BYTES),
        name="pack_signals",
    )(key_proj, value_proj, out_grad, query_proj)
    if owned % SUBLANES:
        send = send.reshape(2, groups, dests, owned, tok_rows)
        send = send.transpose(2, 0, 1, 3, 4).reshape(dests, 2 * groups * owned, tok_rows)
    return send


def spread_tokens(a_ref, b_ref, x_ref):
    tok_rows, width = a_ref.shape
    for tile in range(width // LANES):
        cols = slice(tile * LANES, (tile + 1) * LANES)
        x_ref[tile * tok_rows : (tile + 1) * tok_rows, :] = product(
            a_ref[:, cols], b_ref[:, cols]
        ).astype(F32)


def walk_tokens(ref, coef_ref, tok_rows, tiles, start, move):
    modes = coef_ref.shape[1]
    decay = [coef_ref[0, m] for m in range(modes)]
    weight = [coef_ref[2, m] for m in range(modes)]

    def step(t, held):
        rows = pl.ds(start + move * t, tiles, stride=tok_rows)
        x = ref[rows, :]
        held = tuple(decay[m] * held[m] + x for m in range(modes))
        ref[rows, :] = tree_sum([weight[m] * held[m] for m in range(modes)])
        return held

    zero = tuple(jnp.zeros((tiles, LANES), F32) for _ in range(modes))
    return lax.fori_loop(0, tok_rows, step, zero, unroll=8)


def tree_sum(terms):
    while len(terms) > 1:
        terms = [sum(terms[i : i + 2][1:], terms[i]) for i in range(0, len(terms), 2)]
    return terms[0]


def local_kernel(seq_ref, q_ref, k_ref, v_ref, o_ref, coef_ref, conv_ref, grad_ref, *state_refs):
    tok_rows, width = k_ref.shape
    tiles = width // LANES
    shards = len(state_refs) + 1
    spread_tokens(k_ref, v_ref, conv_ref)
    spread_tokens(o_ref, q_ref, grad_ref)
    ahead = walk_tokens(conv_ref, coef_ref, tok_rows, tiles, 0, 1)
    behind = walk_tokens(grad_ref, coef_ref, tok_rows, tiles, tok_rows - 1, -1)
    ahead = jnp.concatenate(ahead, axis=0).astype(LINK)
    behind = jnp.concatenate(behind, axis=0).astype(LINK)
    for k in range(1, shards):
        stays = seq_ref[0] + k < shards

        @pl.when(stays)
        def _():
            state_refs[k - 1][...] = ahead

        @pl.when(jnp.logical_not(stays))
        def _():
            state_refs[k - 1][...] = behind


def local_parts(seq_index, shards, query_proj, key_proj, value_proj, out_grad, coefs):
    tok_rows, width = key_proj.shape
    modes, tiles = coefs.shape[1:3]
    whole = pl.BlockSpec(memory_space=pltpu.VMEM)
    outs = pl.pallas_call(
        local_kernel,
        in_specs=[pl.BlockSpec(memory_space=pltpu.SMEM)] + [whole] * 5,
        out_specs=[whole] * (shards + 1),
        out_shape=[jax.ShapeDtypeStruct((tok_rows * tiles, LANES), F32)] * 2
        + [jax.ShapeDtypeStruct((modes * tiles, LANES), LINK)] * (shards - 1),
        compiler_params=pltpu.CompilerParams(vmem_limit_bytes=VMEM_BYTES),
        cost_estimate=pl.CostEstimate(
            flops=8 * modes * tok_rows * width, bytes_accessed=8 * tok_rows * width, transcendentals=0
        ),
        name="local_parts",
    )(seq_index, query_proj, key_proj, value_proj, out_grad, coefs)
    return outs[:2], outs[2:]


def send_state(state, shards, k):
    return lax.ppermute(state, "seq", [(i, (i + k) % shards) for i in range(shards)])


def edge_states(seq, state_refs, coef_ref, later):
    shards = len(state_refs) + 1
    modes, tiles = coef_ref.shape[1:3]
    held = [jnp.zeros((tiles, LANES), F32) for _ in range(modes)]
    count = shards - 1 - seq if later else seq
    for k in range(shards - 1, 0, -1):
        ref = state_refs[shards - k - 1 if later else k - 1]
        block = jnp.where(k <= count, ref[...].astype(F32), 0.0)
        held = [
            coef_ref[1, m] * held[m] + block[m * tiles : (m + 1) * tiles] for m in range(modes)
        ]
    return held


def add_edge(ref, held, coef_ref, tok_rows, tiles, start, move):
    modes = coef_ref.shape[1]
    decay = [coef_ref[0, m] for m in range(modes)]

    def step(t, held):
        rows = pl.ds(start + move * t, tiles, stride=tok_rows)
        held = tuple(decay[m] * held[m] for m in range(modes))
        ref[rows, :] = ref[rows, :] + tree_sum(list(held))
        return held

    held = tuple(coef_ref[2, m] * held[m] for m in range(modes))
    lax.fori_loop(0, tok_rows, step, held, unroll=8)


def final_kernel(seq_ref, q_ref, k_ref, v_ref, o_ref, coef_ref, gain_ref, x_ref, g_ref, *refs):
    state_refs, hbm_refs, held_refs, sems = refs[:-7], refs[-7:-4], refs[-4:-1], refs[-1]
    layer_ref, key_ref, value_ref = held_refs
    tok_rows, width = k_ref.shape
    tiles = width // LANES

    def departure(i, tile):
        place = (slice(None), pl.ds(tile * LANES, LANES))
        return pltpu.make_async_copy(
            held_refs[i].at[place], hbm_refs[i].at[place], sems.at[i, tile]
        )

    edge = edge_states(seq_ref[0], state_refs, coef_ref, False)
    add_edge(x_ref, edge, coef_ref, tok_rows, tiles, 0, 1)
    for tile in range(tiles):
        cols = slice(tile * LANES, (tile + 1) * LANES)
        rows = slice(tile * tok_rows, (tile + 1) * tok_rows)
        conv_in = product(k_ref[:, cols], v_ref[:, cols]).astype(F32)
        long_conv = x_ref[rows, :] + gain_ref[:, cols] * conv_in
        layer_ref[:, cols] = (q_ref[:, cols].astype(F32) * long_conv).astype(BF16)
        departure(0, tile).start()
    edge = edge_states(seq_ref[0], state_refs, coef_ref, True)
    add_edge(g_ref, edge, coef_ref, tok_rows, tiles, tok_rows - 1, -1)
    for tile in range(tiles):
        cols = slice(tile * LANES, (tile + 1) * LANES)
        rows = slice(tile * tok_rows, (tile + 1) * tok_rows)
        mid_grad = product(o_ref[:, cols], q_ref[:, cols]).astype(F32)
        conv_grad = g_ref[rows, :] + gain_ref[:, cols] * mid_grad
        key_ref[:, cols] = (conv_grad * v_ref[:, cols].astype(F32)).astype(BF16)
        departure(1, tile).start()
        value_ref[:, cols] = (conv_grad * k_ref[:, cols].astype(F32)).astype(BF16)
        departure(2, tile).start()
    for i in range(3):
        for tile in range(tiles):
            departure(i, tile).wait()


def final_outputs(seq_index, signals, coefs, gain, parts, states):
    tok_rows, width = signals[0].shape
    modes, tiles = coefs.shape[1:3]
    args = (*signals, coefs, gain, *parts, *states)
    whole = pl.BlockSpec(memory_space=pltpu.VMEM)
    return pl.pallas_call(
        final_kernel,
        in_specs=[pl.BlockSpec(memory_space=pltpu.SMEM)] + [whole] * len(args),
        out_specs=[pl.BlockSpec(memory_space=pl.ANY)] * 3,
        out_shape=[jax.ShapeDtypeStruct((tok_rows, width), BF16)] * 3,
        scratch_shapes=[pltpu.VMEM((tok_rows, width), BF16)] * 3
        + [pltpu.SemaphoreType.DMA((3, tiles))],
        compiler_params=pltpu.CompilerParams(vmem_limit_bytes=VMEM_BYTES),
        cost_estimate=pl.CostEstimate(
            flops=8 * modes * tok_rows * width, bytes_accessed=14 * tok_rows * width, transcendentals=0
        ),
        name="final_outputs",
    )(seq_index, *args)


def lag_kernel(shards, chans, groups, owned, scale, *refs):
    in_refs, out_ref, u_all, g_all, turned_all = refs[:-4], *refs[-4:]
    tok_rows = out_ref.shape[2]
    halves = tok_rows // LANES
    blocks = shards * halves
    depth = chans * groups
    full = blocks * depth
    if len(in_refs) == 1:
        take = chans * groups * owned

        def by_filter(row):
            return row % depth * owned + row // depth

        order = one_hot(take, take, by_filter)
        for which, kept in enumerate((u_all, g_all)):
            rows = slice(which * groups * owned, (which + 1) * groups * owned)
            for s in range(shards):
                piece = in_refs[0][s * chans : (s + 1) * chans, rows, :].reshape(take, tok_rows)
                piece = jnp.dot(order, piece, preferred_element_type=F32).astype(BF16)
                piece = piece.reshape(owned, depth, tok_rows)
                for h in range(halves):
                    first = (s * halves + h) * depth
                    kept[:, first : first + depth, :] = piece[:, :, h * LANES : (h + 1) * LANES]
    else:
        u_all[...] = in_refs[0][...]
        g_all[:, :full, :] = in_refs[1][...]
    g_all[:, full:, :] = jnp.zeros((owned, g_all.shape[1] - full, LANES), BF16)
    mirror = one_hot(LANES, LANES, lambda row: LANES - 1 - row)
    row = lax.broadcasted_iota(jnp.int32, (LANES, LANES), 0)
    col = lax.broadcasted_iota(jnp.int32, (LANES, LANES), 1)
    same_block = row + col >= LANES - 1
    filter_row = lax.broadcasted_iota(jnp.int32, (owned, LANES), 0)
    batch = min(blocks, 16)

    def one_filter(f, _):
        turned = turned_all[f]

        def some_lags(first):
            tables = []
            for d in range(0, batch, 2):
                live = full
                if batch == blocks:
                    live = min(full, -(-(blocks - d) * depth // LANES) * LANES)
                pair = jnp.concatenate(
                    [
                        g_all[f, pl.ds(pl.multiple_of((first + d + e) * depth, depth), live), :]
                        for e in range(2)
                    ],
                    axis=1,
                )
                table = jnp.dot(turned[:, :live], pair, preferred_element_type=F32)
                tables += [table[:, :LANES], table[:, LANES:]]
            last = g_all[f, pl.ds(pl.multiple_of((first + batch) * depth, depth), full), :]
            if batch < blocks:
                tables.append(jnp.dot(turned, last, preferred_element_type=F32))
            else:
                tables.append(jnp.zeros((LANES, LANES), F32))
            for d in range(batch):
                joined = jnp.where(same_block, tables[d], tables[d + 1])
                skewed = pltpu.roll(joined, 1, 1, stride=1, stride_axis=0)
                sums = jnp.sum(skewed, axis=0, keepdims=True) * scale
                lane = d % halves * LANES
                place = ((first + d) // halves, slice(None), slice(lane, lane + LANES))
                out_ref[place] = jnp.where(filter_row == f, sums, out_ref[place])

        if batch == blocks:
            some_lags(0)
        else:
            lax.fori_loop(0, blocks // batch, lambda i, c: (some_lags(i * batch), c)[1], 0)
        return 0

    for f in range(owned):
        turned_all[f] = lax.dot_general(
            mirror, u_all[f], (((1,), (1,)), ((), ())), preferred_element_type=F32
        ).astype(BF16)
    lax.fori_loop(0, owned, one_filter, 0, unroll=min(owned, 2))


def filter_lags(received, shards, chans, owned, scale):
    tok_rows = received.shape[2]
    groups = received.shape[1] // (2 * owned)
    halves = tok_rows // LANES
    depth = chans * groups
    full = shards * halves * depth
    args = (received,)
    if owned % SUBLANES:
        split = received.reshape(shards, chans, 2, groups, owned, halves, LANES)
        split = split.transpose(2, 4, 0, 5, 1, 3, 6).reshape(2, owned, full, LANES)
        args = (split[0], split[1])
    return pl.pallas_call(
        functools.partial(lag_kernel, shards, chans, groups, owned, scale),
        out_shape=jax.ShapeDtypeStruct((shards, owned, tok_rows), F32),
        scratch_shapes=[
            pltpu.VMEM((owned, full, LANES), BF16),
            pltpu.VMEM((owned, 2 * full + depth, LANES), BF16),
            pltpu.VMEM((owned, LANES, full), BF16),
        ],
        compiler_params=pltpu.CompilerParams(vmem_limit_bytes=VMEM_BYTES),
        name="filter_lags",
    )(*args)


def per_device(query_proj, key_proj, value_proj, out_grad, residues, decay_rate, skip_gain):
    tok_rows, width = key_proj.shape
    shards = lax.axis_size("seq")
    chans = lax.axis_size("chan")
    length = shards * tok_rows
    owned = FILTERS // (shards * chans)
    modes = residues.shape[1]
    signals = (query_proj, key_proj, value_proj, out_grad)

    send = pack_signals(shards, chans, owned, *signals)
    send, *signals, residues, decay_rate = lax.optimization_barrier(
        (send, *signals, residues, decay_rate)
    )
    received = lax.all_to_all(send, ("seq", "chan"), split_axis=0, concat_axis=0, tiled=True)

    coefs = jnp.stack(
        [
            jnp.exp(-decay_rate),
            jnp.exp(-(decay_rate * float(tok_rows))),
            residues * jnp.sqrt(decay_rate),
        ]
    )
    coefs = coefs.transpose(0, 2, 1).reshape(3, modes, 1, FILTERS // LANES, LANES)
    coefs = jnp.broadcast_to(coefs, (3, modes, width // FILTERS, FILTERS // LANES, LANES))
    coefs = coefs.reshape(3, modes, width // LANES, LANES)
    seq_index = lax.axis_index("seq").reshape(1)
    parts, states = local_parts(seq_index, shards, *signals, coefs)
    early = [send_state(states[k - 1], shards, k) for k in range(1, min(shards, 6))]
    received, *parts = lax.optimization_barrier((received, *parts))

    scale = 1.0 / math.sqrt(length * (CHANNELS // FILTERS))
    lags = filter_lags(received, shards, chans, owned, scale)
    lags, *late = lax.optimization_barrier((lags, *states[5:]))
    late = [send_state(state, shards, 6 + i) for i, state in enumerate(late)]
    lags = lax.all_to_all(lags, "seq", split_axis=0, concat_axis=0, tiled=True)
    filter_grad = lags.reshape(shards * owned, tok_rows).T
    layer_out, key_grad, value_grad = final_outputs(
        seq_index, signals, coefs, skip_gain[None, :], parts, early + late
    )
    return (layer_out, key_grad, value_grad, filter_grad)


def solution(mesh):
    split = P("seq", "chan")
    return jax.shard_map(
        per_device,
        mesh=mesh,
        in_specs=(split, split, split, split, P(), P(), P("chan")),
        out_specs=(split, split, split, split),
        check_vma=False,
    )
```

```python
import functools
import math

import jax
import jax.numpy as jnp
from jax import lax
from jax.experimental import pallas as pl
from jax.experimental.pallas import tpu as pltpu
from jax.sharding import PartitionSpec as P

CHANNELS = 4096
FILTERS = 256
LANES = 128
SUBLANES = 8
VMEM_BYTES = 48 * 1024 * 1024
PACK_VMEM_BYTES = 62 * 1024 * 1024
F32 = jnp.float32
BF16 = jnp.bfloat16
LINK = jnp.bfloat16


def product(first, second):
    return (first.astype(F32) * second.astype(F32)).astype(BF16)


def one_hot(rows, cols, column_of):
    row = lax.broadcasted_iota(jnp.int32, (rows, cols), 0)
    col = lax.broadcasted_iota(jnp.int32, (rows, cols), 1)
    return (col == column_of(row)).astype(F32).astype(BF16)


def pack_kernel(shards, chans, owned, *refs):
    hbm_refs, send_ref, held, packed, in_sems, out_sems = refs[:4], *refs[4:]
    tok_rows, width = held.shape[1:]
    groups = width // FILTERS
    per_chan = FILTERS // chans
    parts = tok_rows // LANES
    rows = groups * owned

    def arrival(i, part):
        place = pl.ds(part * LANES, LANES)
        return pltpu.make_async_copy(
            hbm_refs[i].at[place, :], held.at[i, place, :], in_sems.at[i, part]
        )

    def departure(which, part):
        lanes = pl.ds(part * LANES, LANES)
        if owned % SUBLANES:
            place = (which, slice(None), slice(None), lanes)
        else:
            place = (slice(None), pl.ds(which * rows, rows), lanes)
        return pltpu.make_async_copy(
            packed.at[place], send_ref.at[place], out_sems.at[which, part]
        )

    units = [(which, part) for which in range(2) for part in range(parts)]
    for which, part in units:
        for i in (2 * which, 2 * which + 1):
            arrival(i, part).start()

    def owned_filter(row):
        seq = row // (chans * owned)
        chan = row // owned % chans
        return chan * per_chan + seq * owned + row % owned

    order = one_hot(FILTERS, FILTERS, owned_filter)
    for which, part in units:
        for i in (2 * which, 2 * which + 1):
            arrival(i, part).wait()
        place = slice(part * LANES, (part + 1) * LANES)
        signal = product(held[2 * which, place, :], held[2 * which + 1, place, :])
        pieces = []
        for group in range(groups):
            piece = lax.dot_general(
                order,
                signal[:, group * FILTERS : (group + 1) * FILTERS],
                (((1,), (1,)), ((), ())),
                preferred_element_type=F32,
            )
            if owned % SUBLANES:
                packed[which, group, :, place] = piece.astype(BF16)
            else:
                pieces.append(piece.reshape(shards * chans, owned, LANES))
        if pieces:
            packed[:, which * rows : (which + 1) * rows, place] = jnp.concatenate(
                pieces, axis=1
            ).astype(BF16)
        departure(which, part).start()
    for which, part in units:
        departure(which, part).wait()


def pack_signals(shards, chans, owned, query_proj, key_proj, value_proj, out_grad):
    tok_rows, width = key_proj.shape
    groups = width // FILTERS
    dests = shards * chans
    parts = tok_rows // LANES
    if owned % SUBLANES:
        shape = (2, groups, FILTERS, tok_rows)
    else:
        shape = (dests, 2 * groups * owned, tok_rows)
    send = pl.pallas_call(
        functools.partial(pack_kernel, shards, chans, owned),
        in_specs=[pl.BlockSpec(memory_space=pl.ANY)] * 4,
        out_specs=pl.BlockSpec(memory_space=pl.ANY),
        out_shape=jax.ShapeDtypeStruct(shape, BF16),
        scratch_shapes=[
            pltpu.VMEM((4, tok_rows, width), BF16),
            pltpu.VMEM(shape, BF16),
            pltpu.SemaphoreType.DMA((4, parts)),
            pltpu.SemaphoreType.DMA((2, parts)),
        ],
        compiler_params=pltpu.CompilerParams(vmem_limit_bytes=PACK_VMEM_BYTES),
        name="pack_signals",
    )(key_proj, value_proj, out_grad, query_proj)
    if owned % SUBLANES:
        send = send.reshape(2, groups, dests, owned, tok_rows)
        send = send.transpose(2, 0, 1, 3, 4).reshape(dests, 2 * groups * owned, tok_rows)
    return send


def spread_tokens(a_ref, b_ref, x_ref):
    tok_rows, width = a_ref.shape
    for tile in range(width // LANES):
        cols = slice(tile * LANES, (tile + 1) * LANES)
        x_ref[tile * tok_rows : (tile + 1) * tok_rows, :] = product(
            a_ref[:, cols], b_ref[:, cols]
        ).astype(F32)


def walk_tokens(ref, coef_ref, tok_rows, tiles, start, move):
    modes = coef_ref.shape[1]
    decay = [coef_ref[0, m] for m in range(modes)]
    weight = [coef_ref[2, m] for m in range(modes)]

    def step(t, held):
        rows = pl.ds(start + move * t, tiles, stride=tok_rows)
        x = ref[rows, :]
        held = tuple(decay[m] * held[m] + x for m in range(modes))
        ref[rows, :] = tree_sum([weight[m] * held[m] for m in range(modes)])
        return held

    zero = tuple(jnp.zeros((tiles, LANES), F32) for _ in range(modes))
    return lax.fori_loop(0, tok_rows, step, zero, unroll=8)


def tree_sum(terms):
    while len(terms) > 1:
        terms = [sum(terms[i : i + 2][1:], terms[i]) for i in range(0, len(terms), 2)]
    return terms[0]


def state_kernel(seq_ref, q_ref, k_ref, v_ref, o_ref, coef_ref, *refs):
    state_refs, x_ref, g_ref = refs[:-2], refs[-2], refs[-1]
    tok_rows, width = k_ref.shape
    tiles = width // LANES
    modes = coef_ref.shape[1]
    shards = len(state_refs) + 1
    spread_tokens(k_ref, v_ref, x_ref)
    spread_tokens(o_ref, q_ref, g_ref)
    decay = [coef_ref[0, m] for m in range(modes)]

    def step(t, carry):
        x = x_ref[pl.ds(t, tiles, stride=tok_rows), :]
        g = g_ref[pl.ds(tok_rows - 1 - t, tiles, stride=tok_rows), :]
        ahead = tuple(decay[m] * carry[0][m] + x for m in range(modes))
        behind = tuple(decay[m] * carry[1][m] + g for m in range(modes))
        return (ahead, behind)

    zero = tuple(jnp.zeros((tiles, LANES), F32) for _ in range(modes))
    ahead, behind = lax.fori_loop(0, tok_rows, step, (zero, zero), unroll=8)
    ahead = jnp.concatenate(ahead, axis=0).astype(LINK)
    behind = jnp.concatenate(behind, axis=0).astype(LINK)
    for k in range(1, shards):
        stays = seq_ref[0] + k < shards

        @pl.when(stays)
        def _():
            state_refs[k - 1][...] = ahead

        @pl.when(jnp.logical_not(stays))
        def _():
            state_refs[k - 1][...] = behind


def block_states(seq_index, shards, query_proj, key_proj, value_proj, out_grad, coefs):
    tok_rows, width = key_proj.shape
    modes, tiles = coefs.shape[1:3]
    whole = pl.BlockSpec(memory_space=pltpu.VMEM)
    return pl.pallas_call(
        state_kernel,
        in_specs=[pl.BlockSpec(memory_space=pltpu.SMEM)] + [whole] * 5,
        out_specs=[whole] * (shards - 1),
        out_shape=[jax.ShapeDtypeStruct((modes * tiles, LANES), LINK)] * (shards - 1),
        scratch_shapes=[pltpu.VMEM((tok_rows * tiles, LANES), F32)] * 2,
        compiler_params=pltpu.CompilerParams(vmem_limit_bytes=VMEM_BYTES),
        cost_estimate=pl.CostEstimate(
            flops=4 * modes * tok_rows * width, bytes_accessed=8 * tok_rows * width, transcendentals=0
        ),
        name="block_states",
    )(seq_index, query_proj, key_proj, value_proj, out_grad, coefs)


def local_kernel(q_ref, k_ref, v_ref, o_ref, coef_ref, conv_ref, grad_ref):
    tok_rows, width = k_ref.shape
    tiles = width // LANES
    spread_tokens(k_ref, v_ref, conv_ref)
    spread_tokens(o_ref, q_ref, grad_ref)
    walk_tokens(conv_ref, coef_ref, tok_rows, tiles, 0, 1)
    walk_tokens(grad_ref, coef_ref, tok_rows, tiles, tok_rows - 1, -1)


def local_parts(query_proj, key_proj, value_proj, out_grad, coefs):
    tok_rows, width = key_proj.shape
    modes, tiles = coefs.shape[1:3]
    return pl.pallas_call(
        local_kernel,
        out_shape=[jax.ShapeDtypeStruct((tok_rows * tiles, LANES), F32)] * 2,
        compiler_params=pltpu.CompilerParams(vmem_limit_bytes=VMEM_BYTES),
        cost_estimate=pl.CostEstimate(
            flops=8 * modes * tok_rows * width, bytes_accessed=8 * tok_rows * width, transcendentals=0
        ),
        name="local_parts",
    )(query_proj, key_proj, value_proj, out_grad, coefs)


def send_state(state, shards, k):
    return lax.ppermute(state, "seq", [(i, (i + k) % shards) for i in range(shards)])


def edge_states(seq, state_refs, coef_ref, later):
    shards = len(state_refs) + 1
    modes, tiles = coef_ref.shape[1:3]
    held = [jnp.zeros((tiles, LANES), F32) for _ in range(modes)]
    count = shards - 1 - seq if later else seq
    for k in range(shards - 1, 0, -1):
        ref = state_refs[shards - k - 1 if later else k - 1]
        block = jnp.where(k <= count, ref[...].astype(F32), 0.0)
        held = [
            coef_ref[1, m] * held[m] + block[m * tiles : (m + 1) * tiles] for m in range(modes)
        ]
    return held


def add_edge(ref, held, coef_ref, tok_rows, tiles, start, move):
    modes = coef_ref.shape[1]
    decay = [coef_ref[0, m] for m in range(modes)]

    def step(t, held):
        rows = pl.ds(start + move * t, tiles, stride=tok_rows)
        held = tuple(decay[m] * held[m] for m in range(modes))
        ref[rows, :] = ref[rows, :] + tree_sum(list(held))
        return held

    held = tuple(coef_ref[2, m] * held[m] for m in range(modes))
    lax.fori_loop(0, tok_rows, step, held, unroll=8)


def final_kernel(seq_ref, q_ref, k_ref, v_ref, o_ref, coef_ref, gain_ref, x_ref, g_ref, *refs):
    state_refs, hbm_refs, held_refs, sems = refs[:-7], refs[-7:-4], refs[-4:-1], refs[-1]
    layer_ref, key_ref, value_ref = held_refs
    tok_rows, width = k_ref.shape
    tiles = width // LANES

    def departure(i, tile):
        place = (slice(None), pl.ds(tile * LANES, LANES))
        return pltpu.make_async_copy(
            held_refs[i].at[place], hbm_refs[i].at[place], sems.at[i, tile]
        )

    edge = edge_states(seq_ref[0], state_refs, coef_ref, False)
    add_edge(x_ref, edge, coef_ref, tok_rows, tiles, 0, 1)
    for tile in range(tiles):
        cols = slice(tile * LANES, (tile + 1) * LANES)
        rows = slice(tile * tok_rows, (tile + 1) * tok_rows)
        conv_in = product(k_ref[:, cols], v_ref[:, cols]).astype(F32)
        long_conv = x_ref[rows, :] + gain_ref[:, cols] * conv_in
        layer_ref[:, cols] = (q_ref[:, cols].astype(F32) * long_conv).astype(BF16)
        departure(0, tile).start()
    edge = edge_states(seq_ref[0], state_refs, coef_ref, True)
    add_edge(g_ref, edge, coef_ref, tok_rows, tiles, tok_rows - 1, -1)
    for tile in range(tiles):
        cols = slice(tile * LANES, (tile + 1) * LANES)
        rows = slice(tile * tok_rows, (tile + 1) * tok_rows)
        mid_grad = product(o_ref[:, cols], q_ref[:, cols]).astype(F32)
        conv_grad = g_ref[rows, :] + gain_ref[:, cols] * mid_grad
        key_ref[:, cols] = (conv_grad * v_ref[:, cols].astype(F32)).astype(BF16)
        departure(1, tile).start()
        value_ref[:, cols] = (conv_grad * k_ref[:, cols].astype(F32)).astype(BF16)
        departure(2, tile).start()
    for i in range(3):
        for tile in range(tiles):
            departure(i, tile).wait()


def final_outputs(seq_index, signals, coefs, gain, parts, states):
    tok_rows, width = signals[0].shape
    modes, tiles = coefs.shape[1:3]
    args = (*signals, coefs, gain, *parts, *states)
    whole = pl.BlockSpec(memory_space=pltpu.VMEM)
    return pl.pallas_call(
        final_kernel,
        in_specs=[pl.BlockSpec(memory_space=pltpu.SMEM)] + [whole] * len(args),
        out_specs=[pl.BlockSpec(memory_space=pl.ANY)] * 3,
        out_shape=[jax.ShapeDtypeStruct((tok_rows, width), BF16)] * 3,
        scratch_shapes=[pltpu.VMEM((tok_rows, width), BF16)] * 3
        + [pltpu.SemaphoreType.DMA((3, tiles))],
        compiler_params=pltpu.CompilerParams(vmem_limit_bytes=VMEM_BYTES),
        cost_estimate=pl.CostEstimate(
            flops=8 * modes * tok_rows * width, bytes_accessed=14 * tok_rows * width, transcendentals=0
        ),
        name="final_outputs",
    )(seq_index, *args)


def lag_kernel(shards, chans, groups, owned, scale, *refs):
    in_refs, out_ref, u_all, g_all, turned_all = refs[:-4], *refs[-4:]
    tok_rows = out_ref.shape[2]
    halves = tok_rows // LANES
    blocks = shards * halves
    depth = chans * groups
    full = blocks * depth
    if len(in_refs) == 1:
        take = chans * groups * owned

        def by_filter(row):
            return row % depth * owned + row // depth

        order = one_hot(take, take, by_filter)
        for which, kept in enumerate((u_all, g_all)):
            rows = slice(which * groups * owned, (which + 1) * groups * owned)
            for s in range(shards):
                piece = in_refs[0][s * chans : (s + 1) * chans, rows, :].reshape(take, tok_rows)
                piece = jnp.dot(order, piece, preferred_element_type=F32).astype(BF16)
                piece = piece.reshape(owned, depth, tok_rows)
                for h in range(halves):
                    first = (s * halves + h) * depth
                    kept[:, first : first + depth, :] = piece[:, :, h * LANES : (h + 1) * LANES]
    else:
        u_all[...] = in_refs[0][...]
        g_all[:, :full, :] = in_refs[1][...]
    g_all[:, full:, :] = jnp.zeros((owned, g_all.shape[1] - full, LANES), BF16)
    mirror = one_hot(LANES, LANES, lambda row: LANES - 1 - row)
    row = lax.broadcasted_iota(jnp.int32, (LANES, LANES), 0)
    col = lax.broadcasted_iota(jnp.int32, (LANES, LANES), 1)
    same_block = row + col >= LANES - 1
    filter_row = lax.broadcasted_iota(jnp.int32, (owned, LANES), 0)
    batch = min(blocks, 16)

    def one_filter(f, _):
        turned = turned_all[f]

        def some_lags(first):
            tables = []
            for d in range(0, batch, 2):
                live = full
                if batch == blocks:
                    live = min(full, -(-(blocks - d) * depth // LANES) * LANES)
                pair = jnp.concatenate(
                    [
                        g_all[f, pl.ds(pl.multiple_of((first + d + e) * depth, depth), live), :]
                        for e in range(2)
                    ],
                    axis=1,
                )
                table = jnp.dot(turned[:, :live], pair, preferred_element_type=F32)
                tables += [table[:, :LANES], table[:, LANES:]]
            last = g_all[f, pl.ds(pl.multiple_of((first + batch) * depth, depth), full), :]
            if batch < blocks:
                tables.append(jnp.dot(turned, last, preferred_element_type=F32))
            else:
                tables.append(jnp.zeros((LANES, LANES), F32))
            for d in range(batch):
                joined = jnp.where(same_block, tables[d], tables[d + 1])
                skewed = pltpu.roll(joined, 1, 1, stride=1, stride_axis=0)
                sums = jnp.sum(skewed, axis=0, keepdims=True) * scale
                lane = d % halves * LANES
                place = ((first + d) // halves, slice(None), slice(lane, lane + LANES))
                out_ref[place] = jnp.where(filter_row == f, sums, out_ref[place])

        if batch == blocks:
            some_lags(0)
        else:
            lax.fori_loop(0, blocks // batch, lambda i, c: (some_lags(i * batch), c)[1], 0)
        return 0

    for f in range(owned):
        turned_all[f] = lax.dot_general(
            mirror, u_all[f], (((1,), (1,)), ((), ())), preferred_element_type=F32
        ).astype(BF16)
    lax.fori_loop(0, owned, one_filter, 0, unroll=min(owned, 2))


def filter_lags(received, shards, chans, owned, scale):
    tok_rows = received.shape[2]
    groups = received.shape[1] // (2 * owned)
    halves = tok_rows // LANES
    depth = chans * groups
    full = shards * halves * depth
    args = (received,)
    if owned % SUBLANES:
        split = received.reshape(shards, chans, 2, groups, owned, halves, LANES)
        split = split.transpose(2, 4, 0, 5, 1, 3, 6).reshape(2, owned, full, LANES)
        args = (split[0], split[1])
    return pl.pallas_call(
        functools.partial(lag_kernel, shards, chans, groups, owned, scale),
        out_shape=jax.ShapeDtypeStruct((shards, owned, tok_rows), F32),
        scratch_shapes=[
            pltpu.VMEM((owned, full, LANES), BF16),
            pltpu.VMEM((owned, 2 * full + depth, LANES), BF16),
            pltpu.VMEM((owned, LANES, full), BF16),
        ],
        compiler_params=pltpu.CompilerParams(vmem_limit_bytes=VMEM_BYTES),
        name="filter_lags",
    )(*args)


def per_device(query_proj, key_proj, value_proj, out_grad, residues, decay_rate, skip_gain):
    tok_rows, width = key_proj.shape
    shards = lax.axis_size("seq")
    chans = lax.axis_size("chan")
    length = shards * tok_rows
    owned = FILTERS // (shards * chans)
    modes = residues.shape[1]
    signals = (query_proj, key_proj, value_proj, out_grad)

    send = pack_signals(shards, chans, owned, *signals)
    send, *signals, residues, decay_rate = lax.optimization_barrier(
        (send, *signals, residues, decay_rate)
    )
    received = lax.all_to_all(send, ("seq", "chan"), split_axis=0, concat_axis=0, tiled=True)

    coefs = jnp.stack(
        [
            jnp.exp(-decay_rate),
            jnp.exp(-(decay_rate * float(tok_rows))),
            residues * jnp.sqrt(decay_rate),
        ]
    )
    coefs = coefs.transpose(0, 2, 1).reshape(3, modes, 1, FILTERS // LANES, LANES)
    coefs = jnp.broadcast_to(coefs, (3, modes, width // FILTERS, FILTERS // LANES, LANES))
    coefs = coefs.reshape(3, modes, width // LANES, LANES)
    seq_index = lax.axis_index("seq").reshape(1)
    states = block_states(seq_index, shards, *signals, coefs)
    *states, coefs = lax.optimization_barrier((*states, coefs))
    states = [send_state(state, shards, 1 + i) for i, state in enumerate(states)]
    parts = local_parts(*signals, coefs)
    received, *parts = lax.optimization_barrier((received, *parts, *states))
    parts, states = parts[:2], parts[2:]

    scale = 1.0 / math.sqrt(length * (CHANNELS // FILTERS))
    lags = filter_lags(received, shards, chans, owned, scale)
    lags = lax.all_to_all(lags, "seq", split_axis=0, concat_axis=0, tiled=True)
    filter_grad = lags.reshape(shards * owned, tok_rows).T
    layer_out, key_grad, value_grad = final_outputs(
        seq_index, signals, coefs, skip_gain[None, :], parts, states
    )
    return (layer_out, key_grad, value_grad, filter_grad)


def solution(mesh):
    split = P("seq", "chan")
    return jax.shard_map(
        per_device,
        mesh=mesh,
        in_specs=(split, split, split, split, P(), P(), P("chan")),
        out_specs=(split, split, split, split),
        check_vma=False,
    )
```

```python
import functools
import math

import jax
import jax.numpy as jnp
from jax import lax
from jax.experimental import pallas as pl
from jax.experimental.pallas import tpu as pltpu
from jax.sharding import PartitionSpec as P

CHANNELS = 4096
FILTERS = 256
LANES = 128
SUBLANES = 8
VMEM_BYTES = 16 * 1024 * 1024
PACK_VMEM_BYTES = 62 * 1024 * 1024
F32 = jnp.float32
BF16 = jnp.bfloat16
LINK = jnp.bfloat16


def product(first, second):
    return (first.astype(F32) * second.astype(F32)).astype(BF16)


def one_hot(rows, cols, column_of):
    row = lax.broadcasted_iota(jnp.int32, (rows, cols), 0)
    col = lax.broadcasted_iota(jnp.int32, (rows, cols), 1)
    return (col == column_of(row)).astype(F32).astype(BF16)


def pack_kernel(shards, chans, owned, *refs):
    hbm_refs, send_ref, held, packed, in_sems, out_sems = refs[:4], *refs[4:]
    tok_rows, width = held.shape[1:]
    groups = width // FILTERS
    per_chan = FILTERS // chans
    parts = tok_rows // LANES
    rows = groups * owned

    def arrival(i, part):
        place = pl.ds(part * LANES, LANES)
        return pltpu.make_async_copy(
            hbm_refs[i].at[place, :], held.at[i, place, :], in_sems.at[i, part]
        )

    def departure(which, part):
        lanes = pl.ds(part * LANES, LANES)
        if owned % SUBLANES:
            place = (which, slice(None), slice(None), lanes)
        else:
            place = (slice(None), pl.ds(which * rows, rows), lanes)
        return pltpu.make_async_copy(
            packed.at[place], send_ref.at[place], out_sems.at[which, part]
        )

    units = [(which, part) for which in range(2) for part in range(parts)]
    for which, part in units:
        for i in (2 * which, 2 * which + 1):
            arrival(i, part).start()

    def owned_filter(row):
        seq = row // (chans * owned)
        chan = row // owned % chans
        return chan * per_chan + seq * owned + row % owned

    order = one_hot(FILTERS, FILTERS, owned_filter)
    for which, part in units:
        for i in (2 * which, 2 * which + 1):
            arrival(i, part).wait()
        place = slice(part * LANES, (part + 1) * LANES)
        signal = product(held[2 * which, place, :], held[2 * which + 1, place, :])
        pieces = []
        for group in range(groups):
            piece = lax.dot_general(
                order,
                signal[:, group * FILTERS : (group + 1) * FILTERS],
                (((1,), (1,)), ((), ())),
                preferred_element_type=F32,
            )
            if owned % SUBLANES:
                packed[which, group, :, place] = piece.astype(BF16)
            else:
                pieces.append(piece.reshape(shards * chans, owned, LANES))
        if pieces:
            packed[:, which * rows : (which + 1) * rows, place] = jnp.concatenate(
                pieces, axis=1
            ).astype(BF16)
        departure(which, part).start()
    for which, part in units:
        departure(which, part).wait()


def pack_signals(shards, chans, owned, query_proj, key_proj, value_proj, out_grad):
    tok_rows, width = key_proj.shape
    groups = width // FILTERS
    dests = shards * chans
    parts = tok_rows // LANES
    if owned % SUBLANES:
        shape = (2, groups, FILTERS, tok_rows)
    else:
        shape = (dests, 2 * groups * owned, tok_rows)
    send = pl.pallas_call(
        functools.partial(pack_kernel, shards, chans, owned),
        in_specs=[pl.BlockSpec(memory_space=pl.ANY)] * 4,
        out_specs=pl.BlockSpec(memory_space=pl.ANY),
        out_shape=jax.ShapeDtypeStruct(shape, BF16),
        scratch_shapes=[
            pltpu.VMEM((4, tok_rows, width), BF16),
            pltpu.VMEM(shape, BF16),
            pltpu.SemaphoreType.DMA((4, parts)),
            pltpu.SemaphoreType.DMA((2, parts)),
        ],
        compiler_params=pltpu.CompilerParams(vmem_limit_bytes=PACK_VMEM_BYTES),
        name="pack_signals",
    )(key_proj, value_proj, out_grad, query_proj)
    if owned % SUBLANES:
        send = send.reshape(2, groups, dests, owned, tok_rows)
        send = send.transpose(2, 0, 1, 3, 4).reshape(dests, 2 * groups * owned, tok_rows)
    return send


def spread_tokens(a_ref, b_ref, x_ref):
    tok_rows, width = a_ref.shape
    for tile in range(width // LANES):
        cols = slice(tile * LANES, (tile + 1) * LANES)
        x_ref[tile * tok_rows : (tile + 1) * tok_rows, :] = product(
            a_ref[:, cols], b_ref[:, cols]
        ).astype(F32)


def walk_tokens(ref, coef_ref, tok_rows, tiles, start, move):
    modes = coef_ref.shape[1]
    decay = [coef_ref[0, m] for m in range(modes)]
    weight = [coef_ref[2, m] for m in range(modes)]

    def step(t, held):
        rows = pl.ds(start + move * t, tiles, stride=tok_rows)
        x = ref[rows, :]
        held = tuple(decay[m] * held[m] + x for m in range(modes))
        ref[rows, :] = tree_sum([weight[m] * held[m] for m in range(modes)])
        return held

    zero = tuple(jnp.zeros((tiles, LANES), F32) for _ in range(modes))
    return lax.fori_loop(0, tok_rows, step, zero, unroll=8)


def tree_sum(terms):
    while len(terms) > 1:
        terms = [sum(terms[i : i + 2][1:], terms[i]) for i in range(0, len(terms), 2)]
    return terms[0]


def state_kernel(seq_ref, q_ref, k_ref, v_ref, o_ref, coef_ref, *refs):
    state_refs, own_ref, x_ref, g_ref = refs[:-3], *refs[-3:]
    tok_rows, width = k_ref.shape
    tiles = width // LANES
    modes = coef_ref.shape[1]
    pairs = len(state_refs) + 1
    spread_tokens(k_ref, v_ref, x_ref)
    spread_tokens(o_ref, q_ref, g_ref)
    decay = [coef_ref[0, m] for m in range(modes)]

    def step(t, carry):
        x = x_ref[pl.ds(t, tiles, stride=tok_rows), :]
        g = g_ref[pl.ds(tok_rows - 1 - t, tiles, stride=tok_rows), :]
        ahead = tuple(decay[m] * carry[0][m] + x for m in range(modes))
        behind = tuple(decay[m] * carry[1][m] + g for m in range(modes))
        return (ahead, behind)

    zero = tuple(jnp.zeros((tiles, LANES), F32) for _ in range(modes))
    ahead, behind = lax.fori_loop(0, tok_rows, step, (zero, zero), unroll=8)
    ahead = jnp.concatenate(ahead, axis=0)
    behind = jnp.concatenate(behind, axis=0)
    own_ref[0] = ahead
    own_ref[1] = behind
    for k in range(1, pairs):
        stays = seq_ref[0] // 2 + k < pairs

        @pl.when(stays)
        def _():
            state_refs[k - 1][...] = ahead.astype(LINK)

        @pl.when(jnp.logical_not(stays))
        def _():
            state_refs[k - 1][...] = behind.astype(LINK)


def block_states(seq_index, pairs, query_proj, key_proj, value_proj, out_grad, coefs):
    tok_rows, width = key_proj.shape
    modes, tiles = coefs.shape[1:3]
    whole = pl.BlockSpec(memory_space=pltpu.VMEM)
    *states, own = pl.pallas_call(
        state_kernel,
        in_specs=[pl.BlockSpec(memory_space=pltpu.SMEM)] + [whole] * 5,
        out_specs=[whole] * pairs,
        out_shape=[jax.ShapeDtypeStruct((modes * tiles, LANES), LINK)] * (pairs - 1)
        + [jax.ShapeDtypeStruct((2, modes * tiles, LANES), F32)],
        scratch_shapes=[pltpu.VMEM((tok_rows * tiles, LANES), F32)] * 2,
        compiler_params=pltpu.CompilerParams(vmem_limit_bytes=VMEM_BYTES),
        cost_estimate=pl.CostEstimate(
            flops=4 * modes * tok_rows * width, bytes_accessed=8 * tok_rows * width, transcendentals=0
        ),
        name="block_states",
    )(seq_index, query_proj, key_proj, value_proj, out_grad, coefs)
    return states, own


def pair_kernel(seq_ref, coef_ref, own_ref, *refs):
    state_refs, kept_ref, given_ref = refs[:-2], *refs[-2:]
    pairs = len(state_refs) + 1
    modes, tiles = coef_ref.shape[1:3]
    pair = seq_ref[0] // 2
    second = seq_ref[0] % 2 == 1
    for m in range(modes):
        rows = slice(m * tiles, (m + 1) * tiles)
        decay = coef_ref[1, m]
        both = decay * decay
        before = jnp.zeros((tiles, LANES), F32)
        after = jnp.zeros((tiles, LANES), F32)
        for k in range(pairs - 1, 0, -1):
            block = state_refs[k - 1][...].astype(F32)[rows]
            before = both * before + jnp.where(k <= pair, block, 0.0)
            block = state_refs[pairs - k - 1][...].astype(F32)[rows]
            after = both * after + jnp.where(k <= pairs - 1 - pair, block, 0.0)
        before = jnp.where(second, before, decay * before)
        after = jnp.where(second, decay * after, after)
        kept_ref[0, rows] = jnp.where(second, decay * before, before)
        kept_ref[1, rows] = jnp.where(second, after, decay * after)
        own = own_ref[0, rows]
        given_ref[0, rows] = jnp.where(second, before, decay * before + own).astype(LINK)
        own = own_ref[1, rows]
        given_ref[1, rows] = jnp.where(second, decay * after + own, after).astype(LINK)


def pair_states(seq_index, coefs, own, states):
    whole = pl.BlockSpec(memory_space=pltpu.VMEM)
    return pl.pallas_call(
        pair_kernel,
        in_specs=[pl.BlockSpec(memory_space=pltpu.SMEM)] + [whole] * (2 + len(states)),
        out_specs=[whole] * 2,
        out_shape=[
            jax.ShapeDtypeStruct(own.shape, F32),
            jax.ShapeDtypeStruct(own.shape, LINK),
        ],
        compiler_params=pltpu.CompilerParams(vmem_limit_bytes=VMEM_BYTES),
        name="pair_states",
    )(seq_index, coefs, own, *states)


def local_kernel(q_ref, k_ref, v_ref, o_ref, coef_ref, conv_ref, grad_ref):
    tok_rows, width = k_ref.shape
    tiles = width // LANES
    spread_tokens(k_ref, v_ref, conv_ref)
    spread_tokens(o_ref, q_ref, grad_ref)
    walk_tokens(conv_ref, coef_ref, tok_rows, tiles, 0, 1)
    walk_tokens(grad_ref, coef_ref, tok_rows, tiles, tok_rows - 1, -1)


def local_parts(query_proj, key_proj, value_proj, out_grad, coefs):
    tok_rows, width = key_proj.shape
    modes, tiles = coefs.shape[1:3]
    return pl.pallas_call(
        local_kernel,
        out_shape=[jax.ShapeDtypeStruct((tok_rows * tiles, LANES), F32)] * 2,
        compiler_params=pltpu.CompilerParams(vmem_limit_bytes=VMEM_BYTES),
        cost_estimate=pl.CostEstimate(
            flops=8 * modes * tok_rows * width, bytes_accessed=8 * tok_rows * width, transcendentals=0
        ),
        name="local_parts",
    )(query_proj, key_proj, value_proj, out_grad, coefs)


def along_column(state, pairs, k):
    route = [(2 * p + b, 2 * ((p + k) % pairs) + b) for p in range(pairs) for b in range(2)]
    return lax.ppermute(state, "seq", route)


def inside_pair(state, pairs):
    return lax.ppermute(state, "seq", [(i, i ^ 1) for i in range(2 * pairs)])


def add_edge(ref, held, coef_ref, tok_rows, tiles, start, move):
    modes = coef_ref.shape[1]
    decay = [coef_ref[0, m] for m in range(modes)]

    def step(t, held):
        rows = pl.ds(start + move * t, tiles, stride=tok_rows)
        held = tuple(decay[m] * held[m] for m in range(modes))
        ref[rows, :] = ref[rows, :] + tree_sum(list(held))
        return held

    held = tuple(coef_ref[2, m] * held[m] for m in range(modes))
    lax.fori_loop(0, tok_rows, step, held, unroll=8)


def final_kernel(
    q_ref, k_ref, v_ref, o_ref, coef_ref, gain_ref, x_ref, g_ref, kept_ref, given_ref, *refs
):
    hbm_refs, held_refs, sems = refs[:3], refs[3:6], refs[6]
    layer_ref, key_ref, value_ref = held_refs
    tok_rows, width = k_ref.shape
    tiles = width // LANES
    modes = coef_ref.shape[1]

    def edge(side):
        total = kept_ref[side] + given_ref[side].astype(F32)
        return [total[m * tiles : (m + 1) * tiles] for m in range(modes)]

    def departure(i, tile):
        place = (slice(None), pl.ds(tile * LANES, LANES))
        return pltpu.make_async_copy(
            held_refs[i].at[place], hbm_refs[i].at[place], sems.at[i, tile]
        )

    add_edge(x_ref, edge(0), coef_ref, tok_rows, tiles, 0, 1)
    for tile in range(tiles):
        cols = slice(tile * LANES, (tile + 1) * LANES)
        rows = slice(tile * tok_rows, (tile + 1) * tok_rows)
        conv_in = product(k_ref[:, cols], v_ref[:, cols]).astype(F32)
        long_conv = x_ref[rows, :] + gain_ref[:, cols] * conv_in
        layer_ref[:, cols] = (q_ref[:, cols].astype(F32) * long_conv).astype(BF16)
        departure(0, tile).start()
    add_edge(g_ref, edge(1), coef_ref, tok_rows, tiles, tok_rows - 1, -1)
    for tile in range(tiles):
        cols = slice(tile * LANES, (tile + 1) * LANES)
        rows = slice(tile * tok_rows, (tile + 1) * tok_rows)
        mid_grad = product(o_ref[:, cols], q_ref[:, cols]).astype(F32)
        conv_grad = g_ref[rows, :] + gain_ref[:, cols] * mid_grad
        key_ref[:, cols] = (conv_grad * v_ref[:, cols].astype(F32)).astype(BF16)
        departure(1, tile).start()
        value_ref[:, cols] = (conv_grad * k_ref[:, cols].astype(F32)).astype(BF16)
        departure(2, tile).start()
    for i in range(3):
        for tile in range(tiles):
            departure(i, tile).wait()


def final_outputs(signals, coefs, gain, parts, kept, given):
    tok_rows, width = signals[0].shape
    modes, tiles = coefs.shape[1:3]
    args = (*signals, coefs, gain, *parts, kept, given)
    whole = pl.BlockSpec(memory_space=pltpu.VMEM)
    return pl.pallas_call(
        final_kernel,
        in_specs=[whole] * len(args),
        out_specs=[pl.BlockSpec(memory_space=pl.ANY)] * 3,
        out_shape=[jax.ShapeDtypeStruct((tok_rows, width), BF16)] * 3,
        scratch_shapes=[pltpu.VMEM((tok_rows, width), BF16)] * 3
        + [pltpu.SemaphoreType.DMA((3, tiles))],
        compiler_params=pltpu.CompilerParams(vmem_limit_bytes=VMEM_BYTES),
        cost_estimate=pl.CostEstimate(
            flops=8 * modes * tok_rows * width, bytes_accessed=14 * tok_rows * width, transcendentals=0
        ),
        name="final_outputs",
    )(*args)


def lag_kernel(shards, chans, groups, owned, scale, *refs):
    in_refs, out_ref, u_all, g_all, turned_all = refs[:-4], *refs[-4:]
    tok_rows = out_ref.shape[2]
    halves = tok_rows // LANES
    blocks = shards * halves
    depth = chans * groups
    full = blocks * depth
    if len(in_refs) == 1:
        take = chans * groups * owned

        def by_filter(row):
            return row % depth * owned + row // depth

        order = one_hot(take, take, by_filter)
        for which, kept in enumerate((u_all, g_all)):
            rows = slice(which * groups * owned, (which + 1) * groups * owned)
            for s in range(shards):
                piece = in_refs[0][s * chans : (s + 1) * chans, rows, :].reshape(take, tok_rows)
                piece = jnp.dot(order, piece, preferred_element_type=F32).astype(BF16)
                piece = piece.reshape(owned, depth, tok_rows)
                for h in range(halves):
                    first = (s * halves + h) * depth
                    kept[:, first : first + depth, :] = piece[:, :, h * LANES : (h + 1) * LANES]
    else:
        u_all[...] = in_refs[0][...]
        g_all[:, :full, :] = in_refs[1][...]
    g_all[:, full:, :] = jnp.zeros((owned, g_all.shape[1] - full, LANES), BF16)
    mirror = one_hot(LANES, LANES, lambda row: LANES - 1 - row)
    row = lax.broadcasted_iota(jnp.int32, (LANES, LANES), 0)
    col = lax.broadcasted_iota(jnp.int32, (LANES, LANES), 1)
    same_block = row + col >= LANES - 1
    filter_row = lax.broadcasted_iota(jnp.int32, (owned, LANES), 0)
    batch = min(blocks, 16)

    def one_filter(f, _):
        turned = turned_all[f]

        def some_lags(first):
            tables = []
            for d in range(0, batch, 2):
                live = full
                if batch == blocks:
                    live = min(full, -(-(blocks - d) * depth // LANES) * LANES)
                pair = jnp.concatenate(
                    [
                        g_all[f, pl.ds(pl.multiple_of((first + d + e) * depth, depth), live), :]
                        for e in range(2)
                    ],
                    axis=1,
                )
                table = jnp.dot(turned[:, :live], pair, preferred_element_type=F32)
                tables += [table[:, :LANES], table[:, LANES:]]
            last = g_all[f, pl.ds(pl.multiple_of((first + batch) * depth, depth), full), :]
            if batch < blocks:
                tables.append(jnp.dot(turned, last, preferred_element_type=F32))
            else:
                tables.append(jnp.zeros((LANES, LANES), F32))
            for d in range(batch):
                joined = jnp.where(same_block, tables[d], tables[d + 1])
                skewed = pltpu.roll(joined, 1, 1, stride=1, stride_axis=0)
                sums = jnp.sum(skewed, axis=0, keepdims=True) * scale
                lane = d % halves * LANES
                place = ((first + d) // halves, slice(None), slice(lane, lane + LANES))
                out_ref[place] = jnp.where(filter_row == f, sums, out_ref[place])

        if batch == blocks:
            some_lags(0)
        else:
            lax.fori_loop(0, blocks // batch, lambda i, c: (some_lags(i * batch), c)[1], 0)
        return 0

    for f in range(owned):
        turned_all[f] = lax.dot_general(
            mirror, u_all[f], (((1,), (1,)), ((), ())), preferred_element_type=F32
        ).astype(BF16)
    lax.fori_loop(0, owned, one_filter, 0, unroll=min(owned, 2))


def filter_lags(received, shards, chans, owned, scale):
    tok_rows = received.shape[2]
    groups = received.shape[1] // (2 * owned)
    halves = tok_rows // LANES
    depth = chans * groups
    full = shards * halves * depth
    args = (received,)
    if owned % SUBLANES:
        split = received.reshape(shards, chans, 2, groups, owned, halves, LANES)
        split = split.transpose(2, 4, 0, 5, 1, 3, 6).reshape(2, owned, full, LANES)
        args = (split[0], split[1])
    return pl.pallas_call(
        functools.partial(lag_kernel, shards, chans, groups, owned, scale),
        out_shape=jax.ShapeDtypeStruct((shards, owned, tok_rows), F32),
        scratch_shapes=[
            pltpu.VMEM((owned, full, LANES), BF16),
            pltpu.VMEM((owned, 2 * full + depth, LANES), BF16),
            pltpu.VMEM((owned, LANES, full), BF16),
        ],
        compiler_params=pltpu.CompilerParams(vmem_limit_bytes=VMEM_BYTES),
        name="filter_lags",
    )(*args)


def per_device(query_proj, key_proj, value_proj, out_grad, residues, decay_rate, skip_gain):
    tok_rows, width = key_proj.shape
    shards = lax.axis_size("seq")
    chans = lax.axis_size("chan")
    length = shards * tok_rows
    owned = FILTERS // (shards * chans)
    modes = residues.shape[1]
    signals = (query_proj, key_proj, value_proj, out_grad)

    send = pack_signals(shards, chans, owned, *signals)
    send, *signals, residues, decay_rate = lax.optimization_barrier(
        (send, *signals, residues, decay_rate)
    )
    received = lax.all_to_all(send, ("seq", "chan"), split_axis=0, concat_axis=0, tiled=True)

    coefs = jnp.stack(
        [
            jnp.exp(-decay_rate),
            jnp.exp(-(decay_rate * float(tok_rows))),
            residues * jnp.sqrt(decay_rate),
        ]
    )
    coefs = coefs.transpose(0, 2, 1).reshape(3, modes, 1, FILTERS // LANES, LANES)
    coefs = jnp.broadcast_to(coefs, (3, modes, width // FILTERS, FILTERS // LANES, LANES))
    coefs = coefs.reshape(3, modes, width // LANES, LANES)
    seq_index = lax.axis_index("seq").reshape(1)
    pairs = shards // 2
    states, own = block_states(seq_index, pairs, *signals, coefs)
    *states, coefs = lax.optimization_barrier((*states, coefs))
    states = [along_column(state, pairs, 1 + i) for i, state in enumerate(states)]
    parts = local_parts(*signals, coefs)
    kept, given = pair_states(seq_index, coefs, own, states)
    received, kept, given, *parts = lax.optimization_barrier((received, kept, given, *parts))
    given = inside_pair(given, pairs)

    scale = 1.0 / math.sqrt(length * (CHANNELS // FILTERS))
    lags = filter_lags(received, shards, chans, owned, scale)
    lags = lax.all_to_all(lags, "seq", split_axis=0, concat_axis=0, tiled=True)
    filter_grad = lags.reshape(shards * owned, tok_rows).T
    layer_out, key_grad, value_grad = final_outputs(
        signals, coefs, skip_gain[None, :], parts, kept, given
    )
    return (layer_out, key_grad, value_grad, filter_grad)


def solution(mesh):
    split = P("seq", "chan")
    return jax.shard_map(
        per_device,
        mesh=mesh,
        in_specs=(split, split, split, split, P(), P(), P("chan")),
        out_specs=(split, split, split, split),
        check_vma=False,
    )
```

```python
import functools
import math

import jax
import jax.numpy as jnp
from jax import lax
from jax.experimental import pallas as pl
from jax.experimental.pallas import tpu as pltpu
from jax.sharding import PartitionSpec as P

CHANNELS = 4096
FILTERS = 256
LANES = 128
SUBLANES = 8
GAP = 8
VMEM_BYTES = 16 * 1024 * 1024
PACK_VMEM_BYTES = 62 * 1024 * 1024
F32 = jnp.float32
BF16 = jnp.bfloat16
LINK = jnp.bfloat16


def product(first, second):
    return (first.astype(F32) * second.astype(F32)).astype(BF16)


def one_hot(rows, cols, column_of):
    row = lax.broadcasted_iota(jnp.int32, (rows, cols), 0)
    col = lax.broadcasted_iota(jnp.int32, (rows, cols), 1)
    return (col == column_of(row)).astype(F32).astype(BF16)


def pack_kernel(shards, chans, owned, *refs):
    hbm_refs, send_ref, held, packed, in_sems, out_sems = refs[:4], *refs[4:]
    tok_rows, width = held.shape[1:]
    groups = width // FILTERS
    per_chan = FILTERS // chans
    units = [(which, first) for which in range(2) for first in range(0, groups, 2)]

    def arrival(i, first):
        place = (slice(None), pl.ds(first * FILTERS, 2 * FILTERS))
        return pltpu.make_async_copy(
            hbm_refs[i].at[place], held.at[(i, *place)], in_sems.at[i, first // 2]
        )

    def departure(which, first):
        if owned % SUBLANES:
            place = (which, pl.ds(first, 2))
        else:
            place = (slice(None), pl.ds((which * groups + first) * owned, 2 * owned))
        return pltpu.make_async_copy(
            packed.at[place], send_ref.at[place], out_sems.at[which, first // 2]
        )

    for which, first in units:
        for i in (2 * which, 2 * which + 1):
            arrival(i, first).start()

    def owned_filter(row):
        seq = row // (chans * owned)
        chan = row // owned % chans
        return chan * per_chan + seq * owned + row % owned

    order = one_hot(FILTERS, FILTERS, owned_filter)
    for which, first in units:
        for i in (2 * which, 2 * which + 1):
            arrival(i, first).wait()
        pieces = []
        for group in (first, first + 1):
            cols = slice(group * FILTERS, (group + 1) * FILTERS)
            piece = lax.dot_general(
                order,
                product(held[2 * which, :, cols], held[2 * which + 1, :, cols]),
                (((1,), (1,)), ((), ())),
                preferred_element_type=F32,
            )
            if owned % SUBLANES:
                packed[which, group] = piece.astype(BF16)
            else:
                pieces.append(piece.reshape(shards * chans, owned, tok_rows))
        if pieces:
            row = (which * groups + first) * owned
            packed[:, row : row + 2 * owned, :] = jnp.concatenate(pieces, axis=1).astype(BF16)
        departure(which, first).start()
    for which, first in units:
        departure(which, first).wait()


def pack_signals(shards, chans, owned, query_proj, key_proj, value_proj, out_grad):
    tok_rows, width = key_proj.shape
    groups = width // FILTERS
    dests = shards * chans
    if owned % SUBLANES:
        shape = (2, groups, FILTERS, tok_rows)
    else:
        shape = (dests, 2 * groups * owned, tok_rows)
    send = pl.pallas_call(
        functools.partial(pack_kernel, shards, chans, owned),
        in_specs=[pl.BlockSpec(memory_space=pl.ANY)] * 4,
        out_specs=pl.BlockSpec(memory_space=pl.ANY),
        out_shape=jax.ShapeDtypeStruct(shape, BF16),
        scratch_shapes=[
            pltpu.VMEM((4, tok_rows, width), BF16),
            pltpu.VMEM(shape, BF16),
            pltpu.SemaphoreType.DMA((4, groups // 2)),
            pltpu.SemaphoreType.DMA((2, groups // 2)),
        ],
        compiler_params=pltpu.CompilerParams(vmem_limit_bytes=PACK_VMEM_BYTES),
        name="pack_signals",
    )(key_proj, value_proj, out_grad, query_proj)
    if owned % SUBLANES:
        send = send.reshape(2, groups, dests, owned, tok_rows)
        send = send.transpose(2, 0, 1, 3, 4).reshape(dests, 2 * groups * owned, tok_rows)
    return send


def tile_rows(tok_rows, tile):
    first = tile * (tok_rows + GAP)
    return slice(first, first + tok_rows)


def token_shape(tok_rows, tiles):
    return (tiles * (tok_rows + GAP), LANES)


def token_place(t, tok_rows, tiles):
    return (pl.ds(t, tiles, stride=tok_rows + GAP), slice(None))


def spread_tokens(a_ref, b_ref, x_ref):
    tok_rows, width = a_ref.shape
    for tile in range(width // LANES):
        cols = slice(tile * LANES, (tile + 1) * LANES)
        x_ref[tile_rows(tok_rows, tile), :] = product(a_ref[:, cols], b_ref[:, cols]).astype(F32)


def walk_tokens(ref, coef_ref, tok_rows, tiles, start, move):
    modes = coef_ref.shape[1]
    decay = [coef_ref[0, m] for m in range(modes)]
    weight = [coef_ref[2, m] for m in range(modes)]

    def step(t, held):
        place = token_place(start + move * t, tok_rows, tiles)
        x = ref[place]
        held = tuple(decay[m] * held[m] + x for m in range(modes))
        ref[place] = tree_sum([weight[m] * held[m] for m in range(modes)])
        return held

    zero = tuple(jnp.zeros((tiles, LANES), F32) for _ in range(modes))
    return lax.fori_loop(0, tok_rows, step, zero, unroll=8)


def tree_sum(terms):
    while len(terms) > 1:
        terms = [sum(terms[i : i + 2][1:], terms[i]) for i in range(0, len(terms), 2)]
    return terms[0]


def state_kernel(seq_ref, q_ref, k_ref, v_ref, o_ref, coef_ref, *refs):
    state_refs, own_ref, x_ref, g_ref = refs[:-3], *refs[-3:]
    tok_rows, width = k_ref.shape
    tiles = width // LANES
    modes = coef_ref.shape[1]
    pairs = len(state_refs) + 1
    spread_tokens(k_ref, v_ref, x_ref)
    spread_tokens(o_ref, q_ref, g_ref)
    decay = [coef_ref[0, m] for m in range(modes)]

    def step(t, carry):
        x = x_ref[token_place(t, tok_rows, tiles)]
        g = g_ref[token_place(tok_rows - 1 - t, tok_rows, tiles)]
        ahead = tuple(decay[m] * carry[0][m] + x for m in range(modes))
        behind = tuple(decay[m] * carry[1][m] + g for m in range(modes))
        return (ahead, behind)

    zero = tuple(jnp.zeros((tiles, LANES), F32) for _ in range(modes))
    ahead, behind = lax.fori_loop(0, tok_rows, step, (zero, zero), unroll=8)
    ahead = jnp.concatenate(ahead, axis=0)
    behind = jnp.concatenate(behind, axis=0)
    own_ref[0] = ahead
    own_ref[1] = behind
    for k in range(1, pairs):
        stays = seq_ref[0] // 2 + k < pairs

        @pl.when(stays)
        def _():
            state_refs[k - 1][...] = ahead.astype(LINK)

        @pl.when(jnp.logical_not(stays))
        def _():
            state_refs[k - 1][...] = behind.astype(LINK)


def block_states(seq_index, pairs, query_proj, key_proj, value_proj, out_grad, coefs):
    tok_rows, width = key_proj.shape
    modes, tiles = coefs.shape[1:3]
    whole = pl.BlockSpec(memory_space=pltpu.VMEM)
    *states, own = pl.pallas_call(
        state_kernel,
        in_specs=[pl.BlockSpec(memory_space=pltpu.SMEM)] + [whole] * 5,
        out_specs=[whole] * pairs,
        out_shape=[jax.ShapeDtypeStruct((modes * tiles, LANES), LINK)] * (pairs - 1)
        + [jax.ShapeDtypeStruct((2, modes * tiles, LANES), F32)],
        scratch_shapes=[pltpu.VMEM(token_shape(tok_rows, tiles), F32)] * 2,
        compiler_params=pltpu.CompilerParams(vmem_limit_bytes=VMEM_BYTES),
        cost_estimate=pl.CostEstimate(
            flops=4 * modes * tok_rows * width, bytes_accessed=8 * tok_rows * width, transcendentals=0
        ),
        name="block_states",
    )(seq_index, query_proj, key_proj, value_proj, out_grad, coefs)
    return states, own


def pair_kernel(seq_ref, coef_ref, own_ref, *refs):
    state_refs, kept_ref, given_ref = refs[:-2], *refs[-2:]
    pairs = len(state_refs) + 1
    modes, tiles = coef_ref.shape[1:3]
    pair = seq_ref[0] // 2
    second = seq_ref[0] % 2 == 1
    for m in range(modes):
        rows = slice(m * tiles, (m + 1) * tiles)
        decay = coef_ref[1, m]
        both = decay * decay
        before = jnp.zeros((tiles, LANES), F32)
        after = jnp.zeros((tiles, LANES), F32)
        for k in range(pairs - 1, 0, -1):
            block = state_refs[k - 1][...].astype(F32)[rows]
            before = both * before + jnp.where(k <= pair, block, 0.0)
            block = state_refs[pairs - k - 1][...].astype(F32)[rows]
            after = both * after + jnp.where(k <= pairs - 1 - pair, block, 0.0)
        before = jnp.where(second, before, decay * before)
        after = jnp.where(second, decay * after, after)
        kept_ref[0, rows] = jnp.where(second, decay * before, before)
        kept_ref[1, rows] = jnp.where(second, after, decay * after)
        own = own_ref[0, rows]
        given_ref[0, rows] = jnp.where(second, before, decay * before + own).astype(LINK)
        own = own_ref[1, rows]
        given_ref[1, rows] = jnp.where(second, decay * after + own, after).astype(LINK)


def pair_states(seq_index, coefs, own, states):
    whole = pl.BlockSpec(memory_space=pltpu.VMEM)
    return pl.pallas_call(
        pair_kernel,
        in_specs=[pl.BlockSpec(memory_space=pltpu.SMEM)] + [whole] * (2 + len(states)),
        out_specs=[whole] * 2,
        out_shape=[
            jax.ShapeDtypeStruct(own.shape, F32),
            jax.ShapeDtypeStruct(own.shape, LINK),
        ],
        compiler_params=pltpu.CompilerParams(vmem_limit_bytes=VMEM_BYTES),
        name="pair_states",
    )(seq_index, coefs, own, *states)


def local_kernel(q_ref, k_ref, v_ref, o_ref, coef_ref, conv_ref, grad_ref):
    tok_rows, width = k_ref.shape
    tiles = width // LANES
    spread_tokens(k_ref, v_ref, conv_ref)
    spread_tokens(o_ref, q_ref, grad_ref)
    walk_tokens(conv_ref, coef_ref, tok_rows, tiles, 0, 1)
    walk_tokens(grad_ref, coef_ref, tok_rows, tiles, tok_rows - 1, -1)


def local_parts(query_proj, key_proj, value_proj, out_grad, coefs):
    tok_rows, width = key_proj.shape
    modes, tiles = coefs.shape[1:3]
    return pl.pallas_call(
        local_kernel,
        out_shape=[jax.ShapeDtypeStruct(token_shape(tok_rows, tiles), F32)] * 2,
        compiler_params=pltpu.CompilerParams(vmem_limit_bytes=VMEM_BYTES),
        cost_estimate=pl.CostEstimate(
            flops=8 * modes * tok_rows * width, bytes_accessed=8 * tok_rows * width, transcendentals=0
        ),
        name="local_parts",
    )(query_proj, key_proj, value_proj, out_grad, coefs)


def along_column(state, pairs, k):
    route = [(2 * p + b, 2 * ((p + k) % pairs) + b) for p in range(pairs) for b in range(2)]
    return lax.ppermute(state, "seq", route)


def inside_pair(state, pairs):
    return lax.ppermute(state, "seq", [(i, i ^ 1) for i in range(2 * pairs)])


def fill_edge(ref, held, coef_ref, tok_rows, tiles, start, move):
    modes = coef_ref.shape[1]
    decay = [coef_ref[0, m] for m in range(modes)]

    def step(t, held):
        held = tuple(decay[m] * held[m] for m in range(modes))
        ref[token_place(start + move * t, tok_rows, tiles)] = tree_sum(list(held))
        return held

    held = tuple(coef_ref[2, m] * held[m] for m in range(modes))
    lax.fori_loop(0, tok_rows, step, held, unroll=8)


def final_kernel(
    q_ref, k_ref, v_ref, o_ref, coef_ref, gain_ref, kept_ref, given_ref, *refs
):
    part_refs, hbm_refs, refs = refs[:2], refs[2:5], refs[5:]
    x_ref, g_ref, edge_ref, layer_ref, key_ref, value_ref, in_sems, out_sems = refs
    tok_rows, width = k_ref.shape
    tiles = width // LANES
    modes = coef_ref.shape[1]

    def arrival(i, tile):
        rows = pl.ds(tile * (tok_rows + GAP), tok_rows)
        return pltpu.make_async_copy(
            part_refs[i].at[rows, :], (x_ref, g_ref)[i].at[rows, :], in_sems.at[i, tile]
        )

    def departure(i, tile):
        place = (slice(None), pl.ds(tile * LANES, LANES))
        return pltpu.make_async_copy(
            (layer_ref, key_ref, value_ref)[i].at[place], hbm_refs[i].at[place], out_sems.at[i, tile]
        )

    def edge(side):
        total = kept_ref[side] + given_ref[side].astype(F32)
        return [total[m * tiles : (m + 1) * tiles] for m in range(modes)]

    for i in range(2):
        for tile in range(tiles):
            arrival(i, tile).start()
    fill_edge(edge_ref, edge(0), coef_ref, tok_rows, tiles, 0, 1)
    for tile in range(tiles):
        arrival(0, tile).wait()
    for tile in range(tiles):
        cols = slice(tile * LANES, (tile + 1) * LANES)
        rows = tile_rows(tok_rows, tile)
        conv_in = product(k_ref[:, cols], v_ref[:, cols]).astype(F32)
        long_conv = x_ref[rows, :] + edge_ref[rows, :] + gain_ref[:, cols] * conv_in
        layer_ref[:, cols] = (q_ref[:, cols].astype(F32) * long_conv).astype(BF16)
        departure(0, tile).start()
    fill_edge(edge_ref, edge(1), coef_ref, tok_rows, tiles, tok_rows - 1, -1)
    for tile in range(tiles):
        arrival(1, tile).wait()
    for tile in range(tiles):
        cols = slice(tile * LANES, (tile + 1) * LANES)
        rows = tile_rows(tok_rows, tile)
        mid_grad = product(o_ref[:, cols], q_ref[:, cols]).astype(F32)
        conv_grad = g_ref[rows, :] + edge_ref[rows, :] + gain_ref[:, cols] * mid_grad
        key_ref[:, cols] = (conv_grad * v_ref[:, cols].astype(F32)).astype(BF16)
        departure(1, tile).start()
        value_ref[:, cols] = (conv_grad * k_ref[:, cols].astype(F32)).astype(BF16)
        departure(2, tile).start()
    for i in range(3):
        for tile in range(tiles):
            departure(i, tile).wait()


def final_outputs(signals, coefs, gain, kept, given, parts):
    tok_rows, width = signals[0].shape
    modes, tiles = coefs.shape[1:3]
    args = (*signals, coefs, gain, kept, given)
    whole = pl.BlockSpec(memory_space=pltpu.VMEM)
    away = pl.BlockSpec(memory_space=pl.ANY)
    return pl.pallas_call(
        final_kernel,
        in_specs=[whole] * len(args) + [away] * len(parts),
        out_specs=[away] * 3,
        out_shape=[jax.ShapeDtypeStruct((tok_rows, width), BF16)] * 3,
        scratch_shapes=[pltpu.VMEM(token_shape(tok_rows, tiles), F32)] * 3
        + [pltpu.VMEM((tok_rows, width), BF16)] * 3
        + [pltpu.SemaphoreType.DMA((2, tiles)), pltpu.SemaphoreType.DMA((3, tiles))],
        compiler_params=pltpu.CompilerParams(vmem_limit_bytes=VMEM_BYTES),
        cost_estimate=pl.CostEstimate(
            flops=8 * modes * tok_rows * width, bytes_accessed=14 * tok_rows * width, transcendentals=0
        ),
        name="final_outputs",
    )(*args, *parts)


def lag_kernel(shards, chans, groups, owned, scale, *refs):
    in_refs, out_ref, u_all, g_all, turned_all = refs[:-4], *refs[-4:]
    tok_rows = out_ref.shape[2]
    halves = tok_rows // LANES
    blocks = shards * halves
    depth = chans * groups
    full = blocks * depth
    if len(in_refs) == 1:
        take = chans * groups * owned

        def by_filter(row):
            return row % depth * owned + row // depth

        order = one_hot(take, take, by_filter)
        for which, kept in enumerate((u_all, g_all)):
            rows = slice(which * groups * owned, (which + 1) * groups * owned)
            for s in range(shards):
                piece = in_refs[0][s * chans : (s + 1) * chans, rows, :].reshape(take, tok_rows)
                piece = jnp.dot(order, piece, preferred_element_type=F32).astype(BF16)
                piece = piece.reshape(owned, depth, tok_rows)
                for h in range(halves):
                    first = (s * halves + h) * depth
                    kept[:, first : first + depth, :] = piece[:, :, h * LANES : (h + 1) * LANES]
    else:
        u_all[...] = in_refs[0][...]
        g_all[:, :full, :] = in_refs[1][...]
    g_all[:, full:, :] = jnp.zeros((owned, g_all.shape[1] - full, LANES), BF16)
    mirror = one_hot(LANES, LANES, lambda row: LANES - 1 - row)
    row = lax.broadcasted_iota(jnp.int32, (LANES, LANES), 0)
    col = lax.broadcasted_iota(jnp.int32, (LANES, LANES), 1)
    same_block = row + col >= LANES - 1
    filter_row = lax.broadcasted_iota(jnp.int32, (owned, LANES), 0)
    batch = min(blocks, 16)

    def one_filter(f, _):
        turned = turned_all[f]

        def some_lags(first):
            tables = []
            for d in range(0, batch, 2):
                live = full
                if batch == blocks:
                    live = min(full, -(-(blocks - d) * depth // LANES) * LANES)
                pair = jnp.concatenate(
                    [
                        g_all[f, pl.ds(pl.multiple_of((first + d + e) * depth, depth), live), :]
                        for e in range(2)
                    ],
                    axis=1,
                )
                table = jnp.dot(turned[:, :live], pair, preferred_element_type=F32)
                tables += [table[:, :LANES], table[:, LANES:]]
            last = g_all[f, pl.ds(pl.multiple_of((first + batch) * depth, depth), full), :]
            if batch < blocks:
                tables.append(jnp.dot(turned, last, preferred_element_type=F32))
            else:
                tables.append(jnp.zeros((LANES, LANES), F32))
            for d in range(batch):
                joined = jnp.where(same_block, tables[d], tables[d + 1])
                skewed = pltpu.roll(joined, 1, 1, stride=1, stride_axis=0)
                sums = jnp.sum(skewed, axis=0, keepdims=True) * scale
                lane = d % halves * LANES
                place = ((first + d) // halves, slice(None), slice(lane, lane + LANES))
                out_ref[place] = jnp.where(filter_row == f, sums, out_ref[place])

        if batch == blocks:
            some_lags(0)
        else:
            lax.fori_loop(0, blocks // batch, lambda i, c: (some_lags(i * batch), c)[1], 0)
        return 0

    for f in range(owned):
        turned_all[f] = lax.dot_general(
            mirror, u_all[f], (((1,), (1,)), ((), ())), preferred_element_type=F32
        ).astype(BF16)
    lax.fori_loop(0, owned, one_filter, 0, unroll=min(owned, 2))


def filter_lags(received, shards, chans, owned, scale):
    tok_rows = received.shape[2]
    groups = received.shape[1] // (2 * owned)
    halves = tok_rows // LANES
    depth = chans * groups
    full = shards * halves * depth
    args = (received,)
    if owned % SUBLANES:
        split = received.reshape(shards, chans, 2, groups, owned, halves, LANES)
        split = split.transpose(2, 4, 0, 5, 1, 3, 6).reshape(2, owned, full, LANES)
        args = (split[0], split[1])
    return pl.pallas_call(
        functools.partial(lag_kernel, shards, chans, groups, owned, scale),
        out_shape=jax.ShapeDtypeStruct((shards, owned, tok_rows), F32),
        scratch_shapes=[
            pltpu.VMEM((owned, full, LANES), BF16),
            pltpu.VMEM((owned, 2 * full + depth, LANES), BF16),
            pltpu.VMEM((owned, LANES, full), BF16),
        ],
        compiler_params=pltpu.CompilerParams(vmem_limit_bytes=VMEM_BYTES),
        cost_estimate=pl.CostEstimate(
            flops=4 * owned * LANES * full * full, bytes_accessed=8 * owned * full * LANES, transcendentals=0
        ),
        name="filter_lags",
    )(*args)


def per_device(query_proj, key_proj, value_proj, out_grad, residues, decay_rate, skip_gain):
    tok_rows, width = key_proj.shape
    shards = lax.axis_size("seq")
    chans = lax.axis_size("chan")
    length = shards * tok_rows
    owned = FILTERS // (shards * chans)
    modes = residues.shape[1]
    signals = (query_proj, key_proj, value_proj, out_grad)

    send = pack_signals(shards, chans, owned, *signals)
    send, *signals, residues, decay_rate = lax.optimization_barrier(
        (send, *signals, residues, decay_rate)
    )
    received = lax.all_to_all(send, ("seq", "chan"), split_axis=0, concat_axis=0, tiled=True)

    coefs = jnp.stack(
        [
            jnp.exp(-decay_rate),
            jnp.exp(-(decay_rate * float(tok_rows))),
            residues * jnp.sqrt(decay_rate),
        ]
    )
    coefs = coefs.transpose(0, 2, 1).reshape(3, modes, 1, FILTERS // LANES, LANES)
    coefs = jnp.broadcast_to(coefs, (3, modes, width // FILTERS, FILTERS // LANES, LANES))
    coefs = coefs.reshape(3, modes, width // LANES, LANES)
    seq_index = lax.axis_index("seq").reshape(1)
    pairs = shards // 2
    states, own = block_states(seq_index, pairs, *signals, coefs)
    *states, coefs = lax.optimization_barrier((*states, coefs))
    states = [along_column(state, pairs, 1 + i) for i, state in enumerate(states)]
    parts = local_parts(*signals, coefs)
    kept, given = pair_states(seq_index, coefs, own, states)
    received, kept, given, *parts = lax.optimization_barrier((received, kept, given, *parts))
    given = inside_pair(given, pairs)

    scale = 1.0 / math.sqrt(length * (CHANNELS // FILTERS))
    lags = filter_lags(received, shards, chans, owned, scale)
    lags, given = lax.optimization_barrier((lags, given))
    lags = lax.all_to_all(lags, "seq", split_axis=0, concat_axis=0, tiled=True)
    filter_grad = lags.reshape(shards * owned, tok_rows).T
    layer_out, key_grad, value_grad = final_outputs(
        signals, coefs, skip_gain[None, :], kept, given, parts
    )
    return (layer_out, key_grad, value_grad, filter_grad)


def solution(mesh):
    split = P("seq", "chan")
    return jax.shard_map(
        per_device,
        mesh=mesh,
        in_specs=(split, split, split, split, P(), P(), P("chan")),
        out_specs=(split, split, split, split),
        check_vma=False,
    )
```

```python
import functools
import math

import jax
import jax.numpy as jnp
from jax import lax
from jax.experimental import pallas as pl
from jax.experimental.pallas import tpu as pltpu
from jax.sharding import PartitionSpec as P

CHANNELS = 4096
FILTERS = 256
LANES = 128
SUBLANES = 8
GAP = 8
VMEM_BYTES = 16 * 1024 * 1024
PACK_VMEM_BYTES = 62 * 1024 * 1024
F32 = jnp.float32
BF16 = jnp.bfloat16
LINK = jnp.bfloat16


def product(first, second):
    return (first.astype(F32) * second.astype(F32)).astype(BF16)


def one_hot(rows, cols, column_of):
    row = lax.broadcasted_iota(jnp.int32, (rows, cols), 0)
    col = lax.broadcasted_iota(jnp.int32, (rows, cols), 1)
    return (col == column_of(row)).astype(F32).astype(BF16)


def pack_kernel(shards, chans, owned, *refs):
    hbm_refs, send_ref, held, packed, in_sems, out_sems = refs[:4], *refs[4:]
    tok_rows, width = held.shape[1:]
    groups = width // FILTERS
    per_chan = FILTERS // chans
    units = [(which, first) for which in range(2) for first in range(0, groups, 2)]

    def arrival(i, first):
        place = (slice(None), pl.ds(first * FILTERS, 2 * FILTERS))
        return pltpu.make_async_copy(
            hbm_refs[i].at[place], held.at[(i, *place)], in_sems.at[i, first // 2]
        )

    def departure(which, first):
        if owned % SUBLANES:
            place = (which, pl.ds(first, 2))
        else:
            place = (slice(None), pl.ds((which * groups + first) * owned, 2 * owned))
        return pltpu.make_async_copy(
            packed.at[place], send_ref.at[place], out_sems.at[which, first // 2]
        )

    for which, first in units:
        for i in (2 * which, 2 * which + 1):
            arrival(i, first).start()

    def owned_filter(row):
        seq = row // (chans * owned)
        chan = row // owned % chans
        return chan * per_chan + seq * owned + row % owned

    order = one_hot(FILTERS, FILTERS, owned_filter)
    for which, first in units:
        for i in (2 * which, 2 * which + 1):
            arrival(i, first).wait()
        pieces = []
        for group in (first, first + 1):
            cols = slice(group * FILTERS, (group + 1) * FILTERS)
            piece = lax.dot_general(
                order,
                product(held[2 * which, :, cols], held[2 * which + 1, :, cols]),
                (((1,), (1,)), ((), ())),
                preferred_element_type=F32,
            )
            if owned % SUBLANES:
                packed[which, group] = piece.astype(BF16)
            else:
                pieces.append(piece.reshape(shards * chans, owned, tok_rows))
        if pieces:
            row = (which * groups + first) * owned
            packed[:, row : row + 2 * owned, :] = jnp.concatenate(pieces, axis=1).astype(BF16)
        departure(which, first).start()
    for which, first in units:
        departure(which, first).wait()


def pack_signals(shards, chans, owned, query_proj, key_proj, value_proj, out_grad):
    tok_rows, width = key_proj.shape
    groups = width // FILTERS
    dests = shards * chans
    if owned % SUBLANES:
        shape = (2, groups, FILTERS, tok_rows)
    else:
        shape = (dests, 2 * groups * owned, tok_rows)
    send = pl.pallas_call(
        functools.partial(pack_kernel, shards, chans, owned),
        in_specs=[pl.BlockSpec(memory_space=pl.ANY)] * 4,
        out_specs=pl.BlockSpec(memory_space=pl.ANY),
        out_shape=jax.ShapeDtypeStruct(shape, BF16),
        scratch_shapes=[
            pltpu.VMEM((4, tok_rows, width), BF16),
            pltpu.VMEM(shape, BF16),
            pltpu.SemaphoreType.DMA((4, groups // 2)),
            pltpu.SemaphoreType.DMA((2, groups // 2)),
        ],
        compiler_params=pltpu.CompilerParams(vmem_limit_bytes=PACK_VMEM_BYTES),
        name="pack_signals",
    )(key_proj, value_proj, out_grad, query_proj)
    if owned % SUBLANES:
        send = send.reshape(2, groups, dests, owned, tok_rows)
        send = send.transpose(2, 0, 1, 3, 4).reshape(dests, 2 * groups * owned, tok_rows)
    return send


def tile_rows(tok_rows, tile):
    first = tile * (tok_rows + GAP)
    return slice(first, first + tok_rows)


def token_shape(tok_rows, tiles):
    return (tiles * (tok_rows + GAP), LANES)


def token_place(t, tok_rows, tiles):
    return (pl.ds(t, tiles, stride=tok_rows + GAP), slice(None))


def spread_tokens(a_ref, b_ref, x_ref):
    tok_rows, width = a_ref.shape
    for tile in range(width // LANES):
        cols = slice(tile * LANES, (tile + 1) * LANES)
        x_ref[tile_rows(tok_rows, tile), :] = product(a_ref[:, cols], b_ref[:, cols]).astype(F32)


def walk_tokens(ref, coef_ref, tok_rows, tiles, start, move):
    modes = coef_ref.shape[1]
    decay = [coef_ref[0, m] for m in range(modes)]
    weight = [coef_ref[2, m] for m in range(modes)]

    def step(t, held):
        place = token_place(start + move * t, tok_rows, tiles)
        x = ref[place]
        held = tuple(decay[m] * held[m] + x for m in range(modes))
        ref[place] = tree_sum([weight[m] * held[m] for m in range(modes)])
        return held

    zero = tuple(jnp.zeros((tiles, LANES), F32) for _ in range(modes))
    return lax.fori_loop(0, tok_rows, step, zero, unroll=8)


def tree_sum(terms):
    while len(terms) > 1:
        terms = [sum(terms[i : i + 2][1:], terms[i]) for i in range(0, len(terms), 2)]
    return terms[0]


def state_kernel(seq_ref, q_ref, k_ref, v_ref, o_ref, coef_ref, *refs):
    state_refs, own_ref, x_ref, g_ref = refs[:-3], *refs[-3:]
    tok_rows, width = k_ref.shape
    tiles = width // LANES
    modes = coef_ref.shape[1]
    pairs = len(state_refs) + 1
    spread_tokens(k_ref, v_ref, x_ref)
    spread_tokens(o_ref, q_ref, g_ref)
    decay = [coef_ref[0, m] for m in range(modes)]

    def step(t, carry):
        x = x_ref[token_place(t, tok_rows, tiles)]
        g = g_ref[token_place(tok_rows - 1 - t, tok_rows, tiles)]
        ahead = tuple(decay[m] * carry[0][m] + x for m in range(modes))
        behind = tuple(decay[m] * carry[1][m] + g for m in range(modes))
        return (ahead, behind)

    zero = tuple(jnp.zeros((tiles, LANES), F32) for _ in range(modes))
    ahead, behind = lax.fori_loop(0, tok_rows, step, (zero, zero), unroll=8)
    ahead = jnp.concatenate(ahead, axis=0)
    behind = jnp.concatenate(behind, axis=0)
    own_ref[0] = ahead
    own_ref[1] = behind
    for k in range(1, pairs):
        stays = seq_ref[0] // 2 + k < pairs

        @pl.when(stays)
        def _():
            state_refs[k - 1][...] = ahead.astype(LINK)

        @pl.when(jnp.logical_not(stays))
        def _():
            state_refs[k - 1][...] = behind.astype(LINK)


def block_states(seq_index, pairs, query_proj, key_proj, value_proj, out_grad, coefs):
    tok_rows, width = key_proj.shape
    modes, tiles = coefs.shape[1:3]
    whole = pl.BlockSpec(memory_space=pltpu.VMEM)
    *states, own = pl.pallas_call(
        state_kernel,
        in_specs=[pl.BlockSpec(memory_space=pltpu.SMEM)] + [whole] * 5,
        out_specs=[whole] * pairs,
        out_shape=[jax.ShapeDtypeStruct((modes * tiles, LANES), LINK)] * (pairs - 1)
        + [jax.ShapeDtypeStruct((2, modes * tiles, LANES), F32)],
        scratch_shapes=[pltpu.VMEM(token_shape(tok_rows, tiles), F32)] * 2,
        compiler_params=pltpu.CompilerParams(vmem_limit_bytes=VMEM_BYTES),
        cost_estimate=pl.CostEstimate(
            flops=4 * modes * tok_rows * width, bytes_accessed=8 * tok_rows * width, transcendentals=0
        ),
        name="block_states",
    )(seq_index, query_proj, key_proj, value_proj, out_grad, coefs)
    return states, own


def pair_kernel(seq_ref, coef_ref, own_ref, *refs):
    state_refs, kept_ref, given_ref = refs[:-2], *refs[-2:]
    pairs = len(state_refs) + 1
    modes, tiles = coef_ref.shape[1:3]
    pair = seq_ref[0] // 2
    second = seq_ref[0] % 2 == 1
    for m in range(modes):
        rows = slice(m * tiles, (m + 1) * tiles)
        decay = coef_ref[1, m]
        both = decay * decay
        before = jnp.zeros((tiles, LANES), F32)
        after = jnp.zeros((tiles, LANES), F32)
        for k in range(pairs - 1, 0, -1):
            block = state_refs[k - 1][...].astype(F32)[rows]
            before = both * before + jnp.where(k <= pair, block, 0.0)
            block = state_refs[pairs - k - 1][...].astype(F32)[rows]
            after = both * after + jnp.where(k <= pairs - 1 - pair, block, 0.0)
        before = jnp.where(second, before, decay * before)
        after = jnp.where(second, decay * after, after)
        kept_ref[0, rows] = jnp.where(second, decay * before, before)
        kept_ref[1, rows] = jnp.where(second, after, decay * after)
        own = own_ref[0, rows]
        given_ref[0, rows] = jnp.where(second, before, decay * before + own).astype(LINK)
        own = own_ref[1, rows]
        given_ref[1, rows] = jnp.where(second, decay * after + own, after).astype(LINK)


def pair_states(seq_index, coefs, own, states):
    whole = pl.BlockSpec(memory_space=pltpu.VMEM)
    return pl.pallas_call(
        pair_kernel,
        in_specs=[pl.BlockSpec(memory_space=pltpu.SMEM)] + [whole] * (2 + len(states)),
        out_specs=[whole] * 2,
        out_shape=[
            jax.ShapeDtypeStruct(own.shape, F32),
            jax.ShapeDtypeStruct(own.shape, LINK),
        ],
        compiler_params=pltpu.CompilerParams(vmem_limit_bytes=VMEM_BYTES),
        name="pair_states",
    )(seq_index, coefs, own, *states)


def local_kernel(q_ref, k_ref, v_ref, o_ref, coef_ref, gain_ref, conv_ref, grad_ref):
    tok_rows, width = k_ref.shape
    tiles = width // LANES
    spread_tokens(k_ref, v_ref, conv_ref)
    spread_tokens(o_ref, q_ref, grad_ref)
    walk_tokens(conv_ref, coef_ref, tok_rows, tiles, 0, 1)
    walk_tokens(grad_ref, coef_ref, tok_rows, tiles, tok_rows - 1, -1)
    for tile in range(tiles):
        cols = slice(tile * LANES, (tile + 1) * LANES)
        rows = tile_rows(tok_rows, tile)
        gain = gain_ref[:, cols]
        conv_in = product(k_ref[:, cols], v_ref[:, cols]).astype(F32)
        conv_ref[rows, :] = conv_ref[rows, :] + gain * conv_in
        mid_grad = product(o_ref[:, cols], q_ref[:, cols]).astype(F32)
        grad_ref[rows, :] = grad_ref[rows, :] + gain * mid_grad


def local_parts(query_proj, key_proj, value_proj, out_grad, coefs, gain):
    tok_rows, width = key_proj.shape
    modes, tiles = coefs.shape[1:3]
    return pl.pallas_call(
        local_kernel,
        out_shape=[jax.ShapeDtypeStruct(token_shape(tok_rows, tiles), F32)] * 2,
        compiler_params=pltpu.CompilerParams(vmem_limit_bytes=VMEM_BYTES),
        cost_estimate=pl.CostEstimate(
            flops=8 * modes * tok_rows * width, bytes_accessed=8 * tok_rows * width, transcendentals=0
        ),
        name="local_parts",
    )(query_proj, key_proj, value_proj, out_grad, coefs, gain)


def along_column(state, pairs, k):
    route = [(2 * p + b, 2 * ((p + k) % pairs) + b) for p in range(pairs) for b in range(2)]
    return lax.ppermute(state, "seq", route)


def inside_pair(state, pairs):
    return lax.ppermute(state, "seq", [(i, i ^ 1) for i in range(2 * pairs)])


def fill_edge(ref, held, coef_ref, tok_rows, tiles, start, move):
    modes = coef_ref.shape[1]
    decay = [coef_ref[0, m] for m in range(modes)]

    def step(t, held):
        held = tuple(decay[m] * held[m] for m in range(modes))
        ref[token_place(start + move * t, tok_rows, tiles)] = tree_sum(list(held))
        return held

    held = tuple(coef_ref[2, m] * held[m] for m in range(modes))
    lax.fori_loop(0, tok_rows, step, held, unroll=8)


def final_kernel(
    q_ref, k_ref, v_ref, coef_ref, x_ref, g_ref, kept_ref, given_ref, *refs
):
    hbm_refs, (edge_ref, layer_ref, key_ref, value_ref, sems) = refs[:3], refs[3:]
    tok_rows, width = k_ref.shape
    tiles = width // LANES
    modes = coef_ref.shape[1]

    def departure(i, tile):
        place = (slice(None), pl.ds(tile * LANES, LANES))
        return pltpu.make_async_copy(
            (layer_ref, key_ref, value_ref)[i].at[place], hbm_refs[i].at[place], sems.at[i, tile]
        )

    def edge(side):
        total = kept_ref[side] + given_ref[side].astype(F32)
        return [total[m * tiles : (m + 1) * tiles] for m in range(modes)]

    fill_edge(edge_ref, edge(0), coef_ref, tok_rows, tiles, 0, 1)
    for tile in range(tiles):
        cols = slice(tile * LANES, (tile + 1) * LANES)
        rows = tile_rows(tok_rows, tile)
        long_conv = x_ref[rows, :] + edge_ref[rows, :]
        layer_ref[:, cols] = (q_ref[:, cols].astype(F32) * long_conv).astype(BF16)
        departure(0, tile).start()
    fill_edge(edge_ref, edge(1), coef_ref, tok_rows, tiles, tok_rows - 1, -1)
    for tile in range(tiles):
        cols = slice(tile * LANES, (tile + 1) * LANES)
        rows = tile_rows(tok_rows, tile)
        conv_grad = g_ref[rows, :] + edge_ref[rows, :]
        key_ref[:, cols] = (conv_grad * v_ref[:, cols].astype(F32)).astype(BF16)
        departure(1, tile).start()
        value_ref[:, cols] = (conv_grad * k_ref[:, cols].astype(F32)).astype(BF16)
        departure(2, tile).start()
    for i in range(3):
        for tile in range(tiles):
            departure(i, tile).wait()


def final_outputs(signals, coefs, parts, kept, given):
    tok_rows, width = signals[0].shape
    modes, tiles = coefs.shape[1:3]
    args = (*signals, coefs, *parts, kept, given)
    whole = pl.BlockSpec(memory_space=pltpu.VMEM)
    return pl.pallas_call(
        final_kernel,
        in_specs=[whole] * len(args),
        out_specs=[pl.BlockSpec(memory_space=pl.ANY)] * 3,
        out_shape=[jax.ShapeDtypeStruct((tok_rows, width), BF16)] * 3,
        scratch_shapes=[pltpu.VMEM(token_shape(tok_rows, tiles), F32)]
        + [pltpu.VMEM((tok_rows, width), BF16)] * 3
        + [pltpu.SemaphoreType.DMA((3, tiles))],
        compiler_params=pltpu.CompilerParams(vmem_limit_bytes=VMEM_BYTES),
        cost_estimate=pl.CostEstimate(
            flops=8 * modes * tok_rows * width, bytes_accessed=14 * tok_rows * width, transcendentals=0
        ),
        name="final_outputs",
    )(*args)


def lag_kernel(shards, chans, groups, owned, scale, count, *refs):
    in_refs, (out_ref, u_all, g_all, turned_all) = refs[:count], refs[-4:]
    tok_rows = out_ref.shape[2]
    halves = tok_rows // LANES
    blocks = shards * halves
    depth = chans * groups
    full = blocks * depth
    if len(in_refs) == 1:
        take = chans * groups * owned

        def by_filter(row):
            return row % depth * owned + row // depth

        order = one_hot(take, take, by_filter)
        for which, kept in enumerate((u_all, g_all)):
            rows = slice(which * groups * owned, (which + 1) * groups * owned)
            for s in range(shards):
                piece = in_refs[0][s * chans : (s + 1) * chans, rows, :].reshape(take, tok_rows)
                piece = jnp.dot(order, piece, preferred_element_type=F32).astype(BF16)
                piece = piece.reshape(owned, depth, tok_rows)
                for h in range(halves):
                    first = (s * halves + h) * depth
                    kept[:, first : first + depth, :] = piece[:, :, h * LANES : (h + 1) * LANES]
    else:
        u_all[...] = in_refs[0][...]
        g_all[:, :full, :] = in_refs[1][...]
    g_all[:, full:, :] = jnp.zeros((owned, g_all.shape[1] - full, LANES), BF16)
    mirror = one_hot(LANES, LANES, lambda row: LANES - 1 - row)
    row = lax.broadcasted_iota(jnp.int32, (LANES, LANES), 0)
    col = lax.broadcasted_iota(jnp.int32, (LANES, LANES), 1)
    same_block = row + col >= LANES - 1
    filter_row = lax.broadcasted_iota(jnp.int32, (owned, LANES), 0)
    batch = min(blocks, 16)

    def one_filter(f, _):
        turned = turned_all[f]

        def some_lags(first):
            tables = []
            for d in range(0, batch, 2):
                live = full
                if batch == blocks:
                    live = min(full, -(-(blocks - d) * depth // LANES) * LANES)
                pair = jnp.concatenate(
                    [
                        g_all[f, pl.ds(pl.multiple_of((first + d + e) * depth, depth), live), :]
                        for e in range(2)
                    ],
                    axis=1,
                )
                table = jnp.dot(turned[:, :live], pair, preferred_element_type=F32)
                tables += [table[:, :LANES], table[:, LANES:]]
            last = g_all[f, pl.ds(pl.multiple_of((first + batch) * depth, depth), full), :]
            if batch < blocks:
                tables.append(jnp.dot(turned, last, preferred_element_type=F32))
            else:
                tables.append(jnp.zeros((LANES, LANES), F32))
            for d in range(batch):
                joined = jnp.where(same_block, tables[d], tables[d + 1])
                skewed = pltpu.roll(joined, 1, 1, stride=1, stride_axis=0)
                sums = jnp.sum(skewed, axis=0, keepdims=True) * scale
                lane = d % halves * LANES
                place = ((first + d) // halves, slice(None), slice(lane, lane + LANES))
                out_ref[place] = jnp.where(filter_row == f, sums, out_ref[place])

        if batch == blocks:
            some_lags(0)
        else:
            lax.fori_loop(0, blocks // batch, lambda i, c: (some_lags(i * batch), c)[1], 0)
        return 0

    for f in range(owned):
        turned_all[f] = lax.dot_general(
            mirror, u_all[f], (((1,), (1,)), ((), ())), preferred_element_type=F32
        ).astype(BF16)
    lax.fori_loop(0, owned, one_filter, 0, unroll=min(owned, 4))


def filter_lags(received, held, shards, chans, owned, scale):
    tok_rows = received.shape[2]
    groups = received.shape[1] // (2 * owned)
    halves = tok_rows // LANES
    depth = chans * groups
    full = shards * halves * depth
    args = (received,)
    if owned % SUBLANES:
        split = received.reshape(shards, chans, 2, groups, owned, halves, LANES)
        split = split.transpose(2, 4, 0, 5, 1, 3, 6).reshape(2, owned, full, LANES)
        args = (split[0], split[1])
    return pl.pallas_call(
        functools.partial(lag_kernel, shards, chans, groups, owned, scale, len(args)),
        in_specs=[pl.BlockSpec(memory_space=pltpu.VMEM)] * len(args)
        + [pl.BlockSpec(memory_space=pl.ANY)] * len(held),
        out_specs=pl.BlockSpec(memory_space=pltpu.VMEM),
        out_shape=jax.ShapeDtypeStruct((shards, owned, tok_rows), F32),
        scratch_shapes=[
            pltpu.VMEM((owned, full, LANES), BF16),
            pltpu.VMEM((owned, 2 * full + depth, LANES), BF16),
            pltpu.VMEM((owned, LANES, full), BF16),
        ],
        compiler_params=pltpu.CompilerParams(vmem_limit_bytes=VMEM_BYTES),
        cost_estimate=pl.CostEstimate(
            flops=4 * owned * LANES * full * full, bytes_accessed=8 * owned * full * LANES, transcendentals=0
        ),
        name="filter_lags",
    )(*args, *held)


def per_device(query_proj, key_proj, value_proj, out_grad, residues, decay_rate, skip_gain):
    tok_rows, width = key_proj.shape
    shards = lax.axis_size("seq")
    chans = lax.axis_size("chan")
    length = shards * tok_rows
    owned = FILTERS // (shards * chans)
    modes = residues.shape[1]
    signals = (query_proj, key_proj, value_proj, out_grad)

    send = pack_signals(shards, chans, owned, *signals)
    send, *signals, residues, decay_rate = lax.optimization_barrier(
        (send, *signals, residues, decay_rate)
    )
    received = lax.all_to_all(send, ("seq", "chan"), split_axis=0, concat_axis=0, tiled=True)

    coefs = jnp.stack(
        [
            jnp.exp(-decay_rate),
            jnp.exp(-(decay_rate * float(tok_rows))),
            residues * jnp.sqrt(decay_rate),
        ]
    )
    coefs = coefs.transpose(0, 2, 1).reshape(3, modes, 1, FILTERS // LANES, LANES)
    coefs = jnp.broadcast_to(coefs, (3, modes, width // FILTERS, FILTERS // LANES, LANES))
    coefs = coefs.reshape(3, modes, width // LANES, LANES)
    seq_index = lax.axis_index("seq").reshape(1)
    pairs = shards // 2
    states, own = block_states(seq_index, pairs, *signals, coefs)
    *states, coefs = lax.optimization_barrier((*states, coefs))
    states = [along_column(state, pairs, 1 + i) for i, state in enumerate(states)]
    parts = local_parts(*signals, coefs, skip_gain[None, :])
    kept, given = pair_states(seq_index, coefs, own, states)
    received, kept, given = lax.optimization_barrier((received, kept, given))
    given = inside_pair(given, pairs)

    scale = 1.0 / math.sqrt(length * (CHANNELS // FILTERS))
    lags = filter_lags(received, parts, shards, chans, owned, scale)
    lags, given = lax.optimization_barrier((lags, given))
    lags = lax.all_to_all(lags, "seq", split_axis=0, concat_axis=0, tiled=True)
    filter_grad = lags.reshape(shards * owned, tok_rows).T
    layer_out, key_grad, value_grad = final_outputs(
        signals[:3], coefs, parts, kept, given
    )
    return (layer_out, key_grad, value_grad, filter_grad)


def solution(mesh):
    split = P("seq", "chan")
    return jax.shard_map(
        per_device,
        mesh=mesh,
        in_specs=(split, split, split, split, P(), P(), P("chan")),
        out_specs=(split, split, split, split),
        check_vma=False,
    )
```

```python
import functools
import math

import jax
import jax.numpy as jnp
from jax import lax
from jax.experimental import pallas as pl
from jax.experimental.pallas import tpu as pltpu
from jax.sharding import PartitionSpec as P

CHANNELS = 4096
FILTERS = 256
LANES = 128
SUBLANES = 8
GAP = 8
VMEM_BYTES = 16 * 1024 * 1024
FINAL_VMEM_BYTES = 60 * 1024 * 1024
PACK_VMEM_BYTES = 62 * 1024 * 1024
F32 = jnp.float32
BF16 = jnp.bfloat16
LINK = jnp.bfloat16


def product(first, second):
    return (first.astype(F32) * second.astype(F32)).astype(BF16)


def one_hot(rows, cols, column_of):
    row = lax.broadcasted_iota(jnp.int32, (rows, cols), 0)
    col = lax.broadcasted_iota(jnp.int32, (rows, cols), 1)
    return (col == column_of(row)).astype(F32).astype(BF16)


def pack_kernel(shards, chans, owned, *refs):
    hbm_refs, send_ref, held, packed, in_sems, out_sems = refs[:4], *refs[4:]
    tok_rows, width = held.shape[1:]
    groups = width // FILTERS
    per_chan = FILTERS // chans
    units = [(which, first) for which in range(2) for first in range(0, groups, 2)]

    def arrival(i, first):
        place = (slice(None), pl.ds(first * FILTERS, 2 * FILTERS))
        return pltpu.make_async_copy(
            hbm_refs[i].at[place], held.at[(i, *place)], in_sems.at[i, first // 2]
        )

    def departure(which, first):
        if owned % SUBLANES:
            place = (which, pl.ds(first, 2))
        else:
            place = (slice(None), pl.ds((which * groups + first) * owned, 2 * owned))
        return pltpu.make_async_copy(
            packed.at[place], send_ref.at[place], out_sems.at[which, first // 2]
        )

    for which, first in units:
        for i in (2 * which, 2 * which + 1):
            arrival(i, first).start()

    def owned_filter(row):
        seq = row // (chans * owned)
        chan = row // owned % chans
        return chan * per_chan + seq * owned + row % owned

    order = one_hot(FILTERS, FILTERS, owned_filter)
    for which, first in units:
        for i in (2 * which, 2 * which + 1):
            arrival(i, first).wait()
        pieces = []
        for group in (first, first + 1):
            cols = slice(group * FILTERS, (group + 1) * FILTERS)
            piece = lax.dot_general(
                order,
                product(held[2 * which, :, cols], held[2 * which + 1, :, cols]),
                (((1,), (1,)), ((), ())),
                preferred_element_type=F32,
            )
            if owned % SUBLANES:
                packed[which, group] = piece.astype(BF16)
            else:
                pieces.append(piece.reshape(shards * chans, owned, tok_rows))
        if pieces:
            row = (which * groups + first) * owned
            packed[:, row : row + 2 * owned, :] = jnp.concatenate(pieces, axis=1).astype(BF16)
        departure(which, first).start()
    for which, first in units:
        departure(which, first).wait()


def pack_signals(shards, chans, owned, query_proj, key_proj, value_proj, out_grad):
    tok_rows, width = key_proj.shape
    groups = width // FILTERS
    dests = shards * chans
    if owned % SUBLANES:
        shape = (2, groups, FILTERS, tok_rows)
    else:
        shape = (dests, 2 * groups * owned, tok_rows)
    send = pl.pallas_call(
        functools.partial(pack_kernel, shards, chans, owned),
        in_specs=[pl.BlockSpec(memory_space=pl.ANY)] * 4,
        out_specs=pl.BlockSpec(memory_space=pl.ANY),
        out_shape=jax.ShapeDtypeStruct(shape, BF16),
        scratch_shapes=[
            pltpu.VMEM((4, tok_rows, width), BF16),
            pltpu.VMEM(shape, BF16),
            pltpu.SemaphoreType.DMA((4, groups // 2)),
            pltpu.SemaphoreType.DMA((2, groups // 2)),
        ],
        compiler_params=pltpu.CompilerParams(vmem_limit_bytes=PACK_VMEM_BYTES),
        name="pack_signals",
    )(key_proj, value_proj, out_grad, query_proj)
    if owned % SUBLANES:
        send = send.reshape(2, groups, dests, owned, tok_rows)
        send = send.transpose(2, 0, 1, 3, 4).reshape(dests, 2 * groups * owned, tok_rows)
    return send


def tile_rows(tok_rows, tile):
    first = tile * (tok_rows + GAP)
    return slice(first, first + tok_rows)


def token_shape(tok_rows, tiles):
    return (tiles * (tok_rows + GAP), LANES)


def token_place(t, tok_rows, tiles):
    return (pl.ds(t, tiles, stride=tok_rows + GAP), slice(None))


def spread_tokens(a_ref, b_ref, x_ref):
    tok_rows, width = a_ref.shape
    for tile in range(width // LANES):
        cols = slice(tile * LANES, (tile + 1) * LANES)
        x_ref[tile_rows(tok_rows, tile), :] = product(a_ref[:, cols], b_ref[:, cols]).astype(F32)


def walk_tokens(ref, coef_ref, tok_rows, tiles, start, move):
    modes = coef_ref.shape[1]
    decay = [coef_ref[0, m] for m in range(modes)]
    weight = [coef_ref[2, m] for m in range(modes)]

    def step(t, held):
        place = token_place(start + move * t, tok_rows, tiles)
        x = ref[place]
        held = tuple(decay[m] * held[m] + x for m in range(modes))
        ref[place] = tree_sum([weight[m] * held[m] for m in range(modes)])
        return held

    zero = tuple(jnp.zeros((tiles, LANES), F32) for _ in range(modes))
    return lax.fori_loop(0, tok_rows, step, zero, unroll=8)


def tree_sum(terms):
    while len(terms) > 1:
        terms = [sum(terms[i : i + 2][1:], terms[i]) for i in range(0, len(terms), 2)]
    return terms[0]


def state_kernel(seq_ref, q_ref, k_ref, v_ref, o_ref, coef_ref, *refs):
    state_refs, own_ref, x_ref, g_ref = refs[:-3], *refs[-3:]
    tok_rows, width = k_ref.shape
    tiles = width // LANES
    modes = coef_ref.shape[1]
    pairs = len(state_refs) + 1
    spread_tokens(k_ref, v_ref, x_ref)
    spread_tokens(o_ref, q_ref, g_ref)
    decay = [coef_ref[0, m] for m in range(modes)]

    def step(t, carry):
        x = x_ref[token_place(t, tok_rows, tiles)]
        g = g_ref[token_place(tok_rows - 1 - t, tok_rows, tiles)]
        ahead = tuple(decay[m] * carry[0][m] + x for m in range(modes))
        behind = tuple(decay[m] * carry[1][m] + g for m in range(modes))
        return (ahead, behind)

    zero = tuple(jnp.zeros((tiles, LANES), F32) for _ in range(modes))
    ahead, behind = lax.fori_loop(0, tok_rows, step, (zero, zero), unroll=8)
    ahead = jnp.concatenate(ahead, axis=0)
    behind = jnp.concatenate(behind, axis=0)
    own_ref[0] = ahead
    own_ref[1] = behind
    for k in range(1, pairs):
        stays = seq_ref[0] // 2 + k < pairs

        @pl.when(stays)
        def _():
            state_refs[k - 1][...] = ahead.astype(LINK)

        @pl.when(jnp.logical_not(stays))
        def _():
            state_refs[k - 1][...] = behind.astype(LINK)


def block_states(seq_index, pairs, query_proj, key_proj, value_proj, out_grad, coefs):
    tok_rows, width = key_proj.shape
    modes, tiles = coefs.shape[1:3]
    whole = pl.BlockSpec(memory_space=pltpu.VMEM)
    *states, own = pl.pallas_call(
        state_kernel,
        in_specs=[pl.BlockSpec(memory_space=pltpu.SMEM)] + [whole] * 5,
        out_specs=[whole] * pairs,
        out_shape=[jax.ShapeDtypeStruct((modes * tiles, LANES), LINK)] * (pairs - 1)
        + [jax.ShapeDtypeStruct((2, modes * tiles, LANES), F32)],
        scratch_shapes=[pltpu.VMEM(token_shape(tok_rows, tiles), F32)] * 2,
        compiler_params=pltpu.CompilerParams(vmem_limit_bytes=VMEM_BYTES),
        cost_estimate=pl.CostEstimate(
            flops=4 * modes * tok_rows * width, bytes_accessed=8 * tok_rows * width, transcendentals=0
        ),
        name="block_states",
    )(seq_index, query_proj, key_proj, value_proj, out_grad, coefs)
    return states, own


def pair_kernel(seq_ref, coef_ref, own_ref, _, *refs):
    state_refs, kept_ref, given_ref = refs[:-2], *refs[-2:]
    pairs = len(state_refs) + 1
    modes, tiles = coef_ref.shape[1:3]
    pair = seq_ref[0] // 2
    second = seq_ref[0] % 2 == 1
    for m in range(modes):
        rows = slice(m * tiles, (m + 1) * tiles)
        decay = coef_ref[1, m]
        both = decay * decay
        before = jnp.zeros((tiles, LANES), F32)
        after = jnp.zeros((tiles, LANES), F32)
        for k in range(pairs - 1, 0, -1):
            block = state_refs[k - 1][...].astype(F32)[rows]
            before = both * before + jnp.where(k <= pair, block, 0.0)
            block = state_refs[pairs - k - 1][...].astype(F32)[rows]
            after = both * after + jnp.where(k <= pairs - 1 - pair, block, 0.0)
        before = jnp.where(second, before, decay * before)
        after = jnp.where(second, decay * after, after)
        kept_ref[0, rows] = jnp.where(second, decay * before, before)
        kept_ref[1, rows] = jnp.where(second, after, decay * after)
        own = own_ref[0, rows]
        given_ref[0, rows] = jnp.where(second, before, decay * before + own).astype(LINK)
        own = own_ref[1, rows]
        given_ref[1, rows] = jnp.where(second, decay * after + own, after).astype(LINK)


def pair_states(seq_index, coefs, own, parts, states):
    whole = pl.BlockSpec(memory_space=pltpu.VMEM)
    return pl.pallas_call(
        pair_kernel,
        in_specs=[pl.BlockSpec(memory_space=pltpu.SMEM), whole, whole]
        + [pl.BlockSpec(memory_space=pl.ANY)]
        + [whole] * len(states),
        out_specs=[whole] * 2,
        out_shape=[
            jax.ShapeDtypeStruct(own.shape, F32),
            jax.ShapeDtypeStruct(own.shape, LINK),
        ],
        compiler_params=pltpu.CompilerParams(vmem_limit_bytes=VMEM_BYTES),
        name="pair_states",
    )(seq_index, coefs, own, parts, *states)


def local_kernel(q_ref, k_ref, v_ref, o_ref, coef_ref, gain_ref, part_ref):
    conv_ref, grad_ref = part_ref.at[0], part_ref.at[1]
    tok_rows, width = k_ref.shape
    tiles = width // LANES
    spread_tokens(k_ref, v_ref, conv_ref)
    spread_tokens(o_ref, q_ref, grad_ref)
    walk_tokens(conv_ref, coef_ref, tok_rows, tiles, 0, 1)
    walk_tokens(grad_ref, coef_ref, tok_rows, tiles, tok_rows - 1, -1)
    for tile in range(tiles):
        cols = slice(tile * LANES, (tile + 1) * LANES)
        rows = tile_rows(tok_rows, tile)
        gain = gain_ref[:, cols]
        conv_in = product(k_ref[:, cols], v_ref[:, cols]).astype(F32)
        conv_ref[rows, :] = conv_ref[rows, :] + gain * conv_in
        mid_grad = product(o_ref[:, cols], q_ref[:, cols]).astype(F32)
        grad_ref[rows, :] = grad_ref[rows, :] + gain * mid_grad


def local_parts(query_proj, key_proj, value_proj, out_grad, coefs, gain):
    tok_rows, width = key_proj.shape
    modes, tiles = coefs.shape[1:3]
    return pl.pallas_call(
        local_kernel,
        out_shape=jax.ShapeDtypeStruct((2, *token_shape(tok_rows, tiles)), F32),
        compiler_params=pltpu.CompilerParams(vmem_limit_bytes=VMEM_BYTES),
        cost_estimate=pl.CostEstimate(
            flops=8 * modes * tok_rows * width, bytes_accessed=8 * tok_rows * width, transcendentals=0
        ),
        name="local_parts",
    )(query_proj, key_proj, value_proj, out_grad, coefs, gain)


def along_column(state, pairs, k):
    route = [(2 * p + b, 2 * ((p + k) % pairs) + b) for p in range(pairs) for b in range(2)]
    return lax.ppermute(state, "seq", route)


def inside_pair(state, pairs):
    return lax.ppermute(state, "seq", [(i, i ^ 1) for i in range(2 * pairs)])


def fill_edge(ref, held, coef_ref, tok_rows, tiles, start, move):
    modes = coef_ref.shape[1]
    decay = [coef_ref[0, m] for m in range(modes)]

    def step(t, held):
        held = tuple(decay[m] * held[m] for m in range(modes))
        ref[token_place(start + move * t, tok_rows, tiles)] = tree_sum(list(held))
        return held

    held = tuple(coef_ref[2, m] * held[m] for m in range(modes))
    lax.fori_loop(0, tok_rows, step, held, unroll=8)


def final_kernel(q_ref, k_ref, v_ref, coef_ref, kept_ref, given_ref, part_ref, *refs):
    hbm_refs, refs = refs[:3], refs[3:]
    held_ref, edge_ref, layer_ref, key_ref, value_ref, in_sems, sems = refs
    x_ref, g_ref = held_ref.at[0], held_ref.at[1]
    tok_rows, width = k_ref.shape
    tiles = width // LANES
    modes = coef_ref.shape[1]

    def arrival(i, half):
        rows = pl.ds(half * (part_ref.shape[1] // 2), part_ref.shape[1] // 2)
        return pltpu.make_async_copy(
            part_ref.at[i, rows, :], held_ref.at[i, rows, :], in_sems.at[i, half]
        )

    def departure(i, tile):
        place = (slice(None), pl.ds(tile * LANES, LANES))
        return pltpu.make_async_copy(
            (layer_ref, key_ref, value_ref)[i].at[place], hbm_refs[i].at[place], sems.at[i, tile]
        )

    def edge(side):
        total = kept_ref[side] + given_ref[side].astype(F32)
        return [total[m * tiles : (m + 1) * tiles] for m in range(modes)]

    for i in range(2):
        for half in range(2):
            arrival(i, half).start()
    fill_edge(edge_ref, edge(0), coef_ref, tok_rows, tiles, 0, 1)
    for half in range(2):
        arrival(0, half).wait()
    for tile in range(tiles):
        cols = slice(tile * LANES, (tile + 1) * LANES)
        rows = tile_rows(tok_rows, tile)
        long_conv = x_ref[rows, :] + edge_ref[rows, :]
        layer_ref[:, cols] = (q_ref[:, cols].astype(F32) * long_conv).astype(BF16)
        departure(0, tile).start()
    fill_edge(edge_ref, edge(1), coef_ref, tok_rows, tiles, tok_rows - 1, -1)
    for half in range(2):
        arrival(1, half).wait()
    for tile in range(tiles):
        cols = slice(tile * LANES, (tile + 1) * LANES)
        rows = tile_rows(tok_rows, tile)
        conv_grad = g_ref[rows, :] + edge_ref[rows, :]
        key_ref[:, cols] = (conv_grad * v_ref[:, cols].astype(F32)).astype(BF16)
        departure(1, tile).start()
        value_ref[:, cols] = (conv_grad * k_ref[:, cols].astype(F32)).astype(BF16)
        departure(2, tile).start()
    for i in range(3):
        for tile in range(tiles):
            departure(i, tile).wait()


def final_outputs(signals, coefs, kept, given, parts):
    tok_rows, width = signals[0].shape
    modes, tiles = coefs.shape[1:3]
    args = (*signals, coefs, kept, given)
    whole = pl.BlockSpec(memory_space=pltpu.VMEM)
    away = pl.BlockSpec(memory_space=pl.ANY)
    return pl.pallas_call(
        final_kernel,
        in_specs=[whole] * len(args) + [away],
        out_specs=[away] * 3,
        out_shape=[jax.ShapeDtypeStruct((tok_rows, width), BF16)] * 3,
        scratch_shapes=[
            pltpu.VMEM(parts.shape, F32),
            pltpu.VMEM(parts.shape[1:], F32),
            pltpu.VMEM((tok_rows, width), BF16),
            pltpu.VMEM((tok_rows, width), BF16),
            pltpu.VMEM((tok_rows, width), BF16),
            pltpu.SemaphoreType.DMA((2, 2)),
            pltpu.SemaphoreType.DMA((3, tiles)),
        ],
        compiler_params=pltpu.CompilerParams(vmem_limit_bytes=FINAL_VMEM_BYTES),
        cost_estimate=pl.CostEstimate(
            flops=8 * modes * tok_rows * width, bytes_accessed=14 * tok_rows * width, transcendentals=0
        ),
        name="final_outputs",
    )(*args, parts)


def lag_kernel(shards, chans, groups, owned, scale, *refs):
    in_refs, (out_ref, u_all, g_all, turned_all) = refs[:-4], refs[-4:]
    tok_rows = out_ref.shape[2]
    halves = tok_rows // LANES
    blocks = shards * halves
    depth = chans * groups
    full = blocks * depth
    if len(in_refs) == 1:
        take = chans * groups * owned

        def by_filter(row):
            return row % depth * owned + row // depth

        order = one_hot(take, take, by_filter)
        for which, kept in enumerate((u_all, g_all)):
            rows = slice(which * groups * owned, (which + 1) * groups * owned)
            for s in range(shards):
                piece = in_refs[0][s * chans : (s + 1) * chans, rows, :].reshape(take, tok_rows)
                piece = jnp.dot(order, piece, preferred_element_type=F32).astype(BF16)
                piece = piece.reshape(owned, depth, tok_rows)
                for h in range(halves):
                    first = (s * halves + h) * depth
                    kept[:, first : first + depth, :] = piece[:, :, h * LANES : (h + 1) * LANES]
    else:
        u_all[...] = in_refs[0][...]
        g_all[:, :full, :] = in_refs[1][...]
    g_all[:, full:, :] = jnp.zeros((owned, g_all.shape[1] - full, LANES), BF16)
    mirror = one_hot(LANES, LANES, lambda row: LANES - 1 - row)
    row = lax.broadcasted_iota(jnp.int32, (LANES, LANES), 0)
    col = lax.broadcasted_iota(jnp.int32, (LANES, LANES), 1)
    same_block = row + col >= LANES - 1
    filter_row = lax.broadcasted_iota(jnp.int32, (owned, LANES), 0)
    batch = min(blocks, 16)

    def one_filter(f, _):
        turned = turned_all[f]

        def some_lags(first):
            tables = []
            for d in range(0, batch, 2):
                live = full
                if batch == blocks:
                    live = min(full, -(-(blocks - d) * depth // LANES) * LANES)
                pair = jnp.concatenate(
                    [
                        g_all[f, pl.ds(pl.multiple_of((first + d + e) * depth, depth), live), :]
                        for e in range(2)
                    ],
                    axis=1,
                )
                table = jnp.dot(turned[:, :live], pair, preferred_element_type=F32)
                tables += [table[:, :LANES], table[:, LANES:]]
            last = g_all[f, pl.ds(pl.multiple_of((first + batch) * depth, depth), full), :]
            if batch < blocks:
                tables.append(jnp.dot(turned, last, preferred_element_type=F32))
            else:
                tables.append(jnp.zeros((LANES, LANES), F32))
            for d in range(batch):
                joined = jnp.where(same_block, tables[d], tables[d + 1])
                skewed = pltpu.roll(joined, 1, 1, stride=1, stride_axis=0)
                sums = jnp.sum(skewed, axis=0, keepdims=True) * scale
                lane = d % halves * LANES
                place = ((first + d) // halves, slice(None), slice(lane, lane + LANES))
                out_ref[place] = jnp.where(filter_row == f, sums, out_ref[place])

        if batch == blocks:
            some_lags(0)
        else:
            lax.fori_loop(0, blocks // batch, lambda i, c: (some_lags(i * batch), c)[1], 0)
        return 0

    for f in range(owned):
        turned_all[f] = lax.dot_general(
            mirror, u_all[f], (((1,), (1,)), ((), ())), preferred_element_type=F32
        ).astype(BF16)
    lax.fori_loop(0, owned, one_filter, 0, unroll=min(owned, 4))


def filter_lags(received, shards, chans, owned, scale):
    tok_rows = received.shape[2]
    groups = received.shape[1] // (2 * owned)
    halves = tok_rows // LANES
    depth = chans * groups
    full = shards * halves * depth
    args = (received,)
    if owned % SUBLANES:
        split = received.reshape(shards, chans, 2, groups, owned, halves, LANES)
        split = split.transpose(2, 4, 0, 5, 1, 3, 6).reshape(2, owned, full, LANES)
        args = (split[0], split[1])
    return pl.pallas_call(
        functools.partial(lag_kernel, shards, chans, groups, owned, scale),
        out_shape=jax.ShapeDtypeStruct((shards, owned, tok_rows), F32),
        scratch_shapes=[
            pltpu.VMEM((owned, full, LANES), BF16),
            pltpu.VMEM((owned, 2 * full + depth, LANES), BF16),
            pltpu.VMEM((owned, LANES, full), BF16),
        ],
        compiler_params=pltpu.CompilerParams(vmem_limit_bytes=VMEM_BYTES),
        cost_estimate=pl.CostEstimate(
            flops=4 * owned * LANES * full * full, bytes_accessed=8 * owned * full * LANES, transcendentals=0
        ),
        name="filter_lags",
    )(*args)


def per_device(query_proj, key_proj, value_proj, out_grad, residues, decay_rate, skip_gain):
    tok_rows, width = key_proj.shape
    shards = lax.axis_size("seq")
    chans = lax.axis_size("chan")
    length = shards * tok_rows
    owned = FILTERS // (shards * chans)
    modes = residues.shape[1]
    signals = (query_proj, key_proj, value_proj, out_grad)

    send = pack_signals(shards, chans, owned, *signals)
    send, *signals, residues, decay_rate = lax.optimization_barrier(
        (send, *signals, residues, decay_rate)
    )
    received = lax.all_to_all(send, ("seq", "chan"), split_axis=0, concat_axis=0, tiled=True)

    coefs = jnp.stack(
        [
            jnp.exp(-decay_rate),
            jnp.exp(-(decay_rate * float(tok_rows))),
            residues * jnp.sqrt(decay_rate),
        ]
    )
    coefs = coefs.transpose(0, 2, 1).reshape(3, modes, 1, FILTERS // LANES, LANES)
    coefs = jnp.broadcast_to(coefs, (3, modes, width // FILTERS, FILTERS // LANES, LANES))
    coefs = coefs.reshape(3, modes, width // LANES, LANES)
    seq_index = lax.axis_index("seq").reshape(1)
    pairs = shards // 2
    states, own = block_states(seq_index, pairs, *signals, coefs)
    *states, coefs = lax.optimization_barrier((*states, coefs))
    states = [along_column(state, pairs, 1 + i) for i, state in enumerate(states)]
    parts = local_parts(*signals, coefs, skip_gain[None, :])
    kept, given = pair_states(seq_index, coefs, own, parts, states)
    received, kept, given = lax.optimization_barrier((received, kept, given))
    given = inside_pair(given, pairs)

    scale = 1.0 / math.sqrt(length * (CHANNELS // FILTERS))
    lags = filter_lags(received, shards, chans, owned, scale)
    lags, given = lax.optimization_barrier((lags, given))
    lags = lax.all_to_all(lags, "seq", split_axis=0, concat_axis=0, tiled=True)
    filter_grad = lags.reshape(shards * owned, tok_rows).T
    layer_out, key_grad, value_grad = final_outputs(
        signals[:3], coefs, kept, given, parts
    )
    return (layer_out, key_grad, value_grad, filter_grad)


def solution(mesh):
    split = P("seq", "chan")
    return jax.shard_map(
        per_device,
        mesh=mesh,
        in_specs=(split, split, split, split, P(), P(), P("chan")),
        out_specs=(split, split, split, split),
        check_vma=False,
    )
```

```python
import functools
import math

import jax
import jax.numpy as jnp
from jax import lax
from jax.experimental import pallas as pl
from jax.experimental.pallas import tpu as pltpu
from jax.sharding import PartitionSpec as P

CHANNELS = 4096
FILTERS = 256
LANES = 128
SUBLANES = 8
GAP = 8
VMEM_BYTES = 16 * 1024 * 1024
FULL_VMEM_BYTES = 62 * 1024 * 1024
F32 = jnp.float32
BF16 = jnp.bfloat16
LINK = jnp.bfloat16


def takes(micros):
    return pl.CostEstimate(flops=0, bytes_accessed=int(micros * 3.6e6), transcendentals=0)


def product(first, second):
    return (first.astype(F32) * second.astype(F32)).astype(BF16)


def one_hot(rows, cols, column_of):
    row = lax.broadcasted_iota(jnp.int32, (rows, cols), 0)
    col = lax.broadcasted_iota(jnp.int32, (rows, cols), 1)
    return (col == column_of(row)).astype(F32).astype(BF16)


def pack_kernel(shards, chans, owned, *refs):
    hbm_refs, send_ref, held, packed, in_sems, out_sems = refs[:4], *refs[4:]
    tok_rows, width = held.shape[1:]
    groups = width // FILTERS
    per_chan = FILTERS // chans
    units = [(which, first) for which in range(2) for first in range(0, groups, 2)]

    def arrival(i, first):
        place = (slice(None), pl.ds(first * FILTERS, 2 * FILTERS))
        return pltpu.make_async_copy(
            hbm_refs[i].at[place], held.at[(i, *place)], in_sems.at[i, first // 2]
        )

    def departure(which, first):
        if owned % SUBLANES:
            place = (which, pl.ds(first, 2))
        else:
            place = (slice(None), pl.ds((which * groups + first) * owned, 2 * owned))
        return pltpu.make_async_copy(
            packed.at[place], send_ref.at[place], out_sems.at[which, first // 2]
        )

    for which, first in units:
        for i in (2 * which, 2 * which + 1):
            arrival(i, first).start()

    def owned_filter(row):
        seq = row // (chans * owned)
        chan = row // owned % chans
        return chan * per_chan + seq * owned + row % owned

    order = one_hot(FILTERS, FILTERS, owned_filter)
    for which, first in units:
        for i in (2 * which, 2 * which + 1):
            arrival(i, first).wait()
        pieces = []
        for group in (first, first + 1):
            cols = slice(group * FILTERS, (group + 1) * FILTERS)
            piece = lax.dot_general(
                order,
                product(held[2 * which, :, cols], held[2 * which + 1, :, cols]),
                (((1,), (1,)), ((), ())),
                preferred_element_type=F32,
            )
            if owned % SUBLANES:
                packed[which, group] = piece.astype(BF16)
            else:
                pieces.append(piece.reshape(shards * chans, owned, tok_rows))
        if pieces:
            row = (which * groups + first) * owned
            packed[:, row : row + 2 * owned, :] = jnp.concatenate(pieces, axis=1).astype(BF16)
        departure(which, first).start()
    for which, first in units:
        departure(which, first).wait()


def pack_signals(shards, chans, owned, query_proj, key_proj, value_proj, out_grad):
    tok_rows, width = key_proj.shape
    groups = width // FILTERS
    dests = shards * chans
    if owned % SUBLANES:
        shape = (2, groups, FILTERS, tok_rows)
    else:
        shape = (dests, 2 * groups * owned, tok_rows)
    send = pl.pallas_call(
        functools.partial(pack_kernel, shards, chans, owned),
        in_specs=[pl.BlockSpec(memory_space=pl.ANY)] * 4,
        out_specs=pl.BlockSpec(memory_space=pl.ANY),
        out_shape=jax.ShapeDtypeStruct(shape, BF16),
        scratch_shapes=[
            pltpu.VMEM((4, tok_rows, width), BF16),
            pltpu.VMEM(shape, BF16),
            pltpu.SemaphoreType.DMA((4, groups // 2)),
            pltpu.SemaphoreType.DMA((2, groups // 2)),
        ],
        compiler_params=pltpu.CompilerParams(vmem_limit_bytes=FULL_VMEM_BYTES),
        cost_estimate=takes(3.0),
        name="pack_signals",
    )(key_proj, value_proj, out_grad, query_proj)
    if owned % SUBLANES:
        send = send.reshape(2, groups, dests, owned, tok_rows)
        send = send.transpose(2, 0, 1, 3, 4).reshape(dests, 2 * groups * owned, tok_rows)
    return send


def tile_rows(tok_rows, tile):
    first = tile * (tok_rows + GAP)
    return slice(first, first + tok_rows)


def token_shape(tok_rows, tiles):
    return (tiles * (tok_rows + GAP), LANES)


def token_place(t, tok_rows, tiles):
    return (pl.ds(t, tiles, stride=tok_rows + GAP), slice(None))


def spread_tokens(a_ref, b_ref, x_ref):
    tok_rows, width = a_ref.shape
    for tile in range(width // LANES):
        cols = slice(tile * LANES, (tile + 1) * LANES)
        x_ref[tile_rows(tok_rows, tile), :] = product(a_ref[:, cols], b_ref[:, cols]).astype(F32)


def walk_tokens(ref, coef_ref, tok_rows, tiles, start, move):
    modes = coef_ref.shape[1]
    decay = [coef_ref[0, m] for m in range(modes)]
    weight = [coef_ref[2, m] for m in range(modes)]

    def step(t, held):
        place = token_place(start + move * t, tok_rows, tiles)
        x = ref[place]
        held = tuple(decay[m] * held[m] + x for m in range(modes))
        ref[place] = tree_sum([weight[m] * held[m] for m in range(modes)])
        return held

    zero = tuple(jnp.zeros((tiles, LANES), F32) for _ in range(modes))
    return lax.fori_loop(0, tok_rows, step, zero, unroll=8)


def tree_sum(terms):
    while len(terms) > 1:
        terms = [sum(terms[i : i + 2][1:], terms[i]) for i in range(0, len(terms), 2)]
    return terms[0]


def state_kernel(seq_ref, q_ref, k_ref, v_ref, o_ref, coef_ref, *refs):
    state_refs, own_ref, x_ref, g_ref = refs[:-3], *refs[-3:]
    tok_rows, width = k_ref.shape
    tiles = width // LANES
    modes = coef_ref.shape[1]
    pairs = len(state_refs) + 1
    spread_tokens(k_ref, v_ref, x_ref)
    spread_tokens(o_ref, q_ref, g_ref)
    decay = [coef_ref[0, m] for m in range(modes)]

    def step(t, carry):
        x = x_ref[token_place(t, tok_rows, tiles)]
        g = g_ref[token_place(tok_rows - 1 - t, tok_rows, tiles)]
        ahead = tuple(decay[m] * carry[0][m] + x for m in range(modes))
        behind = tuple(decay[m] * carry[1][m] + g for m in range(modes))
        return (ahead, behind)

    zero = tuple(jnp.zeros((tiles, LANES), F32) for _ in range(modes))
    ahead, behind = lax.fori_loop(0, tok_rows, step, (zero, zero), unroll=8)
    ahead = jnp.concatenate(ahead, axis=0)
    behind = jnp.concatenate(behind, axis=0)
    own_ref[0] = ahead
    own_ref[1] = behind
    for k in range(1, pairs):
        stays = seq_ref[0] // 2 + k < pairs

        @pl.when(stays)
        def _():
            state_refs[k - 1][...] = ahead.astype(LINK)

        @pl.when(jnp.logical_not(stays))
        def _():
            state_refs[k - 1][...] = behind.astype(LINK)


def block_states(seq_index, pairs, query_proj, key_proj, value_proj, out_grad, coefs):
    tok_rows, width = key_proj.shape
    modes, tiles = coefs.shape[1:3]
    whole = pl.BlockSpec(memory_space=pltpu.VMEM)
    *states, own = pl.pallas_call(
        state_kernel,
        in_specs=[pl.BlockSpec(memory_space=pltpu.SMEM)] + [whole] * 5,
        out_specs=[whole] * pairs,
        out_shape=[jax.ShapeDtypeStruct((modes * tiles, LANES), LINK)] * (pairs - 1)
        + [jax.ShapeDtypeStruct((2, modes * tiles, LANES), F32)],
        scratch_shapes=[pltpu.VMEM(token_shape(tok_rows, tiles), F32)] * 2,
        compiler_params=pltpu.CompilerParams(vmem_limit_bytes=VMEM_BYTES),
        cost_estimate=takes(3.0),
        name="block_states",
    )(seq_index, query_proj, key_proj, value_proj, out_grad, coefs)
    return states, own


def pair_kernel(seq_ref, coef_ref, own_ref, _, *refs):
    state_refs, kept_ref, given_ref = refs[:-2], *refs[-2:]
    pairs = len(state_refs) + 1
    modes, tiles = coef_ref.shape[1:3]
    pair = seq_ref[0] // 2
    second = seq_ref[0] % 2 == 1
    for m in range(modes):
        rows = slice(m * tiles, (m + 1) * tiles)
        decay = coef_ref[1, m]
        both = decay * decay
        before = jnp.zeros((tiles, LANES), F32)
        after = jnp.zeros((tiles, LANES), F32)
        for k in range(pairs - 1, 0, -1):
            block = state_refs[k - 1][...].astype(F32)[rows]
            before = both * before + jnp.where(k <= pair, block, 0.0)
            block = state_refs[pairs - k - 1][...].astype(F32)[rows]
            after = both * after + jnp.where(k <= pairs - 1 - pair, block, 0.0)
        before = jnp.where(second, before, decay * before)
        after = jnp.where(second, decay * after, after)
        kept_ref[0, rows] = jnp.where(second, decay * before, before)
        kept_ref[1, rows] = jnp.where(second, after, decay * after)
        own = own_ref[0, rows]
        given_ref[0, rows] = jnp.where(second, before, decay * before + own).astype(LINK)
        own = own_ref[1, rows]
        given_ref[1, rows] = jnp.where(second, decay * after + own, after).astype(LINK)


def pair_states(seq_index, coefs, own, lags, states):
    whole = pl.BlockSpec(memory_space=pltpu.VMEM)
    return pl.pallas_call(
        pair_kernel,
        in_specs=[pl.BlockSpec(memory_space=pltpu.SMEM), whole, whole]
        + [pl.BlockSpec(memory_space=pl.ANY)]
        + [whole] * len(states),
        out_specs=[whole] * 2,
        out_shape=[
            jax.ShapeDtypeStruct(own.shape, F32),
            jax.ShapeDtypeStruct(own.shape, LINK),
        ],
        compiler_params=pltpu.CompilerParams(vmem_limit_bytes=FULL_VMEM_BYTES),
        cost_estimate=takes(0.1),
        name="pair_states",
    )(seq_index, coefs, own, lags, *states)


def local_kernel(q_ref, k_ref, v_ref, o_ref, coef_ref, gain_ref, part_ref):
    conv_ref, grad_ref = part_ref.at[0], part_ref.at[1]
    tok_rows, width = k_ref.shape
    tiles = width // LANES
    spread_tokens(k_ref, v_ref, conv_ref)
    spread_tokens(o_ref, q_ref, grad_ref)
    walk_tokens(conv_ref, coef_ref, tok_rows, tiles, 0, 1)
    walk_tokens(grad_ref, coef_ref, tok_rows, tiles, tok_rows - 1, -1)
    for tile in range(tiles):
        cols = slice(tile * LANES, (tile + 1) * LANES)
        rows = tile_rows(tok_rows, tile)
        gain = gain_ref[:, cols]
        conv_in = product(k_ref[:, cols], v_ref[:, cols]).astype(F32)
        conv_ref[rows, :] = conv_ref[rows, :] + gain * conv_in
        mid_grad = product(o_ref[:, cols], q_ref[:, cols]).astype(F32)
        grad_ref[rows, :] = grad_ref[rows, :] + gain * mid_grad


def local_parts(query_proj, key_proj, value_proj, out_grad, coefs, gain):
    tok_rows, width = key_proj.shape
    modes, tiles = coefs.shape[1:3]
    return pl.pallas_call(
        local_kernel,
        out_shape=jax.ShapeDtypeStruct((2, *token_shape(tok_rows, tiles)), F32),
        compiler_params=pltpu.CompilerParams(vmem_limit_bytes=VMEM_BYTES),
        cost_estimate=takes(6.5),
        name="local_parts",
    )(query_proj, key_proj, value_proj, out_grad, coefs, gain)


def along_column(state, pairs, k):
    route = [(2 * p + b, 2 * ((p + k) % pairs) + b) for p in range(pairs) for b in range(2)]
    return lax.ppermute(state, "seq", route)


def inside_pair(state, pairs):
    return lax.ppermute(state, "seq", [(i, i ^ 1) for i in range(2 * pairs)])


def fill_edge(ref, held, coef_ref, tok_rows, tiles, start, move):
    modes = coef_ref.shape[1]
    decay = [coef_ref[0, m] for m in range(modes)]

    def step(t, held):
        held = tuple(decay[m] * held[m] for m in range(modes))
        ref[token_place(start + move * t, tok_rows, tiles)] = tree_sum(list(held))
        return held

    held = tuple(coef_ref[2, m] * held[m] for m in range(modes))
    lax.fori_loop(0, tok_rows, step, held, unroll=8)


def final_kernel(
    coef_hbm, kept_hbm, given_hbm, part_hbm, q_hbm, v_hbm, k_hbm, layer_hbm, key_hbm, value_hbm,
    coef_ref, kept_ref, given_ref, part_ref, q_ref, v_ref, k_ref, edge_ref,
    layer_ref, key_ref, value_ref, in_sems, out_sems,
):
    tok_rows, width = k_ref.shape
    tiles = width // LANES
    modes = coef_ref.shape[1]
    arrivals = [
        pltpu.make_async_copy(source, target, in_sems.at[i])
        for i, (source, target) in enumerate(
            (
                (kept_hbm, kept_ref),
                (given_hbm, given_ref),
                (coef_hbm, coef_ref),
                (part_hbm.at[0], part_ref.at[0]),
                (q_hbm, q_ref),
                (part_hbm.at[1], part_ref.at[1]),
                (v_hbm, v_ref),
                (k_hbm, k_ref),
            )
        )
    ]

    def departure(i, tile):
        place = (slice(None), pl.ds(tile * LANES, LANES))
        return pltpu.make_async_copy(
            (layer_ref, key_ref, value_ref)[i].at[place],
            (layer_hbm, key_hbm, value_hbm)[i].at[place],
            out_sems.at[i, tile],
        )

    def edge(side):
        total = kept_ref[side] + given_ref[side].astype(F32)
        return [total[m * tiles : (m + 1) * tiles] for m in range(modes)]

    for copy in arrivals:
        copy.start()
    for copy in arrivals[:3]:
        copy.wait()
    fill_edge(edge_ref, edge(0), coef_ref, tok_rows, tiles, 0, 1)
    for copy in arrivals[3:5]:
        copy.wait()
    for tile in range(tiles):
        cols = slice(tile * LANES, (tile + 1) * LANES)
        rows = tile_rows(tok_rows, tile)
        long_conv = part_ref[0, rows, :] + edge_ref[rows, :]
        layer_ref[:, cols] = (q_ref[:, cols].astype(F32) * long_conv).astype(BF16)
        departure(0, tile).start()
    fill_edge(edge_ref, edge(1), coef_ref, tok_rows, tiles, tok_rows - 1, -1)
    for copy in arrivals[5:]:
        copy.wait()
    for tile in range(tiles):
        cols = slice(tile * LANES, (tile + 1) * LANES)
        rows = tile_rows(tok_rows, tile)
        conv_grad = part_ref[1, rows, :] + edge_ref[rows, :]
        key_ref[:, cols] = (conv_grad * v_ref[:, cols].astype(F32)).astype(BF16)
        departure(1, tile).start()
        value_ref[:, cols] = (conv_grad * k_ref[:, cols].astype(F32)).astype(BF16)
        departure(2, tile).start()
    for i in range(3):
        for tile in range(tiles):
            departure(i, tile).wait()


def final_outputs(query_proj, key_proj, value_proj, coefs, kept, given, parts):
    tok_rows, width = key_proj.shape
    tiles = coefs.shape[2]
    args = (coefs, kept, given, parts, query_proj, value_proj, key_proj)
    away = pl.BlockSpec(memory_space=pl.ANY)
    return pl.pallas_call(
        final_kernel,
        in_specs=[away] * len(args),
        out_specs=[away] * 3,
        out_shape=[jax.ShapeDtypeStruct((tok_rows, width), BF16)] * 3,
        scratch_shapes=[pltpu.VMEM(arg.shape, arg.dtype) for arg in args]
        + [pltpu.VMEM(parts.shape[1:], F32)]
        + [pltpu.VMEM((tok_rows, width), BF16)] * 3
        + [pltpu.SemaphoreType.DMA((len(args) + 1,)), pltpu.SemaphoreType.DMA((3, tiles))],
        compiler_params=pltpu.CompilerParams(vmem_limit_bytes=FULL_VMEM_BYTES),
        cost_estimate=takes(5.0),
        name="final_outputs",
    )(*args)


def lag_kernel(shards, chans, groups, owned, scale, *refs):
    in_refs, (out_ref, held, sems, u_all, g_all, turned_all) = refs[1:-6], refs[-6:]
    tok_rows = out_ref.shape[2]
    halves = tok_rows // LANES
    blocks = shards * halves
    depth = chans * groups
    full = blocks * depth
    if len(in_refs) == 1:
        take = chans * groups * owned

        def by_filter(row):
            return row % depth * owned + row // depth

        def arrival(s):
            place = pl.ds(s * chans, chans)
            return pltpu.make_async_copy(in_refs[0].at[place], held.at[place], sems.at[s])

        for s in range(shards):
            arrival(s).start()
        order = one_hot(take, take, by_filter)
        for s in range(shards):
            arrival(s).wait()
            for which, kept in enumerate((u_all, g_all)):
                rows = slice(which * groups * owned, (which + 1) * groups * owned)
                piece = held[s * chans : (s + 1) * chans, rows, :].reshape(take, tok_rows)
                piece = jnp.dot(order, piece, preferred_element_type=F32).astype(BF16)
                piece = piece.reshape(owned, depth, tok_rows)
                for h in range(halves):
                    first = (s * halves + h) * depth
                    kept[:, first : first + depth, :] = piece[:, :, h * LANES : (h + 1) * LANES]
    else:
        copies = [
            pltpu.make_async_copy(in_refs[0], u_all, sems.at[0]),
            pltpu.make_async_copy(in_refs[1], g_all.at[:, pl.ds(0, full), :], sems.at[1]),
        ]
        for copy in copies:
            copy.start()
        for copy in copies:
            copy.wait()
    g_all[:, full:, :] = jnp.zeros((owned, g_all.shape[1] - full, LANES), BF16)
    mirror = one_hot(LANES, LANES, lambda row: LANES - 1 - row)
    row = lax.broadcasted_iota(jnp.int32, (LANES, LANES), 0)
    col = lax.broadcasted_iota(jnp.int32, (LANES, LANES), 1)
    same_block = row + col >= LANES - 1
    filter_row = lax.broadcasted_iota(jnp.int32, (owned, LANES), 0)
    batch = min(blocks, 16)

    def one_filter(f, _):
        turned = turned_all[f]

        def some_lags(first):
            tables = []
            for d in range(0, batch, 2):
                live = full
                if batch == blocks:
                    live = min(full, -(-(blocks - d) * depth // LANES) * LANES)
                pair = jnp.concatenate(
                    [
                        g_all[f, pl.ds(pl.multiple_of((first + d + e) * depth, depth), live), :]
                        for e in range(2)
                    ],
                    axis=1,
                )
                table = jnp.dot(turned[:, :live], pair, preferred_element_type=F32)
                tables += [table[:, :LANES], table[:, LANES:]]
            last = g_all[f, pl.ds(pl.multiple_of((first + batch) * depth, depth), full), :]
            if batch < blocks:
                tables.append(jnp.dot(turned, last, preferred_element_type=F32))
            else:
                tables.append(jnp.zeros((LANES, LANES), F32))
            for d in range(batch):
                joined = jnp.where(same_block, tables[d], tables[d + 1])
                skewed = pltpu.roll(joined, 1, 1, stride=1, stride_axis=0)
                sums = jnp.sum(skewed, axis=0, keepdims=True) * scale
                lane = d % halves * LANES
                place = ((first + d) // halves, slice(None), slice(lane, lane + LANES))
                out_ref[place] = jnp.where(filter_row == f, sums, out_ref[place])

        if batch == blocks:
            some_lags(0)
        else:
            lax.fori_loop(0, blocks // batch, lambda i, c: (some_lags(i * batch), c)[1], 0)
        return 0

    for f in range(owned):
        turned_all[f] = lax.dot_general(
            mirror, u_all[f], (((1,), (1,)), ((), ())), preferred_element_type=F32
        ).astype(BF16)
    lax.fori_loop(0, owned, one_filter, 0, unroll=min(owned, 4))


def filter_lags(received, parts, shards, chans, owned, scale):
    tok_rows = received.shape[2]
    groups = received.shape[1] // (2 * owned)
    halves = tok_rows // LANES
    depth = chans * groups
    full = shards * halves * depth
    args = (received,)
    if owned % SUBLANES:
        split = received.reshape(shards, chans, 2, groups, owned, halves, LANES)
        split = split.transpose(2, 4, 0, 5, 1, 3, 6).reshape(2, owned, full, LANES)
        args = (split[0], split[1])
    away = pl.BlockSpec(memory_space=pl.ANY)
    return pl.pallas_call(
        functools.partial(lag_kernel, shards, chans, groups, owned, scale),
        in_specs=[away] * (len(args) + 1),
        out_specs=pl.BlockSpec(memory_space=pltpu.VMEM),
        out_shape=jax.ShapeDtypeStruct((shards, owned, tok_rows), F32),
        scratch_shapes=[
            pltpu.VMEM(received.shape if len(args) == 1 else (SUBLANES, LANES), BF16),
            pltpu.SemaphoreType.DMA((max(shards, 2),)),
            pltpu.VMEM((owned, full, LANES), BF16),
            pltpu.VMEM((owned, 2 * full + depth, LANES), BF16),
            pltpu.VMEM((owned, LANES, full), BF16),
        ],
        compiler_params=pltpu.CompilerParams(vmem_limit_bytes=VMEM_BYTES),
        cost_estimate=takes(0.1),
        name="filter_lags",
    )(parts, *args)


def per_device(query_proj, key_proj, value_proj, out_grad, residues, decay_rate, skip_gain):
    tok_rows, width = key_proj.shape
    shards = lax.axis_size("seq")
    chans = lax.axis_size("chan")
    length = shards * tok_rows
    owned = FILTERS // (shards * chans)
    modes = residues.shape[1]
    signals = (query_proj, key_proj, value_proj, out_grad)

    send = pack_signals(shards, chans, owned, *signals)
    send, *signals, residues, decay_rate = lax.optimization_barrier(
        (send, *signals, residues, decay_rate)
    )
    received = lax.all_to_all(send, ("seq", "chan"), split_axis=0, concat_axis=0, tiled=True)

    coefs = jnp.stack(
        [
            jnp.exp(-decay_rate),
            jnp.exp(-(decay_rate * float(tok_rows))),
            residues * jnp.sqrt(decay_rate),
        ]
    )
    coefs = coefs.transpose(0, 2, 1).reshape(3, modes, 1, FILTERS // LANES, LANES)
    coefs = jnp.broadcast_to(coefs, (3, modes, width // FILTERS, FILTERS // LANES, LANES))
    coefs = coefs.reshape(3, modes, width // LANES, LANES)
    seq_index = lax.axis_index("seq").reshape(1)
    pairs = shards // 2
    states, own = block_states(seq_index, pairs, *signals, coefs)
    *states, coefs = lax.optimization_barrier((*states, coefs))
    states = [along_column(state, pairs, 1 + i) for i, state in enumerate(states)]
    parts = local_parts(*signals, coefs, skip_gain[None, :])
    scale = 1.0 / math.sqrt(length * (CHANNELS // FILTERS))
    lags = filter_lags(received, parts, shards, chans, owned, scale)
    kept, given = pair_states(seq_index, coefs, own, lags, states)
    given = inside_pair(given, pairs)
    lags = lax.all_to_all(lags, "seq", split_axis=0, concat_axis=0, tiled=True)
    filter_grad = lags.reshape(shards * owned, tok_rows).T
    layer_out, key_grad, value_grad = final_outputs(
        *signals[:3], coefs, kept, given, parts
    )
    return (layer_out, key_grad, value_grad, filter_grad)


def solution(mesh):
    split = P("seq", "chan")
    return jax.shard_map(
        per_device,
        mesh=mesh,
        in_specs=(split, split, split, split, P(), P(), P("chan")),
        out_specs=(split, split, split, split),
        check_vma=False,
    )
```

```python
import functools
import math

import jax
import jax.numpy as jnp
from jax import lax
from jax.experimental import pallas as pl
from jax.experimental.pallas import tpu as pltpu
from jax.sharding import PartitionSpec as P

CHANNELS = 4096
FILTERS = 256
LANES = 128
SUBLANES = 8
GAP = 8
VMEM_BYTES = 16 * 1024 * 1024
PACK_VMEM_BYTES = 62 * 1024 * 1024
F32 = jnp.float32
BF16 = jnp.bfloat16
LINK = jnp.bfloat16


def takes(micros):
    return pl.CostEstimate(flops=0, bytes_accessed=int(micros * 3.6e6), transcendentals=0)


def product(first, second):
    return (first.astype(F32) * second.astype(F32)).astype(BF16)


def one_hot(rows, cols, column_of):
    row = lax.broadcasted_iota(jnp.int32, (rows, cols), 0)
    col = lax.broadcasted_iota(jnp.int32, (rows, cols), 1)
    return (col == column_of(row)).astype(F32).astype(BF16)


def pack_kernel(shards, chans, owned, *refs):
    hbm_refs, send_ref, held, packed, in_sems, out_sems = refs[:4], *refs[4:]
    tok_rows, width = held.shape[1:]
    groups = width // FILTERS
    per_chan = FILTERS // chans
    units = [(which, first) for which in range(2) for first in range(0, groups, 2)]

    def arrival(i, first):
        place = (slice(None), pl.ds(first * FILTERS, 2 * FILTERS))
        return pltpu.make_async_copy(
            hbm_refs[i].at[place], held.at[(i, *place)], in_sems.at[i, first // 2]
        )

    def departure(which, first):
        if owned % SUBLANES:
            place = (which, pl.ds(first, 2))
        else:
            place = (slice(None), pl.ds((which * groups + first) * owned, 2 * owned))
        return pltpu.make_async_copy(
            packed.at[place], send_ref.at[place], out_sems.at[which, first // 2]
        )

    for which, first in units:
        for i in (2 * which, 2 * which + 1):
            arrival(i, first).start()

    def owned_filter(row):
        seq = row // (chans * owned)
        chan = row // owned % chans
        return chan * per_chan + seq * owned + row % owned

    order = one_hot(FILTERS, FILTERS, owned_filter)
    for which, first in units:
        for i in (2 * which, 2 * which + 1):
            arrival(i, first).wait()
        pieces = []
        for group in (first, first + 1):
            cols = slice(group * FILTERS, (group + 1) * FILTERS)
            piece = lax.dot_general(
                order,
                product(held[2 * which, :, cols], held[2 * which + 1, :, cols]),
                (((1,), (1,)), ((), ())),
                preferred_element_type=F32,
            )
            if owned % SUBLANES:
                packed[which, group] = piece.astype(BF16)
            else:
                pieces.append(piece.reshape(shards * chans, owned, tok_rows))
        if pieces:
            row = (which * groups + first) * owned
            packed[:, row : row + 2 * owned, :] = jnp.concatenate(pieces, axis=1).astype(BF16)
        departure(which, first).start()
    for which, first in units:
        departure(which, first).wait()


def pack_signals(shards, chans, owned, query_proj, key_proj, value_proj, out_grad):
    tok_rows, width = key_proj.shape
    groups = width // FILTERS
    dests = shards * chans
    if owned % SUBLANES:
        shape = (2, groups, FILTERS, tok_rows)
    else:
        shape = (dests, 2 * groups * owned, tok_rows)
    send = pl.pallas_call(
        functools.partial(pack_kernel, shards, chans, owned),
        in_specs=[pl.BlockSpec(memory_space=pl.ANY)] * 4,
        out_specs=pl.BlockSpec(memory_space=pl.ANY),
        out_shape=jax.ShapeDtypeStruct(shape, BF16),
        scratch_shapes=[
            pltpu.VMEM((4, tok_rows, width), BF16),
            pltpu.VMEM(shape, BF16),
            pltpu.SemaphoreType.DMA((4, groups // 2)),
            pltpu.SemaphoreType.DMA((2, groups // 2)),
        ],
        compiler_params=pltpu.CompilerParams(vmem_limit_bytes=PACK_VMEM_BYTES),
        cost_estimate=takes(3.0),
        name="pack_signals",
    )(key_proj, value_proj, out_grad, query_proj)
    if owned % SUBLANES:
        send = send.reshape(2, groups, dests, owned, tok_rows)
        send = send.transpose(2, 0, 1, 3, 4).reshape(dests, 2 * groups * owned, tok_rows)
    return send


def tile_rows(tok_rows, tile):
    first = tile * (tok_rows + GAP)
    return slice(first, first + tok_rows)


def token_shape(tok_rows, tiles):
    return (tiles * (tok_rows + GAP), LANES)


def token_place(t, tok_rows, tiles):
    return (pl.ds(t, tiles, stride=tok_rows + GAP), slice(None))


def spread_tokens(a_ref, b_ref, x_ref):
    tok_rows, width = a_ref.shape
    for tile in range(width // LANES):
        cols = slice(tile * LANES, (tile + 1) * LANES)
        x_ref[tile_rows(tok_rows, tile), :] = product(a_ref[:, cols], b_ref[:, cols]).astype(F32)


def walk_tokens(ref, coef_ref, tok_rows, tiles, start, move):
    modes = coef_ref.shape[1]
    decay = [coef_ref[0, m] for m in range(modes)]
    weight = [coef_ref[2, m] for m in range(modes)]

    def step(t, held):
        place = token_place(start + move * t, tok_rows, tiles)
        x = ref[place]
        held = tuple(decay[m] * held[m] + x for m in range(modes))
        ref[place] = tree_sum([weight[m] * held[m] for m in range(modes)])
        return held

    zero = tuple(jnp.zeros((tiles, LANES), F32) for _ in range(modes))
    return lax.fori_loop(0, tok_rows, step, zero, unroll=8)


def tree_sum(terms):
    while len(terms) > 1:
        terms = [sum(terms[i : i + 2][1:], terms[i]) for i in range(0, len(terms), 2)]
    return terms[0]


def state_kernel(seq_ref, q_ref, k_ref, v_ref, o_ref, coef_ref, *refs):
    state_refs, own_ref, x_ref, g_ref = refs[:-3], *refs[-3:]
    tok_rows, width = k_ref.shape
    tiles = width // LANES
    modes = coef_ref.shape[1]
    pairs = len(state_refs) + 1
    spread_tokens(k_ref, v_ref, x_ref)
    spread_tokens(o_ref, q_ref, g_ref)
    decay = [coef_ref[0, m] for m in range(modes)]

    def step(t, carry):
        x = x_ref[token_place(t, tok_rows, tiles)]
        g = g_ref[token_place(tok_rows - 1 - t, tok_rows, tiles)]
        ahead = tuple(decay[m] * carry[0][m] + x for m in range(modes))
        behind = tuple(decay[m] * carry[1][m] + g for m in range(modes))
        return (ahead, behind)

    zero = tuple(jnp.zeros((tiles, LANES), F32) for _ in range(modes))
    ahead, behind = lax.fori_loop(0, tok_rows, step, (zero, zero), unroll=8)
    ahead = jnp.concatenate(ahead, axis=0)
    behind = jnp.concatenate(behind, axis=0)
    own_ref[0] = ahead
    own_ref[1] = behind
    for k in range(1, pairs):
        stays = seq_ref[0] // 2 + k < pairs

        @pl.when(stays)
        def _():
            state_refs[k - 1][...] = ahead.astype(LINK)

        @pl.when(jnp.logical_not(stays))
        def _():
            state_refs[k - 1][...] = behind.astype(LINK)


def block_states(seq_index, pairs, query_proj, key_proj, value_proj, out_grad, coefs):
    tok_rows, width = key_proj.shape
    modes, tiles = coefs.shape[1:3]
    whole = pl.BlockSpec(memory_space=pltpu.VMEM)
    *states, own = pl.pallas_call(
        state_kernel,
        in_specs=[pl.BlockSpec(memory_space=pltpu.SMEM)] + [whole] * 5,
        out_specs=[whole] * pairs,
        out_shape=[jax.ShapeDtypeStruct((modes * tiles, LANES), LINK)] * (pairs - 1)
        + [jax.ShapeDtypeStruct((2, modes * tiles, LANES), F32)],
        scratch_shapes=[pltpu.VMEM(token_shape(tok_rows, tiles), F32)] * 2,
        compiler_params=pltpu.CompilerParams(vmem_limit_bytes=VMEM_BYTES),
        cost_estimate=takes(3.0),
        name="block_states",
    )(seq_index, query_proj, key_proj, value_proj, out_grad, coefs)
    return states, own


def pair_kernel(seq_ref, coef_ref, own_ref, *refs):
    state_refs, kept_ref, given_ref = refs[2:-2], *refs[-2:]
    pairs = len(state_refs) + 1
    modes, tiles = coef_ref.shape[1:3]
    pair = seq_ref[0] // 2
    second = seq_ref[0] % 2 == 1
    for m in range(modes):
        rows = slice(m * tiles, (m + 1) * tiles)
        decay = coef_ref[1, m]
        both = decay * decay
        before = jnp.zeros((tiles, LANES), F32)
        after = jnp.zeros((tiles, LANES), F32)
        for k in range(pairs - 1, 0, -1):
            block = state_refs[k - 1][...].astype(F32)[rows]
            before = both * before + jnp.where(k <= pair, block, 0.0)
            block = state_refs[pairs - k - 1][...].astype(F32)[rows]
            after = both * after + jnp.where(k <= pairs - 1 - pair, block, 0.0)
        before = jnp.where(second, before, decay * before)
        after = jnp.where(second, decay * after, after)
        kept_ref[0, rows] = jnp.where(second, decay * before, before)
        kept_ref[1, rows] = jnp.where(second, after, decay * after)
        own = own_ref[0, rows]
        given_ref[0, rows] = jnp.where(second, before, decay * before + own).astype(LINK)
        own = own_ref[1, rows]
        given_ref[1, rows] = jnp.where(second, decay * after + own, after).astype(LINK)


def pair_states(seq_index, coefs, own, parts, states):
    whole = pl.BlockSpec(memory_space=pltpu.VMEM)
    return pl.pallas_call(
        pair_kernel,
        in_specs=[pl.BlockSpec(memory_space=pltpu.SMEM), whole, whole]
        + [pl.BlockSpec(memory_space=pl.ANY)] * len(parts)
        + [whole] * len(states),
        out_specs=[whole] * 2,
        out_shape=[
            jax.ShapeDtypeStruct(own.shape, F32),
            jax.ShapeDtypeStruct(own.shape, LINK),
        ],
        compiler_params=pltpu.CompilerParams(vmem_limit_bytes=VMEM_BYTES),
        cost_estimate=takes(0.1),
        name="pair_states",
    )(seq_index, coefs, own, *parts, *states)


def local_kernel(
    q_ref, k_ref, v_ref, o_ref, coef_ref, gain_ref, conv_ref, grad_ref, x_ref, g_ref
):
    tok_rows, width = k_ref.shape
    tiles = width // LANES
    spread_tokens(k_ref, v_ref, x_ref)
    spread_tokens(o_ref, q_ref, g_ref)
    walk_tokens(x_ref, coef_ref, tok_rows, tiles, 0, 1)
    walk_tokens(g_ref, coef_ref, tok_rows, tiles, tok_rows - 1, -1)
    for tile in range(tiles):
        cols = slice(tile * LANES, (tile + 1) * LANES)
        rows = tile_rows(tok_rows, tile)
        gain = gain_ref[:, cols]
        conv_in = product(k_ref[:, cols], v_ref[:, cols]).astype(F32)
        conv_ref[:, cols] = (x_ref[rows, :] + gain * conv_in).astype(BF16)
        mid_grad = product(o_ref[:, cols], q_ref[:, cols]).astype(F32)
        grad_ref[:, cols] = (g_ref[rows, :] + gain * mid_grad).astype(BF16)


def local_parts(query_proj, key_proj, value_proj, out_grad, coefs, gain):
    tok_rows, width = key_proj.shape
    tiles = coefs.shape[2]
    return pl.pallas_call(
        local_kernel,
        out_shape=[jax.ShapeDtypeStruct((tok_rows, width), BF16)] * 2,
        scratch_shapes=[pltpu.VMEM(token_shape(tok_rows, tiles), F32)] * 2,
        compiler_params=pltpu.CompilerParams(vmem_limit_bytes=VMEM_BYTES),
        cost_estimate=takes(6.5),
        name="local_parts",
    )(query_proj, key_proj, value_proj, out_grad, coefs, gain)


def along_column(state, pairs, k):
    route = [(2 * p + b, 2 * ((p + k) % pairs) + b) for p in range(pairs) for b in range(2)]
    return lax.ppermute(state, "seq", route)


def inside_pair(state, pairs):
    return lax.ppermute(state, "seq", [(i, i ^ 1) for i in range(2 * pairs)])


def fill_edge(ref, held, coef_ref, tok_rows, tiles, start, move):
    modes = coef_ref.shape[1]
    decay = [coef_ref[0, m] for m in range(modes)]

    def step(t, held):
        held = tuple(decay[m] * held[m] for m in range(modes))
        ref[token_place(start + move * t, tok_rows, tiles)] = tree_sum(list(held))
        return held

    held = tuple(coef_ref[2, m] * held[m] for m in range(modes))
    lax.fori_loop(0, tok_rows, step, held, unroll=8)


def final_kernel(
    q_ref, k_ref, v_ref, conv_ref, grad_ref, coef_ref, kept_ref, given_ref,
    layer_hbm, key_hbm, value_hbm, edge_ref, layer_ref, key_ref, value_ref, sems,
):
    tok_rows, width = k_ref.shape
    tiles = width // LANES
    modes = coef_ref.shape[1]

    def departure(i, tile):
        place = (slice(None), pl.ds(tile * LANES, LANES))
        return pltpu.make_async_copy(
            (layer_ref, key_ref, value_ref)[i].at[place],
            (layer_hbm, key_hbm, value_hbm)[i].at[place],
            sems.at[i, tile],
        )

    def edge(side):
        total = kept_ref[side] + given_ref[side].astype(F32)
        return [total[m * tiles : (m + 1) * tiles] for m in range(modes)]

    fill_edge(edge_ref, edge(0), coef_ref, tok_rows, tiles, 0, 1)
    for tile in range(tiles):
        cols = slice(tile * LANES, (tile + 1) * LANES)
        long_conv = conv_ref[:, cols].astype(F32) + edge_ref[tile_rows(tok_rows, tile), :]
        layer_ref[:, cols] = (q_ref[:, cols].astype(F32) * long_conv).astype(BF16)
        departure(0, tile).start()
    fill_edge(edge_ref, edge(1), coef_ref, tok_rows, tiles, tok_rows - 1, -1)
    for tile in range(tiles):
        cols = slice(tile * LANES, (tile + 1) * LANES)
        conv_grad = grad_ref[:, cols].astype(F32) + edge_ref[tile_rows(tok_rows, tile), :]
        key_ref[:, cols] = (conv_grad * v_ref[:, cols].astype(F32)).astype(BF16)
        departure(1, tile).start()
        value_ref[:, cols] = (conv_grad * k_ref[:, cols].astype(F32)).astype(BF16)
        departure(2, tile).start()
    for i in range(3):
        for tile in range(tiles):
            departure(i, tile).wait()


def final_outputs(signals, parts, coefs, kept, given):
    tok_rows, width = signals[0].shape
    tiles = coefs.shape[2]
    args = (*signals, *parts, coefs, kept, given)
    return pl.pallas_call(
        final_kernel,
        in_specs=[pl.BlockSpec(memory_space=pltpu.VMEM)] * len(args),
        out_specs=[pl.BlockSpec(memory_space=pl.ANY)] * 3,
        out_shape=[jax.ShapeDtypeStruct((tok_rows, width), BF16)] * 3,
        scratch_shapes=[pltpu.VMEM(token_shape(tok_rows, tiles), F32)]
        + [pltpu.VMEM((tok_rows, width), BF16)] * 3
        + [pltpu.SemaphoreType.DMA((3, tiles))],
        compiler_params=pltpu.CompilerParams(vmem_limit_bytes=VMEM_BYTES),
        cost_estimate=takes(4.0),
        name="final_outputs",
    )(*args)


def lag_kernel(shards, chans, groups, owned, scale, *refs):
    in_refs, (out_ref, u_all, g_all, turned_all) = refs[:-4], refs[-4:]
    tok_rows = out_ref.shape[2]
    halves = tok_rows // LANES
    blocks = shards * halves
    depth = chans * groups
    full = blocks * depth
    if len(in_refs) == 1:
        take = chans * groups * owned

        def by_filter(row):
            return row % depth * owned + row // depth

        order = one_hot(take, take, by_filter)
        for which, kept in enumerate((u_all, g_all)):
            rows = slice(which * groups * owned, (which + 1) * groups * owned)
            for s in range(shards):
                piece = in_refs[0][s * chans : (s + 1) * chans, rows, :].reshape(take, tok_rows)
                piece = jnp.dot(order, piece, preferred_element_type=F32).astype(BF16)
                piece = piece.reshape(owned, depth, tok_rows)
                for h in range(halves):
                    first = (s * halves + h) * depth
                    kept[:, first : first + depth, :] = piece[:, :, h * LANES : (h + 1) * LANES]
    else:
        u_all[...] = in_refs[0][...]
        g_all[:, :full, :] = in_refs[1][...]
    g_all[:, full:, :] = jnp.zeros((owned, g_all.shape[1] - full, LANES), BF16)
    mirror = one_hot(LANES, LANES, lambda row: LANES - 1 - row)
    row = lax.broadcasted_iota(jnp.int32, (LANES, LANES), 0)
    col = lax.broadcasted_iota(jnp.int32, (LANES, LANES), 1)
    same_block = row + col >= LANES - 1
    filter_row = lax.broadcasted_iota(jnp.int32, (owned, LANES), 0)
    batch = min(blocks, 16)

    def one_filter(f, _):
        turned = turned_all[f]

        def some_lags(first):
            tables = []
            for d in range(0, batch, 2):
                live = full
                if batch == blocks:
                    live = min(full, -(-(blocks - d) * depth // LANES) * LANES)
                pair = jnp.concatenate(
                    [
                        g_all[f, pl.ds(pl.multiple_of((first + d + e) * depth, depth), live), :]
                        for e in range(2)
                    ],
                    axis=1,
                )
                table = jnp.dot(turned[:, :live], pair, preferred_element_type=F32)
                tables += [table[:, :LANES], table[:, LANES:]]
            last = g_all[f, pl.ds(pl.multiple_of((first + batch) * depth, depth), full), :]
            if batch < blocks:
                tables.append(jnp.dot(turned, last, preferred_element_type=F32))
            else:
                tables.append(jnp.zeros((LANES, LANES), F32))
            for d in range(batch):
                joined = jnp.where(same_block, tables[d], tables[d + 1])
                skewed = pltpu.roll(joined, 1, 1, stride=1, stride_axis=0)
                sums = jnp.sum(skewed, axis=0, keepdims=True) * scale
                lane = d % halves * LANES
                place = ((first + d) // halves, slice(None), slice(lane, lane + LANES))
                out_ref[place] = jnp.where(filter_row == f, sums, out_ref[place])

        if batch == blocks:
            some_lags(0)
        else:
            lax.fori_loop(0, blocks // batch, lambda i, c: (some_lags(i * batch), c)[1], 0)
        return 0

    for f in range(owned):
        turned_all[f] = lax.dot_general(
            mirror, u_all[f], (((1,), (1,)), ((), ())), preferred_element_type=F32
        ).astype(BF16)
    lax.fori_loop(0, owned, one_filter, 0, unroll=min(owned, 4))


def filter_lags(received, shards, chans, owned, scale):
    tok_rows = received.shape[2]
    groups = received.shape[1] // (2 * owned)
    halves = tok_rows // LANES
    depth = chans * groups
    full = shards * halves * depth
    args = (received,)
    if owned % SUBLANES:
        split = received.reshape(shards, chans, 2, groups, owned, halves, LANES)
        split = split.transpose(2, 4, 0, 5, 1, 3, 6).reshape(2, owned, full, LANES)
        args = (split[0], split[1])
    return pl.pallas_call(
        functools.partial(lag_kernel, shards, chans, groups, owned, scale),
        out_shape=jax.ShapeDtypeStruct((shards, owned, tok_rows), F32),
        scratch_shapes=[
            pltpu.VMEM((owned, full, LANES), BF16),
            pltpu.VMEM((owned, 2 * full + depth, LANES), BF16),
            pltpu.VMEM((owned, LANES, full), BF16),
        ],
        compiler_params=pltpu.CompilerParams(vmem_limit_bytes=VMEM_BYTES),
        cost_estimate=takes(4.0),
        name="filter_lags",
    )(*args)


def per_device(query_proj, key_proj, value_proj, out_grad, residues, decay_rate, skip_gain):
    tok_rows, width = key_proj.shape
    shards = lax.axis_size("seq")
    chans = lax.axis_size("chan")
    length = shards * tok_rows
    owned = FILTERS // (shards * chans)
    modes = residues.shape[1]
    signals = (query_proj, key_proj, value_proj, out_grad)

    send = pack_signals(shards, chans, owned, *signals)
    send, *signals, residues, decay_rate = lax.optimization_barrier(
        (send, *signals, residues, decay_rate)
    )
    received = lax.all_to_all(send, ("seq", "chan"), split_axis=0, concat_axis=0, tiled=True)

    coefs = jnp.stack(
        [
            jnp.exp(-decay_rate),
            jnp.exp(-(decay_rate * float(tok_rows))),
            residues * jnp.sqrt(decay_rate),
        ]
    )
    coefs = coefs.transpose(0, 2, 1).reshape(3, modes, 1, FILTERS // LANES, LANES)
    coefs = jnp.broadcast_to(coefs, (3, modes, width // FILTERS, FILTERS // LANES, LANES))
    coefs = coefs.reshape(3, modes, width // LANES, LANES)
    seq_index = lax.axis_index("seq").reshape(1)
    pairs = shards // 2
    states, own = block_states(seq_index, pairs, *signals, coefs)
    *states, coefs = lax.optimization_barrier((*states, coefs))
    states = [along_column(state, pairs, 1 + i) for i, state in enumerate(states)]
    parts = local_parts(*signals, coefs, skip_gain[None, :])
    kept, given = pair_states(seq_index, coefs, own, parts, states)
    received, kept, given = lax.optimization_barrier((received, kept, given))
    given = inside_pair(given, pairs)

    scale = 1.0 / math.sqrt(length * (CHANNELS // FILTERS))
    lags = filter_lags(received, shards, chans, owned, scale)
    lags, given = lax.optimization_barrier((lags, given))
    lags = lax.all_to_all(lags, "seq", split_axis=0, concat_axis=0, tiled=True)
    filter_grad = lags.reshape(shards * owned, tok_rows).T
    layer_out, key_grad, value_grad = final_outputs(
        signals[:3], parts, coefs, kept, given
    )
    return (layer_out, key_grad, value_grad, filter_grad)


def solution(mesh):
    split = P("seq", "chan")
    return jax.shard_map(
        per_device,
        mesh=mesh,
        in_specs=(split, split, split, split, P(), P(), P("chan")),
        out_specs=(split, split, split, split),
        check_vma=False,
    )
```

```python
import functools
import math

import jax
import jax.numpy as jnp
from jax import lax
from jax.experimental import pallas as pl
from jax.experimental.pallas import tpu as pltpu
from jax.sharding import PartitionSpec as P

CHANNELS = 4096
FILTERS = 256
LANES = 128
SUBLANES = 8
GAP = 8
VMEM_BYTES = 16 * 1024 * 1024
PACK_VMEM_BYTES = 62 * 1024 * 1024
F32 = jnp.float32
BF16 = jnp.bfloat16
LINK = jnp.bfloat16


def takes(micros):
    return pl.CostEstimate(flops=0, bytes_accessed=int(micros * 3.6e6), transcendentals=0)


def product(first, second):
    return (first.astype(F32) * second.astype(F32)).astype(BF16)


def one_hot(rows, cols, column_of):
    row = lax.broadcasted_iota(jnp.int32, (rows, cols), 0)
    col = lax.broadcasted_iota(jnp.int32, (rows, cols), 1)
    return (col == column_of(row)).astype(F32).astype(BF16)


def pack_kernel(shards, chans, owned, *refs):
    hbm_refs, send_ref, held, packed, in_sems, out_sems = refs[:4], *refs[4:]
    tok_rows, width = held.shape[1:]
    groups = width // FILTERS
    per_chan = FILTERS // chans
    units = [(which, first) for which in range(2) for first in range(0, groups, 2)]

    def arrival(i, first):
        place = (slice(None), pl.ds(first * FILTERS, 2 * FILTERS))
        return pltpu.make_async_copy(
            hbm_refs[i].at[place], held.at[(i, *place)], in_sems.at[i, first // 2]
        )

    def departure(which, first):
        if owned % SUBLANES:
            place = (which, pl.ds(first, 2))
        else:
            place = (slice(None), pl.ds((which * groups + first) * owned, 2 * owned))
        return pltpu.make_async_copy(
            packed.at[place], send_ref.at[place], out_sems.at[which, first // 2]
        )

    for which, first in units:
        for i in (2 * which, 2 * which + 1):
            arrival(i, first).start()

    def owned_filter(row):
        seq = row // (chans * owned)
        chan = row // owned % chans
        return chan * per_chan + seq * owned + row % owned

    order = one_hot(FILTERS, FILTERS, owned_filter)
    for which, first in units:
        for i in (2 * which, 2 * which + 1):
            arrival(i, first).wait()
        pieces = []
        for group in (first, first + 1):
            cols = slice(group * FILTERS, (group + 1) * FILTERS)
            piece = lax.dot_general(
                order,
                product(held[2 * which, :, cols], held[2 * which + 1, :, cols]),
                (((1,), (1,)), ((), ())),
                preferred_element_type=F32,
            )
            if owned % SUBLANES:
                packed[which, group] = piece.astype(BF16)
            else:
                pieces.append(piece.reshape(shards * chans, owned, tok_rows))
        if pieces:
            row = (which * groups + first) * owned
            packed[:, row : row + 2 * owned, :] = jnp.concatenate(pieces, axis=1).astype(BF16)
        departure(which, first).start()
    for which, first in units:
        departure(which, first).wait()


def pack_signals(shards, chans, owned, query_proj, key_proj, value_proj, out_grad):
    tok_rows, width = key_proj.shape
    groups = width // FILTERS
    dests = shards * chans
    if owned % SUBLANES:
        shape = (2, groups, FILTERS, tok_rows)
    else:
        shape = (dests, 2 * groups * owned, tok_rows)
    send = pl.pallas_call(
        functools.partial(pack_kernel, shards, chans, owned),
        in_specs=[pl.BlockSpec(memory_space=pl.ANY)] * 4,
        out_specs=pl.BlockSpec(memory_space=pl.ANY),
        out_shape=jax.ShapeDtypeStruct(shape, BF16),
        scratch_shapes=[
            pltpu.VMEM((4, tok_rows, width), BF16),
            pltpu.VMEM(shape, BF16),
            pltpu.SemaphoreType.DMA((4, groups // 2)),
            pltpu.SemaphoreType.DMA((2, groups // 2)),
        ],
        compiler_params=pltpu.CompilerParams(vmem_limit_bytes=PACK_VMEM_BYTES),
        cost_estimate=takes(3.0),
        name="pack_signals",
    )(key_proj, value_proj, out_grad, query_proj)
    if owned % SUBLANES:
        send = send.reshape(2, groups, dests, owned, tok_rows)
        send = send.transpose(2, 0, 1, 3, 4).reshape(dests, 2 * groups * owned, tok_rows)
    return send


def tile_rows(tok_rows, tile):
    first = tile * (tok_rows + GAP)
    return slice(first, first + tok_rows)


def token_shape(tok_rows, tiles):
    return (tiles * (tok_rows + GAP), LANES)


def token_place(t, tok_rows, tiles):
    return (pl.ds(t, tiles, stride=tok_rows + GAP), slice(None))


def spread_tokens(a_ref, b_ref, x_ref):
    tok_rows, width = a_ref.shape
    for tile in range(width // LANES):
        cols = slice(tile * LANES, (tile + 1) * LANES)
        x_ref[tile_rows(tok_rows, tile), :] = product(a_ref[:, cols], b_ref[:, cols]).astype(F32)


def walk_tokens(ref, coef_ref, tok_rows, tiles, start, move):
    modes = coef_ref.shape[1]
    decay = [coef_ref[0, m] for m in range(modes)]
    weight = [coef_ref[2, m] for m in range(modes)]

    def step(t, held):
        place = token_place(start + move * t, tok_rows, tiles)
        x = ref[place]
        held = tuple(decay[m] * held[m] + x for m in range(modes))
        ref[place] = tree_sum([weight[m] * held[m] for m in range(modes)])
        return held

    zero = tuple(jnp.zeros((tiles, LANES), F32) for _ in range(modes))
    return lax.fori_loop(0, tok_rows, step, zero, unroll=8)


def tree_sum(terms):
    while len(terms) > 1:
        terms = [sum(terms[i : i + 2][1:], terms[i]) for i in range(0, len(terms), 2)]
    return terms[0]


def state_kernel(seq_ref, q_ref, k_ref, v_ref, o_ref, coef_ref, *refs):
    state_refs, own_ref, x_ref, g_ref = refs[:-3], *refs[-3:]
    tok_rows, width = k_ref.shape
    tiles = width // LANES
    modes = coef_ref.shape[1]
    pairs = len(state_refs) + 1
    spread_tokens(k_ref, v_ref, x_ref)
    spread_tokens(o_ref, q_ref, g_ref)
    decay = [coef_ref[0, m] for m in range(modes)]

    def step(t, carry):
        x = x_ref[token_place(t, tok_rows, tiles)]
        g = g_ref[token_place(tok_rows - 1 - t, tok_rows, tiles)]
        ahead = tuple(decay[m] * carry[0][m] + x for m in range(modes))
        behind = tuple(decay[m] * carry[1][m] + g for m in range(modes))
        return (ahead, behind)

    zero = tuple(jnp.zeros((tiles, LANES), F32) for _ in range(modes))
    ahead, behind = lax.fori_loop(0, tok_rows, step, (zero, zero), unroll=8)
    ahead = jnp.concatenate(ahead, axis=0)
    behind = jnp.concatenate(behind, axis=0)
    own_ref[0] = ahead
    own_ref[1] = behind
    for k in range(1, pairs):
        stays = seq_ref[0] // 2 + k < pairs

        @pl.when(stays)
        def _():
            state_refs[k - 1][...] = ahead.astype(LINK)

        @pl.when(jnp.logical_not(stays))
        def _():
            state_refs[k - 1][...] = behind.astype(LINK)


def block_states(seq_index, pairs, query_proj, key_proj, value_proj, out_grad, coefs):
    tok_rows, width = key_proj.shape
    modes, tiles = coefs.shape[1:3]
    whole = pl.BlockSpec(memory_space=pltpu.VMEM)
    *states, own = pl.pallas_call(
        state_kernel,
        in_specs=[pl.BlockSpec(memory_space=pltpu.SMEM)] + [whole] * 5,
        out_specs=[whole] * pairs,
        out_shape=[jax.ShapeDtypeStruct((modes * tiles, LANES), LINK)] * (pairs - 1)
        + [jax.ShapeDtypeStruct((2, modes * tiles, LANES), F32)],
        scratch_shapes=[pltpu.VMEM(token_shape(tok_rows, tiles), F32)] * 2,
        compiler_params=pltpu.CompilerParams(vmem_limit_bytes=VMEM_BYTES),
        cost_estimate=takes(3.0),
        name="block_states",
    )(seq_index, query_proj, key_proj, value_proj, out_grad, coefs)
    return states, own


def pair_kernel(seq_ref, coef_ref, own_ref, _, *refs):
    state_refs, kept_ref, given_ref = refs[:-2], *refs[-2:]
    pairs = len(state_refs) + 1
    modes, tiles = coef_ref.shape[1:3]
    pair = seq_ref[0] // 2
    second = seq_ref[0] % 2 == 1
    for m in range(modes):
        rows = slice(m * tiles, (m + 1) * tiles)
        decay = coef_ref[1, m]
        both = decay * decay
        before = jnp.zeros((tiles, LANES), F32)
        after = jnp.zeros((tiles, LANES), F32)
        for k in range(pairs - 1, 0, -1):
            block = state_refs[k - 1][...].astype(F32)[rows]
            before = both * before + jnp.where(k <= pair, block, 0.0)
            block = state_refs[pairs - k - 1][...].astype(F32)[rows]
            after = both * after + jnp.where(k <= pairs - 1 - pair, block, 0.0)
        before = jnp.where(second, before, decay * before)
        after = jnp.where(second, decay * after, after)
        kept_ref[0, rows] = jnp.where(second, decay * before, before)
        kept_ref[1, rows] = jnp.where(second, after, decay * after)
        own = own_ref[0, rows]
        given_ref[0, rows] = jnp.where(second, before, decay * before + own).astype(LINK)
        own = own_ref[1, rows]
        given_ref[1, rows] = jnp.where(second, decay * after + own, after).astype(LINK)


def pair_states(seq_index, coefs, own, done, states):
    whole = pl.BlockSpec(memory_space=pltpu.VMEM)
    return pl.pallas_call(
        pair_kernel,
        in_specs=[pl.BlockSpec(memory_space=pltpu.SMEM), whole, whole]
        + [pl.BlockSpec(memory_space=pl.ANY)]
        + [whole] * len(states),
        out_specs=[whole] * 2,
        out_shape=[
            jax.ShapeDtypeStruct(own.shape, F32),
            jax.ShapeDtypeStruct(own.shape, LINK),
        ],
        compiler_params=pltpu.CompilerParams(vmem_limit_bytes=VMEM_BYTES),
        cost_estimate=takes(0.1),
        name="pair_states",
    )(seq_index, coefs, own, done, *states)


def local_kernel(
    q_ref, k_ref, v_ref, o_ref, coef_ref, gain_ref, conv_ref, grad_ref, done_ref, x_ref, g_ref
):
    tok_rows, width = k_ref.shape
    tiles = width // LANES
    spread_tokens(k_ref, v_ref, x_ref)
    spread_tokens(o_ref, q_ref, g_ref)
    walk_tokens(x_ref, coef_ref, tok_rows, tiles, 0, 1)
    walk_tokens(g_ref, coef_ref, tok_rows, tiles, tok_rows - 1, -1)
    for tile in range(tiles):
        cols = slice(tile * LANES, (tile + 1) * LANES)
        rows = tile_rows(tok_rows, tile)
        gain = gain_ref[:, cols]
        conv_in = product(k_ref[:, cols], v_ref[:, cols]).astype(F32)
        conv_ref[:, cols] = x_ref[rows, :] + gain * conv_in
        mid_grad = product(o_ref[:, cols], q_ref[:, cols]).astype(F32)
        grad_ref[:, cols] = g_ref[rows, :] + gain * mid_grad
    done_ref[...] = jnp.zeros(done_ref.shape, F32)


def local_parts(query_proj, key_proj, value_proj, out_grad, coefs, gain):
    tok_rows, width = key_proj.shape
    tiles = coefs.shape[2]
    return pl.pallas_call(
        local_kernel,
        out_shape=[jax.ShapeDtypeStruct((tok_rows, width), F32)] * 2
        + [jax.ShapeDtypeStruct((SUBLANES, LANES), F32)],
        scratch_shapes=[pltpu.VMEM(token_shape(tok_rows, tiles), F32)] * 2,
        compiler_params=pltpu.CompilerParams(vmem_limit_bytes=VMEM_BYTES),
        cost_estimate=takes(6.5),
        name="local_parts",
    )(query_proj, key_proj, value_proj, out_grad, coefs, gain)


def along_column(state, pairs, k):
    route = [(2 * p + b, 2 * ((p + k) % pairs) + b) for p in range(pairs) for b in range(2)]
    return lax.ppermute(state, "seq", route)


def inside_pair(state, pairs):
    return lax.ppermute(state, "seq", [(i, i ^ 1) for i in range(2 * pairs)])


def fill_edge(ref, held, coef_ref, tok_rows, tiles, start, move):
    modes = coef_ref.shape[1]
    decay = [coef_ref[0, m] for m in range(modes)]

    def step(t, held):
        held = tuple(decay[m] * held[m] for m in range(modes))
        ref[token_place(start + move * t, tok_rows, tiles)] = tree_sum(list(held))
        return held

    held = tuple(coef_ref[2, m] * held[m] for m in range(modes))
    lax.fori_loop(0, tok_rows, step, held, unroll=8)


def output_kernel(side, count, *refs):
    part_ref, coef_ref, kept_ref, given_ref = refs[:4]
    factor_refs, hbm_refs = refs[4 : 4 + count], refs[4 + count : 4 + 2 * count]
    edge_ref, out_refs, sems = refs[4 + 2 * count], refs[5 + 2 * count : -1], refs[-1]
    tok_rows, width = part_ref.shape
    tiles = width // LANES

    def departure(i, tile):
        place = (slice(None), pl.ds(tile * LANES, LANES))
        return pltpu.make_async_copy(
            out_refs[i].at[place], hbm_refs[i].at[place], sems.at[i, tile]
        )

    total = kept_ref[side] + given_ref[side].astype(F32)
    held = [total[m * tiles : (m + 1) * tiles] for m in range(coef_ref.shape[1])]
    start, move = ((0, 1), (tok_rows - 1, -1))[side]
    fill_edge(edge_ref, held, coef_ref, tok_rows, tiles, start, move)
    for tile in range(tiles):
        cols = slice(tile * LANES, (tile + 1) * LANES)
        value = part_ref[:, cols] + edge_ref[tile_rows(tok_rows, tile), :]
        for i in range(count):
            out_refs[i][:, cols] = (value * factor_refs[i][:, cols].astype(F32)).astype(BF16)
            departure(i, tile).start()
    for i in range(count):
        for tile in range(tiles):
            departure(i, tile).wait()


def outputs(side, name, part, coefs, kept, given, *factors):
    tok_rows, width = part.shape
    tiles = coefs.shape[2]
    count = len(factors)
    args = (part, coefs, kept, given, *factors)
    return pl.pallas_call(
        functools.partial(output_kernel, side, count),
        in_specs=[pl.BlockSpec(memory_space=pltpu.VMEM)] * len(args),
        out_specs=[pl.BlockSpec(memory_space=pl.ANY)] * count,
        out_shape=[jax.ShapeDtypeStruct((tok_rows, width), BF16)] * count,
        scratch_shapes=[pltpu.VMEM(token_shape(tok_rows, tiles), F32)]
        + [pltpu.VMEM((tok_rows, width), BF16)] * count
        + [pltpu.SemaphoreType.DMA((count, tiles))],
        compiler_params=pltpu.CompilerParams(vmem_limit_bytes=VMEM_BYTES),
        cost_estimate=takes(2.0),
        name=name,
    )(*args)


def lag_kernel(shards, chans, groups, owned, scale, *refs):
    in_refs, (out_ref, u_all, g_all, turned_all) = refs[:-4], refs[-4:]
    tok_rows = out_ref.shape[2]
    halves = tok_rows // LANES
    blocks = shards * halves
    depth = chans * groups
    full = blocks * depth
    if len(in_refs) == 1:
        take = chans * groups * owned

        def by_filter(row):
            return row % depth * owned + row // depth

        order = one_hot(take, take, by_filter)
        for which, kept in enumerate((u_all, g_all)):
            rows = slice(which * groups * owned, (which + 1) * groups * owned)
            for s in range(shards):
                piece = in_refs[0][s * chans : (s + 1) * chans, rows, :].reshape(take, tok_rows)
                piece = jnp.dot(order, piece, preferred_element_type=F32).astype(BF16)
                piece = piece.reshape(owned, depth, tok_rows)
                for h in range(halves):
                    first = (s * halves + h) * depth
                    kept[:, first : first + depth, :] = piece[:, :, h * LANES : (h + 1) * LANES]
    else:
        u_all[...] = in_refs[0][...]
        g_all[:, :full, :] = in_refs[1][...]
    g_all[:, full:, :] = jnp.zeros((owned, g_all.shape[1] - full, LANES), BF16)
    mirror = one_hot(LANES, LANES, lambda row: LANES - 1 - row)
    row = lax.broadcasted_iota(jnp.int32, (LANES, LANES), 0)
    col = lax.broadcasted_iota(jnp.int32, (LANES, LANES), 1)
    same_block = row + col >= LANES - 1
    filter_row = lax.broadcasted_iota(jnp.int32, (owned, LANES), 0)
    batch = min(blocks, 16)

    def one_filter(f, _):
        turned = turned_all[f]

        def some_lags(first):
            tables = []
            for d in range(0, batch, 2):
                live = full
                if batch == blocks:
                    live = min(full, -(-(blocks - d) * depth // LANES) * LANES)
                pair = jnp.concatenate(
                    [
                        g_all[f, pl.ds(pl.multiple_of((first + d + e) * depth, depth), live), :]
                        for e in range(2)
                    ],
                    axis=1,
                )
                table = jnp.dot(turned[:, :live], pair, preferred_element_type=F32)
                tables += [table[:, :LANES], table[:, LANES:]]
            last = g_all[f, pl.ds(pl.multiple_of((first + batch) * depth, depth), full), :]
            if batch < blocks:
                tables.append(jnp.dot(turned, last, preferred_element_type=F32))
            else:
                tables.append(jnp.zeros((LANES, LANES), F32))
            for d in range(batch):
                joined = jnp.where(same_block, tables[d], tables[d + 1])
                skewed = pltpu.roll(joined, 1, 1, stride=1, stride_axis=0)
                sums = jnp.sum(skewed, axis=0, keepdims=True) * scale
                lane = d % halves * LANES
                place = ((first + d) // halves, slice(None), slice(lane, lane + LANES))
                out_ref[place] = jnp.where(filter_row == f, sums, out_ref[place])

        if batch == blocks:
            some_lags(0)
        else:
            lax.fori_loop(0, blocks // batch, lambda i, c: (some_lags(i * batch), c)[1], 0)
        return 0

    for f in range(owned):
        turned_all[f] = lax.dot_general(
            mirror, u_all[f], (((1,), (1,)), ((), ())), preferred_element_type=F32
        ).astype(BF16)
    lax.fori_loop(0, owned, one_filter, 0, unroll=min(owned, 4))


def filter_lags(received, shards, chans, owned, scale):
    tok_rows = received.shape[2]
    groups = received.shape[1] // (2 * owned)
    halves = tok_rows // LANES
    depth = chans * groups
    full = shards * halves * depth
    args = (received,)
    if owned % SUBLANES:
        split = received.reshape(shards, chans, 2, groups, owned, halves, LANES)
        split = split.transpose(2, 4, 0, 5, 1, 3, 6).reshape(2, owned, full, LANES)
        args = (split[0], split[1])
    return pl.pallas_call(
        functools.partial(lag_kernel, shards, chans, groups, owned, scale),
        out_shape=jax.ShapeDtypeStruct((shards, owned, tok_rows), F32),
        scratch_shapes=[
            pltpu.VMEM((owned, full, LANES), BF16),
            pltpu.VMEM((owned, 2 * full + depth, LANES), BF16),
            pltpu.VMEM((owned, LANES, full), BF16),
        ],
        compiler_params=pltpu.CompilerParams(vmem_limit_bytes=VMEM_BYTES),
        cost_estimate=takes(4.0),
        name="filter_lags",
    )(*args)


def per_device(query_proj, key_proj, value_proj, out_grad, residues, decay_rate, skip_gain):
    tok_rows, width = key_proj.shape
    shards = lax.axis_size("seq")
    chans = lax.axis_size("chan")
    length = shards * tok_rows
    owned = FILTERS // (shards * chans)
    modes = residues.shape[1]
    signals = (query_proj, key_proj, value_proj, out_grad)

    send = pack_signals(shards, chans, owned, *signals)
    send, *signals, residues, decay_rate = lax.optimization_barrier(
        (send, *signals, residues, decay_rate)
    )
    received = lax.all_to_all(send, ("seq", "chan"), split_axis=0, concat_axis=0, tiled=True)

    coefs = jnp.stack(
        [
            jnp.exp(-decay_rate),
            jnp.exp(-(decay_rate * float(tok_rows))),
            residues * jnp.sqrt(decay_rate),
        ]
    )
    coefs = coefs.transpose(0, 2, 1).reshape(3, modes, 1, FILTERS // LANES, LANES)
    coefs = jnp.broadcast_to(coefs, (3, modes, width // FILTERS, FILTERS // LANES, LANES))
    coefs = coefs.reshape(3, modes, width // LANES, LANES)
    seq_index = lax.axis_index("seq").reshape(1)
    pairs = shards // 2
    states, own = block_states(seq_index, pairs, *signals, coefs)
    *states, coefs = lax.optimization_barrier((*states, coefs))
    states = [along_column(state, pairs, 1 + i) for i, state in enumerate(states)]
    conv_part, grad_part, done = local_parts(*signals, coefs, skip_gain[None, :])
    kept, given = pair_states(seq_index, coefs, own, done, states)
    received, kept, given = lax.optimization_barrier((received, kept, given))
    given = inside_pair(given, pairs)

    scale = 1.0 / math.sqrt(length * (CHANNELS // FILTERS))
    lags = filter_lags(received, shards, chans, owned, scale)
    lags, given = lax.optimization_barrier((lags, given))
    lags = lax.all_to_all(lags, "seq", split_axis=0, concat_axis=0, tiled=True)
    filter_grad = lags.reshape(shards * owned, tok_rows).T
    query_proj, key_proj, value_proj, _ = signals
    (layer_out,) = outputs(0, "conv_outputs", conv_part, coefs, kept, given, query_proj)
    key_grad, value_grad = outputs(
        1, "grad_outputs", grad_part, coefs, kept, given, value_proj, key_proj
    )
    return (layer_out, key_grad, value_grad, filter_grad)


def solution(mesh):
    split = P("seq", "chan")
    return jax.shard_map(
        per_device,
        mesh=mesh,
        in_specs=(split, split, split, split, P(), P(), P("chan")),
        out_specs=(split, split, split, split),
        check_vma=False,
    )
```

```python
import functools
import math

import jax
import jax.numpy as jnp
from jax import lax
from jax.experimental import pallas as pl
from jax.experimental.pallas import tpu as pltpu
from jax.sharding import PartitionSpec as P

CHANNELS = 4096
FILTERS = 256
LANES = 128
SUBLANES = 8
GAP = 8
VMEM_BYTES = 16 * 1024 * 1024
PACK_VMEM_BYTES = 62 * 1024 * 1024
F32 = jnp.float32
BF16 = jnp.bfloat16
LINK = jnp.bfloat16


def takes(micros):
    return pl.CostEstimate(flops=0, bytes_accessed=int(micros * 3.6e6), transcendentals=0)


def product(first, second):
    return first * second


def one_hot(rows, cols, column_of):
    row = lax.broadcasted_iota(jnp.int32, (rows, cols), 0)
    col = lax.broadcasted_iota(jnp.int32, (rows, cols), 1)
    return (col == column_of(row)).astype(F32).astype(BF16)


def pack_kernel(shards, chans, owned, *refs):
    hbm_refs, send_ref, held, packed, in_sems, out_sems = refs[:4], *refs[4:]
    tok_rows, width = held.shape[1:]
    groups = width // FILTERS
    per_chan = FILTERS // chans
    units = [(which, first) for which in range(2) for first in range(0, groups, 2)]

    def arrival(i, first):
        place = (slice(None), pl.ds(first * FILTERS, 2 * FILTERS))
        return pltpu.make_async_copy(
            hbm_refs[i].at[place], held.at[(i, *place)], in_sems.at[i, first // 2]
        )

    def departure(which, first):
        if owned % SUBLANES:
            place = (which, pl.ds(first, 2))
        else:
            place = (slice(None), pl.ds((which * groups + first) * owned, 2 * owned))
        return pltpu.make_async_copy(
            packed.at[place], send_ref.at[place], out_sems.at[which, first // 2]
        )

    for which, first in units:
        for i in (2 * which, 2 * which + 1):
            arrival(i, first).start()

    def owned_filter(row):
        seq = row // (chans * owned)
        chan = row // owned % chans
        return chan * per_chan + seq * owned + row % owned

    order = one_hot(FILTERS, FILTERS, owned_filter)
    for which, first in units:
        for i in (2 * which, 2 * which + 1):
            arrival(i, first).wait()
        pieces = []
        for group in (first, first + 1):
            cols = slice(group * FILTERS, (group + 1) * FILTERS)
            piece = lax.dot_general(
                order,
                product(held[2 * which, :, cols], held[2 * which + 1, :, cols]),
                (((1,), (1,)), ((), ())),
                preferred_element_type=F32,
            )
            if owned % SUBLANES:
                packed[which, group] = piece.astype(BF16)
            else:
                pieces.append(piece.reshape(shards * chans, owned, tok_rows))
        if pieces:
            row = (which * groups + first) * owned
            packed[:, row : row + 2 * owned, :] = jnp.concatenate(pieces, axis=1).astype(BF16)
        departure(which, first).start()
    for which, first in units:
        departure(which, first).wait()


def pack_signals(shards, chans, owned, query_proj, key_proj, value_proj, out_grad):
    tok_rows, width = key_proj.shape
    groups = width // FILTERS
    dests = shards * chans
    if owned % SUBLANES:
        shape = (2, groups, FILTERS, tok_rows)
    else:
        shape = (dests, 2 * groups * owned, tok_rows)
    send = pl.pallas_call(
        functools.partial(pack_kernel, shards, chans, owned),
        in_specs=[pl.BlockSpec(memory_space=pl.ANY)] * 4,
        out_specs=pl.BlockSpec(memory_space=pl.ANY),
        out_shape=jax.ShapeDtypeStruct(shape, BF16),
        scratch_shapes=[
            pltpu.VMEM((4, tok_rows, width), BF16),
            pltpu.VMEM(shape, BF16),
            pltpu.SemaphoreType.DMA((4, groups // 2)),
            pltpu.SemaphoreType.DMA((2, groups // 2)),
        ],
        compiler_params=pltpu.CompilerParams(vmem_limit_bytes=PACK_VMEM_BYTES),
        cost_estimate=takes(3.0),
        name="pack_signals",
    )(key_proj, value_proj, out_grad, query_proj)
    if owned % SUBLANES:
        send = send.reshape(2, groups, dests, owned, tok_rows)
        send = send.transpose(2, 0, 1, 3, 4).reshape(dests, 2 * groups * owned, tok_rows)
    return send


def tile_rows(tok_rows, tile):
    first = tile * (tok_rows + GAP)
    return slice(first, first + tok_rows)


def token_shape(tok_rows, tiles):
    return (tiles * (tok_rows + GAP), LANES)


def token_place(t, tok_rows, tiles):
    return (pl.ds(t, tiles, stride=tok_rows + GAP), slice(None))


def spread_tokens(a_ref, b_ref, x_ref):
    tok_rows, width = a_ref.shape
    for tile in range(width // LANES):
        cols = slice(tile * LANES, (tile + 1) * LANES)
        x_ref[tile_rows(tok_rows, tile), :] = product(a_ref[:, cols], b_ref[:, cols]).astype(F32)


def walk_tokens(ref, coef_ref, tok_rows, tiles, start, move):
    modes = coef_ref.shape[1]
    decay = [coef_ref[0, m] for m in range(modes)]
    weight = [coef_ref[2, m] for m in range(modes)]

    def step(t, held):
        place = token_place(start + move * t, tok_rows, tiles)
        x = ref[place]
        held = tuple(decay[m] * held[m] + x for m in range(modes))
        ref[place] = tree_sum([weight[m] * held[m] for m in range(modes)])
        return held

    zero = tuple(jnp.zeros((tiles, LANES), F32) for _ in range(modes))
    return lax.fori_loop(0, tok_rows, step, zero, unroll=8)


def tree_sum(terms):
    while len(terms) > 1:
        terms = [sum(terms[i : i + 2][1:], terms[i]) for i in range(0, len(terms), 2)]
    return terms[0]


def state_kernel(seq_ref, q_ref, k_ref, v_ref, o_ref, coef_ref, *refs):
    state_refs, own_ref, x_ref, g_ref = refs[:-3], *refs[-3:]
    tok_rows, width = k_ref.shape
    tiles = width // LANES
    modes = coef_ref.shape[1]
    pairs = len(state_refs) + 1
    spread_tokens(k_ref, v_ref, x_ref)
    spread_tokens(o_ref, q_ref, g_ref)
    decay = [coef_ref[0, m] for m in range(modes)]

    def step(t, carry):
        x = x_ref[token_place(t, tok_rows, tiles)]
        g = g_ref[token_place(tok_rows - 1 - t, tok_rows, tiles)]
        ahead = tuple(decay[m] * carry[0][m] + x for m in range(modes))
        behind = tuple(decay[m] * carry[1][m] + g for m in range(modes))
        return (ahead, behind)

    zero = tuple(jnp.zeros((tiles, LANES), F32) for _ in range(modes))
    ahead, behind = lax.fori_loop(0, tok_rows, step, (zero, zero), unroll=8)
    ahead = jnp.concatenate(ahead, axis=0)
    behind = jnp.concatenate(behind, axis=0)
    own_ref[0] = ahead
    own_ref[1] = behind
    for k in range(1, pairs):
        stays = seq_ref[0] // 2 + k < pairs

        @pl.when(stays)
        def _():
            state_refs[k - 1][...] = ahead.astype(LINK)

        @pl.when(jnp.logical_not(stays))
        def _():
            state_refs[k - 1][...] = behind.astype(LINK)


def block_states(seq_index, pairs, query_proj, key_proj, value_proj, out_grad, coefs):
    tok_rows, width = key_proj.shape
    modes, tiles = coefs.shape[1:3]
    whole = pl.BlockSpec(memory_space=pltpu.VMEM)
    *states, own = pl.pallas_call(
        state_kernel,
        in_specs=[pl.BlockSpec(memory_space=pltpu.SMEM)] + [whole] * 5,
        out_specs=[whole] * pairs,
        out_shape=[jax.ShapeDtypeStruct((modes * tiles, LANES), LINK)] * (pairs - 1)
        + [jax.ShapeDtypeStruct((2, modes * tiles, LANES), F32)],
        scratch_shapes=[pltpu.VMEM(token_shape(tok_rows, tiles), F32)] * 2,
        compiler_params=pltpu.CompilerParams(vmem_limit_bytes=VMEM_BYTES),
        cost_estimate=takes(3.0),
        name="block_states",
    )(seq_index, query_proj, key_proj, value_proj, out_grad, coefs)
    return states, own


def pair_kernel(seq_ref, coef_ref, own_ref, _, *refs):
    state_refs, kept_ref, given_ref = refs[:-2], *refs[-2:]
    pairs = len(state_refs) + 1
    modes, tiles = coef_ref.shape[1:3]
    pair = seq_ref[0] // 2
    second = seq_ref[0] % 2 == 1
    for m in range(modes):
        rows = slice(m * tiles, (m + 1) * tiles)
        decay = coef_ref[1, m]
        both = decay * decay
        before = jnp.zeros((tiles, LANES), F32)
        after = jnp.zeros((tiles, LANES), F32)
        for k in range(pairs - 1, 0, -1):
            block = state_refs[k - 1][...].astype(F32)[rows]
            before = both * before + jnp.where(k <= pair, block, 0.0)
            block = state_refs[pairs - k - 1][...].astype(F32)[rows]
            after = both * after + jnp.where(k <= pairs - 1 - pair, block, 0.0)
        before = jnp.where(second, before, decay * before)
        after = jnp.where(second, decay * after, after)
        kept_ref[0, rows] = jnp.where(second, decay * before, before)
        kept_ref[1, rows] = jnp.where(second, after, decay * after)
        own = own_ref[0, rows]
        given_ref[0, rows] = jnp.where(second, before, decay * before + own).astype(LINK)
        own = own_ref[1, rows]
        given_ref[1, rows] = jnp.where(second, decay * after + own, after).astype(LINK)


def pair_states(seq_index, coefs, own, done, states):
    whole = pl.BlockSpec(memory_space=pltpu.VMEM)
    return pl.pallas_call(
        pair_kernel,
        in_specs=[pl.BlockSpec(memory_space=pltpu.SMEM), whole, whole]
        + [pl.BlockSpec(memory_space=pl.ANY)]
        + [whole] * len(states),
        out_specs=[whole] * 2,
        out_shape=[
            jax.ShapeDtypeStruct(own.shape, F32),
            jax.ShapeDtypeStruct(own.shape, LINK),
        ],
        compiler_params=pltpu.CompilerParams(vmem_limit_bytes=VMEM_BYTES),
        cost_estimate=takes(0.1),
        name="pair_states",
    )(seq_index, coefs, own, done, *states)


def local_kernel(
    q_ref, k_ref, v_ref, o_ref, coef_ref, gain_ref, conv_ref, grad_ref, done_ref, x_ref, g_ref
):
    tok_rows, width = k_ref.shape
    tiles = width // LANES
    spread_tokens(k_ref, v_ref, x_ref)
    spread_tokens(o_ref, q_ref, g_ref)
    walk_tokens(x_ref, coef_ref, tok_rows, tiles, 0, 1)
    walk_tokens(g_ref, coef_ref, tok_rows, tiles, tok_rows - 1, -1)
    for tile in range(tiles):
        cols = slice(tile * LANES, (tile + 1) * LANES)
        rows = tile_rows(tok_rows, tile)
        gain = gain_ref[:, cols]
        conv_in = product(k_ref[:, cols], v_ref[:, cols]).astype(F32)
        conv_ref[:, cols] = x_ref[rows, :] + gain * conv_in
        mid_grad = product(o_ref[:, cols], q_ref[:, cols]).astype(F32)
        grad_ref[:, cols] = g_ref[rows, :] + gain * mid_grad
    done_ref[...] = jnp.zeros(done_ref.shape, F32)


def local_parts(query_proj, key_proj, value_proj, out_grad, coefs, gain):
    tok_rows, width = key_proj.shape
    tiles = coefs.shape[2]
    return pl.pallas_call(
        local_kernel,
        out_shape=[jax.ShapeDtypeStruct((tok_rows, width), F32)] * 2
        + [jax.ShapeDtypeStruct((SUBLANES, LANES), F32)],
        scratch_shapes=[pltpu.VMEM(token_shape(tok_rows, tiles), F32)] * 2,
        compiler_params=pltpu.CompilerParams(vmem_limit_bytes=VMEM_BYTES),
        cost_estimate=takes(6.5),
        name="local_parts",
    )(query_proj, key_proj, value_proj, out_grad, coefs, gain)


def along_column(state, pairs, k):
    route = [(2 * p + b, 2 * ((p + k) % pairs) + b) for p in range(pairs) for b in range(2)]
    return lax.ppermute(state, "seq", route)


def inside_pair(state, pairs):
    return lax.ppermute(state, "seq", [(i, i ^ 1) for i in range(2 * pairs)])


def fill_edge(ref, held, coef_ref, tok_rows, tiles, start, move):
    modes = coef_ref.shape[1]
    decay = [coef_ref[0, m] for m in range(modes)]

    def step(t, held):
        held = tuple(decay[m] * held[m] for m in range(modes))
        ref[token_place(start + move * t, tok_rows, tiles)] = tree_sum(list(held))
        return held

    held = tuple(coef_ref[2, m] * held[m] for m in range(modes))
    lax.fori_loop(0, tok_rows, step, held, unroll=8)


def edge_kernel(coef_ref, kept_ref, given_ref, edge_ref):
    modes, tiles = coef_ref.shape[1:3]
    tok_rows = edge_ref.shape[0] // tiles - GAP
    fill_side(0, edge_ref, coef_ref, kept_ref, given_ref, tok_rows, tiles)


def fill_side(side, edge_ref, coef_ref, kept_ref, given_ref, tok_rows, tiles):
    total = kept_ref[side] + given_ref[side].astype(F32)
    held = [total[m * tiles : (m + 1) * tiles] for m in range(coef_ref.shape[1])]
    start, move = ((0, 1), (tok_rows - 1, -1))[side]
    fill_edge(edge_ref, held, coef_ref, tok_rows, tiles, start, move)


def edge_terms(tok_rows, coefs, kept, given):
    return pl.pallas_call(
        edge_kernel,
        out_shape=jax.ShapeDtypeStruct(token_shape(tok_rows, coefs.shape[2]), F32),
        compiler_params=pltpu.CompilerParams(vmem_limit_bytes=VMEM_BYTES),
        cost_estimate=takes(1.3),
        name="edge_terms",
    )(coefs, kept, given)


def multiply_out(part_ref, edge_ref, factor_refs, out_refs, hbm_refs, sems):
    tok_rows, width = part_ref.shape
    copies = []
    for tile in range(width // LANES):
        cols = slice(tile * LANES, (tile + 1) * LANES)
        value = part_ref[:, cols] + edge_ref[tile_rows(tok_rows, tile), :]
        for i, (factor_ref, out_ref, hbm_ref) in enumerate(zip(factor_refs, out_refs, hbm_refs)):
            out_ref[:, cols] = (value * factor_ref[:, cols].astype(F32)).astype(BF16)
            place = (slice(None), pl.ds(tile * LANES, LANES))
            copies.append(
                pltpu.make_async_copy(out_ref.at[place], hbm_ref.at[place], sems.at[i, tile])
            )
            copies[-1].start()
    return copies


def conv_kernel(
    part_ref, edge_ref, q_ref, coef_ref, kept_ref, given_ref,
    layer_hbm, next_ref, layer_ref, sems,
):
    tok_rows, width = part_ref.shape
    copies = multiply_out(part_ref, edge_ref, [q_ref], [layer_ref], [layer_hbm], sems)
    fill_side(1, next_ref, coef_ref, kept_ref, given_ref, tok_rows, width // LANES)
    for copy in copies:
        copy.wait()


def conv_outputs(part, edge, query_proj, coefs, kept, given):
    tok_rows, width = part.shape
    whole = pl.BlockSpec(memory_space=pltpu.VMEM)
    return pl.pallas_call(
        conv_kernel,
        in_specs=[whole] * 6,
        out_specs=[pl.BlockSpec(memory_space=pl.ANY), whole],
        out_shape=[
            jax.ShapeDtypeStruct((tok_rows, width), BF16),
            jax.ShapeDtypeStruct(edge.shape, F32),
        ],
        scratch_shapes=[
            pltpu.VMEM((tok_rows, width), BF16),
            pltpu.SemaphoreType.DMA((1, width // LANES)),
        ],
        compiler_params=pltpu.CompilerParams(vmem_limit_bytes=VMEM_BYTES),
        cost_estimate=takes(2.0),
        name="conv_outputs",
    )(part, edge, query_proj, coefs, kept, given)


def grad_kernel(
    part_ref, edge_ref, v_ref, k_ref, key_hbm, value_hbm, key_ref, value_ref, sems
):
    copies = multiply_out(
        part_ref, edge_ref, [v_ref, k_ref], [key_ref, value_ref], [key_hbm, value_hbm], sems
    )
    for copy in copies:
        copy.wait()


def grad_outputs(part, edge, value_proj, key_proj):
    tok_rows, width = part.shape
    return pl.pallas_call(
        grad_kernel,
        in_specs=[pl.BlockSpec(memory_space=pltpu.VMEM)] * 4,
        out_specs=[pl.BlockSpec(memory_space=pl.ANY)] * 2,
        out_shape=[jax.ShapeDtypeStruct((tok_rows, width), BF16)] * 2,
        scratch_shapes=[pltpu.VMEM((tok_rows, width), BF16)] * 2
        + [pltpu.SemaphoreType.DMA((2, width // LANES))],
        compiler_params=pltpu.CompilerParams(vmem_limit_bytes=VMEM_BYTES),
        cost_estimate=takes(1.2),
        name="grad_outputs",
    )(part, edge, value_proj, key_proj)


def lag_kernel(shards, chans, groups, owned, scale, *refs):
    in_refs, (out_ref, u_all, g_all, turned_all) = refs[:-4], refs[-4:]
    tok_rows = out_ref.shape[2]
    halves = tok_rows // LANES
    blocks = shards * halves
    depth = chans * groups
    full = blocks * depth
    if len(in_refs) == 1:
        take = chans * groups * owned

        def by_filter(row):
            return row % depth * owned + row // depth

        order = one_hot(take, take, by_filter)
        for which, kept in enumerate((u_all, g_all)):
            rows = slice(which * groups * owned, (which + 1) * groups * owned)
            for s in range(shards):
                piece = in_refs[0][s * chans : (s + 1) * chans, rows, :].reshape(take, tok_rows)
                piece = jnp.dot(order, piece, preferred_element_type=F32).astype(BF16)
                piece = piece.reshape(owned, depth, tok_rows)
                for h in range(halves):
                    first = (s * halves + h) * depth
                    kept[:, first : first + depth, :] = piece[:, :, h * LANES : (h + 1) * LANES]
    else:
        u_all[...] = in_refs[0][...]
        g_all[:, :full, :] = in_refs[1][...]
    g_all[:, full:, :] = jnp.zeros((owned, g_all.shape[1] - full, LANES), BF16)
    mirror = one_hot(LANES, LANES, lambda row: LANES - 1 - row)
    row = lax.broadcasted_iota(jnp.int32, (LANES, LANES), 0)
    col = lax.broadcasted_iota(jnp.int32, (LANES, LANES), 1)
    same_block = row + col >= LANES - 1
    filter_row = lax.broadcasted_iota(jnp.int32, (owned, LANES), 0)
    batch = min(blocks, 16)

    def one_filter(f, _):
        turned = turned_all[f]

        def some_lags(first):
            tables = []
            for d in range(0, batch, 2):
                live = full
                if batch == blocks:
                    live = min(full, -(-(blocks - d) * depth // LANES) * LANES)
                pair = jnp.concatenate(
                    [
                        g_all[f, pl.ds(pl.multiple_of((first + d + e) * depth, depth), live), :]
                        for e in range(2)
                    ],
                    axis=1,
                )
                table = jnp.dot(turned[:, :live], pair, preferred_element_type=F32)
                tables += [table[:, :LANES], table[:, LANES:]]
            last = g_all[f, pl.ds(pl.multiple_of((first + batch) * depth, depth), full), :]
            if batch < blocks:
                tables.append(jnp.dot(turned, last, preferred_element_type=F32))
            else:
                tables.append(jnp.zeros((LANES, LANES), F32))
            for d in range(batch):
                joined = jnp.where(same_block, tables[d], tables[d + 1])
                skewed = pltpu.roll(joined, 1, 1, stride=1, stride_axis=0)
                sums = jnp.sum(skewed, axis=0, keepdims=True) * scale
                lane = d % halves * LANES
                place = ((first + d) // halves, slice(None), slice(lane, lane + LANES))
                out_ref[place] = jnp.where(filter_row == f, sums, out_ref[place])

        if batch == blocks:
            some_lags(0)
        else:
            lax.fori_loop(0, blocks // batch, lambda i, c: (some_lags(i * batch), c)[1], 0)
        return 0

    for f in range(owned):
        turned_all[f] = lax.dot_general(
            mirror, u_all[f], (((1,), (1,)), ((), ())), preferred_element_type=F32
        ).astype(BF16)
    lax.fori_loop(0, owned, one_filter, 0, unroll=min(owned, 4))


def filter_lags(received, shards, chans, owned, scale):
    tok_rows = received.shape[2]
    groups = received.shape[1] // (2 * owned)
    halves = tok_rows // LANES
    depth = chans * groups
    full = shards * halves * depth
    args = (received,)
    if owned % SUBLANES:
        split = received.reshape(shards, chans, 2, groups, owned, halves, LANES)
        split = split.transpose(2, 4, 0, 5, 1, 3, 6).reshape(2, owned, full, LANES)
        args = (split[0], split[1])
    return pl.pallas_call(
        functools.partial(lag_kernel, shards, chans, groups, owned, scale),
        out_shape=jax.ShapeDtypeStruct((shards, owned, tok_rows), F32),
        scratch_shapes=[
            pltpu.VMEM((owned, full, LANES), BF16),
            pltpu.VMEM((owned, 2 * full + depth, LANES), BF16),
            pltpu.VMEM((owned, LANES, full), BF16),
        ],
        compiler_params=pltpu.CompilerParams(vmem_limit_bytes=VMEM_BYTES),
        cost_estimate=takes(4.0),
        name="filter_lags",
    )(*args)


def per_device(query_proj, key_proj, value_proj, out_grad, residues, decay_rate, skip_gain):
    tok_rows, width = key_proj.shape
    shards = lax.axis_size("seq")
    chans = lax.axis_size("chan")
    length = shards * tok_rows
    owned = FILTERS // (shards * chans)
    modes = residues.shape[1]
    signals = (query_proj, key_proj, value_proj, out_grad)

    send = pack_signals(shards, chans, owned, *signals)
    send, *signals, residues, decay_rate = lax.optimization_barrier(
        (send, *signals, residues, decay_rate)
    )
    received = lax.all_to_all(send, ("seq", "chan"), split_axis=0, concat_axis=0, tiled=True)

    coefs = jnp.stack(
        [
            jnp.exp(-decay_rate),
            jnp.exp(-(decay_rate * float(tok_rows))),
            residues * jnp.sqrt(decay_rate),
        ]
    )
    coefs = coefs.transpose(0, 2, 1).reshape(3, modes, 1, FILTERS // LANES, LANES)
    coefs = jnp.broadcast_to(coefs, (3, modes, width // FILTERS, FILTERS // LANES, LANES))
    coefs = coefs.reshape(3, modes, width // LANES, LANES)
    seq_index = lax.axis_index("seq").reshape(1)
    pairs = shards // 2
    states, own = block_states(seq_index, pairs, *signals, coefs)
    *states, coefs = lax.optimization_barrier((*states, coefs))
    states = [along_column(state, pairs, 1 + i) for i, state in enumerate(states)]
    conv_part, grad_part, done = local_parts(*signals, coefs, skip_gain[None, :])
    kept, given = pair_states(seq_index, coefs, own, done, states)
    received, kept, given = lax.optimization_barrier((received, kept, given))
    given = inside_pair(given, pairs)

    scale = 1.0 / math.sqrt(length * (CHANNELS // FILTERS))
    lags = filter_lags(received, shards, chans, owned, scale)
    lags, given = lax.optimization_barrier((lags, given))
    lags = lax.all_to_all(lags, "seq", split_axis=0, concat_axis=0, tiled=True)
    filter_grad = lags.reshape(shards * owned, tok_rows).T
    query_proj, key_proj, value_proj, _ = signals
    edge = edge_terms(tok_rows, coefs, kept, given)
    layer_out, edge = conv_outputs(conv_part, edge, query_proj, coefs, kept, given)
    key_grad, value_grad = grad_outputs(grad_part, edge, value_proj, key_proj)
    return (layer_out, key_grad, value_grad, filter_grad)


def solution(mesh):
    split = P("seq", "chan")
    return jax.shard_map(
        per_device,
        mesh=mesh,
        in_specs=(split, split, split, split, P(), P(), P("chan")),
        out_specs=(split, split, split, split),
        check_vma=False,
    )
```

```python
import functools
import math

import jax
import jax.numpy as jnp
from jax import lax
from jax.experimental import pallas as pl
from jax.experimental.pallas import tpu as pltpu
from jax.sharding import PartitionSpec as P

CHANNELS = 4096
FILTERS = 256
LANES = 128
SUBLANES = 8
GAP = 8
VMEM_BYTES = 16 * 1024 * 1024
FULL_VMEM_BYTES = 62 * 1024 * 1024
F32 = jnp.float32
BF16 = jnp.bfloat16
LINK = jnp.bfloat16


def takes(micros):
    return pl.CostEstimate(flops=0, bytes_accessed=int(micros * 3.6e6), transcendentals=0)


def product(first, second):
    return first * second


def one_hot(rows, cols, column_of):
    row = lax.broadcasted_iota(jnp.int32, (rows, cols), 0)
    col = lax.broadcasted_iota(jnp.int32, (rows, cols), 1)
    return (col == column_of(row)).astype(F32).astype(BF16)


def pack_kernel(shards, chans, owned, *refs):
    hbm_refs, send_ref, held, packed, in_sems, out_sems = refs[:4], *refs[4:]
    tok_rows, width = held.shape[1:]
    groups = width // FILTERS
    per_chan = FILTERS // chans
    units = [(which, first) for which in range(2) for first in range(0, groups, 2)]

    def arrival(i, first):
        place = (slice(None), pl.ds(first * FILTERS, 2 * FILTERS))
        return pltpu.make_async_copy(
            hbm_refs[i].at[place], held.at[(i, *place)], in_sems.at[i, first // 2]
        )

    def departure(which, first):
        if owned % SUBLANES:
            place = (which, pl.ds(first, 2))
        else:
            place = (slice(None), pl.ds((which * groups + first) * owned, 2 * owned))
        return pltpu.make_async_copy(
            packed.at[place], send_ref.at[place], out_sems.at[which, first // 2]
        )

    for which, first in units:
        for i in (2 * which, 2 * which + 1):
            arrival(i, first).start()

    def owned_filter(row):
        seq = row // (chans * owned)
        chan = row // owned % chans
        return chan * per_chan + seq * owned + row % owned

    order = one_hot(FILTERS, FILTERS, owned_filter)
    for which, first in units:
        for i in (2 * which, 2 * which + 1):
            arrival(i, first).wait()
        pieces = []
        for group in (first, first + 1):
            cols = slice(group * FILTERS, (group + 1) * FILTERS)
            piece = lax.dot_general(
                order,
                product(held[2 * which, :, cols], held[2 * which + 1, :, cols]),
                (((1,), (1,)), ((), ())),
                preferred_element_type=F32,
            )
            if owned % SUBLANES:
                packed[which, group] = piece.astype(BF16)
            else:
                pieces.append(piece.reshape(shards * chans, owned, tok_rows))
        if pieces:
            row = (which * groups + first) * owned
            packed[:, row : row + 2 * owned, :] = jnp.concatenate(pieces, axis=1).astype(BF16)
        departure(which, first).start()
    for which, first in units:
        departure(which, first).wait()


def pack_signals(shards, chans, owned, query_proj, key_proj, value_proj, out_grad):
    tok_rows, width = key_proj.shape
    groups = width // FILTERS
    dests = shards * chans
    if owned % SUBLANES:
        shape = (2, groups, FILTERS, tok_rows)
    else:
        shape = (dests, 2 * groups * owned, tok_rows)
    send = pl.pallas_call(
        functools.partial(pack_kernel, shards, chans, owned),
        in_specs=[pl.BlockSpec(memory_space=pl.ANY)] * 4,
        out_specs=pl.BlockSpec(memory_space=pl.ANY),
        out_shape=jax.ShapeDtypeStruct(shape, BF16),
        scratch_shapes=[
            pltpu.VMEM((4, tok_rows, width), BF16),
            pltpu.VMEM(shape, BF16),
            pltpu.SemaphoreType.DMA((4, groups // 2)),
            pltpu.SemaphoreType.DMA((2, groups // 2)),
        ],
        compiler_params=pltpu.CompilerParams(vmem_limit_bytes=FULL_VMEM_BYTES),
        cost_estimate=takes(3.0),
        name="pack_signals",
    )(key_proj, value_proj, out_grad, query_proj)
    if owned % SUBLANES:
        send = send.reshape(2, groups, dests, owned, tok_rows)
        send = send.transpose(2, 0, 1, 3, 4).reshape(dests, 2 * groups * owned, tok_rows)
    return send


def tile_rows(tok_rows, tile):
    first = tile * (tok_rows + GAP)
    return slice(first, first + tok_rows)


def token_shape(tok_rows, tiles):
    return (tiles * (tok_rows + GAP), LANES)


def token_place(t, tok_rows, tiles):
    return (pl.ds(t, tiles, stride=tok_rows + GAP), slice(None))


def spread_tokens(a_ref, b_ref, x_ref):
    tok_rows, width = a_ref.shape
    for tile in range(width // LANES):
        cols = slice(tile * LANES, (tile + 1) * LANES)
        x_ref[tile_rows(tok_rows, tile), :] = product(a_ref[:, cols], b_ref[:, cols]).astype(F32)


def walk_tokens(ref, coef_ref, tok_rows, tiles, start, move):
    modes = coef_ref.shape[1]
    decay = [coef_ref[0, m] for m in range(modes)]
    weight = [coef_ref[2, m] for m in range(modes)]

    def step(t, held):
        place = token_place(start + move * t, tok_rows, tiles)
        x = ref[place]
        held = tuple(decay[m] * held[m] + x for m in range(modes))
        ref[place] = tree_sum([weight[m] * held[m] for m in range(modes)])
        return held

    zero = tuple(jnp.zeros((tiles, LANES), F32) for _ in range(modes))
    return lax.fori_loop(0, tok_rows, step, zero, unroll=8)


def tree_sum(terms):
    while len(terms) > 1:
        terms = [sum(terms[i : i + 2][1:], terms[i]) for i in range(0, len(terms), 2)]
    return terms[0]


def state_kernel(q_ref, k_ref, v_ref, o_ref, coef_ref, own_ref, sent_ref, x_ref, g_ref):
    tok_rows, width = k_ref.shape
    tiles = width // LANES
    modes = coef_ref.shape[1]
    spread_tokens(k_ref, v_ref, x_ref)
    spread_tokens(o_ref, q_ref, g_ref)
    decay = [coef_ref[0, m] for m in range(modes)]

    def step(t, carry):
        x = x_ref[token_place(t, tok_rows, tiles)]
        g = g_ref[token_place(tok_rows - 1 - t, tok_rows, tiles)]
        ahead = tuple(decay[m] * carry[0][m] + x for m in range(modes))
        behind = tuple(decay[m] * carry[1][m] + g for m in range(modes))
        return (ahead, behind)

    zero = tuple(jnp.zeros((tiles, LANES), F32) for _ in range(modes))
    for side, held in enumerate(lax.fori_loop(0, tok_rows, step, (zero, zero), unroll=8)):
        held = jnp.concatenate(held, axis=0)
        own_ref[side] = held
        sent_ref[side] = held.astype(LINK)


def block_states(query_proj, key_proj, value_proj, out_grad, coefs):
    tok_rows, width = key_proj.shape
    modes, tiles = coefs.shape[1:3]
    return pl.pallas_call(
        state_kernel,
        out_shape=[
            jax.ShapeDtypeStruct((2, modes * tiles, LANES), F32),
            jax.ShapeDtypeStruct((2, modes * tiles, LANES), LINK),
        ],
        scratch_shapes=[pltpu.VMEM(token_shape(tok_rows, tiles), F32)] * 2,
        compiler_params=pltpu.CompilerParams(vmem_limit_bytes=VMEM_BYTES),
        cost_estimate=takes(3.0),
        name="block_states",
    )(query_proj, key_proj, value_proj, out_grad, coefs)


def pair_kernel(seq_ref, coef_ref, own_ref, near_ref, *state_refs):
    pairs = len(state_refs) + 1
    modes, tiles = coef_ref.shape[1:3]
    pair = seq_ref[0] // 2
    second = seq_ref[0] % 2 == 1
    for m in range(modes):
        rows = slice(m * tiles, (m + 1) * tiles)
        decay = coef_ref[1, m]
        own, near = own_ref[0, rows], near_ref[0].astype(F32)[rows]
        ahead = jnp.where(second, own + decay * near, near + decay * own)
        own, near = own_ref[1, rows], near_ref[1].astype(F32)[rows]
        behind = jnp.where(second, near + decay * own, own + decay * near)
        for k in range(1, pairs):
            state_refs[k - 1][rows] = jnp.where(pair + k < pairs, ahead, behind)


def pair_states(seq_index, pairs, coefs, own, near):
    whole = pl.BlockSpec(memory_space=pltpu.VMEM)
    states = pl.pallas_call(
        pair_kernel,
        in_specs=[pl.BlockSpec(memory_space=pltpu.SMEM)] + [whole] * 3,
        out_specs=[whole] * (pairs - 1),
        out_shape=[jax.ShapeDtypeStruct(own.shape[1:], F32)] * (pairs - 1),
        compiler_params=pltpu.CompilerParams(vmem_limit_bytes=VMEM_BYTES),
        cost_estimate=takes(0.1),
        name="pair_states",
    )(seq_index, coefs, own, near)
    return [state.astype(LINK) for state in states]


def sum_pairs(side, seq, coef_ref, near_ref, state_refs):
    pairs = len(state_refs) + 1
    modes, tiles = coef_ref.shape[1:3]
    pair, count = seq // 2, (seq // 2, pairs - 1 - seq // 2)[side]
    beside = seq % 2 == 1 - side
    held = []
    for m in range(modes):
        rows = slice(m * tiles, (m + 1) * tiles)
        decay = coef_ref[1, m]
        total = jnp.zeros((tiles, LANES), F32)
        for k in range(pairs - 1, 0, -1):
            state_ref = state_refs[k - 1 if side == 0 else pairs - k - 1]
            block = state_ref[...].astype(F32)[rows]
            total = decay * decay * total + jnp.where(k <= count, block, 0.0)
        near = near_ref[side].astype(F32)[rows]
        held.append(jnp.where(beside, decay * total + near, total))
    return held


def local_kernel(
    q_ref, k_ref, v_ref, o_ref, coef_ref, gain_ref, part_ref, done_ref
):
    conv_ref, grad_ref = part_ref.at[0], part_ref.at[1]
    tok_rows, width = k_ref.shape
    tiles = width // LANES
    spread_tokens(k_ref, v_ref, conv_ref)
    spread_tokens(o_ref, q_ref, grad_ref)
    walk_tokens(conv_ref, coef_ref, tok_rows, tiles, 0, 1)
    walk_tokens(grad_ref, coef_ref, tok_rows, tiles, tok_rows - 1, -1)
    for tile in range(tiles):
        cols = slice(tile * LANES, (tile + 1) * LANES)
        rows = tile_rows(tok_rows, tile)
        gain = gain_ref[:, cols]
        conv_in = product(k_ref[:, cols], v_ref[:, cols]).astype(F32)
        conv_ref[rows, :] = conv_ref[rows, :] + gain * conv_in
        mid_grad = product(o_ref[:, cols], q_ref[:, cols]).astype(F32)
        grad_ref[rows, :] = grad_ref[rows, :] + gain * mid_grad
    done_ref[...] = jnp.zeros(done_ref.shape, F32)


def local_parts(query_proj, key_proj, value_proj, out_grad, coefs, gain):
    tok_rows, width = key_proj.shape
    tiles = coefs.shape[2]
    return pl.pallas_call(
        local_kernel,
        out_shape=[
            jax.ShapeDtypeStruct((2, *token_shape(tok_rows, tiles)), F32),
            jax.ShapeDtypeStruct((SUBLANES, LANES), F32),
        ],
        compiler_params=pltpu.CompilerParams(vmem_limit_bytes=VMEM_BYTES),
        cost_estimate=takes(6.5),
        name="local_parts",
    )(query_proj, key_proj, value_proj, out_grad, coefs, gain)


def along_column(state, pairs, k):
    route = [(2 * p + b, 2 * ((p + k) % pairs) + b) for p in range(pairs) for b in range(2)]
    return lax.ppermute(state, "seq", route)


def inside_pair(state, pairs):
    return lax.ppermute(state, "seq", [(i, i ^ 1) for i in range(2 * pairs)])


def fill_edge(ref, held, coef_ref, tok_rows, tiles, start, move):
    modes = coef_ref.shape[1]
    decay = [coef_ref[0, m] for m in range(modes)]

    def step(t, held):
        held = tuple(decay[m] * held[m] for m in range(modes))
        ref[token_place(start + move * t, tok_rows, tiles)] = tree_sum(list(held))
        return held

    held = tuple(coef_ref[2, m] * held[m] for m in range(modes))
    lax.fori_loop(0, tok_rows, step, held, unroll=8)


def final_kernel(count, *refs):
    seq_ref, hbm_refs, refs = refs[0], refs[1 : 1 + count], refs[1 + count :]
    out_hbm, held_refs, refs = refs[:3], refs[3 : 3 + count], refs[3 + count :]
    edge_ref, out_refs, in_sems, out_sems = refs[0], refs[1:4], refs[4], refs[5]
    coef_ref, near_ref, *state_refs = held_refs[:-4]
    part_ref, q_ref, v_ref, k_ref = held_refs[-4:]
    tok_rows, width = k_ref.shape
    tiles = width // LANES
    pieces = list(zip(hbm_refs[:-4], held_refs[:-4]))
    small = len(pieces)
    pieces += [(hbm_refs[-4].at[0], part_ref.at[0]), (hbm_refs[-3], q_ref)]
    pieces += [(hbm_refs[-4].at[1], part_ref.at[1])] + list(zip(hbm_refs[-2:], held_refs[-2:]))
    arrivals = [
        pltpu.make_async_copy(source, target, in_sems.at[i])
        for i, (source, target) in enumerate(pieces)
    ]
    departures = []

    def multiply_out(side, outs):
        for tile in range(tiles):
            cols = slice(tile * LANES, (tile + 1) * LANES)
            rows = tile_rows(tok_rows, tile)
            value = part_ref[side, rows, :] + edge_ref[rows, :]
            for i, factor_ref in outs:
                out_refs[i][:, cols] = (value * factor_ref[:, cols].astype(F32)).astype(BF16)
                place = (slice(None), pl.ds(tile * LANES, LANES))
                copy = pltpu.make_async_copy(
                    out_refs[i].at[place], out_hbm[i].at[place], out_sems.at[i, tile]
                )
                copy.start()
                departures.append(copy)

    for copy in arrivals:
        copy.start()
    for copy in arrivals[:small]:
        copy.wait()
    held = sum_pairs(0, seq_ref[0], coef_ref, near_ref, state_refs)
    fill_edge(edge_ref, held, coef_ref, tok_rows, tiles, 0, 1)
    for copy in arrivals[small : small + 2]:
        copy.wait()
    multiply_out(0, [(0, q_ref)])
    held = sum_pairs(1, seq_ref[0], coef_ref, near_ref, state_refs)
    fill_edge(edge_ref, held, coef_ref, tok_rows, tiles, tok_rows - 1, -1)
    for copy in arrivals[small + 2 :]:
        copy.wait()
    multiply_out(1, [(1, v_ref), (2, k_ref)])
    for copy in departures:
        copy.wait()


def final_outputs(seq_index, coefs, near, states, parts, query_proj, value_proj, key_proj):
    tok_rows, width = key_proj.shape
    tiles = coefs.shape[2]
    args = (coefs, near, *states, parts, query_proj, value_proj, key_proj)
    away = pl.BlockSpec(memory_space=pl.ANY)
    return pl.pallas_call(
        functools.partial(final_kernel, len(args)),
        in_specs=[pl.BlockSpec(memory_space=pltpu.SMEM)] + [away] * len(args),
        out_specs=[away] * 3,
        out_shape=[jax.ShapeDtypeStruct((tok_rows, width), BF16)] * 3,
        scratch_shapes=[pltpu.VMEM(arg.shape, arg.dtype) for arg in args]
        + [pltpu.VMEM(token_shape(tok_rows, tiles), F32)]
        + [pltpu.VMEM((tok_rows, width), BF16)] * 3
        + [pltpu.SemaphoreType.DMA((len(args) + 1,)), pltpu.SemaphoreType.DMA((3, tiles))],
        compiler_params=pltpu.CompilerParams(vmem_limit_bytes=FULL_VMEM_BYTES),
        cost_estimate=takes(100.0),
        name="final_outputs",
    )(seq_index, *args)


def lag_kernel(shards, chans, groups, owned, scale, *refs):
    in_refs, (out_ref, u_all, g_all, turned_all) = refs[1:-4], refs[-4:]
    tok_rows = out_ref.shape[2]
    halves = tok_rows // LANES
    blocks = shards * halves
    depth = chans * groups
    full = blocks * depth
    if len(in_refs) == 1:
        take = chans * groups * owned

        def by_filter(row):
            return row % depth * owned + row // depth

        order = one_hot(take, take, by_filter)
        for which, kept in enumerate((u_all, g_all)):
            rows = slice(which * groups * owned, (which + 1) * groups * owned)
            for s in range(shards):
                piece = in_refs[0][s * chans : (s + 1) * chans, rows, :].reshape(take, tok_rows)
                piece = jnp.dot(order, piece, preferred_element_type=F32).astype(BF16)
                piece = piece.reshape(owned, depth, tok_rows)
                for h in range(halves):
                    first = (s * halves + h) * depth
                    kept[:, first : first + depth, :] = piece[:, :, h * LANES : (h + 1) * LANES]
    else:
        u_all[...] = in_refs[0][...]
        g_all[:, :full, :] = in_refs[1][...]
    g_all[:, full:, :] = jnp.zeros((owned, g_all.shape[1] - full, LANES), BF16)
    mirror = one_hot(LANES, LANES, lambda row: LANES - 1 - row)
    row = lax.broadcasted_iota(jnp.int32, (LANES, LANES), 0)
    col = lax.broadcasted_iota(jnp.int32, (LANES, LANES), 1)
    same_block = row + col >= LANES - 1
    filter_row = lax.broadcasted_iota(jnp.int32, (owned, LANES), 0)
    batch = min(blocks, 16)

    def one_filter(f, _):
        turned = turned_all[f]

        def some_lags(first):
            tables = []
            for d in range(0, batch, 2):
                live = full
                if batch == blocks:
                    live = min(full, -(-(blocks - d) * depth // LANES) * LANES)
                pair = jnp.concatenate(
                    [
                        g_all[f, pl.ds(pl.multiple_of((first + d + e) * depth, depth), live), :]
                        for e in range(2)
                    ],
                    axis=1,
                )
                table = jnp.dot(turned[:, :live], pair, preferred_element_type=F32)
                tables += [table[:, :LANES], table[:, LANES:]]
            last = g_all[f, pl.ds(pl.multiple_of((first + batch) * depth, depth), full), :]
            if batch < blocks:
                tables.append(jnp.dot(turned, last, preferred_element_type=F32))
            else:
                tables.append(jnp.zeros((LANES, LANES), F32))
            for d in range(batch):
                joined = jnp.where(same_block, tables[d], tables[d + 1])
                skewed = pltpu.roll(joined, 1, 1, stride=1, stride_axis=0)
                sums = jnp.sum(skewed, axis=0, keepdims=True) * scale
                lane = d % halves * LANES
                place = ((first + d) // halves, slice(None), slice(lane, lane + LANES))
                out_ref[place] = jnp.where(filter_row == f, sums, out_ref[place])

        if batch == blocks:
            some_lags(0)
        else:
            lax.fori_loop(0, blocks // batch, lambda i, c: (some_lags(i * batch), c)[1], 0)
        return 0

    for f in range(owned):
        turned_all[f] = lax.dot_general(
            mirror, u_all[f], (((1,), (1,)), ((), ())), preferred_element_type=F32
        ).astype(BF16)
    lax.fori_loop(0, owned, one_filter, 0, unroll=min(owned, 4))


def filter_lags(received, done, shards, chans, owned, scale):
    tok_rows = received.shape[2]
    groups = received.shape[1] // (2 * owned)
    halves = tok_rows // LANES
    depth = chans * groups
    full = shards * halves * depth
    args = (received,)
    if owned % SUBLANES:
        split = received.reshape(shards, chans, 2, groups, owned, halves, LANES)
        split = split.transpose(2, 4, 0, 5, 1, 3, 6).reshape(2, owned, full, LANES)
        args = (split[0], split[1])
    whole = pl.BlockSpec(memory_space=pltpu.VMEM)
    return pl.pallas_call(
        functools.partial(lag_kernel, shards, chans, groups, owned, scale),
        in_specs=[pl.BlockSpec(memory_space=pl.ANY)] + [whole] * len(args),
        out_specs=whole,
        out_shape=jax.ShapeDtypeStruct((shards, owned, tok_rows), F32),
        scratch_shapes=[
            pltpu.VMEM((owned, full, LANES), BF16),
            pltpu.VMEM((owned, 2 * full + depth, LANES), BF16),
            pltpu.VMEM((owned, LANES, full), BF16),
        ],
        compiler_params=pltpu.CompilerParams(vmem_limit_bytes=VMEM_BYTES),
        cost_estimate=takes(0.1),
        name="filter_lags",
    )(done, *args)


def per_device(query_proj, key_proj, value_proj, out_grad, residues, decay_rate, skip_gain):
    tok_rows, width = key_proj.shape
    shards = lax.axis_size("seq")
    chans = lax.axis_size("chan")
    length = shards * tok_rows
    owned = FILTERS // (shards * chans)
    modes = residues.shape[1]
    signals = (query_proj, key_proj, value_proj, out_grad)

    send = pack_signals(shards, chans, owned, *signals)
    send, *signals, residues, decay_rate = lax.optimization_barrier(
        (send, *signals, residues, decay_rate)
    )
    received = lax.all_to_all(send, ("seq", "chan"), split_axis=0, concat_axis=0, tiled=True)

    coefs = jnp.stack(
        [
            jnp.exp(-decay_rate),
            jnp.exp(-(decay_rate * float(tok_rows))),
            residues * jnp.sqrt(decay_rate),
        ]
    )
    coefs = coefs.transpose(0, 2, 1).reshape(3, modes, 1, FILTERS // LANES, LANES)
    coefs = jnp.broadcast_to(coefs, (3, modes, width // FILTERS, FILTERS // LANES, LANES))
    coefs = coefs.reshape(3, modes, width // LANES, LANES)
    seq_index = lax.axis_index("seq").reshape(1)
    pairs = shards // 2
    own, sent = block_states(*signals, coefs)
    near = inside_pair(sent, pairs)
    states = pair_states(seq_index, pairs, coefs, own, near)
    *states, coefs, near = lax.optimization_barrier((*states, coefs, near))
    states = [along_column(state, pairs, 1 + i) for i, state in enumerate(states)]
    parts, done = local_parts(*signals, coefs, skip_gain[None, :])

    scale = 1.0 / math.sqrt(length * (CHANNELS // FILTERS))
    lags = filter_lags(received, done, shards, chans, owned, scale)
    lags = lax.all_to_all(lags, "seq", split_axis=0, concat_axis=0, tiled=True)
    filter_grad = lags.reshape(shards * owned, tok_rows).T
    query_proj, key_proj, value_proj, _ = signals
    layer_out, key_grad, value_grad = final_outputs(
        seq_index, coefs, near, states, parts, query_proj, value_proj, key_proj
    )
    return (layer_out, key_grad, value_grad, filter_grad)


def solution(mesh):
    split = P("seq", "chan")
    return jax.shard_map(
        per_device,
        mesh=mesh,
        in_specs=(split, split, split, split, P(), P(), P("chan")),
        out_specs=(split, split, split, split),
        check_vma=False,
    )
```

```python
import functools
import math

import jax
import jax.numpy as jnp
from jax import lax
from jax.experimental import pallas as pl
from jax.experimental.pallas import tpu as pltpu
from jax.sharding import PartitionSpec as P

CHANNELS = 4096
FILTERS = 256
LANES = 128
SUBLANES = 8
GAP = 8
VMEM_BYTES = 16 * 1024 * 1024
FULL_VMEM_BYTES = 62 * 1024 * 1024
F32 = jnp.float32
BF16 = jnp.bfloat16
LINK = jnp.bfloat16


def takes(micros):
    return pl.CostEstimate(flops=0, bytes_accessed=int(micros * 3.6e6), transcendentals=0)


def product(first, second):
    return first * second


def one_hot(rows, cols, column_of):
    row = lax.broadcasted_iota(jnp.int32, (rows, cols), 0)
    col = lax.broadcasted_iota(jnp.int32, (rows, cols), 1)
    return (col == column_of(row)).astype(F32).astype(BF16)


def pack_kernel(shards, chans, owned, *refs):
    hbm_refs, send_ref, held, packed, in_sems, out_sems = refs[:4], *refs[4:]
    tok_rows, width = held.shape[1:]
    groups = width // FILTERS
    per_chan = FILTERS // chans
    units = [(which, first) for which in range(2) for first in range(0, groups, 2)]

    def arrival(i, first):
        place = (slice(None), pl.ds(first * FILTERS, 2 * FILTERS))
        return pltpu.make_async_copy(
            hbm_refs[i].at[place], held.at[(i, *place)], in_sems.at[i, first // 2]
        )

    def departure(which, first):
        if owned % SUBLANES:
            place = (which, pl.ds(first, 2))
        else:
            place = (slice(None), pl.ds((which * groups + first) * owned, 2 * owned))
        return pltpu.make_async_copy(
            packed.at[place], send_ref.at[place], out_sems.at[which, first // 2]
        )

    for which, first in units:
        for i in (2 * which, 2 * which + 1):
            arrival(i, first).start()

    def owned_filter(row):
        seq = row // (chans * owned)
        chan = row // owned % chans
        return chan * per_chan + seq * owned + row % owned

    order = one_hot(FILTERS, FILTERS, owned_filter)
    for which, first in units:
        for i in (2 * which, 2 * which + 1):
            arrival(i, first).wait()
        pieces = []
        for group in (first, first + 1):
            cols = slice(group * FILTERS, (group + 1) * FILTERS)
            piece = lax.dot_general(
                order,
                product(held[2 * which, :, cols], held[2 * which + 1, :, cols]),
                (((1,), (1,)), ((), ())),
                preferred_element_type=F32,
            )
            if owned % SUBLANES:
                packed[which, group] = piece.astype(BF16)
            else:
                pieces.append(piece.reshape(shards * chans, owned, tok_rows))
        if pieces:
            row = (which * groups + first) * owned
            packed[:, row : row + 2 * owned, :] = jnp.concatenate(pieces, axis=1).astype(BF16)
        departure(which, first).start()
    for which, first in units:
        departure(which, first).wait()


def pack_signals(shards, chans, owned, query_proj, key_proj, value_proj, out_grad):
    tok_rows, width = key_proj.shape
    groups = width // FILTERS
    dests = shards * chans
    if owned % SUBLANES:
        shape = (2, groups, FILTERS, tok_rows)
    else:
        shape = (dests, 2 * groups * owned, tok_rows)
    send = pl.pallas_call(
        functools.partial(pack_kernel, shards, chans, owned),
        in_specs=[pl.BlockSpec(memory_space=pl.ANY)] * 4,
        out_specs=pl.BlockSpec(memory_space=pl.ANY),
        out_shape=jax.ShapeDtypeStruct(shape, BF16),
        scratch_shapes=[
            pltpu.VMEM((4, tok_rows, width), BF16),
            pltpu.VMEM(shape, BF16),
            pltpu.SemaphoreType.DMA((4, groups // 2)),
            pltpu.SemaphoreType.DMA((2, groups // 2)),
        ],
        compiler_params=pltpu.CompilerParams(vmem_limit_bytes=FULL_VMEM_BYTES),
        cost_estimate=takes(3.0),
        name="pack_signals",
    )(key_proj, value_proj, out_grad, query_proj)
    if owned % SUBLANES:
        send = send.reshape(2, groups, dests, owned, tok_rows)
        send = send.transpose(2, 0, 1, 3, 4).reshape(dests, 2 * groups * owned, tok_rows)
    return send


def tile_rows(tok_rows, tile):
    first = tile * (tok_rows + GAP)
    return slice(first, first + tok_rows)


def token_shape(tok_rows, tiles):
    return (tiles * (tok_rows + GAP), LANES)


def token_place(t, tok_rows, tiles):
    return (pl.ds(t, tiles, stride=tok_rows + GAP), slice(None))


def spread_tokens(a_ref, b_ref, x_ref):
    tok_rows, width = a_ref.shape
    for tile in range(width // LANES):
        cols = slice(tile * LANES, (tile + 1) * LANES)
        x_ref[tile_rows(tok_rows, tile), :] = product(a_ref[:, cols], b_ref[:, cols]).astype(F32)


def walk_tokens(ref, coef_ref, tok_rows, tiles, start, move):
    modes = coef_ref.shape[1]
    decay = [coef_ref[0, m] for m in range(modes)]
    weight = [coef_ref[2, m] for m in range(modes)]

    def step(t, held):
        place = token_place(start + move * t, tok_rows, tiles)
        x = ref[place]
        held = tuple(decay[m] * held[m] + x for m in range(modes))
        ref[place] = tree_sum([weight[m] * held[m] for m in range(modes)])
        return held

    zero = tuple(jnp.zeros((tiles, LANES), F32) for _ in range(modes))
    return lax.fori_loop(0, tok_rows, step, zero, unroll=8)


def tree_sum(terms):
    while len(terms) > 1:
        terms = [sum(terms[i : i + 2][1:], terms[i]) for i in range(0, len(terms), 2)]
    return terms[0]


def state_kernel(q_ref, k_ref, v_ref, o_ref, coef_ref, own_ref, sent_ref, x_ref, g_ref):
    tok_rows, width = k_ref.shape
    tiles = width // LANES
    modes = coef_ref.shape[1]
    spread_tokens(k_ref, v_ref, x_ref)
    spread_tokens(o_ref, q_ref, g_ref)
    decay = [coef_ref[0, m] for m in range(modes)]

    def step(t, carry):
        x = x_ref[token_place(t, tok_rows, tiles)]
        g = g_ref[token_place(tok_rows - 1 - t, tok_rows, tiles)]
        ahead = tuple(decay[m] * carry[0][m] + x for m in range(modes))
        behind = tuple(decay[m] * carry[1][m] + g for m in range(modes))
        return (ahead, behind)

    zero = tuple(jnp.zeros((tiles, LANES), F32) for _ in range(modes))
    for side, held in enumerate(lax.fori_loop(0, tok_rows, step, (zero, zero), unroll=8)):
        held = jnp.concatenate(held, axis=0)
        own_ref[side] = held
        sent_ref[side] = held.astype(LINK)


def block_states(query_proj, key_proj, value_proj, out_grad, coefs):
    tok_rows, width = key_proj.shape
    modes, tiles = coefs.shape[1:3]
    return pl.pallas_call(
        state_kernel,
        out_shape=[
            jax.ShapeDtypeStruct((2, modes * tiles, LANES), F32),
            jax.ShapeDtypeStruct((2, modes * tiles, LANES), LINK),
        ],
        scratch_shapes=[pltpu.VMEM(token_shape(tok_rows, tiles), F32)] * 2,
        compiler_params=pltpu.CompilerParams(vmem_limit_bytes=VMEM_BYTES),
        cost_estimate=takes(3.0),
        name="block_states",
    )(query_proj, key_proj, value_proj, out_grad, coefs)


def pair_kernel(seq_ref, coef_ref, own_ref, near_ref, *state_refs):
    pairs = len(state_refs) + 1
    modes, tiles = coef_ref.shape[1:3]
    pair = seq_ref[0] // 2
    second = seq_ref[0] % 2 == 1
    for m in range(modes):
        rows = slice(m * tiles, (m + 1) * tiles)
        decay = coef_ref[1, m]
        own, near = own_ref[0, rows], near_ref[0].astype(F32)[rows]
        ahead = jnp.where(second, own + decay * near, near + decay * own)
        own, near = own_ref[1, rows], near_ref[1].astype(F32)[rows]
        behind = jnp.where(second, near + decay * own, own + decay * near)
        for k in range(1, pairs):
            state_refs[k - 1][rows] = jnp.where(pair + k < pairs, ahead, behind)


def pair_states(seq_index, pairs, coefs, own, near):
    whole = pl.BlockSpec(memory_space=pltpu.VMEM)
    states = pl.pallas_call(
        pair_kernel,
        in_specs=[pl.BlockSpec(memory_space=pltpu.SMEM)] + [whole] * 3,
        out_specs=[whole] * (pairs - 1),
        out_shape=[jax.ShapeDtypeStruct(own.shape[1:], F32)] * (pairs - 1),
        compiler_params=pltpu.CompilerParams(vmem_limit_bytes=VMEM_BYTES),
        cost_estimate=takes(0.1),
        name="pair_states",
    )(seq_index, coefs, own, near)
    return [state.astype(LINK) for state in states]


def sum_pairs(side, seq, coef_ref, near_ref, state_refs):
    pairs = len(state_refs) + 1
    modes, tiles = coef_ref.shape[1:3]
    pair, count = seq // 2, (seq // 2, pairs - 1 - seq // 2)[side]
    beside = seq % 2 == 1 - side
    held = []
    for m in range(modes):
        rows = slice(m * tiles, (m + 1) * tiles)
        decay = coef_ref[1, m]
        total = jnp.zeros((tiles, LANES), F32)
        for k in range(pairs - 1, 0, -1):
            state_ref = state_refs[k - 1 if side == 0 else pairs - k - 1]
            block = state_ref[...].astype(F32)[rows]
            total = decay * decay * total + jnp.where(k <= count, block, 0.0)
        near = near_ref[side].astype(F32)[rows]
        held.append(jnp.where(beside, decay * total + near, total))
    return held


def local_kernel(
    q_ref, k_ref, v_ref, o_ref, coef_ref, gain_ref, part_ref, done_ref
):
    conv_ref, grad_ref = part_ref.at[0], part_ref.at[1]
    tok_rows, width = k_ref.shape
    tiles = width // LANES
    spread_tokens(k_ref, v_ref, conv_ref)
    spread_tokens(o_ref, q_ref, grad_ref)
    walk_tokens(conv_ref, coef_ref, tok_rows, tiles, 0, 1)
    walk_tokens(grad_ref, coef_ref, tok_rows, tiles, tok_rows - 1, -1)
    for tile in range(tiles):
        cols = slice(tile * LANES, (tile + 1) * LANES)
        rows = tile_rows(tok_rows, tile)
        gain = gain_ref[:, cols]
        conv_in = product(k_ref[:, cols], v_ref[:, cols]).astype(F32)
        conv_ref[rows, :] = conv_ref[rows, :] + gain * conv_in
        mid_grad = product(o_ref[:, cols], q_ref[:, cols]).astype(F32)
        grad_ref[rows, :] = grad_ref[rows, :] + gain * mid_grad
    done_ref[...] = jnp.zeros(done_ref.shape, F32)


def local_parts(query_proj, key_proj, value_proj, out_grad, coefs, gain):
    tok_rows, width = key_proj.shape
    tiles = coefs.shape[2]
    return pl.pallas_call(
        local_kernel,
        out_shape=[
            jax.ShapeDtypeStruct((2, *token_shape(tok_rows, tiles)), F32),
            jax.ShapeDtypeStruct((SUBLANES, LANES), F32),
        ],
        compiler_params=pltpu.CompilerParams(vmem_limit_bytes=VMEM_BYTES),
        cost_estimate=takes(6.5),
        name="local_parts",
    )(query_proj, key_proj, value_proj, out_grad, coefs, gain)


def along_column(state, pairs, k):
    route = [(2 * p + b, 2 * ((p + k) % pairs) + b) for p in range(pairs) for b in range(2)]
    return lax.ppermute(state, "seq", route)


def inside_pair(state, pairs):
    return lax.ppermute(state, "seq", [(i, i ^ 1) for i in range(2 * pairs)])


def fill_edge(ref, held, coef_ref, tok_rows, tiles, start, move):
    modes = coef_ref.shape[1]
    decay = [coef_ref[0, m] for m in range(modes)]

    def step(t, held):
        held = tuple(decay[m] * held[m] for m in range(modes))
        ref[token_place(start + move * t, tok_rows, tiles)] = tree_sum(list(held))
        return held

    held = tuple(coef_ref[2, m] * held[m] for m in range(modes))
    lax.fori_loop(0, tok_rows, step, held, unroll=8)


def final_kernel(count, *refs):
    seq_ref, hbm_refs, refs = refs[0], refs[1 : 1 + count], refs[1 + count :]
    out_hbm, held_refs, refs = refs[:3], refs[3 : 3 + count], refs[3 + count :]
    edge_ref, out_refs, in_sems, out_sems = refs[0], refs[1:4], refs[4], refs[5]
    coef_ref, near_ref, *state_refs = held_refs[:-4]
    part_ref, q_ref, v_ref, k_ref = held_refs[-4:]
    tok_rows, width = k_ref.shape
    tiles = width // LANES
    pieces = list(zip(hbm_refs[:-4], held_refs[:-4]))
    small = len(pieces)
    pieces += [(hbm_refs[-4].at[0], part_ref.at[0]), (hbm_refs[-3], q_ref)]
    pieces += [(hbm_refs[-4].at[1], part_ref.at[1])] + list(zip(hbm_refs[-2:], held_refs[-2:]))
    arrivals = [
        pltpu.make_async_copy(source, target, in_sems.at[i])
        for i, (source, target) in enumerate(pieces)
    ]
    departures = []

    def multiply_out(side, outs):
        for tile in range(tiles):
            cols = slice(tile * LANES, (tile + 1) * LANES)
            rows = tile_rows(tok_rows, tile)
            value = part_ref[side, rows, :] + edge_ref[rows, :]
            for i, factor_ref in outs:
                out_refs[i][:, cols] = (value * factor_ref[:, cols].astype(F32)).astype(BF16)
                place = (slice(None), pl.ds(tile * LANES, LANES))
                copy = pltpu.make_async_copy(
                    out_refs[i].at[place], out_hbm[i].at[place], out_sems.at[i, tile]
                )
                copy.start()
                departures.append(copy)

    for copy in arrivals:
        copy.start()
    for copy in arrivals[:small]:
        copy.wait()
    held = sum_pairs(0, seq_ref[0], coef_ref, near_ref, state_refs)
    fill_edge(edge_ref, held, coef_ref, tok_rows, tiles, 0, 1)
    for copy in arrivals[small : small + 2]:
        copy.wait()
    multiply_out(0, [(0, q_ref)])
    held = sum_pairs(1, seq_ref[0], coef_ref, near_ref, state_refs)
    fill_edge(edge_ref, held, coef_ref, tok_rows, tiles, tok_rows - 1, -1)
    for copy in arrivals[small + 2 :]:
        copy.wait()
    multiply_out(1, [(1, v_ref), (2, k_ref)])
    for copy in departures:
        copy.wait()


def final_outputs(seq_index, coefs, near, states, parts, query_proj, value_proj, key_proj):
    tok_rows, width = key_proj.shape
    tiles = coefs.shape[2]
    args = (coefs, near, *states, parts, query_proj, value_proj, key_proj)
    away = pl.BlockSpec(memory_space=pl.ANY)
    return pl.pallas_call(
        functools.partial(final_kernel, len(args)),
        in_specs=[pl.BlockSpec(memory_space=pltpu.SMEM)] + [away] * len(args),
        out_specs=[away] * 3,
        out_shape=[jax.ShapeDtypeStruct((tok_rows, width), BF16)] * 3,
        scratch_shapes=[pltpu.VMEM(arg.shape, arg.dtype) for arg in args]
        + [pltpu.VMEM(token_shape(tok_rows, tiles), F32)]
        + [pltpu.VMEM((tok_rows, width), BF16)] * 3
        + [pltpu.SemaphoreType.DMA((len(args) + 1,)), pltpu.SemaphoreType.DMA((3, tiles))],
        compiler_params=pltpu.CompilerParams(vmem_limit_bytes=FULL_VMEM_BYTES),
        cost_estimate=takes(5.0),
        name="final_outputs",
    )(seq_index, *args)


def lag_kernel(shards, chans, groups, owned, scale, *refs):
    in_refs, (out_ref, u_all, g_all, turned_all) = refs[1:-4], refs[-4:]
    tok_rows = out_ref.shape[2]
    halves = tok_rows // LANES
    blocks = shards * halves
    depth = chans * groups
    full = blocks * depth
    if len(in_refs) == 1:
        take = chans * groups * owned

        def by_filter(row):
            return row % depth * owned + row // depth

        order = one_hot(take, take, by_filter)
        for which, kept in enumerate((u_all, g_all)):
            rows = slice(which * groups * owned, (which + 1) * groups * owned)
            for s in range(shards):
                piece = in_refs[0][s * chans : (s + 1) * chans, rows, :].reshape(take, tok_rows)
                piece = jnp.dot(order, piece, preferred_element_type=F32).astype(BF16)
                piece = piece.reshape(owned, depth, tok_rows)
                for h in range(halves):
                    first = (s * halves + h) * depth
                    kept[:, first : first + depth, :] = piece[:, :, h * LANES : (h + 1) * LANES]
    else:
        u_all[...] = in_refs[0][...]
        g_all[:, :full, :] = in_refs[1][...]
    g_all[:, full:, :] = jnp.zeros((owned, g_all.shape[1] - full, LANES), BF16)
    mirror = one_hot(LANES, LANES, lambda row: LANES - 1 - row)
    row = lax.broadcasted_iota(jnp.int32, (LANES, LANES), 0)
    col = lax.broadcasted_iota(jnp.int32, (LANES, LANES), 1)
    same_block = row + col >= LANES - 1
    filter_row = lax.broadcasted_iota(jnp.int32, (owned, LANES), 0)
    batch = min(blocks, 16)

    def one_filter(f, _):
        turned = turned_all[f]

        def some_lags(first):
            tables = []
            for d in range(0, batch, 2):
                live = full
                if batch == blocks:
                    live = min(full, -(-(blocks - d) * depth // LANES) * LANES)
                pair = jnp.concatenate(
                    [
                        g_all[f, pl.ds(pl.multiple_of((first + d + e) * depth, depth), live), :]
                        for e in range(2)
                    ],
                    axis=1,
                )
                table = jnp.dot(turned[:, :live], pair, preferred_element_type=F32)
                tables += [table[:, :LANES], table[:, LANES:]]
            last = g_all[f, pl.ds(pl.multiple_of((first + batch) * depth, depth), full), :]
            if batch < blocks:
                tables.append(jnp.dot(turned, last, preferred_element_type=F32))
            else:
                tables.append(jnp.zeros((LANES, LANES), F32))
            for d in range(batch):
                joined = jnp.where(same_block, tables[d], tables[d + 1])
                skewed = pltpu.roll(joined, 1, 1, stride=1, stride_axis=0)
                sums = jnp.sum(skewed, axis=0, keepdims=True) * scale
                lane = d % halves * LANES
                place = ((first + d) // halves, slice(None), slice(lane, lane + LANES))
                out_ref[place] = jnp.where(filter_row == f, sums, out_ref[place])

        if batch == blocks:
            some_lags(0)
        else:
            lax.fori_loop(0, blocks // batch, lambda i, c: (some_lags(i * batch), c)[1], 0)
        return 0

    for f in range(owned):
        turned_all[f] = lax.dot_general(
            mirror, u_all[f], (((1,), (1,)), ((), ())), preferred_element_type=F32
        ).astype(BF16)
    lax.fori_loop(0, owned, one_filter, 0, unroll=min(owned, 4))


def filter_lags(received, done, shards, chans, owned, scale):
    tok_rows = received.shape[2]
    groups = received.shape[1] // (2 * owned)
    halves = tok_rows // LANES
    depth = chans * groups
    full = shards * halves * depth
    args = (received,)
    if owned % SUBLANES:
        split = received.reshape(shards, chans, 2, groups, owned, halves, LANES)
        split = split.transpose(2, 4, 0, 5, 1, 3, 6).reshape(2, owned, full, LANES)
        args = (split[0], split[1])
    whole = pl.BlockSpec(memory_space=pltpu.VMEM)
    return pl.pallas_call(
        functools.partial(lag_kernel, shards, chans, groups, owned, scale),
        in_specs=[pl.BlockSpec(memory_space=pl.ANY)] + [whole] * len(args),
        out_specs=whole,
        out_shape=jax.ShapeDtypeStruct((shards, owned, tok_rows), F32),
        scratch_shapes=[
            pltpu.VMEM((owned, full, LANES), BF16),
            pltpu.VMEM((owned, 2 * full + depth, LANES), BF16),
            pltpu.VMEM((owned, LANES, full), BF16),
        ],
        compiler_params=pltpu.CompilerParams(vmem_limit_bytes=VMEM_BYTES),
        cost_estimate=takes(0.1),
        name="filter_lags",
    )(done, *args)


def per_device(query_proj, key_proj, value_proj, out_grad, residues, decay_rate, skip_gain):
    tok_rows, width = key_proj.shape
    shards = lax.axis_size("seq")
    chans = lax.axis_size("chan")
    length = shards * tok_rows
    owned = FILTERS // (shards * chans)
    modes = residues.shape[1]
    signals = (query_proj, key_proj, value_proj, out_grad)

    send = pack_signals(shards, chans, owned, *signals)
    send, *signals, residues, decay_rate = lax.optimization_barrier(
        (send, *signals, residues, decay_rate)
    )
    received = lax.all_to_all(send, ("seq", "chan"), split_axis=0, concat_axis=0, tiled=True)

    coefs = jnp.stack(
        [
            jnp.exp(-decay_rate),
            jnp.exp(-(decay_rate * float(tok_rows))),
            residues * jnp.sqrt(decay_rate),
        ]
    )
    coefs = coefs.transpose(0, 2, 1).reshape(3, modes, 1, FILTERS // LANES, LANES)
    coefs = jnp.broadcast_to(coefs, (3, modes, width // FILTERS, FILTERS // LANES, LANES))
    coefs = coefs.reshape(3, modes, width // LANES, LANES)
    seq_index = lax.axis_index("seq").reshape(1)
    pairs = shards // 2
    own, sent = block_states(*signals, coefs)
    near = inside_pair(sent, pairs)
    states = pair_states(seq_index, pairs, coefs, own, near)
    *states, coefs, near = lax.optimization_barrier((*states, coefs, near))
    states = [along_column(state, pairs, 1 + i) for i, state in enumerate(states)]
    parts, done = local_parts(*signals, coefs, skip_gain[None, :])

    scale = 1.0 / math.sqrt(length * (CHANNELS // FILTERS))
    lags = filter_lags(received, done, shards, chans, owned, scale)
    lags, *states = lax.optimization_barrier((lags, *states))
    lags = lax.all_to_all(lags, "seq", split_axis=0, concat_axis=0, tiled=True)
    filter_grad = lags.reshape(shards * owned, tok_rows).T
    query_proj, key_proj, value_proj, _ = signals
    layer_out, key_grad, value_grad = final_outputs(
        seq_index, coefs, near, states, parts, query_proj, value_proj, key_proj
    )
    return (layer_out, key_grad, value_grad, filter_grad)


def solution(mesh):
    split = P("seq", "chan")
    return jax.shard_map(
        per_device,
        mesh=mesh,
        in_specs=(split, split, split, split, P(), P(), P("chan")),
        out_specs=(split, split, split, split),
        check_vma=False,
    )
```

```python
import functools
import math

import jax
import jax.numpy as jnp
from jax import lax
from jax.experimental import pallas as pl
from jax.experimental.pallas import tpu as pltpu
from jax.sharding import PartitionSpec as P

CHANNELS = 4096
FILTERS = 256
LANES = 128
SUBLANES = 8
GAP = 8
VMEM_BYTES = 16 * 1024 * 1024
FULL_VMEM_BYTES = 62 * 1024 * 1024
F32 = jnp.float32
BF16 = jnp.bfloat16
LINK = jnp.bfloat16


def takes(micros):
    return pl.CostEstimate(flops=0, bytes_accessed=int(micros * 3.6e6), transcendentals=0)


def product(first, second):
    return first * second


def one_hot(rows, cols, column_of):
    row = lax.broadcasted_iota(jnp.int32, (rows, cols), 0)
    col = lax.broadcasted_iota(jnp.int32, (rows, cols), 1)
    return (col == column_of(row)).astype(F32).astype(BF16)


def pack_kernel(shards, chans, owned, *refs):
    hbm_refs, send_ref, held, packed, in_sems, out_sems = refs[:4], *refs[4:]
    tok_rows, width = held.shape[1:]
    groups = width // FILTERS
    per_chan = FILTERS // chans
    units = [(which, first) for which in range(2) for first in range(0, groups, 2)]

    def arrival(i, first):
        place = (slice(None), pl.ds(first * FILTERS, 2 * FILTERS))
        return pltpu.make_async_copy(
            hbm_refs[i].at[place], held.at[(i, *place)], in_sems.at[i, first // 2]
        )

    def departure(which, first):
        if owned % SUBLANES:
            place = (which, pl.ds(first, 2))
        else:
            place = (slice(None), pl.ds((which * groups + first) * owned, 2 * owned))
        return pltpu.make_async_copy(
            packed.at[place], send_ref.at[place], out_sems.at[which, first // 2]
        )

    for which, first in units:
        for i in (2 * which, 2 * which + 1):
            arrival(i, first).start()

    def owned_filter(row):
        seq = row // (chans * owned)
        chan = row // owned % chans
        return chan * per_chan + seq * owned + row % owned

    order = one_hot(FILTERS, FILTERS, owned_filter)
    for which, first in units:
        for i in (2 * which, 2 * which + 1):
            arrival(i, first).wait()
        pieces = []
        for group in (first, first + 1):
            cols = slice(group * FILTERS, (group + 1) * FILTERS)
            piece = lax.dot_general(
                order,
                product(held[2 * which, :, cols], held[2 * which + 1, :, cols]),
                (((1,), (1,)), ((), ())),
                preferred_element_type=F32,
            )
            if owned % SUBLANES:
                packed[which, group] = piece.astype(BF16)
            else:
                pieces.append(piece.reshape(shards * chans, owned, tok_rows))
        if pieces:
            row = (which * groups + first) * owned
            packed[:, row : row + 2 * owned, :] = jnp.concatenate(pieces, axis=1).astype(BF16)
        departure(which, first).start()
    for which, first in units:
        departure(which, first).wait()


def pack_signals(shards, chans, owned, query_proj, key_proj, value_proj, out_grad):
    tok_rows, width = key_proj.shape
    groups = width // FILTERS
    dests = shards * chans
    if owned % SUBLANES:
        shape = (2, groups, FILTERS, tok_rows)
    else:
        shape = (dests, 2 * groups * owned, tok_rows)
    send = pl.pallas_call(
        functools.partial(pack_kernel, shards, chans, owned),
        in_specs=[pl.BlockSpec(memory_space=pl.ANY)] * 4,
        out_specs=pl.BlockSpec(memory_space=pl.ANY),
        out_shape=jax.ShapeDtypeStruct(shape, BF16),
        scratch_shapes=[
            pltpu.VMEM((4, tok_rows, width), BF16),
            pltpu.VMEM(shape, BF16),
            pltpu.SemaphoreType.DMA((4, groups // 2)),
            pltpu.SemaphoreType.DMA((2, groups // 2)),
        ],
        compiler_params=pltpu.CompilerParams(vmem_limit_bytes=FULL_VMEM_BYTES),
        cost_estimate=takes(3.0),
        name="pack_signals",
    )(key_proj, value_proj, out_grad, query_proj)
    if owned % SUBLANES:
        send = send.reshape(2, groups, dests, owned, tok_rows)
        send = send.transpose(2, 0, 1, 3, 4).reshape(dests, 2 * groups * owned, tok_rows)
    return send


def tile_rows(tok_rows, tile):
    first = tile * (tok_rows + GAP)
    return slice(first, first + tok_rows)


def token_shape(tok_rows, tiles):
    return (tiles * (tok_rows + GAP), LANES)


def token_place(t, tok_rows, tiles):
    return (pl.ds(t, tiles, stride=tok_rows + GAP), slice(None))


def spread_tokens(a_ref, b_ref, x_ref):
    tok_rows, width = a_ref.shape
    for tile in range(width // LANES):
        cols = slice(tile * LANES, (tile + 1) * LANES)
        x_ref[tile_rows(tok_rows, tile), :] = product(a_ref[:, cols], b_ref[:, cols]).astype(F32)


def walk_tokens(ref, coef_ref, tok_rows, tiles, start, move):
    modes = coef_ref.shape[1]
    decay = [coef_ref[0, m] for m in range(modes)]
    weight = [coef_ref[2, m] for m in range(modes)]

    def step(t, held):
        place = token_place(start + move * t, tok_rows, tiles)
        x = ref[place]
        held = tuple(decay[m] * held[m] + x for m in range(modes))
        ref[place] = tree_sum([weight[m] * held[m] for m in range(modes)])
        return held

    zero = tuple(jnp.zeros((tiles, LANES), F32) for _ in range(modes))
    return lax.fori_loop(0, tok_rows, step, zero, unroll=8)


def tree_sum(terms):
    while len(terms) > 1:
        terms = [sum(terms[i : i + 2][1:], terms[i]) for i in range(0, len(terms), 2)]
    return terms[0]


def state_kernel(q_ref, k_ref, v_ref, o_ref, coef_ref, own_ref, sent_ref, x_ref, g_ref):
    tok_rows, width = k_ref.shape
    tiles = width // LANES
    modes = coef_ref.shape[1]
    spread_tokens(k_ref, v_ref, x_ref)
    spread_tokens(o_ref, q_ref, g_ref)
    decay = [coef_ref[0, m] for m in range(modes)]

    def step(t, carry):
        x = x_ref[token_place(t, tok_rows, tiles)]
        g = g_ref[token_place(tok_rows - 1 - t, tok_rows, tiles)]
        ahead = tuple(decay[m] * carry[0][m] + x for m in range(modes))
        behind = tuple(decay[m] * carry[1][m] + g for m in range(modes))
        return (ahead, behind)

    zero = tuple(jnp.zeros((tiles, LANES), F32) for _ in range(modes))
    for side, held in enumerate(lax.fori_loop(0, tok_rows, step, (zero, zero), unroll=8)):
        held = jnp.concatenate(held, axis=0)
        own_ref[side] = held
        sent_ref[side] = held.astype(LINK)


def block_states(query_proj, key_proj, value_proj, out_grad, coefs):
    tok_rows, width = key_proj.shape
    modes, tiles = coefs.shape[1:3]
    return pl.pallas_call(
        state_kernel,
        out_shape=[
            jax.ShapeDtypeStruct((2, modes * tiles, LANES), F32),
            jax.ShapeDtypeStruct((2, modes * tiles, LANES), LINK),
        ],
        scratch_shapes=[pltpu.VMEM(token_shape(tok_rows, tiles), F32)] * 2,
        compiler_params=pltpu.CompilerParams(vmem_limit_bytes=VMEM_BYTES),
        cost_estimate=takes(3.0),
        name="block_states",
    )(query_proj, key_proj, value_proj, out_grad, coefs)


def pair_kernel(seq_ref, coef_ref, own_ref, near_ref, *state_refs):
    pairs = len(state_refs) + 1
    modes, tiles = coef_ref.shape[1:3]
    pair = seq_ref[0] // 2
    second = seq_ref[0] % 2 == 1
    for m in range(modes):
        rows = slice(m * tiles, (m + 1) * tiles)
        decay = coef_ref[1, m]
        own, near = own_ref[0, rows], near_ref[0].astype(F32)[rows]
        ahead = jnp.where(second, own + decay * near, near + decay * own)
        own, near = own_ref[1, rows], near_ref[1].astype(F32)[rows]
        behind = jnp.where(second, near + decay * own, own + decay * near)
        for k in range(1, pairs):
            state_refs[k - 1][rows] = jnp.where(pair + k < pairs, ahead, behind)


def pair_states(seq_index, pairs, coefs, own, near):
    whole = pl.BlockSpec(memory_space=pltpu.VMEM)
    states = pl.pallas_call(
        pair_kernel,
        in_specs=[pl.BlockSpec(memory_space=pltpu.SMEM)] + [whole] * 3,
        out_specs=[whole] * (pairs - 1),
        out_shape=[jax.ShapeDtypeStruct(own.shape[1:], F32)] * (pairs - 1),
        compiler_params=pltpu.CompilerParams(vmem_limit_bytes=VMEM_BYTES),
        cost_estimate=takes(0.1),
        name="pair_states",
    )(seq_index, coefs, own, near)
    return [state.astype(LINK) for state in states]


def sum_pairs(side, seq, coef_ref, near_ref, state_refs):
    pairs = len(state_refs) + 1
    modes, tiles = coef_ref.shape[1:3]
    pair, count = seq // 2, (seq // 2, pairs - 1 - seq // 2)[side]
    beside = seq % 2 == 1 - side
    held = []
    for m in range(modes):
        rows = slice(m * tiles, (m + 1) * tiles)
        decay = coef_ref[1, m]
        total = jnp.zeros((tiles, LANES), F32)
        for k in range(pairs - 1, 0, -1):
            state_ref = state_refs[k - 1 if side == 0 else pairs - k - 1]
            block = state_ref[...].astype(F32)[rows]
            total = decay * decay * total + jnp.where(k <= count, block, 0.0)
        near = near_ref[side].astype(F32)[rows]
        held.append(jnp.where(beside, decay * total + near, total))
    return held


def local_kernel(
    q_ref, k_ref, v_ref, o_ref, coef_ref, gain_ref, part_ref, done_ref
):
    conv_ref, grad_ref = part_ref.at[0], part_ref.at[1]
    tok_rows, width = k_ref.shape
    tiles = width // LANES
    spread_tokens(k_ref, v_ref, conv_ref)
    spread_tokens(o_ref, q_ref, grad_ref)
    walk_tokens(conv_ref, coef_ref, tok_rows, tiles, 0, 1)
    walk_tokens(grad_ref, coef_ref, tok_rows, tiles, tok_rows - 1, -1)
    for tile in range(tiles):
        cols = slice(tile * LANES, (tile + 1) * LANES)
        rows = tile_rows(tok_rows, tile)
        gain = gain_ref[:, cols]
        conv_in = product(k_ref[:, cols], v_ref[:, cols]).astype(F32)
        conv_ref[rows, :] = conv_ref[rows, :] + gain * conv_in
        mid_grad = product(o_ref[:, cols], q_ref[:, cols]).astype(F32)
        grad_ref[rows, :] = grad_ref[rows, :] + gain * mid_grad
    done_ref[...] = jnp.zeros(done_ref.shape, F32)


def local_parts(query_proj, key_proj, value_proj, out_grad, coefs, gain):
    tok_rows, width = key_proj.shape
    tiles = coefs.shape[2]
    return pl.pallas_call(
        local_kernel,
        out_shape=[
            jax.ShapeDtypeStruct((2, *token_shape(tok_rows, tiles)), F32),
            jax.ShapeDtypeStruct((SUBLANES, LANES), F32),
        ],
        compiler_params=pltpu.CompilerParams(vmem_limit_bytes=FULL_VMEM_BYTES),
        cost_estimate=takes(6.5),
        name="local_parts",
    )(query_proj, key_proj, value_proj, out_grad, coefs, gain)


def along_column(state, pairs, k):
    route = [(2 * p + b, 2 * ((p + k) % pairs) + b) for p in range(pairs) for b in range(2)]
    return lax.ppermute(state, "seq", route)


def inside_pair(state, pairs):
    return lax.ppermute(state, "seq", [(i, i ^ 1) for i in range(2 * pairs)])


def fill_edge(ref, held, coef_ref, tok_rows, tiles, start, move):
    modes = coef_ref.shape[1]
    decay = [coef_ref[0, m] for m in range(modes)]

    def step(t, held):
        held = tuple(decay[m] * held[m] for m in range(modes))
        ref[token_place(start + move * t, tok_rows, tiles)] = tree_sum(list(held))
        return held

    held = tuple(coef_ref[2, m] * held[m] for m in range(modes))
    lax.fori_loop(0, tok_rows, step, held, unroll=8)


def final_kernel(count, *refs):
    seq_ref, hbm_refs, refs = refs[0], refs[1 : 1 + count], refs[1 + count :]
    out_hbm, held_refs, refs = refs[:3], refs[3 : 3 + count], refs[3 + count :]
    edge_ref, out_refs, in_sems, out_sems = refs[0], refs[1:4], refs[4], refs[5]
    coef_ref, near_ref, *state_refs = held_refs[:-4]
    part_ref, q_ref, v_ref, k_ref = held_refs[-4:]
    tok_rows, width = k_ref.shape
    tiles = width // LANES
    pieces = list(zip(hbm_refs[:-4], held_refs[:-4]))
    small = len(pieces)
    pieces += [(hbm_refs[-4].at[0], part_ref.at[0]), (hbm_refs[-3], q_ref)]
    pieces += [(hbm_refs[-4].at[1], part_ref.at[1])] + list(zip(hbm_refs[-2:], held_refs[-2:]))
    arrivals = [
        pltpu.make_async_copy(source, target, in_sems.at[i])
        for i, (source, target) in enumerate(pieces)
    ]
    departures = []

    def multiply_out(side, outs):
        for tile in range(tiles):
            cols = slice(tile * LANES, (tile + 1) * LANES)
            rows = tile_rows(tok_rows, tile)
            value = part_ref[side, rows, :] + edge_ref[rows, :]
            for i, factor_ref in outs:
                out_refs[i][:, cols] = (value * factor_ref[:, cols].astype(F32)).astype(BF16)
                place = (slice(None), pl.ds(tile * LANES, LANES))
                copy = pltpu.make_async_copy(
                    out_refs[i].at[place], out_hbm[i].at[place], out_sems.at[i, tile]
                )
                copy.start()
                departures.append(copy)

    for copy in arrivals:
        copy.start()
    for copy in arrivals[:small]:
        copy.wait()
    held = sum_pairs(0, seq_ref[0], coef_ref, near_ref, state_refs)
    fill_edge(edge_ref, held, coef_ref, tok_rows, tiles, 0, 1)
    for copy in arrivals[small : small + 2]:
        copy.wait()
    multiply_out(0, [(0, q_ref)])
    held = sum_pairs(1, seq_ref[0], coef_ref, near_ref, state_refs)
    fill_edge(edge_ref, held, coef_ref, tok_rows, tiles, tok_rows - 1, -1)
    for copy in arrivals[small + 2 :]:
        copy.wait()
    multiply_out(1, [(1, v_ref), (2, k_ref)])
    for copy in departures:
        copy.wait()


def final_outputs(seq_index, coefs, near, states, parts, query_proj, value_proj, key_proj):
    tok_rows, width = key_proj.shape
    tiles = coefs.shape[2]
    args = (coefs, near, *states, parts, query_proj, value_proj, key_proj)
    away = pl.BlockSpec(memory_space=pl.ANY)
    return pl.pallas_call(
        functools.partial(final_kernel, len(args)),
        in_specs=[pl.BlockSpec(memory_space=pltpu.SMEM)] + [away] * len(args),
        out_specs=[away] * 3,
        out_shape=[jax.ShapeDtypeStruct((tok_rows, width), BF16)] * 3,
        scratch_shapes=[pltpu.VMEM(arg.shape, arg.dtype) for arg in args]
        + [pltpu.VMEM(token_shape(tok_rows, tiles), F32)]
        + [pltpu.VMEM((tok_rows, width), BF16)] * 3
        + [pltpu.SemaphoreType.DMA((len(args) + 1,)), pltpu.SemaphoreType.DMA((3, tiles))],
        compiler_params=pltpu.CompilerParams(vmem_limit_bytes=FULL_VMEM_BYTES),
        cost_estimate=takes(5.0),
        name="final_outputs",
    )(seq_index, *args)


def lag_kernel(shards, chans, groups, owned, scale, *refs):
    in_refs, (out_ref, u_all, g_all, turned_all) = refs[1:-4], refs[-4:]
    tok_rows = out_ref.shape[2]
    halves = tok_rows // LANES
    blocks = shards * halves
    depth = chans * groups
    full = blocks * depth
    if len(in_refs) == 1:
        take = chans * groups * owned

        def by_filter(row):
            return row % depth * owned + row // depth

        order = one_hot(take, take, by_filter)
        for which, kept in enumerate((u_all, g_all)):
            rows = slice(which * groups * owned, (which + 1) * groups * owned)
            for s in range(shards):
                piece = in_refs[0][s * chans : (s + 1) * chans, rows, :].reshape(take, tok_rows)
                piece = jnp.dot(order, piece, preferred_element_type=F32).astype(BF16)
                piece = piece.reshape(owned, depth, tok_rows)
                for h in range(halves):
                    first = (s * halves + h) * depth
                    kept[:, first : first + depth, :] = piece[:, :, h * LANES : (h + 1) * LANES]
    else:
        u_all[...] = in_refs[0][...]
        g_all[:, :full, :] = in_refs[1][...]
    g_all[:, full:, :] = jnp.zeros((owned, g_all.shape[1] - full, LANES), BF16)
    mirror = one_hot(LANES, LANES, lambda row: LANES - 1 - row)
    row = lax.broadcasted_iota(jnp.int32, (LANES, LANES), 0)
    col = lax.broadcasted_iota(jnp.int32, (LANES, LANES), 1)
    same_block = row + col >= LANES - 1
    filter_row = lax.broadcasted_iota(jnp.int32, (owned, LANES), 0)
    batch = min(blocks, 16)

    def one_filter(f, _):
        turned = turned_all[f]

        def some_lags(first):
            tables = []
            for d in range(0, batch, 2):
                live = full
                if batch == blocks:
                    live = min(full, -(-(blocks - d) * depth // LANES) * LANES)
                pair = jnp.concatenate(
                    [
                        g_all[f, pl.ds(pl.multiple_of((first + d + e) * depth, depth), live), :]
                        for e in range(2)
                    ],
                    axis=1,
                )
                table = jnp.dot(turned[:, :live], pair, preferred_element_type=F32)
                tables += [table[:, :LANES], table[:, LANES:]]
            last = g_all[f, pl.ds(pl.multiple_of((first + batch) * depth, depth), full), :]
            if batch < blocks:
                tables.append(jnp.dot(turned, last, preferred_element_type=F32))
            else:
                tables.append(jnp.zeros((LANES, LANES), F32))
            for d in range(batch):
                joined = jnp.where(same_block, tables[d], tables[d + 1])
                skewed = pltpu.roll(joined, 1, 1, stride=1, stride_axis=0)
                sums = jnp.sum(skewed, axis=0, keepdims=True) * scale
                lane = d % halves * LANES
                place = ((first + d) // halves, slice(None), slice(lane, lane + LANES))
                out_ref[place] = jnp.where(filter_row == f, sums, out_ref[place])

        if batch == blocks:
            some_lags(0)
        else:
            lax.fori_loop(0, blocks // batch, lambda i, c: (some_lags(i * batch), c)[1], 0)
        return 0

    for f in range(owned):
        turned_all[f] = lax.dot_general(
            mirror, u_all[f], (((1,), (1,)), ((), ())), preferred_element_type=F32
        ).astype(BF16)
    lax.fori_loop(0, owned, one_filter, 0, unroll=min(owned, 8))


def filter_lags(received, done, shards, chans, owned, scale):
    tok_rows = received.shape[2]
    groups = received.shape[1] // (2 * owned)
    halves = tok_rows // LANES
    depth = chans * groups
    full = shards * halves * depth
    args = (received,)
    if owned % SUBLANES:
        split = received.reshape(shards, chans, 2, groups, owned, halves, LANES)
        split = split.transpose(2, 4, 0, 5, 1, 3, 6).reshape(2, owned, full, LANES)
        args = (split[0], split[1])
    whole = pl.BlockSpec(memory_space=pltpu.VMEM)
    return pl.pallas_call(
        functools.partial(lag_kernel, shards, chans, groups, owned, scale),
        in_specs=[pl.BlockSpec(memory_space=pl.ANY)] + [whole] * len(args),
        out_specs=whole,
        out_shape=jax.ShapeDtypeStruct((shards, owned, tok_rows), F32),
        scratch_shapes=[
            pltpu.VMEM((owned, full, LANES), BF16),
            pltpu.VMEM((owned, 2 * full + depth, LANES), BF16),
            pltpu.VMEM((owned, LANES, full), BF16),
        ],
        compiler_params=pltpu.CompilerParams(vmem_limit_bytes=VMEM_BYTES),
        cost_estimate=takes(0.1),
        name="filter_lags",
    )(done, *args)


def per_device(query_proj, key_proj, value_proj, out_grad, residues, decay_rate, skip_gain):
    tok_rows, width = key_proj.shape
    shards = lax.axis_size("seq")
    chans = lax.axis_size("chan")
    length = shards * tok_rows
    owned = FILTERS // (shards * chans)
    modes = residues.shape[1]
    signals = (query_proj, key_proj, value_proj, out_grad)

    send = pack_signals(shards, chans, owned, *signals)
    send, *signals, residues, decay_rate = lax.optimization_barrier(
        (send, *signals, residues, decay_rate)
    )
    received = lax.all_to_all(send, ("seq", "chan"), split_axis=0, concat_axis=0, tiled=True)

    coefs = jnp.stack(
        [
            jnp.exp(-decay_rate),
            jnp.exp(-(decay_rate * float(tok_rows))),
            residues * jnp.sqrt(decay_rate),
        ]
    )
    coefs = coefs.transpose(0, 2, 1).reshape(3, modes, 1, FILTERS // LANES, LANES)
    coefs = jnp.broadcast_to(coefs, (3, modes, width // FILTERS, FILTERS // LANES, LANES))
    coefs = coefs.reshape(3, modes, width // LANES, LANES)
    seq_index = lax.axis_index("seq").reshape(1)
    pairs = shards // 2
    own, sent = block_states(*signals, coefs)
    near = inside_pair(sent, pairs)
    states = pair_states(seq_index, pairs, coefs, own, near)
    *states, coefs, near = lax.optimization_barrier((*states, coefs, near))
    states = [along_column(state, pairs, 1 + i) for i, state in enumerate(states)]
    parts, done = local_parts(*signals, coefs, skip_gain[None, :])

    scale = 1.0 / math.sqrt(length * (CHANNELS // FILTERS))
    lags = filter_lags(received, done, shards, chans, owned, scale)
    lags, *states = lax.optimization_barrier((lags, *states))
    lags = lax.all_to_all(lags, "seq", split_axis=0, concat_axis=0, tiled=True)
    filter_grad = lags.reshape(shards * owned, tok_rows).T
    query_proj, key_proj, value_proj, _ = signals
    layer_out, key_grad, value_grad = final_outputs(
        seq_index, coefs, near, states, parts, query_proj, value_proj, key_proj
    )
    return (layer_out, key_grad, value_grad, filter_grad)


def solution(mesh):
    split = P("seq", "chan")
    return jax.shard_map(
        per_device,
        mesh=mesh,
        in_specs=(split, split, split, split, P(), P(), P("chan")),
        out_specs=(split, split, split, split),
        check_vma=False,
    )
```

```python
import functools
import math

import jax
import jax.numpy as jnp
from jax import lax
from jax.experimental import pallas as pl
from jax.experimental.pallas import tpu as pltpu
from jax.sharding import PartitionSpec as P

CHANNELS = 4096
FILTERS = 256
LANES = 128
SUBLANES = 8
GAP = 8
VMEM_BYTES = 16 * 1024 * 1024
FULL_VMEM_BYTES = 62 * 1024 * 1024
F32 = jnp.float32
BF16 = jnp.bfloat16
LINK = jnp.bfloat16


def takes(micros):
    return pl.CostEstimate(flops=0, bytes_accessed=int(micros * 3.6e6), transcendentals=0)


def product(first, second):
    return first * second


def one_hot(rows, cols, column_of):
    row = lax.broadcasted_iota(jnp.int32, (rows, cols), 0)
    col = lax.broadcasted_iota(jnp.int32, (rows, cols), 1)
    return (col == column_of(row)).astype(F32).astype(BF16)


def pack_kernel(shards, chans, owned, *refs):
    hbm_refs, send_ref, held, packed, in_sems, out_sems = refs[:4], *refs[4:]
    tok_rows, width = held.shape[1:]
    groups = width // FILTERS
    per_chan = FILTERS // chans
    units = [(which, first) for which in range(2) for first in range(0, groups, 2)]

    def arrival(i, first):
        place = (slice(None), pl.ds(first * FILTERS, 2 * FILTERS))
        return pltpu.make_async_copy(
            hbm_refs[i].at[place], held.at[(i, *place)], in_sems.at[i, first // 2]
        )

    def departure(which, first):
        if owned % SUBLANES:
            place = (which, pl.ds(first, 2))
        else:
            place = (slice(None), pl.ds((which * groups + first) * owned, 2 * owned))
        return pltpu.make_async_copy(
            packed.at[place], send_ref.at[place], out_sems.at[which, first // 2]
        )

    for which, first in units:
        for i in (2 * which, 2 * which + 1):
            arrival(i, first).start()

    def owned_filter(row):
        seq = row // (chans * owned)
        chan = row // owned % chans
        return chan * per_chan + seq * owned + row % owned

    order = one_hot(FILTERS, FILTERS, owned_filter)
    for which, first in units:
        for i in (2 * which, 2 * which + 1):
            arrival(i, first).wait()
        pieces = []
        for group in (first, first + 1):
            cols = slice(group * FILTERS, (group + 1) * FILTERS)
            piece = lax.dot_general(
                order,
                product(held[2 * which, :, cols], held[2 * which + 1, :, cols]),
                (((1,), (1,)), ((), ())),
                preferred_element_type=F32,
            )
            if owned % SUBLANES:
                packed[which, group] = piece.astype(BF16)
            else:
                pieces.append(piece.reshape(shards * chans, owned, tok_rows))
        if pieces:
            row = (which * groups + first) * owned
            packed[:, row : row + 2 * owned, :] = jnp.concatenate(pieces, axis=1).astype(BF16)
        departure(which, first).start()
    for which, first in units:
        departure(which, first).wait()


def pack_signals(shards, chans, owned, query_proj, key_proj, value_proj, out_grad):
    tok_rows, width = key_proj.shape
    groups = width // FILTERS
    dests = shards * chans
    if owned % SUBLANES:
        shape = (2, groups, FILTERS, tok_rows)
    else:
        shape = (dests, 2 * groups * owned, tok_rows)
    send = pl.pallas_call(
        functools.partial(pack_kernel, shards, chans, owned),
        in_specs=[pl.BlockSpec(memory_space=pl.ANY)] * 4,
        out_specs=pl.BlockSpec(memory_space=pl.ANY),
        out_shape=jax.ShapeDtypeStruct(shape, BF16),
        scratch_shapes=[
            pltpu.VMEM((4, tok_rows, width), BF16),
            pltpu.VMEM(shape, BF16),
            pltpu.SemaphoreType.DMA((4, groups // 2)),
            pltpu.SemaphoreType.DMA((2, groups // 2)),
        ],
        compiler_params=pltpu.CompilerParams(vmem_limit_bytes=FULL_VMEM_BYTES),
        cost_estimate=takes(3.0),
        name="pack_signals",
    )(key_proj, value_proj, out_grad, query_proj)
    if owned % SUBLANES:
        send = send.reshape(2, groups, dests, owned, tok_rows)
        send = send.transpose(2, 0, 1, 3, 4).reshape(dests, 2 * groups * owned, tok_rows)
    return send


def tile_rows(tok_rows, tile):
    first = tile * (tok_rows + GAP)
    return slice(first, first + tok_rows)


def token_shape(tok_rows, tiles):
    return (tiles * (tok_rows + GAP), LANES)


def token_place(t, tok_rows, tiles):
    return (pl.ds(t, tiles, stride=tok_rows + GAP), slice(None))


def spread_tokens(a_ref, b_ref, x_ref):
    tok_rows, width = a_ref.shape
    for tile in range(width // LANES):
        cols = slice(tile * LANES, (tile + 1) * LANES)
        x_ref[tile_rows(tok_rows, tile), :] = product(a_ref[:, cols], b_ref[:, cols]).astype(F32)


def walk_tokens(ref, coef_ref, tok_rows, tiles, start, move):
    modes = coef_ref.shape[1]
    decay = [coef_ref[0, m] for m in range(modes)]
    weight = [coef_ref[2, m] for m in range(modes)]

    def step(t, held):
        place = token_place(start + move * t, tok_rows, tiles)
        x = ref[place]
        held = tuple(decay[m] * held[m] + x for m in range(modes))
        ref[place] = tree_sum([weight[m] * held[m] for m in range(modes)])
        return held

    zero = tuple(jnp.zeros((tiles, LANES), F32) for _ in range(modes))
    return lax.fori_loop(0, tok_rows, step, zero, unroll=8)


def tree_sum(terms):
    while len(terms) > 1:
        terms = [sum(terms[i : i + 2][1:], terms[i]) for i in range(0, len(terms), 2)]
    return terms[0]


def state_kernel(q_ref, k_ref, v_ref, o_ref, coef_ref, own_ref, sent_ref, x_ref, g_ref):
    tok_rows, width = k_ref.shape
    tiles = width // LANES
    modes = coef_ref.shape[1]
    spread_tokens(k_ref, v_ref, x_ref)
    spread_tokens(o_ref, q_ref, g_ref)
    decay = [coef_ref[0, m] for m in range(modes)]

    def step(t, carry):
        x = x_ref[token_place(t, tok_rows, tiles)]
        g = g_ref[token_place(tok_rows - 1 - t, tok_rows, tiles)]
        ahead = tuple(decay[m] * carry[0][m] + x for m in range(modes))
        behind = tuple(decay[m] * carry[1][m] + g for m in range(modes))
        return (ahead, behind)

    zero = tuple(jnp.zeros((tiles, LANES), F32) for _ in range(modes))
    for side, held in enumerate(lax.fori_loop(0, tok_rows, step, (zero, zero), unroll=8)):
        held = jnp.concatenate(held, axis=0)
        own_ref[side] = held
        sent_ref[side] = held.astype(LINK)


def block_states(query_proj, key_proj, value_proj, out_grad, coefs):
    tok_rows, width = key_proj.shape
    modes, tiles = coefs.shape[1:3]
    return pl.pallas_call(
        state_kernel,
        out_shape=[
            jax.ShapeDtypeStruct((2, modes * tiles, LANES), F32),
            jax.ShapeDtypeStruct((2, modes * tiles, LANES), LINK),
        ],
        scratch_shapes=[pltpu.VMEM(token_shape(tok_rows, tiles), F32)] * 2,
        compiler_params=pltpu.CompilerParams(vmem_limit_bytes=VMEM_BYTES),
        cost_estimate=takes(3.0),
        name="block_states",
    )(query_proj, key_proj, value_proj, out_grad, coefs)


def pair_kernel(seq_ref, coef_ref, own_ref, near_ref, *state_refs):
    pairs = len(state_refs) + 1
    modes, tiles = coef_ref.shape[1:3]
    pair = seq_ref[0] // 2
    second = seq_ref[0] % 2 == 1
    for m in range(modes):
        rows = slice(m * tiles, (m + 1) * tiles)
        decay = coef_ref[1, m]
        own, near = own_ref[0, rows], near_ref[0].astype(F32)[rows]
        ahead = jnp.where(second, own + decay * near, near + decay * own)
        own, near = own_ref[1, rows], near_ref[1].astype(F32)[rows]
        behind = jnp.where(second, near + decay * own, own + decay * near)
        for k in range(1, pairs):
            state_refs[k - 1][rows] = jnp.where(pair + k < pairs, ahead, behind)


def pair_states(seq_index, pairs, coefs, own, near):
    whole = pl.BlockSpec(memory_space=pltpu.VMEM)
    states = pl.pallas_call(
        pair_kernel,
        in_specs=[pl.BlockSpec(memory_space=pltpu.SMEM)] + [whole] * 3,
        out_specs=[whole] * (pairs - 1),
        out_shape=[jax.ShapeDtypeStruct(own.shape[1:], F32)] * (pairs - 1),
        compiler_params=pltpu.CompilerParams(vmem_limit_bytes=VMEM_BYTES),
        cost_estimate=takes(0.1),
        name="pair_states",
    )(seq_index, coefs, own, near)
    return [state.astype(LINK) for state in states]


def sum_pairs(side, seq, coef_ref, near_ref, state_refs):
    pairs = len(state_refs) + 1
    modes, tiles = coef_ref.shape[1:3]
    pair, count = seq // 2, (seq // 2, pairs - 1 - seq // 2)[side]
    beside = seq % 2 == 1 - side
    held = []
    for m in range(modes):
        rows = slice(m * tiles, (m + 1) * tiles)
        decay = coef_ref[1, m]
        total = jnp.zeros((tiles, LANES), F32)
        for k in range(pairs - 1, 0, -1):
            state_ref = state_refs[k - 1 if side == 0 else pairs - k - 1]
            block = state_ref[...].astype(F32)[rows]
            total = decay * decay * total + jnp.where(k <= count, block, 0.0)
        near = near_ref[side].astype(F32)[rows]
        held.append(jnp.where(beside, decay * total + near, total))
    return held


def local_kernel(
    q_ref, k_ref, v_ref, o_ref, coef_ref, gain_ref, conv_ref, grad_ref, done_ref
):
    tok_rows, width = k_ref.shape
    tiles = width // LANES
    spread_tokens(k_ref, v_ref, conv_ref)
    spread_tokens(o_ref, q_ref, grad_ref)
    walk_tokens(conv_ref, coef_ref, tok_rows, tiles, 0, 1)
    walk_tokens(grad_ref, coef_ref, tok_rows, tiles, tok_rows - 1, -1)
    for tile in range(tiles):
        cols = slice(tile * LANES, (tile + 1) * LANES)
        rows = tile_rows(tok_rows, tile)
        gain = gain_ref[:, cols]
        conv_in = product(k_ref[:, cols], v_ref[:, cols]).astype(F32)
        conv_ref[rows, :] = conv_ref[rows, :] + gain * conv_in
        mid_grad = product(o_ref[:, cols], q_ref[:, cols]).astype(F32)
        grad_ref[rows, :] = grad_ref[rows, :] + gain * mid_grad
    done_ref[...] = jnp.zeros(done_ref.shape, F32)


def local_parts(query_proj, key_proj, value_proj, out_grad, coefs, gain):
    tok_rows, width = key_proj.shape
    tiles = coefs.shape[2]
    return pl.pallas_call(
        local_kernel,
        out_shape=[jax.ShapeDtypeStruct(token_shape(tok_rows, tiles), F32)] * 2
        + [jax.ShapeDtypeStruct((SUBLANES, LANES), F32)],
        compiler_params=pltpu.CompilerParams(vmem_limit_bytes=VMEM_BYTES),
        cost_estimate=takes(6.5),
        name="local_parts",
    )(query_proj, key_proj, value_proj, out_grad, coefs, gain)


def along_column(state, pairs, k):
    route = [(2 * p + b, 2 * ((p + k) % pairs) + b) for p in range(pairs) for b in range(2)]
    return lax.ppermute(state, "seq", route)


def inside_pair(state, pairs):
    return lax.ppermute(state, "seq", [(i, i ^ 1) for i in range(2 * pairs)])


def fill_edge(ref, held, coef_ref, tok_rows, tiles, start, move):
    modes = coef_ref.shape[1]
    decay = [coef_ref[0, m] for m in range(modes)]

    def step(t, held):
        held = tuple(decay[m] * held[m] for m in range(modes))
        ref[token_place(start + move * t, tok_rows, tiles)] = tree_sum(list(held))
        return held

    held = tuple(coef_ref[2, m] * held[m] for m in range(modes))
    lax.fori_loop(0, tok_rows, step, held, unroll=8)


def final_kernel(count, *refs):
    seq_ref, hbm_refs, refs = refs[0], refs[1 : 1 + count], refs[1 + count :]
    out_hbm, held_refs, refs = refs[:3], refs[3 : 3 + count], refs[3 + count :]
    edge_ref, out_refs, in_sems, out_sems = refs[0], refs[1:4], refs[4], refs[5]
    coef_ref, near_ref, *state_refs = held_refs[:-5]
    conv_ref, q_ref, grad_ref, v_ref, k_ref = held_refs[-5:]
    tok_rows, width = k_ref.shape
    tiles = width // LANES
    small = count - 5
    arrivals = [
        pltpu.make_async_copy(source, target, in_sems.at[i])
        for i, (source, target) in enumerate(zip(hbm_refs, held_refs))
    ]
    departures = []

    def multiply_out(part_ref, outs):
        for tile in range(tiles):
            cols = slice(tile * LANES, (tile + 1) * LANES)
            rows = tile_rows(tok_rows, tile)
            value = part_ref[rows, :] + edge_ref[rows, :]
            for i, factor_ref in outs:
                out_refs[i][:, cols] = (value * factor_ref[:, cols].astype(F32)).astype(BF16)
                place = (slice(None), pl.ds(tile * LANES, LANES))
                copy = pltpu.make_async_copy(
                    out_refs[i].at[place], out_hbm[i].at[place], out_sems.at[i, tile]
                )
                copy.start()
                departures.append(copy)

    for copy in arrivals:
        copy.start()
    for copy in arrivals[:small]:
        copy.wait()
    held = sum_pairs(0, seq_ref[0], coef_ref, near_ref, state_refs)
    fill_edge(edge_ref, held, coef_ref, tok_rows, tiles, 0, 1)
    for copy in arrivals[small : small + 2]:
        copy.wait()
    multiply_out(conv_ref, [(0, q_ref)])
    held = sum_pairs(1, seq_ref[0], coef_ref, near_ref, state_refs)
    fill_edge(edge_ref, held, coef_ref, tok_rows, tiles, tok_rows - 1, -1)
    for copy in arrivals[small + 2 :]:
        copy.wait()
    multiply_out(grad_ref, [(1, v_ref), (2, k_ref)])
    for copy in departures:
        copy.wait()


def final_outputs(
    seq_index, coefs, near, states, conv_part, grad_part, query_proj, value_proj, key_proj
):
    tok_rows, width = key_proj.shape
    tiles = coefs.shape[2]
    args = (coefs, near, *states, conv_part, query_proj, grad_part, value_proj, key_proj)
    away = pl.BlockSpec(memory_space=pl.ANY)
    return pl.pallas_call(
        functools.partial(final_kernel, len(args)),
        in_specs=[pl.BlockSpec(memory_space=pltpu.SMEM)] + [away] * len(args),
        out_specs=[away] * 3,
        out_shape=[jax.ShapeDtypeStruct((tok_rows, width), BF16)] * 3,
        scratch_shapes=[pltpu.VMEM(arg.shape, arg.dtype) for arg in args]
        + [pltpu.VMEM(token_shape(tok_rows, tiles), F32)]
        + [pltpu.VMEM((tok_rows, width), BF16)] * 3
        + [pltpu.SemaphoreType.DMA((len(args),)), pltpu.SemaphoreType.DMA((3, tiles))],
        compiler_params=pltpu.CompilerParams(vmem_limit_bytes=FULL_VMEM_BYTES),
        cost_estimate=takes(5.0),
        name="final_outputs",
    )(seq_index, *args)


def lag_kernel(shards, chans, groups, owned, scale, *refs):
    in_refs, (out_ref, u_all, g_all, turned_all) = refs[1:-4], refs[-4:]
    tok_rows = out_ref.shape[2]
    halves = tok_rows // LANES
    blocks = shards * halves
    depth = chans * groups
    full = blocks * depth
    if len(in_refs) == 1:
        take = chans * groups * owned

        def by_filter(row):
            return row % depth * owned + row // depth

        order = one_hot(take, take, by_filter)
        for which, kept in enumerate((u_all, g_all)):
            rows = slice(which * groups * owned, (which + 1) * groups * owned)
            for s in range(shards):
                piece = in_refs[0][s * chans : (s + 1) * chans, rows, :].reshape(take, tok_rows)
                piece = jnp.dot(order, piece, preferred_element_type=F32).astype(BF16)
                piece = piece.reshape(owned, depth, tok_rows)
                for h in range(halves):
                    first = (s * halves + h) * depth
                    kept[:, first : first + depth, :] = piece[:, :, h * LANES : (h + 1) * LANES]
    else:
        u_all[...] = in_refs[0][...]
        g_all[:, :full, :] = in_refs[1][...]
    g_all[:, full:, :] = jnp.zeros((owned, g_all.shape[1] - full, LANES), BF16)
    mirror = one_hot(LANES, LANES, lambda row: LANES - 1 - row)
    row = lax.broadcasted_iota(jnp.int32, (LANES, LANES), 0)
    col = lax.broadcasted_iota(jnp.int32, (LANES, LANES), 1)
    same_block = row + col >= LANES - 1
    filter_row = lax.broadcasted_iota(jnp.int32, (owned, LANES), 0)
    batch = min(blocks, 16)

    def one_filter(f, _):
        turned = turned_all[f]

        def some_lags(first):
            tables = []
            for d in range(0, batch, 2):
                live = full
                if batch == blocks:
                    live = min(full, -(-(blocks - d) * depth // LANES) * LANES)
                pair = jnp.concatenate(
                    [
                        g_all[f, pl.ds(pl.multiple_of((first + d + e) * depth, depth), live), :]
                        for e in range(2)
                    ],
                    axis=1,
                )
                table = jnp.dot(turned[:, :live], pair, preferred_element_type=F32)
                tables += [table[:, :LANES], table[:, LANES:]]
            last = g_all[f, pl.ds(pl.multiple_of((first + batch) * depth, depth), full), :]
            if batch < blocks:
                tables.append(jnp.dot(turned, last, preferred_element_type=F32))
            else:
                tables.append(jnp.zeros((LANES, LANES), F32))
            for d in range(batch):
                joined = jnp.where(same_block, tables[d], tables[d + 1])
                skewed = pltpu.roll(joined, 1, 1, stride=1, stride_axis=0)
                sums = jnp.sum(skewed, axis=0, keepdims=True) * scale
                lane = d % halves * LANES
                place = ((first + d) // halves, slice(None), slice(lane, lane + LANES))
                out_ref[place] = jnp.where(filter_row == f, sums, out_ref[place])

        if batch == blocks:
            some_lags(0)
        else:
            lax.fori_loop(0, blocks // batch, lambda i, c: (some_lags(i * batch), c)[1], 0)
        return 0

    for f in range(owned):
        turned_all[f] = lax.dot_general(
            mirror, u_all[f], (((1,), (1,)), ((), ())), preferred_element_type=F32
        ).astype(BF16)
    lax.fori_loop(0, owned, one_filter, 0, unroll=min(owned, 8))


def filter_lags(received, done, shards, chans, owned, scale):
    tok_rows = received.shape[2]
    groups = received.shape[1] // (2 * owned)
    halves = tok_rows // LANES
    depth = chans * groups
    full = shards * halves * depth
    args = (received,)
    if owned % SUBLANES:
        split = received.reshape(shards, chans, 2, groups, owned, halves, LANES)
        split = split.transpose(2, 4, 0, 5, 1, 3, 6).reshape(2, owned, full, LANES)
        args = (split[0], split[1])
    whole = pl.BlockSpec(memory_space=pltpu.VMEM)
    return pl.pallas_call(
        functools.partial(lag_kernel, shards, chans, groups, owned, scale),
        in_specs=[pl.BlockSpec(memory_space=pl.ANY)] + [whole] * len(args),
        out_specs=whole,
        out_shape=jax.ShapeDtypeStruct((shards, owned, tok_rows), F32),
        scratch_shapes=[
            pltpu.VMEM((owned, full, LANES), BF16),
            pltpu.VMEM((owned, 2 * full + depth, LANES), BF16),
            pltpu.VMEM((owned, LANES, full), BF16),
        ],
        compiler_params=pltpu.CompilerParams(vmem_limit_bytes=VMEM_BYTES),
        cost_estimate=takes(0.1),
        name="filter_lags",
    )(done, *args)


def per_device(query_proj, key_proj, value_proj, out_grad, residues, decay_rate, skip_gain):
    tok_rows, width = key_proj.shape
    shards = lax.axis_size("seq")
    chans = lax.axis_size("chan")
    length = shards * tok_rows
    owned = FILTERS // (shards * chans)
    modes = residues.shape[1]
    signals = (query_proj, key_proj, value_proj, out_grad)

    send = pack_signals(shards, chans, owned, *signals)
    send, *signals, residues, decay_rate = lax.optimization_barrier(
        (send, *signals, residues, decay_rate)
    )
    received = lax.all_to_all(send, ("seq", "chan"), split_axis=0, concat_axis=0, tiled=True)

    coefs = jnp.stack(
        [
            jnp.exp(-decay_rate),
            jnp.exp(-(decay_rate * float(tok_rows))),
            residues * jnp.sqrt(decay_rate),
        ]
    )
    coefs = coefs.transpose(0, 2, 1).reshape(3, modes, 1, FILTERS // LANES, LANES)
    coefs = jnp.broadcast_to(coefs, (3, modes, width // FILTERS, FILTERS // LANES, LANES))
    coefs = coefs.reshape(3, modes, width // LANES, LANES)
    seq_index = lax.axis_index("seq").reshape(1)
    pairs = shards // 2
    own, sent = block_states(*signals, coefs)
    near = inside_pair(sent, pairs)
    states = pair_states(seq_index, pairs, coefs, own, near)
    *states, coefs, near = lax.optimization_barrier((*states, coefs, near))
    states = [along_column(state, pairs, 1 + i) for i, state in enumerate(states)]
    conv_part, grad_part, done = local_parts(*signals, coefs, skip_gain[None, :])

    scale = 1.0 / math.sqrt(length * (CHANNELS // FILTERS))
    lags = filter_lags(received, done, shards, chans, owned, scale)
    lags, *states = lax.optimization_barrier((lags, *states))
    lags = lax.all_to_all(lags, "seq", split_axis=0, concat_axis=0, tiled=True)
    filter_grad = lags.reshape(shards * owned, tok_rows).T
    query_proj, key_proj, value_proj, _ = signals
    layer_out, key_grad, value_grad = final_outputs(
        seq_index, coefs, near, states, conv_part, grad_part, query_proj, value_proj, key_proj
    )
    return (layer_out, key_grad, value_grad, filter_grad)


def solution(mesh):
    split = P("seq", "chan")
    return jax.shard_map(
        per_device,
        mesh=mesh,
        in_specs=(split, split, split, split, P(), P(), P("chan")),
        out_specs=(split, split, split, split),
        check_vma=False,
    )
```

```python
import functools
import math

import jax
import jax.numpy as jnp
from jax import lax
from jax.experimental import pallas as pl
from jax.experimental.pallas import tpu as pltpu
from jax.sharding import PartitionSpec as P

CHANNELS = 4096
FILTERS = 256
LANES = 128
SUBLANES = 8
GAP = 8
VMEM_BYTES = 16 * 1024 * 1024
FULL_VMEM_BYTES = 62 * 1024 * 1024
F32 = jnp.float32
BF16 = jnp.bfloat16
LINK = jnp.bfloat16


def takes(micros):
    return pl.CostEstimate(flops=0, bytes_accessed=int(micros * 3.6e6), transcendentals=0)


def product(first, second):
    return first * second


def one_hot(rows, cols, column_of):
    row = lax.broadcasted_iota(jnp.int32, (rows, cols), 0)
    col = lax.broadcasted_iota(jnp.int32, (rows, cols), 1)
    return (col == column_of(row)).astype(F32).astype(BF16)


def pack_kernel(shards, chans, owned, *refs):
    hbm_refs, send_ref, held, packed, in_sems, out_sems = refs[:4], *refs[4:]
    tok_rows, width = held.shape[1:]
    groups = width // FILTERS
    per_chan = FILTERS // chans
    units = [(which, first) for which in range(2) for first in range(0, groups, 2)]

    def arrival(i, first):
        place = (slice(None), pl.ds(first * FILTERS, 2 * FILTERS))
        return pltpu.make_async_copy(
            hbm_refs[i].at[place], held.at[(i, *place)], in_sems.at[i, first // 2]
        )

    def departure(which, first):
        if owned % SUBLANES:
            place = (which, pl.ds(first, 2))
        else:
            place = (slice(None), pl.ds((which * groups + first) * owned, 2 * owned))
        return pltpu.make_async_copy(
            packed.at[place], send_ref.at[place], out_sems.at[which, first // 2]
        )

    for which, first in units:
        for i in (2 * which, 2 * which + 1):
            arrival(i, first).start()

    def owned_filter(row):
        chan = row // (shards * owned)
        seq = row // owned % shards
        return chan * per_chan + seq * owned + row % owned

    order = one_hot(FILTERS, FILTERS, owned_filter)
    for which, first in units:
        for i in (2 * which, 2 * which + 1):
            arrival(i, first).wait()
        pieces = []
        for group in (first, first + 1):
            cols = slice(group * FILTERS, (group + 1) * FILTERS)
            piece = lax.dot_general(
                order,
                product(held[2 * which, :, cols], held[2 * which + 1, :, cols]),
                (((1,), (1,)), ((), ())),
                preferred_element_type=F32,
            )
            if owned % SUBLANES:
                packed[which, group] = piece.astype(BF16)
            else:
                pieces.append(piece.reshape(shards * chans, owned, tok_rows))
        if pieces:
            row = (which * groups + first) * owned
            packed[:, row : row + 2 * owned, :] = jnp.concatenate(pieces, axis=1).astype(BF16)
        departure(which, first).start()
    for which, first in units:
        departure(which, first).wait()


def pack_signals(shards, chans, owned, query_proj, key_proj, value_proj, out_grad):
    tok_rows, width = key_proj.shape
    groups = width // FILTERS
    dests = shards * chans
    if owned % SUBLANES:
        shape = (2, groups, FILTERS, tok_rows)
    else:
        shape = (dests, 2 * groups * owned, tok_rows)
    send = pl.pallas_call(
        functools.partial(pack_kernel, shards, chans, owned),
        in_specs=[pl.BlockSpec(memory_space=pl.ANY)] * 4,
        out_specs=pl.BlockSpec(memory_space=pl.ANY),
        out_shape=jax.ShapeDtypeStruct(shape, BF16),
        scratch_shapes=[
            pltpu.VMEM((4, tok_rows, width), BF16),
            pltpu.VMEM(shape, BF16),
            pltpu.SemaphoreType.DMA((4, groups // 2)),
            pltpu.SemaphoreType.DMA((2, groups // 2)),
        ],
        compiler_params=pltpu.CompilerParams(vmem_limit_bytes=FULL_VMEM_BYTES),
        cost_estimate=takes(3.0),
        name="pack_signals",
    )(key_proj, value_proj, out_grad, query_proj)
    if owned % SUBLANES:
        send = send.reshape(2, groups, dests, owned, tok_rows)
        send = send.transpose(2, 0, 1, 3, 4).reshape(dests, 2 * groups * owned, tok_rows)
    return send


def tile_rows(tok_rows, tile):
    first = tile * (tok_rows + GAP)
    return slice(first, first + tok_rows)


def token_shape(tok_rows, tiles):
    return (tiles * (tok_rows + GAP), LANES)


def token_place(t, tok_rows, tiles):
    return (pl.ds(t, tiles, stride=tok_rows + GAP), slice(None))


def spread_tokens(a_ref, b_ref, x_ref):
    tok_rows, width = a_ref.shape
    for tile in range(width // LANES):
        cols = slice(tile * LANES, (tile + 1) * LANES)
        x_ref[tile_rows(tok_rows, tile), :] = product(a_ref[:, cols], b_ref[:, cols]).astype(F32)


def walk_tokens(ref, coef_ref, tok_rows, tiles, start, move):
    modes = coef_ref.shape[1]
    decay = [coef_ref[0, m] for m in range(modes)]
    weight = [coef_ref[2, m] for m in range(modes)]

    def step(t, held):
        place = token_place(start + move * t, tok_rows, tiles)
        x = ref[place]
        held = tuple(decay[m] * held[m] + x for m in range(modes))
        ref[place] = tree_sum([weight[m] * held[m] for m in range(modes)])
        return held

    zero = tuple(jnp.zeros((tiles, LANES), F32) for _ in range(modes))
    return lax.fori_loop(0, tok_rows, step, zero, unroll=8)


def tree_sum(terms):
    while len(terms) > 1:
        terms = [sum(terms[i : i + 2][1:], terms[i]) for i in range(0, len(terms), 2)]
    return terms[0]


def state_kernel(q_ref, k_ref, v_ref, o_ref, coef_ref, own_ref, sent_ref, x_ref, g_ref):
    tok_rows, width = k_ref.shape
    tiles = width // LANES
    modes = coef_ref.shape[1]
    spread_tokens(k_ref, v_ref, x_ref)
    spread_tokens(o_ref, q_ref, g_ref)
    decay = [coef_ref[0, m] for m in range(modes)]

    def step(t, carry):
        x = x_ref[token_place(t, tok_rows, tiles)]
        g = g_ref[token_place(tok_rows - 1 - t, tok_rows, tiles)]
        ahead = tuple(decay[m] * carry[0][m] + x for m in range(modes))
        behind = tuple(decay[m] * carry[1][m] + g for m in range(modes))
        return (ahead, behind)

    zero = tuple(jnp.zeros((tiles, LANES), F32) for _ in range(modes))
    for side, held in enumerate(lax.fori_loop(0, tok_rows, step, (zero, zero), unroll=8)):
        held = jnp.concatenate(held, axis=0)
        own_ref[side] = held
        sent_ref[side] = held.astype(LINK)


def block_states(query_proj, key_proj, value_proj, out_grad, coefs):
    tok_rows, width = key_proj.shape
    modes, tiles = coefs.shape[1:3]
    return pl.pallas_call(
        state_kernel,
        out_shape=[
            jax.ShapeDtypeStruct((2, modes * tiles, LANES), F32),
            jax.ShapeDtypeStruct((2, modes * tiles, LANES), LINK),
        ],
        scratch_shapes=[pltpu.VMEM(token_shape(tok_rows, tiles), F32)] * 2,
        compiler_params=pltpu.CompilerParams(vmem_limit_bytes=VMEM_BYTES),
        cost_estimate=takes(3.0),
        name="block_states",
    )(query_proj, key_proj, value_proj, out_grad, coefs)


def pair_kernel(seq_ref, coef_ref, own_ref, near_ref, *state_refs):
    pairs = len(state_refs) + 1
    modes, tiles = coef_ref.shape[1:3]
    pair = seq_ref[0] // 2
    second = seq_ref[0] % 2 == 1
    for m in range(modes):
        rows = slice(m * tiles, (m + 1) * tiles)
        decay = coef_ref[1, m]
        own, near = own_ref[0, rows], near_ref[0].astype(F32)[rows]
        ahead = jnp.where(second, own + decay * near, near + decay * own)
        own, near = own_ref[1, rows], near_ref[1].astype(F32)[rows]
        behind = jnp.where(second, near + decay * own, own + decay * near)
        for k in range(1, pairs):
            state_refs[k - 1][rows] = jnp.where(pair + k < pairs, ahead, behind)


def pair_states(seq_index, pairs, coefs, own, near):
    whole = pl.BlockSpec(memory_space=pltpu.VMEM)
    states = pl.pallas_call(
        pair_kernel,
        in_specs=[pl.BlockSpec(memory_space=pltpu.SMEM)] + [whole] * 3,
        out_specs=[whole] * (pairs - 1),
        out_shape=[jax.ShapeDtypeStruct(own.shape[1:], F32)] * (pairs - 1),
        compiler_params=pltpu.CompilerParams(vmem_limit_bytes=VMEM_BYTES),
        cost_estimate=takes(0.1),
        name="pair_states",
    )(seq_index, coefs, own, near)
    return [state.astype(LINK) for state in states]


def sum_pairs(side, seq, coef_ref, near_ref, state_refs):
    pairs = len(state_refs) + 1
    modes, tiles = coef_ref.shape[1:3]
    pair, count = seq // 2, (seq // 2, pairs - 1 - seq // 2)[side]
    beside = seq % 2 == 1 - side
    held = []
    for m in range(modes):
        rows = slice(m * tiles, (m + 1) * tiles)
        decay = coef_ref[1, m]
        total = jnp.zeros((tiles, LANES), F32)
        for k in range(pairs - 1, 0, -1):
            state_ref = state_refs[k - 1 if side == 0 else pairs - k - 1]
            block = state_ref[...].astype(F32)[rows]
            total = decay * decay * total + jnp.where(k <= count, block, 0.0)
        near = near_ref[side].astype(F32)[rows]
        held.append(jnp.where(beside, decay * total + near, total))
    return held


def local_kernel(
    q_ref, k_ref, v_ref, o_ref, coef_ref, gain_ref, conv_ref, grad_ref, done_ref
):
    tok_rows, width = k_ref.shape
    tiles = width // LANES
    spread_tokens(k_ref, v_ref, conv_ref)
    spread_tokens(o_ref, q_ref, grad_ref)
    walk_tokens(conv_ref, coef_ref, tok_rows, tiles, 0, 1)
    walk_tokens(grad_ref, coef_ref, tok_rows, tiles, tok_rows - 1, -1)
    for tile in range(tiles):
        cols = slice(tile * LANES, (tile + 1) * LANES)
        rows = tile_rows(tok_rows, tile)
        gain = gain_ref[:, cols]
        conv_in = product(k_ref[:, cols], v_ref[:, cols]).astype(F32)
        conv_ref[rows, :] = conv_ref[rows, :] + gain * conv_in
        mid_grad = product(o_ref[:, cols], q_ref[:, cols]).astype(F32)
        grad_ref[rows, :] = grad_ref[rows, :] + gain * mid_grad
    done_ref[...] = jnp.zeros(done_ref.shape, F32)


def local_parts(query_proj, key_proj, value_proj, out_grad, coefs, gain):
    tok_rows, width = key_proj.shape
    tiles = coefs.shape[2]
    return pl.pallas_call(
        local_kernel,
        out_shape=[jax.ShapeDtypeStruct(token_shape(tok_rows, tiles), F32)] * 2
        + [jax.ShapeDtypeStruct((SUBLANES, LANES), F32)],
        compiler_params=pltpu.CompilerParams(vmem_limit_bytes=VMEM_BYTES),
        cost_estimate=takes(6.5),
        name="local_parts",
    )(query_proj, key_proj, value_proj, out_grad, coefs, gain)


def along_column(state, pairs, k):
    route = [(2 * p + b, 2 * ((p + k) % pairs) + b) for p in range(pairs) for b in range(2)]
    return lax.ppermute(state, "seq", route)


def inside_pair(state, pairs):
    return lax.ppermute(state, "seq", [(i, i ^ 1) for i in range(2 * pairs)])


def fill_edge(ref, held, coef_ref, tok_rows, tiles, start, move):
    modes = coef_ref.shape[1]
    decay = [coef_ref[0, m] for m in range(modes)]

    def step(t, held):
        held = tuple(decay[m] * held[m] for m in range(modes))
        ref[token_place(start + move * t, tok_rows, tiles)] = tree_sum(list(held))
        return held

    held = tuple(coef_ref[2, m] * held[m] for m in range(modes))
    lax.fori_loop(0, tok_rows, step, held, unroll=8)


def final_kernel(count, *refs):
    seq_ref, hbm_refs, refs = refs[0], refs[1 : 1 + count], refs[1 + count :]
    out_hbm, held_refs, refs = refs[:3], refs[3 : 3 + count], refs[3 + count :]
    edge_ref, out_refs, in_sems, out_sems = refs[0], refs[1:4], refs[4], refs[5]
    coef_ref, near_ref, *state_refs = held_refs[:-5]
    conv_ref, q_ref, grad_ref, v_ref, k_ref = held_refs[-5:]
    tok_rows, width = k_ref.shape
    tiles = width // LANES
    small = count - 5
    arrivals = [
        pltpu.make_async_copy(source, target, in_sems.at[i])
        for i, (source, target) in enumerate(zip(hbm_refs, held_refs))
    ]
    departures = []

    def multiply_out(part_ref, outs):
        for tile in range(tiles):
            cols = slice(tile * LANES, (tile + 1) * LANES)
            rows = tile_rows(tok_rows, tile)
            value = part_ref[rows, :] + edge_ref[rows, :]
            for i, factor_ref in outs:
                out_refs[i][:, cols] = (value * factor_ref[:, cols].astype(F32)).astype(BF16)
                place = (slice(None), pl.ds(tile * LANES, LANES))
                copy = pltpu.make_async_copy(
                    out_refs[i].at[place], out_hbm[i].at[place], out_sems.at[i, tile]
                )
                copy.start()
                departures.append(copy)

    for copy in arrivals:
        copy.start()
    for copy in arrivals[:small]:
        copy.wait()
    held = sum_pairs(0, seq_ref[0], coef_ref, near_ref, state_refs)
    fill_edge(edge_ref, held, coef_ref, tok_rows, tiles, 0, 1)
    for copy in arrivals[small : small + 2]:
        copy.wait()
    multiply_out(conv_ref, [(0, q_ref)])
    held = sum_pairs(1, seq_ref[0], coef_ref, near_ref, state_refs)
    fill_edge(edge_ref, held, coef_ref, tok_rows, tiles, tok_rows - 1, -1)
    for copy in arrivals[small + 2 :]:
        copy.wait()
    multiply_out(grad_ref, [(1, v_ref), (2, k_ref)])
    for copy in departures:
        copy.wait()


def final_outputs(
    seq_index, coefs, near, states, conv_part, grad_part, query_proj, value_proj, key_proj
):
    tok_rows, width = key_proj.shape
    tiles = coefs.shape[2]
    args = (coefs, near, *states, conv_part, query_proj, grad_part, value_proj, key_proj)
    away = pl.BlockSpec(memory_space=pl.ANY)
    return pl.pallas_call(
        functools.partial(final_kernel, len(args)),
        in_specs=[pl.BlockSpec(memory_space=pltpu.SMEM)] + [away] * len(args),
        out_specs=[away] * 3,
        out_shape=[jax.ShapeDtypeStruct((tok_rows, width), BF16)] * 3,
        scratch_shapes=[pltpu.VMEM(arg.shape, arg.dtype) for arg in args]
        + [pltpu.VMEM(token_shape(tok_rows, tiles), F32)]
        + [pltpu.VMEM((tok_rows, width), BF16)] * 3
        + [pltpu.SemaphoreType.DMA((len(args),)), pltpu.SemaphoreType.DMA((3, tiles))],
        compiler_params=pltpu.CompilerParams(vmem_limit_bytes=FULL_VMEM_BYTES),
        cost_estimate=takes(5.0),
        name="final_outputs",
    )(seq_index, *args)


def lag_kernel(shards, chans, groups, owned, scale, *refs):
    in_refs, (out_ref, held, sems, u_all, g_all, turned_all) = refs[1:-6], refs[-6:]
    tok_rows = out_ref.shape[2]
    halves = tok_rows // LANES
    blocks = shards * halves
    depth = chans * groups
    full = blocks * depth
    if len(in_refs) == 1:
        take = chans * groups * owned

        def by_filter(row):
            return row % depth * owned + row // depth

        half = shards // 2
        copies = []
        for i in range(2):
            place = (slice(None), pl.ds(i * half, half))
            copies.append(
                pltpu.make_async_copy(in_refs[0].at[place], held.at[place], sems.at[i])
            )
            copies[i].start()
        order = one_hot(take, take, by_filter)
        g_all[:, full:, :] = jnp.zeros((owned, g_all.shape[1] - full, LANES), BF16)
        for i in range(2):
            copies[i].wait()
            for which, kept in enumerate((u_all, g_all)):
                rows = slice(which * groups * owned, (which + 1) * groups * owned)
                for s in range(i * half, (i + 1) * half):
                    piece = held[:, s, rows, :].reshape(take, tok_rows)
                    piece = jnp.dot(order, piece, preferred_element_type=F32).astype(BF16)
                    piece = piece.reshape(owned, depth, tok_rows)
                    for h in range(halves):
                        first = (s * halves + h) * depth
                        kept[:, first : first + depth, :] = piece[:, :, h * LANES : (h + 1) * LANES]
    else:
        u_all[...] = in_refs[0][...]
        g_all[:, :full, :] = in_refs[1][...]
        g_all[:, full:, :] = jnp.zeros((owned, g_all.shape[1] - full, LANES), BF16)
    mirror = one_hot(LANES, LANES, lambda row: LANES - 1 - row)
    row = lax.broadcasted_iota(jnp.int32, (LANES, LANES), 0)
    col = lax.broadcasted_iota(jnp.int32, (LANES, LANES), 1)
    same_block = row + col >= LANES - 1
    filter_row = lax.broadcasted_iota(jnp.int32, (owned, LANES), 0)
    batch = min(blocks, 16)

    def one_filter(f, _):
        turned = turned_all[f]

        def some_lags(first):
            tables = []
            for d in range(0, batch, 2):
                live = full
                if batch == blocks:
                    live = min(full, -(-(blocks - d) * depth // LANES) * LANES)
                pair = jnp.concatenate(
                    [
                        g_all[f, pl.ds(pl.multiple_of((first + d + e) * depth, depth), live), :]
                        for e in range(2)
                    ],
                    axis=1,
                )
                table = jnp.dot(turned[:, :live], pair, preferred_element_type=F32)
                tables += [table[:, :LANES], table[:, LANES:]]
            last = g_all[f, pl.ds(pl.multiple_of((first + batch) * depth, depth), full), :]
            if batch < blocks:
                tables.append(jnp.dot(turned, last, preferred_element_type=F32))
            else:
                tables.append(jnp.zeros((LANES, LANES), F32))
            for d in range(batch):
                joined = jnp.where(same_block, tables[d], tables[d + 1])
                skewed = pltpu.roll(joined, 1, 1, stride=1, stride_axis=0)
                sums = jnp.sum(skewed, axis=0, keepdims=True) * scale
                lane = d % halves * LANES
                place = ((first + d) // halves, slice(None), slice(lane, lane + LANES))
                out_ref[place] = jnp.where(filter_row == f, sums, out_ref[place])

        if batch == blocks:
            some_lags(0)
        else:
            lax.fori_loop(0, blocks // batch, lambda i, c: (some_lags(i * batch), c)[1], 0)
        return 0

    for f in range(owned):
        turned_all[f] = lax.dot_general(
            mirror, u_all[f], (((1,), (1,)), ((), ())), preferred_element_type=F32
        ).astype(BF16)
    lax.fori_loop(0, owned, one_filter, 0, unroll=min(owned, 8))


def filter_lags(received, done, shards, chans, owned, scale):
    tok_rows = received.shape[2]
    groups = received.shape[1] // (2 * owned)
    halves = tok_rows // LANES
    depth = chans * groups
    full = shards * halves * depth
    args = (received.reshape(chans, shards, *received.shape[1:]),)
    if owned % SUBLANES:
        split = received.reshape(chans, shards, 2, groups, owned, halves, LANES)
        split = split.transpose(2, 4, 1, 5, 0, 3, 6).reshape(2, owned, full, LANES)
        args = (split[0], split[1])
    away, whole = pl.BlockSpec(memory_space=pl.ANY), pl.BlockSpec(memory_space=pltpu.VMEM)
    fetched = len(args) == 1
    return pl.pallas_call(
        functools.partial(lag_kernel, shards, chans, groups, owned, scale),
        in_specs=[away] + [away if fetched else whole] * len(args),
        out_specs=whole,
        out_shape=jax.ShapeDtypeStruct((shards, owned, tok_rows), F32),
        scratch_shapes=[
            pltpu.VMEM(args[0].shape if fetched else (2 * SUBLANES, LANES), BF16),
            pltpu.SemaphoreType.DMA((2,)),
            pltpu.VMEM((owned, full, LANES), BF16),
            pltpu.VMEM((owned, 2 * full + depth, LANES), BF16),
            pltpu.VMEM((owned, LANES, full), BF16),
        ],
        compiler_params=pltpu.CompilerParams(vmem_limit_bytes=VMEM_BYTES),
        cost_estimate=takes(0.1),
        name="filter_lags",
    )(done, *args)


def per_device(query_proj, key_proj, value_proj, out_grad, residues, decay_rate, skip_gain):
    tok_rows, width = key_proj.shape
    shards = lax.axis_size("seq")
    chans = lax.axis_size("chan")
    length = shards * tok_rows
    owned = FILTERS // (shards * chans)
    modes = residues.shape[1]
    signals = (query_proj, key_proj, value_proj, out_grad)

    send = pack_signals(shards, chans, owned, *signals)
    send, *signals, residues, decay_rate = lax.optimization_barrier(
        (send, *signals, residues, decay_rate)
    )
    received = lax.all_to_all(send, ("chan", "seq"), split_axis=0, concat_axis=0, tiled=True)

    coefs = jnp.stack(
        [
            jnp.exp(-decay_rate),
            jnp.exp(-(decay_rate * float(tok_rows))),
            residues * jnp.sqrt(decay_rate),
        ]
    )
    coefs = coefs.transpose(0, 2, 1).reshape(3, modes, 1, FILTERS // LANES, LANES)
    coefs = jnp.broadcast_to(coefs, (3, modes, width // FILTERS, FILTERS // LANES, LANES))
    coefs = coefs.reshape(3, modes, width // LANES, LANES)
    seq_index = lax.axis_index("seq").reshape(1)
    pairs = shards // 2
    own, sent = block_states(*signals, coefs)
    near = inside_pair(sent, pairs)
    states = pair_states(seq_index, pairs, coefs, own, near)
    *states, coefs, near = lax.optimization_barrier((*states, coefs, near))
    states = [along_column(state, pairs, 1 + i) for i, state in enumerate(states)]
    conv_part, grad_part, done = local_parts(*signals, coefs, skip_gain[None, :])

    scale = 1.0 / math.sqrt(length * (CHANNELS // FILTERS))
    lags = filter_lags(received, done, shards, chans, owned, scale)
    lags, *states = lax.optimization_barrier((lags, *states))
    lags = lax.all_to_all(lags, "seq", split_axis=0, concat_axis=0, tiled=True)
    filter_grad = lags.reshape(shards * owned, tok_rows).T
    query_proj, key_proj, value_proj, _ = signals
    layer_out, key_grad, value_grad = final_outputs(
        seq_index, coefs, near, states, conv_part, grad_part, query_proj, value_proj, key_proj
    )
    return (layer_out, key_grad, value_grad, filter_grad)


def solution(mesh):
    split = P("seq", "chan")
    return jax.shard_map(
        per_device,
        mesh=mesh,
        in_specs=(split, split, split, split, P(), P(), P("chan")),
        out_specs=(split, split, split, split),
        check_vma=False,
    )
```

```python
import functools
import math

import jax
import jax.numpy as jnp
from jax import lax
from jax.experimental import pallas as pl
from jax.experimental.pallas import tpu as pltpu
from jax.sharding import PartitionSpec as P

CHANNELS = 4096
FILTERS = 256
LANES = 128
SUBLANES = 8
GAP = 8
VMEM_BYTES = 16 * 1024 * 1024
FULL_VMEM_BYTES = 62 * 1024 * 1024
F32 = jnp.float32
BF16 = jnp.bfloat16
LINK = jnp.bfloat16


def takes(micros):
    return pl.CostEstimate(flops=0, bytes_accessed=int(micros * 3.6e6), transcendentals=0)


def product(first, second):
    return first * second


def one_hot(rows, cols, column_of):
    row = lax.broadcasted_iota(jnp.int32, (rows, cols), 0)
    col = lax.broadcasted_iota(jnp.int32, (rows, cols), 1)
    return (col == column_of(row)).astype(F32).astype(BF16)


def pack_kernel(shards, chans, owned, *refs):
    hbm_refs, send_ref, held, packed, in_sems, out_sems = refs[:4], *refs[4:]
    tok_rows, width = held.shape[1:]
    groups = width // FILTERS
    per_chan = FILTERS // chans
    units = [(which, first) for which in range(2) for first in range(0, groups, 2)]

    def arrival(i, first):
        place = (slice(None), pl.ds(first * FILTERS, 2 * FILTERS))
        return pltpu.make_async_copy(
            hbm_refs[i].at[place], held.at[(i, *place)], in_sems.at[i, first // 2]
        )

    def departure(which, first):
        if owned % SUBLANES:
            place = (which, pl.ds(first, 2))
        else:
            place = (slice(None), pl.ds((which * groups + first) * owned, 2 * owned))
        return pltpu.make_async_copy(
            packed.at[place], send_ref.at[place], out_sems.at[which, first // 2]
        )

    for which, first in units:
        for i in (2 * which, 2 * which + 1):
            arrival(i, first).start()

    def owned_filter(row):
        seq = row // (chans * owned)
        chan = row // owned % chans
        return chan * per_chan + seq * owned + row % owned

    order = one_hot(FILTERS, FILTERS, owned_filter)
    for which, first in units:
        for i in (2 * which, 2 * which + 1):
            arrival(i, first).wait()
        pieces = []
        for group in (first, first + 1):
            cols = slice(group * FILTERS, (group + 1) * FILTERS)
            piece = lax.dot_general(
                order,
                product(held[2 * which, :, cols], held[2 * which + 1, :, cols]),
                (((1,), (1,)), ((), ())),
                preferred_element_type=F32,
            )
            if owned % SUBLANES:
                packed[which, group] = piece.astype(BF16)
            else:
                pieces.append(piece.reshape(shards * chans, owned, tok_rows))
        if pieces:
            row = (which * groups + first) * owned
            packed[:, row : row + 2 * owned, :] = jnp.concatenate(pieces, axis=1).astype(BF16)
        departure(which, first).start()
    for which, first in units:
        departure(which, first).wait()


def pack_signals(shards, chans, owned, query_proj, key_proj, value_proj, out_grad):
    tok_rows, width = key_proj.shape
    groups = width // FILTERS
    dests = shards * chans
    if owned % SUBLANES:
        shape = (2, groups, FILTERS, tok_rows)
    else:
        shape = (dests, 2 * groups * owned, tok_rows)
    send = pl.pallas_call(
        functools.partial(pack_kernel, shards, chans, owned),
        in_specs=[pl.BlockSpec(memory_space=pl.ANY)] * 4,
        out_specs=pl.BlockSpec(memory_space=pl.ANY),
        out_shape=jax.ShapeDtypeStruct(shape, BF16),
        scratch_shapes=[
            pltpu.VMEM((4, tok_rows, width), BF16),
            pltpu.VMEM(shape, BF16),
            pltpu.SemaphoreType.DMA((4, groups // 2)),
            pltpu.SemaphoreType.DMA((2, groups // 2)),
        ],
        compiler_params=pltpu.CompilerParams(vmem_limit_bytes=FULL_VMEM_BYTES),
        cost_estimate=takes(3.0),
        name="pack_signals",
    )(key_proj, value_proj, out_grad, query_proj)
    if owned % SUBLANES:
        send = send.reshape(2, groups, dests, owned, tok_rows)
        send = send.transpose(2, 0, 1, 3, 4).reshape(dests, 2 * groups * owned, tok_rows)
    return send


def tile_rows(tok_rows, tile):
    first = tile * (tok_rows + GAP)
    return slice(first, first + tok_rows)


def token_shape(tok_rows, tiles):
    return (tiles * (tok_rows + GAP), LANES)


def token_place(t, tok_rows, tiles):
    return (pl.ds(t, tiles, stride=tok_rows + GAP), slice(None))


def spread_tokens(a_ref, b_ref, x_ref):
    tok_rows, width = a_ref.shape
    for tile in range(width // LANES):
        cols = slice(tile * LANES, (tile + 1) * LANES)
        x_ref[tile_rows(tok_rows, tile), :] = product(a_ref[:, cols], b_ref[:, cols]).astype(F32)


def walk_tokens(ref, coef_ref, tok_rows, tiles, start, move):
    modes = coef_ref.shape[1]
    decay = [coef_ref[0, m] for m in range(modes)]
    weight = [coef_ref[2, m] for m in range(modes)]

    def step(t, held):
        place = token_place(start + move * t, tok_rows, tiles)
        x = ref[place]
        held = tuple(decay[m] * held[m] + x for m in range(modes))
        ref[place] = tree_sum([weight[m] * held[m] for m in range(modes)])
        return held

    zero = tuple(jnp.zeros((tiles, LANES), F32) for _ in range(modes))
    return lax.fori_loop(0, tok_rows, step, zero, unroll=8)


def tree_sum(terms):
    while len(terms) > 1:
        terms = [sum(terms[i : i + 2][1:], terms[i]) for i in range(0, len(terms), 2)]
    return terms[0]


def state_kernel(q_ref, k_ref, v_ref, o_ref, coef_ref, own_ref, sent_ref, x_ref, g_ref):
    tok_rows, width = k_ref.shape
    tiles = width // LANES
    modes = coef_ref.shape[1]
    spread_tokens(k_ref, v_ref, x_ref)
    spread_tokens(o_ref, q_ref, g_ref)
    decay = [coef_ref[0, m] for m in range(modes)]

    def step(t, carry):
        x = x_ref[token_place(t, tok_rows, tiles)]
        g = g_ref[token_place(tok_rows - 1 - t, tok_rows, tiles)]
        ahead = tuple(decay[m] * carry[0][m] + x for m in range(modes))
        behind = tuple(decay[m] * carry[1][m] + g for m in range(modes))
        return (ahead, behind)

    zero = tuple(jnp.zeros((tiles, LANES), F32) for _ in range(modes))
    for side, held in enumerate(lax.fori_loop(0, tok_rows, step, (zero, zero), unroll=8)):
        held = jnp.concatenate(held, axis=0)
        own_ref[side] = held
        sent_ref[side] = held.astype(LINK)


def block_states(query_proj, key_proj, value_proj, out_grad, coefs):
    tok_rows, width = key_proj.shape
    modes, tiles = coefs.shape[1:3]
    return pl.pallas_call(
        state_kernel,
        out_shape=[
            jax.ShapeDtypeStruct((2, modes * tiles, LANES), F32),
            jax.ShapeDtypeStruct((2, modes * tiles, LANES), LINK),
        ],
        scratch_shapes=[pltpu.VMEM(token_shape(tok_rows, tiles), F32)] * 2,
        compiler_params=pltpu.CompilerParams(vmem_limit_bytes=VMEM_BYTES),
        cost_estimate=takes(3.0),
        name="block_states",
    )(query_proj, key_proj, value_proj, out_grad, coefs)


def pair_kernel(seq_ref, coef_ref, own_ref, near_ref, *state_refs):
    pairs = len(state_refs) + 1
    modes, tiles = coef_ref.shape[1:3]
    pair = seq_ref[0] // 2
    second = seq_ref[0] % 2 == 1
    for m in range(modes):
        rows = slice(m * tiles, (m + 1) * tiles)
        decay = coef_ref[1, m]
        own, near = own_ref[0, rows], near_ref[0].astype(F32)[rows]
        ahead = jnp.where(second, own + decay * near, near + decay * own)
        own, near = own_ref[1, rows], near_ref[1].astype(F32)[rows]
        behind = jnp.where(second, near + decay * own, own + decay * near)
        for k in range(1, pairs):
            state_refs[k - 1][rows] = jnp.where(pair + k < pairs, ahead, behind)


def pair_states(seq_index, pairs, coefs, own, near):
    whole = pl.BlockSpec(memory_space=pltpu.VMEM)
    states = pl.pallas_call(
        pair_kernel,
        in_specs=[pl.BlockSpec(memory_space=pltpu.SMEM)] + [whole] * 3,
        out_specs=[whole] * (pairs - 1),
        out_shape=[jax.ShapeDtypeStruct(own.shape[1:], F32)] * (pairs - 1),
        compiler_params=pltpu.CompilerParams(vmem_limit_bytes=VMEM_BYTES),
        cost_estimate=takes(0.1),
        name="pair_states",
    )(seq_index, coefs, own, near)
    return [state.astype(LINK) for state in states]


def sum_pairs(side, seq, coef_ref, near_ref, state_refs):
    pairs = len(state_refs) + 1
    modes, tiles = coef_ref.shape[1:3]
    pair, count = seq // 2, (seq // 2, pairs - 1 - seq // 2)[side]
    beside = seq % 2 == 1 - side
    held = []
    for m in range(modes):
        rows = slice(m * tiles, (m + 1) * tiles)
        decay = coef_ref[1, m]
        total = jnp.zeros((tiles, LANES), F32)
        for k in range(pairs - 1, 0, -1):
            state_ref = state_refs[k - 1 if side == 0 else pairs - k - 1]
            block = state_ref[...].astype(F32)[rows]
            total = decay * decay * total + jnp.where(k <= count, block, 0.0)
        near = near_ref[side].astype(F32)[rows]
        held.append(jnp.where(beside, decay * total + near, total))
    return held


def local_kernel(
    q_ref, k_ref, v_ref, o_ref, coef_ref, gain_ref, conv_ref, grad_ref, done_ref
):
    tok_rows, width = k_ref.shape
    tiles = width // LANES
    spread_tokens(k_ref, v_ref, conv_ref)
    spread_tokens(o_ref, q_ref, grad_ref)
    walk_tokens(conv_ref, coef_ref, tok_rows, tiles, 0, 1)
    walk_tokens(grad_ref, coef_ref, tok_rows, tiles, tok_rows - 1, -1)
    for tile in range(tiles):
        cols = slice(tile * LANES, (tile + 1) * LANES)
        rows = tile_rows(tok_rows, tile)
        gain = gain_ref[:, cols]
        conv_in = product(k_ref[:, cols], v_ref[:, cols]).astype(F32)
        conv_ref[rows, :] = conv_ref[rows, :] + gain * conv_in
        mid_grad = product(o_ref[:, cols], q_ref[:, cols]).astype(F32)
        grad_ref[rows, :] = grad_ref[rows, :] + gain * mid_grad
    done_ref[...] = jnp.zeros(done_ref.shape, F32)


def local_parts(query_proj, key_proj, value_proj, out_grad, coefs, gain):
    tok_rows, width = key_proj.shape
    tiles = coefs.shape[2]
    return pl.pallas_call(
        local_kernel,
        out_shape=[jax.ShapeDtypeStruct(token_shape(tok_rows, tiles), F32)] * 2
        + [jax.ShapeDtypeStruct((SUBLANES, LANES), F32)],
        compiler_params=pltpu.CompilerParams(vmem_limit_bytes=VMEM_BYTES),
        cost_estimate=takes(6.5),
        name="local_parts",
    )(query_proj, key_proj, value_proj, out_grad, coefs, gain)


def along_column(state, pairs, k):
    route = [(2 * p + b, 2 * ((p + k) % pairs) + b) for p in range(pairs) for b in range(2)]
    return lax.ppermute(state, "seq", route)


def inside_pair(state, pairs):
    return lax.ppermute(state, "seq", [(i, i ^ 1) for i in range(2 * pairs)])


def fill_edge(ref, held, coef_ref, tok_rows, tiles, start, move):
    modes = coef_ref.shape[1]
    decay = [coef_ref[0, m] for m in range(modes)]

    def step(t, held):
        held = tuple(decay[m] * held[m] for m in range(modes))
        ref[token_place(start + move * t, tok_rows, tiles)] = tree_sum(list(held))
        return held

    held = tuple(coef_ref[2, m] * held[m] for m in range(modes))
    lax.fori_loop(0, tok_rows, step, held, unroll=8)


def final_kernel(count, *refs):
    seq_ref, hbm_refs, refs = refs[0], refs[1 : 1 + count], refs[1 + count :]
    out_hbm, held_refs, refs = refs[:3], refs[3 : 3 + count], refs[3 + count :]
    edge_ref, out_refs, in_sems, out_sems = refs[0], refs[1:4], refs[4], refs[5]
    coef_ref, near_ref, *state_refs = held_refs[:-5]
    conv_ref, q_ref, grad_ref, v_ref, k_ref = held_refs[-5:]
    tok_rows, width = k_ref.shape
    tiles = width // LANES
    small = count - 5
    arrivals = [
        pltpu.make_async_copy(source, target, in_sems.at[i])
        for i, (source, target) in enumerate(zip(hbm_refs, held_refs))
    ]
    departures = []

    def multiply_out(part_ref, outs):
        for tile in range(tiles):
            cols = slice(tile * LANES, (tile + 1) * LANES)
            rows = tile_rows(tok_rows, tile)
            value = part_ref[rows, :] + edge_ref[rows, :]
            for i, factor_ref in outs:
                out_refs[i][:, cols] = (value * factor_ref[:, cols].astype(F32)).astype(BF16)
                place = (slice(None), pl.ds(tile * LANES, LANES))
                copy = pltpu.make_async_copy(
                    out_refs[i].at[place], out_hbm[i].at[place], out_sems.at[i, tile]
                )
                copy.start()
                departures.append(copy)

    for copy in arrivals:
        copy.start()
    for copy in arrivals[:small]:
        copy.wait()
    held = sum_pairs(0, seq_ref[0], coef_ref, near_ref, state_refs)
    fill_edge(edge_ref, held, coef_ref, tok_rows, tiles, 0, 1)
    for copy in arrivals[small : small + 2]:
        copy.wait()
    multiply_out(conv_ref, [(0, q_ref)])
    held = sum_pairs(1, seq_ref[0], coef_ref, near_ref, state_refs)
    fill_edge(edge_ref, held, coef_ref, tok_rows, tiles, tok_rows - 1, -1)
    for copy in arrivals[small + 2 :]:
        copy.wait()
    multiply_out(grad_ref, [(1, v_ref), (2, k_ref)])
    for copy in departures:
        copy.wait()


def final_outputs(
    seq_index, coefs, near, states, conv_part, grad_part, query_proj, value_proj, key_proj
):
    tok_rows, width = key_proj.shape
    tiles = coefs.shape[2]
    args = (coefs, near, *states, conv_part, query_proj, grad_part, value_proj, key_proj)
    away = pl.BlockSpec(memory_space=pl.ANY)
    return pl.pallas_call(
        functools.partial(final_kernel, len(args)),
        in_specs=[pl.BlockSpec(memory_space=pltpu.SMEM)] + [away] * len(args),
        out_specs=[away] * 3,
        out_shape=[jax.ShapeDtypeStruct((tok_rows, width), BF16)] * 3,
        scratch_shapes=[pltpu.VMEM(arg.shape, arg.dtype) for arg in args]
        + [pltpu.VMEM(token_shape(tok_rows, tiles), F32)]
        + [pltpu.VMEM((tok_rows, width), BF16)] * 3
        + [pltpu.SemaphoreType.DMA((len(args),)), pltpu.SemaphoreType.DMA((3, tiles))],
        compiler_params=pltpu.CompilerParams(vmem_limit_bytes=FULL_VMEM_BYTES),
        cost_estimate=takes(5.0),
        name="final_outputs",
    )(seq_index, *args)


def lag_kernel(shards, chans, groups, owned, scale, *refs):
    in_refs, (out_ref, u_all, g_all, turned_all) = refs[1:-4], refs[-4:]
    tok_rows = out_ref.shape[2]
    halves = tok_rows // LANES
    blocks = shards * halves
    depth = chans * groups
    full = blocks * depth
    if len(in_refs) == 1:
        take = chans * groups * owned

        def by_filter(row):
            return row % depth * owned + row // depth

        order = one_hot(take, take, by_filter)
        for which, kept in enumerate((u_all, g_all)):
            rows = slice(which * groups * owned, (which + 1) * groups * owned)
            for s in range(shards):
                piece = in_refs[0][s * chans : (s + 1) * chans, rows, :].reshape(take, tok_rows)
                piece = jnp.dot(order, piece, preferred_element_type=F32).astype(BF16)
                piece = piece.reshape(owned, depth, tok_rows)
                for h in range(halves):
                    first = (s * halves + h) * depth
                    kept[:, first : first + depth, :] = piece[:, :, h * LANES : (h + 1) * LANES]
    else:
        u_all[...] = in_refs[0][...]
        g_all[:, :full, :] = in_refs[1][...]
    g_all[:, full:, :] = jnp.zeros((owned, g_all.shape[1] - full, LANES), BF16)
    mirror = one_hot(LANES, LANES, lambda row: LANES - 1 - row)
    row = lax.broadcasted_iota(jnp.int32, (LANES, LANES), 0)
    col = lax.broadcasted_iota(jnp.int32, (LANES, LANES), 1)
    same_block = row + col >= LANES - 1
    filter_row = lax.broadcasted_iota(jnp.int32, (owned, LANES), 0)
    batch = min(blocks, 16)

    def one_filter(f, _):
        turned = turned_all[f]

        def some_lags(first):
            tables = []
            for d in range(0, batch, 2):
                live = full
                if batch == blocks:
                    live = min(full, -(-(blocks - d) * depth // LANES) * LANES)
                pair = jnp.concatenate(
                    [
                        g_all[f, pl.ds(pl.multiple_of((first + d + e) * depth, depth), live), :]
                        for e in range(2)
                    ],
                    axis=1,
                )
                table = jnp.dot(turned[:, :live], pair, preferred_element_type=F32)
                tables += [table[:, :LANES], table[:, LANES:]]
            last = g_all[f, pl.ds(pl.multiple_of((first + batch) * depth, depth), full), :]
            if batch < blocks:
                tables.append(jnp.dot(turned, last, preferred_element_type=F32))
            else:
                tables.append(jnp.zeros((LANES, LANES), F32))
            for d in range(batch):
                joined = jnp.where(same_block, tables[d], tables[d + 1])
                skewed = pltpu.roll(joined, 1, 1, stride=1, stride_axis=0)
                sums = jnp.sum(skewed, axis=0, keepdims=True) * scale
                lane = d % halves * LANES
                place = ((first + d) // halves, slice(None), slice(lane, lane + LANES))
                out_ref[place] = jnp.where(filter_row == f, sums, out_ref[place])

        if batch == blocks:
            some_lags(0)
        else:
            lax.fori_loop(0, blocks // batch, lambda i, c: (some_lags(i * batch), c)[1], 0)
        return 0

    for f in range(owned):
        turned_all[f] = lax.dot_general(
            mirror, u_all[f], (((1,), (1,)), ((), ())), preferred_element_type=F32
        ).astype(BF16)
    lax.fori_loop(0, owned, one_filter, 0, unroll=min(owned, 8))


def filter_lags(received, done, shards, chans, owned, scale):
    tok_rows = received.shape[2]
    groups = received.shape[1] // (2 * owned)
    halves = tok_rows // LANES
    depth = chans * groups
    full = shards * halves * depth
    args = (received,)
    if owned % SUBLANES:
        split = received.reshape(shards, chans, 2, groups, owned, halves, LANES)
        split = split.transpose(2, 4, 0, 5, 1, 3, 6).reshape(2, owned, full, LANES)
        args = (split[0], split[1])
    whole = pl.BlockSpec(memory_space=pltpu.VMEM)
    return pl.pallas_call(
        functools.partial(lag_kernel, shards, chans, groups, owned, scale),
        in_specs=[pl.BlockSpec(memory_space=pl.ANY)] + [whole] * len(args),
        out_specs=whole,
        out_shape=jax.ShapeDtypeStruct((shards, owned, tok_rows), F32),
        scratch_shapes=[
            pltpu.VMEM((owned, full, LANES), BF16),
            pltpu.VMEM((owned, 2 * full + depth, LANES), BF16),
            pltpu.VMEM((owned, LANES, full), BF16),
        ],
        compiler_params=pltpu.CompilerParams(vmem_limit_bytes=VMEM_BYTES),
        cost_estimate=takes(2.5),
        name="filter_lags",
    )(done, *args)


def per_device(query_proj, key_proj, value_proj, out_grad, residues, decay_rate, skip_gain):
    tok_rows, width = key_proj.shape
    shards = lax.axis_size("seq")
    chans = lax.axis_size("chan")
    length = shards * tok_rows
    owned = FILTERS // (shards * chans)
    modes = residues.shape[1]
    signals = (query_proj, key_proj, value_proj, out_grad)

    send = pack_signals(shards, chans, owned, *signals)
    send, *signals, residues, decay_rate = lax.optimization_barrier(
        (send, *signals, residues, decay_rate)
    )
    received = lax.all_to_all(send, ("seq", "chan"), split_axis=0, concat_axis=0, tiled=True)

    coefs = jnp.stack(
        [
            jnp.exp(-decay_rate),
            jnp.exp(-(decay_rate * float(tok_rows))),
            residues * jnp.sqrt(decay_rate),
        ]
    )
    coefs = coefs.transpose(0, 2, 1).reshape(3, modes, 1, FILTERS // LANES, LANES)
    coefs = jnp.broadcast_to(coefs, (3, modes, width // FILTERS, FILTERS // LANES, LANES))
    coefs = coefs.reshape(3, modes, width // LANES, LANES)
    seq_index = lax.axis_index("seq").reshape(1)
    pairs = shards // 2
    own, sent = block_states(*signals, coefs)
    near = inside_pair(sent, pairs)
    states = pair_states(seq_index, pairs, coefs, own, near)
    *states, coefs, near = lax.optimization_barrier((*states, coefs, near))
    states = [along_column(state, pairs, 1 + i) for i, state in enumerate(states)]
    conv_part, grad_part, done = local_parts(*signals, coefs, skip_gain[None, :])

    scale = 1.0 / math.sqrt(length * (CHANNELS // FILTERS))
    lags = filter_lags(received, done, shards, chans, owned, scale)
    lags, *states = lax.optimization_barrier((lags, *states))
    lags = lax.all_to_all(lags, "seq", split_axis=0, concat_axis=0, tiled=True)
    filter_grad = lags.reshape(shards * owned, tok_rows).T
    query_proj, key_proj, value_proj, _ = signals
    layer_out, key_grad, value_grad = final_outputs(
        seq_index, coefs, near, states, conv_part, grad_part, query_proj, value_proj, key_proj
    )
    return (layer_out, key_grad, value_grad, filter_grad)


def solution(mesh):
    split = P("seq", "chan")
    return jax.shard_map(
        per_device,
        mesh=mesh,
        in_specs=(split, split, split, split, P(), P(), P("chan")),
        out_specs=(split, split, split, split),
        check_vma=False,
    )
```

```python
import functools
import math

import jax
import jax.numpy as jnp
from jax import lax
from jax.experimental import pallas as pl
from jax.experimental.pallas import tpu as pltpu
from jax.sharding import PartitionSpec as P

CHANNELS = 4096
FILTERS = 256
LANES = 128
SUBLANES = 8
GAP = 8
VMEM_BYTES = 16 * 1024 * 1024
FULL_VMEM_BYTES = 62 * 1024 * 1024
F32 = jnp.float32
BF16 = jnp.bfloat16
LINK = jnp.bfloat16


def product(first, second):
    return first * second


def one_hot(rows, cols, column_of):
    row = lax.broadcasted_iota(jnp.int32, (rows, cols), 0)
    col = lax.broadcasted_iota(jnp.int32, (rows, cols), 1)
    return (col == column_of(row)).astype(F32).astype(BF16)


def pack_kernel(shards, chans, owned, *refs):
    hbm_refs, send_ref, held, packed, in_sems, out_sems = refs[:4], *refs[4:]
    tok_rows, width = held.shape[1:]
    groups = width // FILTERS
    per_chan = FILTERS // chans
    units = [(which, first) for which in range(2) for first in range(0, groups, 2)]

    def arrival(i, first):
        place = (slice(None), pl.ds(first * FILTERS, 2 * FILTERS))
        return pltpu.make_async_copy(
            hbm_refs[i].at[place], held.at[(i, *place)], in_sems.at[i, first // 2]
        )

    def departure(which, first):
        if owned % SUBLANES:
            place = (which, pl.ds(first, 2))
        else:
            place = (slice(None), pl.ds((which * groups + first) * owned, 2 * owned))
        return pltpu.make_async_copy(
            packed.at[place], send_ref.at[place], out_sems.at[which, first // 2]
        )

    for which, first in units:
        for i in (2 * which, 2 * which + 1):
            arrival(i, first).start()

    def owned_filter(row):
        seq = row // (chans * owned)
        chan = row // owned % chans
        return chan * per_chan + seq * owned + row % owned

    order = one_hot(FILTERS, FILTERS, owned_filter)
    for which, first in units:
        for i in (2 * which, 2 * which + 1):
            arrival(i, first).wait()
        pieces = []
        for group in (first, first + 1):
            cols = slice(group * FILTERS, (group + 1) * FILTERS)
            piece = lax.dot_general(
                order,
                product(held[2 * which, :, cols], held[2 * which + 1, :, cols]),
                (((1,), (1,)), ((), ())),
                preferred_element_type=F32,
            )
            if owned % SUBLANES:
                packed[which, group] = piece.astype(BF16)
            else:
                pieces.append(piece.reshape(shards * chans, owned, tok_rows))
        if pieces:
            row = (which * groups + first) * owned
            packed[:, row : row + 2 * owned, :] = jnp.concatenate(pieces, axis=1).astype(BF16)
        departure(which, first).start()
    for which, first in units:
        departure(which, first).wait()


def pack_signals(shards, chans, owned, query_proj, key_proj, value_proj, out_grad):
    tok_rows, width = key_proj.shape
    groups = width // FILTERS
    dests = shards * chans
    if owned % SUBLANES:
        shape = (2, groups, FILTERS, tok_rows)
    else:
        shape = (dests, 2 * groups * owned, tok_rows)
    send = pl.pallas_call(
        functools.partial(pack_kernel, shards, chans, owned),
        in_specs=[pl.BlockSpec(memory_space=pl.ANY)] * 4,
        out_specs=pl.BlockSpec(memory_space=pl.ANY),
        out_shape=jax.ShapeDtypeStruct(shape, BF16),
        scratch_shapes=[
            pltpu.VMEM((4, tok_rows, width), BF16),
            pltpu.VMEM(shape, BF16),
            pltpu.SemaphoreType.DMA((4, groups // 2)),
            pltpu.SemaphoreType.DMA((2, groups // 2)),
        ],
        compiler_params=pltpu.CompilerParams(vmem_limit_bytes=FULL_VMEM_BYTES),
        name="pack_signals",
    )(key_proj, value_proj, out_grad, query_proj)
    if owned % SUBLANES:
        send = send.reshape(2, groups, dests, owned, tok_rows)
        send = send.transpose(2, 0, 1, 3, 4).reshape(dests, 2 * groups * owned, tok_rows)
    return send


def tile_rows(tok_rows, tile):
    first = tile * (tok_rows + GAP)
    return slice(first, first + tok_rows)


def token_shape(tok_rows, tiles):
    return (tiles * (tok_rows + GAP), LANES)


def token_place(t, tok_rows, tiles):
    return (pl.ds(t, tiles, stride=tok_rows + GAP), slice(None))


def spread_tokens(a_ref, b_ref, x_ref):
    tok_rows, width = a_ref.shape
    for tile in range(width // LANES):
        cols = slice(tile * LANES, (tile + 1) * LANES)
        x_ref[tile_rows(tok_rows, tile), :] = product(a_ref[:, cols], b_ref[:, cols]).astype(F32)


def walk_tokens(ref, coef_ref, tok_rows, tiles, start, move):
    modes = coef_ref.shape[1]
    decay = [coef_ref[0, m] for m in range(modes)]
    weight = [coef_ref[2, m] for m in range(modes)]

    def step(t, held):
        place = token_place(start + move * t, tok_rows, tiles)
        x = ref[place]
        held = tuple(decay[m] * held[m] + x for m in range(modes))
        ref[place] = tree_sum([weight[m] * held[m] for m in range(modes)])
        return held

    zero = tuple(jnp.zeros((tiles, LANES), F32) for _ in range(modes))
    return lax.fori_loop(0, tok_rows, step, zero, unroll=8)


def tree_sum(terms):
    while len(terms) > 1:
        terms = [sum(terms[i : i + 2][1:], terms[i]) for i in range(0, len(terms), 2)]
    return terms[0]


def state_kernel(q_ref, k_ref, v_ref, o_ref, coef_ref, own_ref, sent_ref, x_ref, g_ref):
    tok_rows, width = k_ref.shape
    tiles = width // LANES
    modes = coef_ref.shape[1]
    spread_tokens(k_ref, v_ref, x_ref)
    spread_tokens(o_ref, q_ref, g_ref)
    decay = [coef_ref[0, m] for m in range(modes)]

    def step(t, carry):
        x = x_ref[token_place(t, tok_rows, tiles)]
        g = g_ref[token_place(tok_rows - 1 - t, tok_rows, tiles)]
        ahead = tuple(decay[m] * carry[0][m] + x for m in range(modes))
        behind = tuple(decay[m] * carry[1][m] + g for m in range(modes))
        return (ahead, behind)

    zero = tuple(jnp.zeros((tiles, LANES), F32) for _ in range(modes))
    for side, held in enumerate(lax.fori_loop(0, tok_rows, step, (zero, zero), unroll=8)):
        held = jnp.concatenate(held, axis=0)
        own_ref[side] = held
        sent_ref[side] = held.astype(LINK)


def block_states(query_proj, key_proj, value_proj, out_grad, coefs):
    tok_rows, width = key_proj.shape
    modes, tiles = coefs.shape[1:3]
    return pl.pallas_call(
        state_kernel,
        out_shape=[
            jax.ShapeDtypeStruct((2, modes * tiles, LANES), F32),
            jax.ShapeDtypeStruct((2, modes * tiles, LANES), LINK),
        ],
        scratch_shapes=[pltpu.VMEM(token_shape(tok_rows, tiles), F32)] * 2,
        compiler_params=pltpu.CompilerParams(vmem_limit_bytes=VMEM_BYTES),
        name="block_states",
    )(query_proj, key_proj, value_proj, out_grad, coefs)


def pair_kernel(seq_ref, coef_ref, own_ref, near_ref, *state_refs):
    pairs = len(state_refs) + 1
    modes, tiles = coef_ref.shape[1:3]
    pair = seq_ref[0] // 2
    second = seq_ref[0] % 2 == 1
    for m in range(modes):
        rows = slice(m * tiles, (m + 1) * tiles)
        decay = coef_ref[1, m]
        own, near = own_ref[0, rows], near_ref[0].astype(F32)[rows]
        ahead = jnp.where(second, own + decay * near, near + decay * own)
        own, near = own_ref[1, rows], near_ref[1].astype(F32)[rows]
        behind = jnp.where(second, near + decay * own, own + decay * near)
        for k in range(1, pairs):
            state_refs[k - 1][rows] = jnp.where(pair + k < pairs, ahead, behind)


def pair_states(seq_index, pairs, coefs, own, near):
    whole = pl.BlockSpec(memory_space=pltpu.VMEM)
    states = pl.pallas_call(
        pair_kernel,
        in_specs=[pl.BlockSpec(memory_space=pltpu.SMEM)] + [whole] * 3,
        out_specs=[whole] * (pairs - 1),
        out_shape=[jax.ShapeDtypeStruct(own.shape[1:], F32)] * (pairs - 1),
        compiler_params=pltpu.CompilerParams(vmem_limit_bytes=VMEM_BYTES),
        name="pair_states",
    )(seq_index, coefs, own, near)
    return [state.astype(LINK) for state in states]


def sum_pairs(side, seq, coef_ref, near_ref, state_refs):
    pairs = len(state_refs) + 1
    modes, tiles = coef_ref.shape[1:3]
    pair, count = seq // 2, (seq // 2, pairs - 1 - seq // 2)[side]
    beside = seq % 2 == 1 - side
    held = []
    for m in range(modes):
        rows = slice(m * tiles, (m + 1) * tiles)
        decay = coef_ref[1, m]
        total = jnp.zeros((tiles, LANES), F32)
        for k in range(pairs - 1, 0, -1):
            state_ref = state_refs[k - 1 if side == 0 else pairs - k - 1]
            block = state_ref[...].astype(F32)[rows]
            total = decay * decay * total + jnp.where(k <= count, block, 0.0)
        near = near_ref[side].astype(F32)[rows]
        held.append(jnp.where(beside, decay * total + near, total))
    return held


def local_kernel(
    q_ref, k_ref, v_ref, o_ref, coef_ref, gain_ref, conv_ref, grad_ref, done_ref, x_ref, g_ref
):
    tok_rows, width = k_ref.shape
    tiles = width // LANES
    spread_tokens(k_ref, v_ref, x_ref)
    spread_tokens(o_ref, q_ref, g_ref)
    walk_tokens(x_ref, coef_ref, tok_rows, tiles, 0, 1)
    walk_tokens(g_ref, coef_ref, tok_rows, tiles, tok_rows - 1, -1)
    for tile in range(tiles):
        cols = slice(tile * LANES, (tile + 1) * LANES)
        rows = tile_rows(tok_rows, tile)
        gain = gain_ref[:, cols]
        conv_in = product(k_ref[:, cols], v_ref[:, cols]).astype(F32)
        conv_ref[:, cols] = x_ref[rows, :] + gain * conv_in
        mid_grad = product(o_ref[:, cols], q_ref[:, cols]).astype(F32)
        grad_ref[:, cols] = g_ref[rows, :] + gain * mid_grad
    done_ref[...] = jnp.zeros(done_ref.shape, F32)


def local_parts(query_proj, key_proj, value_proj, out_grad, coefs, gain):
    tok_rows, width = key_proj.shape
    tiles = coefs.shape[2]
    return pl.pallas_call(
        local_kernel,
        out_shape=[jax.ShapeDtypeStruct((tok_rows, width), F32)] * 2
        + [jax.ShapeDtypeStruct((SUBLANES, LANES), F32)],
        scratch_shapes=[pltpu.VMEM(token_shape(tok_rows, tiles), F32)] * 2,
        compiler_params=pltpu.CompilerParams(vmem_limit_bytes=VMEM_BYTES),
        name="local_parts",
    )(query_proj, key_proj, value_proj, out_grad, coefs, gain)


def along_column(state, pairs, k):
    route = [(2 * p + b, 2 * ((p + k) % pairs) + b) for p in range(pairs) for b in range(2)]
    return lax.ppermute(state, "seq", route)


def inside_pair(state, pairs):
    return lax.ppermute(state, "seq", [(i, i ^ 1) for i in range(2 * pairs)])


def fill_edge(ref, held, coef_ref, tok_rows, tiles, start, move):
    modes = coef_ref.shape[1]
    decay = [coef_ref[0, m] for m in range(modes)]

    def step(t, held):
        held = tuple(decay[m] * held[m] for m in range(modes))
        ref[token_place(start + move * t, tok_rows, tiles)] = tree_sum(list(held))
        return held

    held = tuple(coef_ref[2, m] * held[m] for m in range(modes))
    lax.fori_loop(0, tok_rows, step, held, unroll=8)


def edge_kernel(seq_ref, coef_ref, near_ref, *refs):
    state_refs, edge_ref = refs[:-1], refs[-1]
    fill_side(0, edge_ref, seq_ref, coef_ref, near_ref, state_refs)


def fill_side(side, edge_ref, seq_ref, coef_ref, near_ref, state_refs):
    tiles = coef_ref.shape[2]
    tok_rows = edge_ref.shape[0] // tiles - GAP
    held = sum_pairs(side, seq_ref[0], coef_ref, near_ref, state_refs)
    start, move = ((0, 1), (tok_rows - 1, -1))[side]
    fill_edge(edge_ref, held, coef_ref, tok_rows, tiles, start, move)


def edge_terms(tok_rows, seq_index, coefs, near, states):
    whole = pl.BlockSpec(memory_space=pltpu.VMEM)
    return pl.pallas_call(
        edge_kernel,
        in_specs=[pl.BlockSpec(memory_space=pltpu.SMEM)] + [whole] * (2 + len(states)),
        out_shape=jax.ShapeDtypeStruct(token_shape(tok_rows, coefs.shape[2]), F32),
        compiler_params=pltpu.CompilerParams(vmem_limit_bytes=VMEM_BYTES),
        name="edge_terms",
    )(seq_index, coefs, near, *states)


def multiply_out(part_ref, edge_ref, factor_refs, out_refs, hbm_refs, sems):
    tok_rows, width = part_ref.shape
    copies = []
    for tile in range(width // LANES):
        cols = slice(tile * LANES, (tile + 1) * LANES)
        value = part_ref[:, cols] + edge_ref[tile_rows(tok_rows, tile), :]
        for i, (factor_ref, out_ref, hbm_ref) in enumerate(zip(factor_refs, out_refs, hbm_refs)):
            out_ref[:, cols] = (value * factor_ref[:, cols].astype(F32)).astype(BF16)
            place = (slice(None), pl.ds(tile * LANES, LANES))
            copies.append(
                pltpu.make_async_copy(out_ref.at[place], hbm_ref.at[place], sems.at[i, tile])
            )
            copies[-1].start()
    return copies


def conv_kernel(seq_ref, part_ref, edge_ref, q_ref, coef_ref, near_ref, *refs):
    state_refs, (layer_hbm, next_ref, layer_ref, sems) = refs[:-4], refs[-4:]
    copies = multiply_out(part_ref, edge_ref, [q_ref], [layer_ref], [layer_hbm], sems)
    fill_side(1, next_ref, seq_ref, coef_ref, near_ref, state_refs)
    for copy in copies:
        copy.wait()


def conv_outputs(seq_index, part, edge, query_proj, coefs, near, states):
    tok_rows, width = part.shape
    whole = pl.BlockSpec(memory_space=pltpu.VMEM)
    return pl.pallas_call(
        conv_kernel,
        in_specs=[pl.BlockSpec(memory_space=pltpu.SMEM)] + [whole] * (5 + len(states)),
        out_specs=[pl.BlockSpec(memory_space=pl.ANY), whole],
        out_shape=[
            jax.ShapeDtypeStruct((tok_rows, width), BF16),
            jax.ShapeDtypeStruct(edge.shape, F32),
        ],
        scratch_shapes=[
            pltpu.VMEM((tok_rows, width), BF16),
            pltpu.SemaphoreType.DMA((1, width // LANES)),
        ],
        compiler_params=pltpu.CompilerParams(vmem_limit_bytes=VMEM_BYTES),
        name="conv_outputs",
    )(seq_index, part, edge, query_proj, coefs, near, *states)


def grad_kernel(
    part_ref, edge_ref, v_ref, k_ref, key_hbm, value_hbm, key_ref, value_ref, sems
):
    copies = multiply_out(
        part_ref, edge_ref, [v_ref, k_ref], [key_ref, value_ref], [key_hbm, value_hbm], sems
    )
    for copy in copies:
        copy.wait()


def grad_outputs(part, edge, value_proj, key_proj):
    tok_rows, width = part.shape
    return pl.pallas_call(
        grad_kernel,
        in_specs=[pl.BlockSpec(memory_space=pltpu.VMEM)] * 4,
        out_specs=[pl.BlockSpec(memory_space=pl.ANY)] * 2,
        out_shape=[jax.ShapeDtypeStruct((tok_rows, width), BF16)] * 2,
        scratch_shapes=[pltpu.VMEM((tok_rows, width), BF16)] * 2
        + [pltpu.SemaphoreType.DMA((2, width // LANES))],
        compiler_params=pltpu.CompilerParams(vmem_limit_bytes=VMEM_BYTES),
        name="grad_outputs",
    )(part, edge, value_proj, key_proj)


def lag_kernel(shards, chans, groups, owned, scale, *refs):
    in_refs, (out_ref, u_all, g_all, turned_all) = refs[1:-4], refs[-4:]
    tok_rows = out_ref.shape[2]
    halves = tok_rows // LANES
    blocks = shards * halves
    depth = chans * groups
    full = blocks * depth
    if len(in_refs) == 1:
        take = chans * groups * owned

        def by_filter(row):
            return row % depth * owned + row // depth

        order = one_hot(take, take, by_filter)
        for which, kept in enumerate((u_all, g_all)):
            rows = slice(which * groups * owned, (which + 1) * groups * owned)
            for s in range(shards):
                piece = in_refs[0][s * chans : (s + 1) * chans, rows, :].reshape(take, tok_rows)
                piece = jnp.dot(order, piece, preferred_element_type=F32).astype(BF16)
                piece = piece.reshape(owned, depth, tok_rows)
                for h in range(halves):
                    first = (s * halves + h) * depth
                    kept[:, first : first + depth, :] = piece[:, :, h * LANES : (h + 1) * LANES]
    else:
        u_all[...] = in_refs[0][...]
        g_all[:, :full, :] = in_refs[1][...]
    g_all[:, full:, :] = jnp.zeros((owned, g_all.shape[1] - full, LANES), BF16)
    mirror = one_hot(LANES, LANES, lambda row: LANES - 1 - row)
    row = lax.broadcasted_iota(jnp.int32, (LANES, LANES), 0)
    col = lax.broadcasted_iota(jnp.int32, (LANES, LANES), 1)
    same_block = row + col >= LANES - 1
    filter_row = lax.broadcasted_iota(jnp.int32, (owned, LANES), 0)
    batch = min(blocks, 16)

    def one_filter(f, _):
        turned = turned_all[f]

        def some_lags(first):
            tables = []
            for d in range(0, batch, 2):
                live = full
                if batch == blocks:
                    live = min(full, -(-(blocks - d) * depth // LANES) * LANES)
                pair = jnp.concatenate(
                    [
                        g_all[f, pl.ds(pl.multiple_of((first + d + e) * depth, depth), live), :]
                        for e in range(2)
                    ],
                    axis=1,
                )
                table = jnp.dot(turned[:, :live], pair, preferred_element_type=F32)
                tables += [table[:, :LANES], table[:, LANES:]]
            last = g_all[f, pl.ds(pl.multiple_of((first + batch) * depth, depth), full), :]
            if batch < blocks:
                tables.append(jnp.dot(turned, last, preferred_element_type=F32))
            else:
                tables.append(jnp.zeros((LANES, LANES), F32))
            for d in range(batch):
                joined = jnp.where(same_block, tables[d], tables[d + 1])
                skewed = pltpu.roll(joined, 1, 1, stride=1, stride_axis=0)
                sums = jnp.sum(skewed, axis=0, keepdims=True) * scale
                lane = d % halves * LANES
                place = ((first + d) // halves, slice(None), slice(lane, lane + LANES))
                out_ref[place] = jnp.where(filter_row == f, sums, out_ref[place])

        if batch == blocks:
            some_lags(0)
        else:
            lax.fori_loop(0, blocks // batch, lambda i, c: (some_lags(i * batch), c)[1], 0)
        return 0

    for f in range(owned):
        turned_all[f] = lax.dot_general(
            mirror, u_all[f], (((1,), (1,)), ((), ())), preferred_element_type=F32
        ).astype(BF16)
    lax.fori_loop(0, owned, one_filter, 0, unroll=min(owned, 8))


def filter_lags(received, done, shards, chans, owned, scale):
    tok_rows = received.shape[2]
    groups = received.shape[1] // (2 * owned)
    halves = tok_rows // LANES
    depth = chans * groups
    full = shards * halves * depth
    args = (received,)
    if owned % SUBLANES:
        split = received.reshape(shards, chans, 2, groups, owned, halves, LANES)
        split = split.transpose(2, 4, 0, 5, 1, 3, 6).reshape(2, owned, full, LANES)
        args = (split[0], split[1])
    whole = pl.BlockSpec(memory_space=pltpu.VMEM)
    return pl.pallas_call(
        functools.partial(lag_kernel, shards, chans, groups, owned, scale),
        in_specs=[pl.BlockSpec(memory_space=pl.ANY)] + [whole] * len(args),
        out_specs=whole,
        out_shape=jax.ShapeDtypeStruct((shards, owned, tok_rows), F32),
        scratch_shapes=[
            pltpu.VMEM((owned, full, LANES), BF16),
            pltpu.VMEM((owned, 2 * full + depth, LANES), BF16),
            pltpu.VMEM((owned, LANES, full), BF16),
        ],
        compiler_params=pltpu.CompilerParams(vmem_limit_bytes=VMEM_BYTES),
        name="filter_lags",
    )(done, *args)


def per_device(query_proj, key_proj, value_proj, out_grad, residues, decay_rate, skip_gain):
    tok_rows, width = key_proj.shape
    shards = lax.axis_size("seq")
    chans = lax.axis_size("chan")
    length = shards * tok_rows
    owned = FILTERS // (shards * chans)
    modes = residues.shape[1]
    signals = (query_proj, key_proj, value_proj, out_grad)

    send = pack_signals(shards, chans, owned, *signals)
    send, *signals, residues, decay_rate = lax.optimization_barrier(
        (send, *signals, residues, decay_rate)
    )
    received = lax.all_to_all(send, ("seq", "chan"), split_axis=0, concat_axis=0, tiled=True)

    coefs = jnp.stack(
        [
            jnp.exp(-decay_rate),
            jnp.exp(-(decay_rate * float(tok_rows))),
            residues * jnp.sqrt(decay_rate),
        ]
    )
    coefs = coefs.transpose(0, 2, 1).reshape(3, modes, 1, FILTERS // LANES, LANES)
    coefs = jnp.broadcast_to(coefs, (3, modes, width // FILTERS, FILTERS // LANES, LANES))
    coefs = coefs.reshape(3, modes, width // LANES, LANES)
    seq_index = lax.axis_index("seq").reshape(1)
    pairs = shards // 2
    own, sent = block_states(*signals, coefs)
    near = inside_pair(sent, pairs)
    states = pair_states(seq_index, pairs, coefs, own, near)
    *states, coefs, near = lax.optimization_barrier((*states, coefs, near))
    states = [along_column(state, pairs, 1 + i) for i, state in enumerate(states)]
    conv_part, grad_part, done = local_parts(*signals, coefs, skip_gain[None, :])

    scale = 1.0 / math.sqrt(length * (CHANNELS // FILTERS))
    lags = filter_lags(received, done, shards, chans, owned, scale)
    lags, *states = lax.optimization_barrier((lags, *states))
    lags = lax.all_to_all(lags, "seq", split_axis=0, concat_axis=0, tiled=True)
    filter_grad = lags.reshape(shards * owned, tok_rows).T
    query_proj, key_proj, value_proj, _ = signals
    edge = edge_terms(tok_rows, seq_index, coefs, near, states)
    layer_out, edge = conv_outputs(seq_index, conv_part, edge, query_proj, coefs, near, states)
    key_grad, value_grad = grad_outputs(grad_part, edge, value_proj, key_proj)
    return (layer_out, key_grad, value_grad, filter_grad)


def solution(mesh):
    split = P("seq", "chan")
    return jax.shard_map(
        per_device,
        mesh=mesh,
        in_specs=(split, split, split, split, P(), P(), P("chan")),
        out_specs=(split, split, split, split),
        check_vma=False,
    )
```

```python
import functools
import math

import jax
import jax.numpy as jnp
from jax import lax
from jax.experimental import pallas as pl
from jax.experimental.pallas import tpu as pltpu
from jax.sharding import PartitionSpec as P

CHANNELS = 4096
FILTERS = 256
LANES = 128
SUBLANES = 8
GAP = 8
VMEM_BYTES = 16 * 1024 * 1024
FULL_VMEM_BYTES = 62 * 1024 * 1024
F32 = jnp.float32
BF16 = jnp.bfloat16
LINK = jnp.bfloat16


def product(first, second):
    return first * second


def one_hot(rows, cols, column_of):
    row = lax.broadcasted_iota(jnp.int32, (rows, cols), 0)
    col = lax.broadcasted_iota(jnp.int32, (rows, cols), 1)
    return (col == column_of(row)).astype(F32).astype(BF16)


def pack_kernel(shards, chans, owned, *refs):
    hbm_refs, send_ref, held, packed, in_sems, out_sems = refs[:4], *refs[4:]
    tok_rows, width = held.shape[1:]
    groups = width // FILTERS
    per_chan = FILTERS // chans
    units = [(w, first, 0, tok_rows) for w in range(2) for first in range(0, groups, 2)]
    which, first, _, _ = units.pop()
    units += [(which, first, 0, tok_rows // 2), (which, first, tok_rows // 2, tok_rows // 2)]

    def arrival(i, unit, n):
        place = (pl.ds(unit[2], unit[3]), pl.ds(unit[1] * FILTERS, 2 * FILTERS))
        return pltpu.make_async_copy(
            hbm_refs[i].at[place], held.at[(i, *place)], in_sems.at[i % 2, n]
        )

    def departure(unit, n):
        which, first, token, count = unit
        lanes = pl.ds(token, count)
        if owned % SUBLANES:
            place = (which, pl.ds(first, 2), slice(None), lanes)
        else:
            place = (slice(None), pl.ds((which * groups + first) * owned, 2 * owned), lanes)
        return pltpu.make_async_copy(packed.at[place], send_ref.at[place], out_sems.at[n])

    for n, unit in enumerate(units):
        for i in (2 * unit[0], 2 * unit[0] + 1):
            arrival(i, unit, n).start()

    def owned_filter(row):
        seq = row // (chans * owned)
        chan = row // owned % chans
        return chan * per_chan + seq * owned + row % owned

    order = one_hot(FILTERS, FILTERS, owned_filter)
    for n, unit in enumerate(units):
        which, first, token, count = unit
        rows = slice(token, token + count)
        for i in (2 * which, 2 * which + 1):
            arrival(i, unit, n).wait()
        pieces = []
        for group in (first, first + 1):
            cols = slice(group * FILTERS, (group + 1) * FILTERS)
            piece = lax.dot_general(
                order,
                product(held[2 * which, rows, cols], held[2 * which + 1, rows, cols]),
                (((1,), (1,)), ((), ())),
                preferred_element_type=F32,
            )
            if owned % SUBLANES:
                packed[which, group, :, rows] = piece.astype(BF16)
            else:
                pieces.append(piece.reshape(shards * chans, owned, count))
        if pieces:
            row = (which * groups + first) * owned
            packed[:, row : row + 2 * owned, rows] = jnp.concatenate(pieces, axis=1).astype(BF16)
        departure(unit, n).start()
    for n, unit in enumerate(units):
        departure(unit, n).wait()


def pack_signals(shards, chans, owned, query_proj, key_proj, value_proj, out_grad):
    tok_rows, width = key_proj.shape
    groups = width // FILTERS
    dests = shards * chans
    if owned % SUBLANES:
        shape = (2, groups, FILTERS, tok_rows)
    else:
        shape = (dests, 2 * groups * owned, tok_rows)
    send = pl.pallas_call(
        functools.partial(pack_kernel, shards, chans, owned),
        in_specs=[pl.BlockSpec(memory_space=pl.ANY)] * 4,
        out_specs=pl.BlockSpec(memory_space=pl.ANY),
        out_shape=jax.ShapeDtypeStruct(shape, BF16),
        scratch_shapes=[
            pltpu.VMEM((4, tok_rows, width), BF16),
            pltpu.VMEM(shape, BF16),
            pltpu.SemaphoreType.DMA((2, groups + 1)),
            pltpu.SemaphoreType.DMA((groups + 1,)),
        ],
        compiler_params=pltpu.CompilerParams(vmem_limit_bytes=FULL_VMEM_BYTES),
        name="pack_signals",
    )(key_proj, value_proj, out_grad, query_proj)
    if owned % SUBLANES:
        send = send.reshape(2, groups, dests, owned, tok_rows)
        send = send.transpose(2, 0, 1, 3, 4).reshape(dests, 2 * groups * owned, tok_rows)
    return send


def tile_rows(tok_rows, tile):
    first = tile * (tok_rows + GAP)
    return slice(first, first + tok_rows)


def token_shape(tok_rows, tiles):
    return (tiles * (tok_rows + GAP), LANES)


def token_place(t, tok_rows, tiles):
    return (pl.ds(t, tiles, stride=tok_rows + GAP), slice(None))


def spread_tokens(a_ref, b_ref, x_ref):
    tok_rows, width = a_ref.shape
    for tile in range(width // LANES):
        cols = slice(tile * LANES, (tile + 1) * LANES)
        x_ref[tile_rows(tok_rows, tile), :] = product(a_ref[:, cols], b_ref[:, cols]).astype(F32)


def walk_tokens(ref, coef_ref, tok_rows, tiles, start, move):
    modes = coef_ref.shape[1]
    decay = [coef_ref[0, m] for m in range(modes)]
    weight = [coef_ref[2, m] for m in range(modes)]

    def step(t, held):
        place = token_place(start + move * t, tok_rows, tiles)
        x = ref[place]
        held = tuple(decay[m] * held[m] + x for m in range(modes))
        ref[place] = tree_sum([weight[m] * held[m] for m in range(modes)])
        return held

    zero = tuple(jnp.zeros((tiles, LANES), F32) for _ in range(modes))
    return lax.fori_loop(0, tok_rows, step, zero, unroll=8)


def tree_sum(terms):
    while len(terms) > 1:
        terms = [sum(terms[i : i + 2][1:], terms[i]) for i in range(0, len(terms), 2)]
    return terms[0]


def state_kernel(q_ref, k_ref, v_ref, o_ref, coef_ref, own_ref, sent_ref, x_ref, g_ref):
    tok_rows, width = k_ref.shape
    tiles = width // LANES
    modes = coef_ref.shape[1]
    spread_tokens(k_ref, v_ref, x_ref)
    spread_tokens(o_ref, q_ref, g_ref)
    decay = [coef_ref[0, m] for m in range(modes)]

    def step(t, carry):
        x = x_ref[token_place(t, tok_rows, tiles)]
        g = g_ref[token_place(tok_rows - 1 - t, tok_rows, tiles)]
        ahead = tuple(decay[m] * carry[0][m] + x for m in range(modes))
        behind = tuple(decay[m] * carry[1][m] + g for m in range(modes))
        return (ahead, behind)

    zero = tuple(jnp.zeros((tiles, LANES), F32) for _ in range(modes))
    for side, held in enumerate(lax.fori_loop(0, tok_rows, step, (zero, zero), unroll=8)):
        held = jnp.concatenate(held, axis=0)
        own_ref[side] = held
        sent_ref[side] = held.astype(LINK)


def block_states(query_proj, key_proj, value_proj, out_grad, coefs):
    tok_rows, width = key_proj.shape
    modes, tiles = coefs.shape[1:3]
    return pl.pallas_call(
        state_kernel,
        out_shape=[
            jax.ShapeDtypeStruct((2, modes * tiles, LANES), F32),
            jax.ShapeDtypeStruct((2, modes * tiles, LANES), LINK),
        ],
        scratch_shapes=[pltpu.VMEM(token_shape(tok_rows, tiles), F32)] * 2,
        compiler_params=pltpu.CompilerParams(vmem_limit_bytes=VMEM_BYTES),
        name="block_states",
    )(query_proj, key_proj, value_proj, out_grad, coefs)


def pair_kernel(seq_ref, coef_ref, own_ref, near_ref, *state_refs):
    pairs = len(state_refs) + 1
    modes, tiles = coef_ref.shape[1:3]
    pair = seq_ref[0] // 2
    second = seq_ref[0] % 2 == 1
    for m in range(modes):
        rows = slice(m * tiles, (m + 1) * tiles)
        decay = coef_ref[1, m]
        own, near = own_ref[0, rows], near_ref[0].astype(F32)[rows]
        ahead = jnp.where(second, own + decay * near, near + decay * own)
        own, near = own_ref[1, rows], near_ref[1].astype(F32)[rows]
        behind = jnp.where(second, near + decay * own, own + decay * near)
        for k in range(1, pairs):
            state_refs[k - 1][rows] = jnp.where(pair + k < pairs, ahead, behind)


def pair_states(seq_index, pairs, coefs, own, near):
    whole = pl.BlockSpec(memory_space=pltpu.VMEM)
    states = pl.pallas_call(
        pair_kernel,
        in_specs=[pl.BlockSpec(memory_space=pltpu.SMEM)] + [whole] * 3,
        out_specs=[whole] * (pairs - 1),
        out_shape=[jax.ShapeDtypeStruct(own.shape[1:], F32)] * (pairs - 1),
        compiler_params=pltpu.CompilerParams(vmem_limit_bytes=VMEM_BYTES),
        name="pair_states",
    )(seq_index, coefs, own, near)
    return [state.astype(LINK) for state in states]


def sum_pairs(side, seq, coef_ref, near_ref, state_refs):
    pairs = len(state_refs) + 1
    modes, tiles = coef_ref.shape[1:3]
    pair, count = seq // 2, (seq // 2, pairs - 1 - seq // 2)[side]
    beside = seq % 2 == 1 - side
    held = []
    for m in range(modes):
        rows = slice(m * tiles, (m + 1) * tiles)
        decay = coef_ref[1, m]
        total = jnp.zeros((tiles, LANES), F32)
        for k in range(pairs - 1, 0, -1):
            state_ref = state_refs[k - 1 if side == 0 else pairs - k - 1]
            block = state_ref[...].astype(F32)[rows]
            total = decay * decay * total + jnp.where(k <= count, block, 0.0)
        near = near_ref[side].astype(F32)[rows]
        held.append(jnp.where(beside, decay * total + near, total))
    return held


def local_kernel(
    q_ref, k_ref, v_ref, o_ref, coef_ref, gain_ref, conv_ref, grad_ref, done_ref, x_ref, g_ref
):
    tok_rows, width = k_ref.shape
    tiles = width // LANES
    spread_tokens(k_ref, v_ref, x_ref)
    spread_tokens(o_ref, q_ref, g_ref)
    walk_tokens(x_ref, coef_ref, tok_rows, tiles, 0, 1)
    walk_tokens(g_ref, coef_ref, tok_rows, tiles, tok_rows - 1, -1)
    for tile in range(tiles):
        cols = slice(tile * LANES, (tile + 1) * LANES)
        rows = tile_rows(tok_rows, tile)
        gain = gain_ref[:, cols]
        conv_in = product(k_ref[:, cols], v_ref[:, cols]).astype(F32)
        conv_ref[:, cols] = x_ref[rows, :] + gain * conv_in
        mid_grad = product(o_ref[:, cols], q_ref[:, cols]).astype(F32)
        grad_ref[:, cols] = g_ref[rows, :] + gain * mid_grad
    done_ref[...] = jnp.zeros(done_ref.shape, F32)


def local_parts(query_proj, key_proj, value_proj, out_grad, coefs, gain):
    tok_rows, width = key_proj.shape
    tiles = coefs.shape[2]
    return pl.pallas_call(
        local_kernel,
        out_shape=[jax.ShapeDtypeStruct((tok_rows, width), F32)] * 2
        + [jax.ShapeDtypeStruct((SUBLANES, LANES), F32)],
        scratch_shapes=[pltpu.VMEM(token_shape(tok_rows, tiles), F32)] * 2,
        compiler_params=pltpu.CompilerParams(vmem_limit_bytes=VMEM_BYTES),
        name="local_parts",
    )(query_proj, key_proj, value_proj, out_grad, coefs, gain)


def along_column(state, pairs, k):
    route = [(2 * p + b, 2 * ((p + k) % pairs) + b) for p in range(pairs) for b in range(2)]
    return lax.ppermute(state, "seq", route)


def inside_pair(state, pairs):
    return lax.ppermute(state, "seq", [(i, i ^ 1) for i in range(2 * pairs)])


def fill_edge(ref, held, coef_ref, tok_rows, tiles, start, move):
    modes = coef_ref.shape[1]
    decay = [coef_ref[0, m] for m in range(modes)]

    def step(t, held):
        held = tuple(decay[m] * held[m] for m in range(modes))
        ref[token_place(start + move * t, tok_rows, tiles)] = tree_sum(list(held))
        return held

    held = tuple(coef_ref[2, m] * held[m] for m in range(modes))
    lax.fori_loop(0, tok_rows, step, held, unroll=8)


def edge_kernel(seq_ref, coef_ref, near_ref, *refs):
    state_refs, edge_ref = refs[:-1], refs[-1]
    fill_side(0, edge_ref, seq_ref, coef_ref, near_ref, state_refs)


def fill_side(side, edge_ref, seq_ref, coef_ref, near_ref, state_refs):
    tiles = coef_ref.shape[2]
    tok_rows = edge_ref.shape[0] // tiles - GAP
    held = sum_pairs(side, seq_ref[0], coef_ref, near_ref, state_refs)
    start, move = ((0, 1), (tok_rows - 1, -1))[side]
    fill_edge(edge_ref, held, coef_ref, tok_rows, tiles, start, move)


def edge_terms(tok_rows, seq_index, coefs, near, states):
    whole = pl.BlockSpec(memory_space=pltpu.VMEM)
    return pl.pallas_call(
        edge_kernel,
        in_specs=[pl.BlockSpec(memory_space=pltpu.SMEM)] + [whole] * (2 + len(states)),
        out_shape=jax.ShapeDtypeStruct(token_shape(tok_rows, coefs.shape[2]), F32),
        compiler_params=pltpu.CompilerParams(vmem_limit_bytes=VMEM_BYTES),
        name="edge_terms",
    )(seq_index, coefs, near, *states)


def multiply_out(part_ref, edge_ref, factor_refs, out_refs, hbm_refs, sems):
    tok_rows, width = part_ref.shape
    copies = []
    for tile in range(width // LANES):
        cols = slice(tile * LANES, (tile + 1) * LANES)
        value = part_ref[:, cols] + edge_ref[tile_rows(tok_rows, tile), :]
        for i, (factor_ref, out_ref, hbm_ref) in enumerate(zip(factor_refs, out_refs, hbm_refs)):
            out_ref[:, cols] = (value * factor_ref[:, cols].astype(F32)).astype(BF16)
            place = (slice(None), pl.ds(tile * LANES, LANES))
            copies.append(
                pltpu.make_async_copy(out_ref.at[place], hbm_ref.at[place], sems.at[i, tile])
            )
            copies[-1].start()
    return copies


def conv_kernel(seq_ref, part_ref, edge_ref, q_ref, coef_ref, near_ref, *refs):
    state_refs, (layer_hbm, next_ref, layer_ref, sems) = refs[:-4], refs[-4:]
    copies = multiply_out(part_ref, edge_ref, [q_ref], [layer_ref], [layer_hbm], sems)
    fill_side(1, next_ref, seq_ref, coef_ref, near_ref, state_refs)
    for copy in copies:
        copy.wait()


def conv_outputs(seq_index, part, edge, query_proj, coefs, near, states):
    tok_rows, width = part.shape
    whole = pl.BlockSpec(memory_space=pltpu.VMEM)
    return pl.pallas_call(
        conv_kernel,
        in_specs=[pl.BlockSpec(memory_space=pltpu.SMEM)] + [whole] * (5 + len(states)),
        out_specs=[pl.BlockSpec(memory_space=pl.ANY), whole],
        out_shape=[
            jax.ShapeDtypeStruct((tok_rows, width), BF16),
            jax.ShapeDtypeStruct(edge.shape, F32),
        ],
        scratch_shapes=[
            pltpu.VMEM((tok_rows, width), BF16),
            pltpu.SemaphoreType.DMA((1, width // LANES)),
        ],
        compiler_params=pltpu.CompilerParams(vmem_limit_bytes=VMEM_BYTES),
        name="conv_outputs",
    )(seq_index, part, edge, query_proj, coefs, near, *states)


def grad_kernel(
    part_ref, edge_ref, v_ref, k_ref, key_hbm, value_hbm, key_ref, value_ref, sems
):
    copies = multiply_out(
        part_ref, edge_ref, [v_ref, k_ref], [key_ref, value_ref], [key_hbm, value_hbm], sems
    )
    for copy in copies:
        copy.wait()


def grad_outputs(part, edge, value_proj, key_proj):
    tok_rows, width = part.shape
    return pl.pallas_call(
        grad_kernel,
        in_specs=[pl.BlockSpec(memory_space=pltpu.VMEM)] * 4,
        out_specs=[pl.BlockSpec(memory_space=pl.ANY)] * 2,
        out_shape=[jax.ShapeDtypeStruct((tok_rows, width), BF16)] * 2,
        scratch_shapes=[pltpu.VMEM((tok_rows, width), BF16)] * 2
        + [pltpu.SemaphoreType.DMA((2, width // LANES))],
        compiler_params=pltpu.CompilerParams(vmem_limit_bytes=VMEM_BYTES),
        name="grad_outputs",
    )(part, edge, value_proj, key_proj)


def lag_kernel(shards, chans, groups, owned, scale, *refs):
    in_refs, (out_ref, u_all, g_all, turned_all) = refs[1:-4], refs[-4:]
    tok_rows = out_ref.shape[2]
    halves = tok_rows // LANES
    blocks = shards * halves
    depth = chans * groups
    full = blocks * depth
    if len(in_refs) == 1:
        take = chans * groups * owned

        def by_filter(row):
            return row % depth * owned + row // depth

        order = one_hot(take, take, by_filter)
        for which, kept in enumerate((u_all, g_all)):
            rows = slice(which * groups * owned, (which + 1) * groups * owned)
            for s in range(shards):
                piece = in_refs[0][s * chans : (s + 1) * chans, rows, :].reshape(take, tok_rows)
                piece = jnp.dot(order, piece, preferred_element_type=F32).astype(BF16)
                piece = piece.reshape(owned, depth, tok_rows)
                for h in range(halves):
                    first = (s * halves + h) * depth
                    kept[:, first : first + depth, :] = piece[:, :, h * LANES : (h + 1) * LANES]
    else:
        u_all[...] = in_refs[0][...]
        g_all[:, :full, :] = in_refs[1][...]
    g_all[:, full:, :] = jnp.zeros((owned, g_all.shape[1] - full, LANES), BF16)
    mirror = one_hot(LANES, LANES, lambda row: LANES - 1 - row)
    row = lax.broadcasted_iota(jnp.int32, (LANES, LANES), 0)
    col = lax.broadcasted_iota(jnp.int32, (LANES, LANES), 1)
    same_block = row + col >= LANES - 1
    filter_row = lax.broadcasted_iota(jnp.int32, (owned, LANES), 0)
    batch = min(blocks, 16)

    def one_filter(f, _):
        turned = turned_all[f]

        def some_lags(first):
            tables = []
            for d in range(0, batch, 2):
                live = full
                if batch == blocks:
                    live = min(full, -(-(blocks - d) * depth // LANES) * LANES)
                pair = jnp.concatenate(
                    [
                        g_all[f, pl.ds(pl.multiple_of((first + d + e) * depth, depth), live), :]
                        for e in range(2)
                    ],
                    axis=1,
                )
                table = jnp.dot(turned[:, :live], pair, preferred_element_type=F32)
                tables += [table[:, :LANES], table[:, LANES:]]
            last = g_all[f, pl.ds(pl.multiple_of((first + batch) * depth, depth), full), :]
            if batch < blocks:
                tables.append(jnp.dot(turned, last, preferred_element_type=F32))
            else:
                tables.append(jnp.zeros((LANES, LANES), F32))
            for d in range(batch):
                joined = jnp.where(same_block, tables[d], tables[d + 1])
                folded = tree_sum(
                    [
                        pltpu.roll(joined[r : r + SUBLANES], r, 1) if r else joined[:SUBLANES]
                        for r in range(0, LANES, SUBLANES)
                    ]
                )
                skewed = pltpu.roll(folded, 1, 1, stride=1, stride_axis=0)
                sums = jnp.sum(skewed, axis=0, keepdims=True) * scale
                lane = d % halves * LANES
                place = ((first + d) // halves, slice(None), slice(lane, lane + LANES))
                out_ref[place] = jnp.where(filter_row == f, sums, out_ref[place])

        if batch == blocks:
            some_lags(0)
        else:
            lax.fori_loop(0, blocks // batch, lambda i, c: (some_lags(i * batch), c)[1], 0)
        return 0

    for f in range(owned):
        turned_all[f] = lax.dot_general(
            mirror, u_all[f], (((1,), (1,)), ((), ())), preferred_element_type=F32
        ).astype(BF16)
    lax.fori_loop(0, owned, one_filter, 0, unroll=min(owned, 8))


def filter_lags(received, done, shards, chans, owned, scale):
    tok_rows = received.shape[2]
    groups = received.shape[1] // (2 * owned)
    halves = tok_rows // LANES
    depth = chans * groups
    full = shards * halves * depth
    args = (received,)
    if owned % SUBLANES:
        split = received.reshape(shards, chans, 2, groups, owned, halves, LANES)
        split = split.transpose(2, 4, 0, 5, 1, 3, 6).reshape(2, owned, full, LANES)
        args = (split[0], split[1])
    whole = pl.BlockSpec(memory_space=pltpu.VMEM)
    return pl.pallas_call(
        functools.partial(lag_kernel, shards, chans, groups, owned, scale),
        in_specs=[pl.BlockSpec(memory_space=pl.ANY)] + [whole] * len(args),
        out_specs=whole,
        out_shape=jax.ShapeDtypeStruct((shards, owned, tok_rows), F32),
        scratch_shapes=[
            pltpu.VMEM((owned, full, LANES), BF16),
            pltpu.VMEM((owned, 2 * full + depth, LANES), BF16),
            pltpu.VMEM((owned, LANES, full), BF16),
        ],
        compiler_params=pltpu.CompilerParams(vmem_limit_bytes=VMEM_BYTES),
        name="filter_lags",
    )(done, *args)


def per_device(query_proj, key_proj, value_proj, out_grad, residues, decay_rate, skip_gain):
    tok_rows, width = key_proj.shape
    shards = lax.axis_size("seq")
    chans = lax.axis_size("chan")
    length = shards * tok_rows
    owned = FILTERS // (shards * chans)
    modes = residues.shape[1]
    signals = (query_proj, key_proj, value_proj, out_grad)

    send = pack_signals(shards, chans, owned, *signals)
    send, *signals, residues, decay_rate = lax.optimization_barrier(
        (send, *signals, residues, decay_rate)
    )
    received = lax.all_to_all(send, ("seq", "chan"), split_axis=0, concat_axis=0, tiled=True)

    coefs = jnp.stack(
        [
            jnp.exp(-decay_rate),
            jnp.exp(-(decay_rate * float(tok_rows))),
            residues * jnp.sqrt(decay_rate),
        ]
    )
    coefs = coefs.transpose(0, 2, 1).reshape(3, modes, 1, FILTERS // LANES, LANES)
    coefs = jnp.broadcast_to(coefs, (3, modes, width // FILTERS, FILTERS // LANES, LANES))
    coefs = coefs.reshape(3, modes, width // LANES, LANES)
    seq_index = lax.axis_index("seq").reshape(1)
    pairs = shards // 2
    own, sent = block_states(*signals, coefs)
    near = inside_pair(sent, pairs)
    states = pair_states(seq_index, pairs, coefs, own, near)
    *states, coefs, near = lax.optimization_barrier((*states, coefs, near))
    states = [along_column(state, pairs, 1 + i) for i, state in enumerate(states)]
    conv_part, grad_part, done = local_parts(*signals, coefs, skip_gain[None, :])

    scale = 1.0 / math.sqrt(length * (CHANNELS // FILTERS))
    lags = filter_lags(received, done, shards, chans, owned, scale)
    lags, *states = lax.optimization_barrier((lags, *states))
    lags = lax.all_to_all(lags, "seq", split_axis=0, concat_axis=0, tiled=True)
    filter_grad = lags.reshape(shards * owned, tok_rows).T
    query_proj, key_proj, value_proj, _ = signals
    edge = edge_terms(tok_rows, seq_index, coefs, near, states)
    layer_out, edge = conv_outputs(seq_index, conv_part, edge, query_proj, coefs, near, states)
    key_grad, value_grad = grad_outputs(grad_part, edge, value_proj, key_proj)
    return (layer_out, key_grad, value_grad, filter_grad)


def solution(mesh):
    split = P("seq", "chan")
    return jax.shard_map(
        per_device,
        mesh=mesh,
        in_specs=(split, split, split, split, P(), P(), P("chan")),
        out_specs=(split, split, split, split),
        check_vma=False,
    )
```

```python
import functools
import math

import jax
import jax.numpy as jnp
from jax import lax
from jax.experimental import pallas as pl
from jax.experimental.pallas import tpu as pltpu
from jax.sharding import PartitionSpec as P

CHANNELS = 4096
FILTERS = 256
LANES = 128
SUBLANES = 8
GAP = 8
VMEM_BYTES = 16 * 1024 * 1024
FULL_VMEM_BYTES = 62 * 1024 * 1024
F32 = jnp.float32
BF16 = jnp.bfloat16
LINK = jnp.bfloat16


def product(first, second):
    return first * second


def one_hot(rows, cols, column_of):
    row = lax.broadcasted_iota(jnp.int32, (rows, cols), 0)
    col = lax.broadcasted_iota(jnp.int32, (rows, cols), 1)
    return (col == column_of(row)).astype(F32).astype(BF16)


def pack_kernel(shards, chans, owned, *refs):
    hbm_refs, send_ref, held, packed, in_sems, out_sems = refs[:4], *refs[4:]
    tok_rows, width = held.shape[1:]
    groups = width // FILTERS
    per_chan = FILTERS // chans
    units = [(which, first) for which in range(2) for first in range(0, groups, 2)]

    def arrival(i, first):
        place = (slice(None), pl.ds(first * FILTERS, 2 * FILTERS))
        return pltpu.make_async_copy(
            hbm_refs[i].at[place], held.at[(i, *place)], in_sems.at[i, first // 2]
        )

    def departure(which, first):
        if owned % SUBLANES:
            place = (which, pl.ds(first, 2))
        else:
            place = (slice(None), pl.ds((which * groups + first) * owned, 2 * owned))
        return pltpu.make_async_copy(
            packed.at[place], send_ref.at[place], out_sems.at[which, first // 2]
        )

    for which, first in units:
        for i in (2 * which, 2 * which + 1):
            arrival(i, first).start()

    def owned_filter(row):
        seq = row // (chans * owned)
        chan = row // owned % chans
        return chan * per_chan + seq * owned + row % owned

    order = one_hot(FILTERS, FILTERS, owned_filter)
    for which, first in units:
        for i in (2 * which, 2 * which + 1):
            arrival(i, first).wait()
        pieces = []
        for group in (first, first + 1):
            cols = slice(group * FILTERS, (group + 1) * FILTERS)
            piece = lax.dot_general(
                order,
                product(held[2 * which, :, cols], held[2 * which + 1, :, cols]),
                (((1,), (1,)), ((), ())),
                preferred_element_type=F32,
            )
            if owned % SUBLANES:
                packed[which, group] = piece.astype(BF16)
            else:
                pieces.append(piece.reshape(shards * chans, owned, tok_rows))
        if pieces:
            row = (which * groups + first) * owned
            packed[:, row : row + 2 * owned, :] = jnp.concatenate(pieces, axis=1).astype(BF16)
        departure(which, first).start()
    for which, first in units:
        departure(which, first).wait()


def pack_signals(shards, chans, owned, query_proj, key_proj, value_proj, out_grad):
    tok_rows, width = key_proj.shape
    groups = width // FILTERS
    dests = shards * chans
    if owned % SUBLANES:
        shape = (2, groups, FILTERS, tok_rows)
    else:
        shape = (dests, 2 * groups * owned, tok_rows)
    send = pl.pallas_call(
        functools.partial(pack_kernel, shards, chans, owned),
        in_specs=[pl.BlockSpec(memory_space=pl.ANY)] * 4,
        out_specs=pl.BlockSpec(memory_space=pl.ANY),
        out_shape=jax.ShapeDtypeStruct(shape, BF16),
        scratch_shapes=[
            pltpu.VMEM((4, tok_rows, width), BF16),
            pltpu.VMEM(shape, BF16),
            pltpu.SemaphoreType.DMA((4, groups // 2)),
            pltpu.SemaphoreType.DMA((2, groups // 2)),
        ],
        compiler_params=pltpu.CompilerParams(vmem_limit_bytes=FULL_VMEM_BYTES),
        name="pack_signals",
    )(key_proj, value_proj, out_grad, query_proj)
    if owned % SUBLANES:
        send = send.reshape(2, groups, dests, owned, tok_rows)
        send = send.transpose(2, 0, 1, 3, 4).reshape(dests, 2 * groups * owned, tok_rows)
    return send


def tile_rows(tok_rows, tile):
    first = tile * (tok_rows + GAP)
    return slice(first, first + tok_rows)


def token_shape(tok_rows, tiles):
    return (tiles * (tok_rows + GAP), LANES)


def token_place(t, tok_rows, tiles):
    return (pl.ds(t, tiles, stride=tok_rows + GAP), slice(None))


def spread_tokens(a_ref, b_ref, x_ref):
    tok_rows, width = a_ref.shape
    for tile in range(width // LANES):
        cols = slice(tile * LANES, (tile + 1) * LANES)
        x_ref[tile_rows(tok_rows, tile), :] = product(a_ref[:, cols], b_ref[:, cols]).astype(F32)


def walk_tokens(ref, coef_ref, tok_rows, tiles, start, move):
    modes = coef_ref.shape[1]
    decay = [coef_ref[0, m] for m in range(modes)]
    weight = [coef_ref[2, m] for m in range(modes)]

    def step(t, held):
        place = token_place(start + move * t, tok_rows, tiles)
        x = ref[place]
        held = tuple(decay[m] * held[m] + x for m in range(modes))
        ref[place] = tree_sum([weight[m] * held[m] for m in range(modes)])
        return held

    zero = tuple(jnp.zeros((tiles, LANES), F32) for _ in range(modes))
    return lax.fori_loop(0, tok_rows, step, zero, unroll=8)


def tree_sum(terms):
    while len(terms) > 1:
        terms = [sum(terms[i : i + 2][1:], terms[i]) for i in range(0, len(terms), 2)]
    return terms[0]


def state_kernel(q_ref, k_ref, v_ref, o_ref, coef_ref, own_ref, sent_ref, x_ref, g_ref):
    tok_rows, width = k_ref.shape
    tiles = width // LANES
    modes = coef_ref.shape[1]
    spread_tokens(k_ref, v_ref, x_ref)
    spread_tokens(o_ref, q_ref, g_ref)
    decay = [coef_ref[0, m] for m in range(modes)]

    def step(t, carry):
        x = x_ref[token_place(t, tok_rows, tiles)]
        g = g_ref[token_place(tok_rows - 1 - t, tok_rows, tiles)]
        ahead = tuple(decay[m] * carry[0][m] + x for m in range(modes))
        behind = tuple(decay[m] * carry[1][m] + g for m in range(modes))
        return (ahead, behind)

    zero = tuple(jnp.zeros((tiles, LANES), F32) for _ in range(modes))
    for side, held in enumerate(lax.fori_loop(0, tok_rows, step, (zero, zero), unroll=8)):
        held = jnp.concatenate(held, axis=0)
        own_ref[side] = held
        sent_ref[side] = held.astype(LINK)


def block_states(query_proj, key_proj, value_proj, out_grad, coefs):
    tok_rows, width = key_proj.shape
    modes, tiles = coefs.shape[1:3]
    return pl.pallas_call(
        state_kernel,
        out_shape=[
            jax.ShapeDtypeStruct((2, modes * tiles, LANES), F32),
            jax.ShapeDtypeStruct((2, modes * tiles, LANES), LINK),
        ],
        scratch_shapes=[pltpu.VMEM(token_shape(tok_rows, tiles), F32)] * 2,
        compiler_params=pltpu.CompilerParams(vmem_limit_bytes=VMEM_BYTES),
        name="block_states",
    )(query_proj, key_proj, value_proj, out_grad, coefs)


def pair_kernel(seq_ref, coef_ref, own_ref, near_ref, *state_refs):
    pairs = len(state_refs) + 1
    modes, tiles = coef_ref.shape[1:3]
    pair = seq_ref[0] // 2
    second = seq_ref[0] % 2 == 1
    for m in range(modes):
        rows = slice(m * tiles, (m + 1) * tiles)
        decay = coef_ref[1, m]
        own, near = own_ref[0, rows], near_ref[0].astype(F32)[rows]
        ahead = jnp.where(second, own + decay * near, near + decay * own)
        own, near = own_ref[1, rows], near_ref[1].astype(F32)[rows]
        behind = jnp.where(second, near + decay * own, own + decay * near)
        for k in range(1, pairs):
            state_refs[k - 1][rows] = jnp.where(pair + k < pairs, ahead, behind)


def pair_states(seq_index, pairs, coefs, own, near):
    whole = pl.BlockSpec(memory_space=pltpu.VMEM)
    states = pl.pallas_call(
        pair_kernel,
        in_specs=[pl.BlockSpec(memory_space=pltpu.SMEM)] + [whole] * 3,
        out_specs=[whole] * (pairs - 1),
        out_shape=[jax.ShapeDtypeStruct(own.shape[1:], F32)] * (pairs - 1),
        compiler_params=pltpu.CompilerParams(vmem_limit_bytes=VMEM_BYTES),
        name="pair_states",
    )(seq_index, coefs, own, near)
    return [state.astype(LINK) for state in states]


def sum_pairs(side, seq, coef_ref, near_ref, state_refs):
    pairs = len(state_refs) + 1
    modes, tiles = coef_ref.shape[1:3]
    pair, count = seq // 2, (seq // 2, pairs - 1 - seq // 2)[side]
    beside = seq % 2 == 1 - side
    held = []
    for m in range(modes):
        rows = slice(m * tiles, (m + 1) * tiles)
        decay = coef_ref[1, m]
        total = jnp.zeros((tiles, LANES), F32)
        for k in range(pairs - 1, 0, -1):
            state_ref = state_refs[k - 1 if side == 0 else pairs - k - 1]
            block = state_ref[...].astype(F32)[rows]
            total = decay * decay * total + jnp.where(k <= count, block, 0.0)
        near = near_ref[side].astype(F32)[rows]
        held.append(jnp.where(beside, decay * total + near, total))
    return held


def local_kernel(
    q_ref, k_ref, v_ref, o_ref, coef_ref, gain_ref, conv_ref, grad_ref, done_ref, x_ref, g_ref
):
    tok_rows, width = k_ref.shape
    tiles = width // LANES
    spread_tokens(k_ref, v_ref, x_ref)
    spread_tokens(o_ref, q_ref, g_ref)
    walk_tokens(x_ref, coef_ref, tok_rows, tiles, 0, 1)
    walk_tokens(g_ref, coef_ref, tok_rows, tiles, tok_rows - 1, -1)
    for tile in range(tiles):
        cols = slice(tile * LANES, (tile + 1) * LANES)
        rows = tile_rows(tok_rows, tile)
        gain = gain_ref[:, cols]
        conv_in = product(k_ref[:, cols], v_ref[:, cols]).astype(F32)
        conv_ref[:, cols] = x_ref[rows, :] + gain * conv_in
        mid_grad = product(o_ref[:, cols], q_ref[:, cols]).astype(F32)
        grad_ref[:, cols] = g_ref[rows, :] + gain * mid_grad
    done_ref[...] = jnp.zeros(done_ref.shape, F32)


def local_parts(query_proj, key_proj, value_proj, out_grad, coefs, gain):
    tok_rows, width = key_proj.shape
    tiles = coefs.shape[2]
    return pl.pallas_call(
        local_kernel,
        out_shape=[jax.ShapeDtypeStruct((tok_rows, width), F32)] * 2
        + [jax.ShapeDtypeStruct((SUBLANES, LANES), F32)],
        scratch_shapes=[pltpu.VMEM(token_shape(tok_rows, tiles), F32)] * 2,
        compiler_params=pltpu.CompilerParams(vmem_limit_bytes=VMEM_BYTES),
        name="local_parts",
    )(query_proj, key_proj, value_proj, out_grad, coefs, gain)


def along_column(state, pairs, k):
    route = [(2 * p + b, 2 * ((p + k) % pairs) + b) for p in range(pairs) for b in range(2)]
    return lax.ppermute(state, "seq", route)


def inside_pair(state, pairs):
    return lax.ppermute(state, "seq", [(i, i ^ 1) for i in range(2 * pairs)])


def fill_edge(ref, held, coef_ref, tok_rows, tiles, start, move):
    modes = coef_ref.shape[1]
    decay = [coef_ref[0, m] for m in range(modes)]

    def step(t, held):
        held = tuple(decay[m] * held[m] for m in range(modes))
        ref[token_place(start + move * t, tok_rows, tiles)] = tree_sum(list(held))
        return held

    held = tuple(coef_ref[2, m] * held[m] for m in range(modes))
    lax.fori_loop(0, tok_rows, step, held, unroll=8)


def edge_kernel(seq_ref, coef_ref, near_ref, *refs):
    state_refs, edge_ref = refs[:-1], refs[-1]
    fill_side(0, edge_ref, seq_ref, coef_ref, near_ref, state_refs)


def fill_side(side, edge_ref, seq_ref, coef_ref, near_ref, state_refs):
    tiles = coef_ref.shape[2]
    tok_rows = edge_ref.shape[0] // tiles - GAP
    held = sum_pairs(side, seq_ref[0], coef_ref, near_ref, state_refs)
    start, move = ((0, 1), (tok_rows - 1, -1))[side]
    fill_edge(edge_ref, held, coef_ref, tok_rows, tiles, start, move)


def edge_terms(tok_rows, seq_index, coefs, near, states):
    whole = pl.BlockSpec(memory_space=pltpu.VMEM)
    return pl.pallas_call(
        edge_kernel,
        in_specs=[pl.BlockSpec(memory_space=pltpu.SMEM)] + [whole] * (2 + len(states)),
        out_shape=jax.ShapeDtypeStruct(token_shape(tok_rows, coefs.shape[2]), F32),
        compiler_params=pltpu.CompilerParams(vmem_limit_bytes=VMEM_BYTES),
        name="edge_terms",
    )(seq_index, coefs, near, *states)


def multiply_out(part_ref, edge_ref, factor_refs, out_refs, hbm_refs, sems):
    tok_rows, width = part_ref.shape
    copies = []
    for tile in range(width // LANES):
        cols = slice(tile * LANES, (tile + 1) * LANES)
        value = part_ref[:, cols] + edge_ref[tile_rows(tok_rows, tile), :]
        for i, (factor_ref, out_ref, hbm_ref) in enumerate(zip(factor_refs, out_refs, hbm_refs)):
            out_ref[:, cols] = (value * factor_ref[:, cols].astype(F32)).astype(BF16)
            place = (slice(None), pl.ds(tile * LANES, LANES))
            copies.append(
                pltpu.make_async_copy(out_ref.at[place], hbm_ref.at[place], sems.at[i, tile])
            )
            copies[-1].start()
    return copies


def conv_kernel(seq_ref, part_ref, edge_ref, q_ref, coef_ref, near_ref, *refs):
    state_refs, (layer_hbm, next_ref, layer_ref, sems) = refs[:-4], refs[-4:]
    copies = multiply_out(part_ref, edge_ref, [q_ref], [layer_ref], [layer_hbm], sems)
    fill_side(1, next_ref, seq_ref, coef_ref, near_ref, state_refs)
    for copy in copies:
        copy.wait()


def conv_outputs(seq_index, part, edge, query_proj, coefs, near, states):
    tok_rows, width = part.shape
    whole = pl.BlockSpec(memory_space=pltpu.VMEM)
    return pl.pallas_call(
        conv_kernel,
        in_specs=[pl.BlockSpec(memory_space=pltpu.SMEM)] + [whole] * (5 + len(states)),
        out_specs=[pl.BlockSpec(memory_space=pl.ANY), whole],
        out_shape=[
            jax.ShapeDtypeStruct((tok_rows, width), BF16),
            jax.ShapeDtypeStruct(edge.shape, F32),
        ],
        scratch_shapes=[
            pltpu.VMEM((tok_rows, width), BF16),
            pltpu.SemaphoreType.DMA((1, width // LANES)),
        ],
        compiler_params=pltpu.CompilerParams(vmem_limit_bytes=VMEM_BYTES),
        name="conv_outputs",
    )(seq_index, part, edge, query_proj, coefs, near, *states)


def grad_kernel(
    part_ref, edge_ref, v_ref, k_ref, key_hbm, value_hbm, key_ref, value_ref, sems
):
    copies = multiply_out(
        part_ref, edge_ref, [v_ref, k_ref], [key_ref, value_ref], [key_hbm, value_hbm], sems
    )
    for copy in copies:
        copy.wait()


def grad_outputs(part, edge, value_proj, key_proj):
    tok_rows, width = part.shape
    return pl.pallas_call(
        grad_kernel,
        in_specs=[pl.BlockSpec(memory_space=pltpu.VMEM)] * 4,
        out_specs=[pl.BlockSpec(memory_space=pl.ANY)] * 2,
        out_shape=[jax.ShapeDtypeStruct((tok_rows, width), BF16)] * 2,
        scratch_shapes=[pltpu.VMEM((tok_rows, width), BF16)] * 2
        + [pltpu.SemaphoreType.DMA((2, width // LANES))],
        compiler_params=pltpu.CompilerParams(vmem_limit_bytes=VMEM_BYTES),
        name="grad_outputs",
    )(part, edge, value_proj, key_proj)


def lag_kernel(shards, chans, groups, owned, *refs):
    in_refs, (out_ref, lag_sums, u_all, g_all, turned_all) = refs[1:-5], refs[-5:]
    halves = out_ref.shape[1] // owned
    tok_rows = halves * LANES
    blocks = shards * halves
    depth = chans * groups
    full = blocks * depth
    if len(in_refs) == 1:
        take = chans * groups * owned

        def by_filter(row):
            return row % depth * owned + row // depth

        order = one_hot(take, take, by_filter)
        for which, kept in enumerate((u_all, g_all)):
            rows = slice(which * groups * owned, (which + 1) * groups * owned)
            for s in range(shards):
                piece = in_refs[0][s * chans : (s + 1) * chans, rows, :].reshape(take, tok_rows)
                piece = jnp.dot(order, piece, preferred_element_type=F32).astype(BF16)
                piece = piece.reshape(owned, depth, tok_rows)
                for h in range(halves):
                    first = (s * halves + h) * depth
                    kept[:, first : first + depth, :] = piece[:, :, h * LANES : (h + 1) * LANES]
    else:
        u_all[...] = in_refs[0][...]
        g_all[:, :full, :] = in_refs[1][...]
    g_all[:, full:, :] = jnp.zeros((owned, g_all.shape[1] - full, LANES), BF16)
    mirror = one_hot(LANES, LANES, lambda row: LANES - 1 - row)
    row = lax.broadcasted_iota(jnp.int32, (LANES, LANES), 0)
    col = lax.broadcasted_iota(jnp.int32, (LANES, LANES), 1)
    same_block = row + col >= LANES - 1
    filter_row = lax.broadcasted_iota(jnp.int32, (owned, LANES), 0)
    batch = min(blocks, 16)

    def one_filter(f, _):
        turned = turned_all[f]

        def some_lags(first):
            tables = []
            for d in range(0, batch, 2):
                live = full
                if batch == blocks:
                    live = min(full, -(-(blocks - d) * depth // LANES) * LANES)
                pair = jnp.concatenate(
                    [
                        g_all[f, pl.ds(pl.multiple_of((first + d + e) * depth, depth), live), :]
                        for e in range(2)
                    ],
                    axis=1,
                )
                table = jnp.dot(turned[:, :live], pair, preferred_element_type=F32)
                tables += [table[:, :LANES], table[:, LANES:]]
            last = g_all[f, pl.ds(pl.multiple_of((first + batch) * depth, depth), full), :]
            if batch < blocks:
                tables.append(jnp.dot(turned, last, preferred_element_type=F32))
            else:
                tables.append(jnp.zeros((LANES, LANES), F32))
            for d in range(batch):
                joined = jnp.where(same_block, tables[d], tables[d + 1])
                skewed = pltpu.roll(joined, 1, 1, stride=1, stride_axis=0)
                sums = jnp.sum(skewed, axis=0, keepdims=True)
                row = d % halves * owned
                place = ((first + d) // halves, slice(row, row + owned), slice(None))
                lag_sums[place] = jnp.where(filter_row == f, sums, lag_sums[place])

        if batch == blocks:
            some_lags(0)
        else:
            lax.fori_loop(0, blocks // batch, lambda i, c: (some_lags(i * batch), c)[1], 0)
        return 0

    for f in range(owned):
        turned_all[f] = lax.dot_general(
            mirror, u_all[f], (((1,), (1,)), ((), ())), preferred_element_type=F32
        ).astype(BF16)
    lax.fori_loop(0, owned, one_filter, 0, unroll=min(owned, 8))
    out_ref[...] = lag_sums[...].astype(LINK)


def filter_lags(received, done, shards, chans, owned):
    tok_rows = received.shape[2]
    groups = received.shape[1] // (2 * owned)
    halves = tok_rows // LANES
    depth = chans * groups
    full = shards * halves * depth
    args = (received,)
    if owned % SUBLANES:
        split = received.reshape(shards, chans, 2, groups, owned, halves, LANES)
        split = split.transpose(2, 4, 0, 5, 1, 3, 6).reshape(2, owned, full, LANES)
        args = (split[0], split[1])
    whole = pl.BlockSpec(memory_space=pltpu.VMEM)
    return pl.pallas_call(
        functools.partial(lag_kernel, shards, chans, groups, owned),
        in_specs=[pl.BlockSpec(memory_space=pl.ANY)] + [whole] * len(args),
        out_specs=whole,
        out_shape=jax.ShapeDtypeStruct((shards, halves * owned, LANES), LINK),
        scratch_shapes=[
            pltpu.VMEM((shards, halves * owned, LANES), F32),
            pltpu.VMEM((owned, full, LANES), BF16),
            pltpu.VMEM((owned, 2 * full + depth, LANES), BF16),
            pltpu.VMEM((owned, LANES, full), BF16),
        ],
        compiler_params=pltpu.CompilerParams(vmem_limit_bytes=VMEM_BYTES),
        name="filter_lags",
    )(done, *args)


def per_device(query_proj, key_proj, value_proj, out_grad, residues, decay_rate, skip_gain):
    tok_rows, width = key_proj.shape
    shards = lax.axis_size("seq")
    chans = lax.axis_size("chan")
    length = shards * tok_rows
    owned = FILTERS // (shards * chans)
    modes = residues.shape[1]
    signals = (query_proj, key_proj, value_proj, out_grad)

    send = pack_signals(shards, chans, owned, *signals)
    send, *signals, residues, decay_rate = lax.optimization_barrier(
        (send, *signals, residues, decay_rate)
    )
    received = lax.all_to_all(send, ("seq", "chan"), split_axis=0, concat_axis=0, tiled=True)

    coefs = jnp.stack(
        [
            jnp.exp(-decay_rate),
            jnp.exp(-(decay_rate * float(tok_rows))),
            residues * jnp.sqrt(decay_rate),
        ]
    )
    coefs = coefs.transpose(0, 2, 1).reshape(3, modes, 1, FILTERS // LANES, LANES)
    coefs = jnp.broadcast_to(coefs, (3, modes, width // FILTERS, FILTERS // LANES, LANES))
    coefs = coefs.reshape(3, modes, width // LANES, LANES)
    seq_index = lax.axis_index("seq").reshape(1)
    pairs = shards // 2
    own, sent = block_states(*signals, coefs)
    near = inside_pair(sent, pairs)
    states = pair_states(seq_index, pairs, coefs, own, near)
    *states, coefs, near = lax.optimization_barrier((*states, coefs, near))
    states = [along_column(state, pairs, 1 + i) for i, state in enumerate(states)]
    conv_part, grad_part, done = local_parts(*signals, coefs, skip_gain[None, :])

    scale = 1.0 / math.sqrt(length * (CHANNELS // FILTERS))
    lags = filter_lags(received, done, shards, chans, owned)
    lags, *states = lax.optimization_barrier((lags, *states))
    lags = lax.all_to_all(lags, "seq", split_axis=0, concat_axis=0, tiled=True)
    lags = lags.reshape(shards, tok_rows // LANES, owned, LANES).transpose(0, 2, 1, 3)
    filter_grad = lags.reshape(shards * owned, tok_rows).T.astype(F32) * scale
    query_proj, key_proj, value_proj, _ = signals
    edge = edge_terms(tok_rows, seq_index, coefs, near, states)
    layer_out, edge = conv_outputs(seq_index, conv_part, edge, query_proj, coefs, near, states)
    key_grad, value_grad = grad_outputs(grad_part, edge, value_proj, key_proj)
    return (layer_out, key_grad, value_grad, filter_grad)


def solution(mesh):
    split = P("seq", "chan")
    return jax.shard_map(
        per_device,
        mesh=mesh,
        in_specs=(split, split, split, split, P(), P(), P("chan")),
        out_specs=(split, split, split, split),
        check_vma=False,
    )
```

```python
import functools
import math

import jax
import jax.numpy as jnp
from jax import lax
from jax.experimental import pallas as pl
from jax.experimental.pallas import tpu as pltpu
from jax.sharding import PartitionSpec as P

CHANNELS = 4096
FILTERS = 256
LANES = 128
SUBLANES = 8
GAP = 8
VMEM_BYTES = 16 * 1024 * 1024
FULL_VMEM_BYTES = 62 * 1024 * 1024
F32 = jnp.float32
BF16 = jnp.bfloat16
LINK = jnp.bfloat16


def product(first, second):
    return first * second


def one_hot(rows, cols, column_of):
    row = lax.broadcasted_iota(jnp.int32, (rows, cols), 0)
    col = lax.broadcasted_iota(jnp.int32, (rows, cols), 1)
    return (col == column_of(row)).astype(F32).astype(BF16)


def pack_kernel(shards, chans, owned, *refs):
    hbm_refs, send_ref, held, packed, in_sems, out_sems = refs[:4], *refs[4:]
    tok_rows, width = held.shape[1:]
    groups = width // FILTERS
    per_chan = FILTERS // chans
    units = [(which, first) for which in range(2) for first in range(0, groups, 2)]

    def arrival(i, first):
        place = (slice(None), pl.ds(first * FILTERS, 2 * FILTERS))
        return pltpu.make_async_copy(
            hbm_refs[i].at[place], held.at[(i, *place)], in_sems.at[i, first // 2]
        )

    def departure(which, first):
        if owned % SUBLANES:
            place = (which, pl.ds(first, 2))
        else:
            place = (slice(None), pl.ds((which * groups + first) * owned, 2 * owned))
        return pltpu.make_async_copy(
            packed.at[place], send_ref.at[place], out_sems.at[which, first // 2]
        )

    for which, first in units:
        for i in (2 * which, 2 * which + 1):
            arrival(i, first).start()

    def owned_filter(row):
        seq = row // (chans * owned)
        chan = row // owned % chans
        return chan * per_chan + seq * owned + row % owned

    order = one_hot(FILTERS, FILTERS, owned_filter)
    for which, first in units:
        for i in (2 * which, 2 * which + 1):
            arrival(i, first).wait()
        pieces = []
        for group in (first, first + 1):
            cols = slice(group * FILTERS, (group + 1) * FILTERS)
            piece = lax.dot_general(
                order,
                product(held[2 * which, :, cols], held[2 * which + 1, :, cols]),
                (((1,), (1,)), ((), ())),
                preferred_element_type=F32,
            )
            if owned % SUBLANES:
                packed[which, group] = piece.astype(BF16)
            else:
                pieces.append(piece.reshape(shards * chans, owned, tok_rows))
        if pieces:
            row = (which * groups + first) * owned
            packed[:, row : row + 2 * owned, :] = jnp.concatenate(pieces, axis=1).astype(BF16)
        departure(which, first).start()
    for which, first in units:
        departure(which, first).wait()


def pack_signals(shards, chans, owned, query_proj, key_proj, value_proj, out_grad):
    tok_rows, width = key_proj.shape
    groups = width // FILTERS
    dests = shards * chans
    if owned % SUBLANES:
        shape = (2, groups, FILTERS, tok_rows)
    else:
        shape = (dests, 2 * groups * owned, tok_rows)
    send = pl.pallas_call(
        functools.partial(pack_kernel, shards, chans, owned),
        in_specs=[pl.BlockSpec(memory_space=pl.ANY)] * 4,
        out_specs=pl.BlockSpec(memory_space=pl.ANY),
        out_shape=jax.ShapeDtypeStruct(shape, BF16),
        scratch_shapes=[
            pltpu.VMEM((4, tok_rows, width), BF16),
            pltpu.VMEM(shape, BF16),
            pltpu.SemaphoreType.DMA((4, groups // 2)),
            pltpu.SemaphoreType.DMA((2, groups // 2)),
        ],
        compiler_params=pltpu.CompilerParams(vmem_limit_bytes=FULL_VMEM_BYTES),
        name="pack_signals",
    )(key_proj, value_proj, out_grad, query_proj)
    if owned % SUBLANES:
        send = send.reshape(2, groups, dests, owned, tok_rows)
        send = send.transpose(2, 0, 1, 3, 4).reshape(dests, 2 * groups * owned, tok_rows)
    return send


def tile_rows(tok_rows, tile):
    first = tile * (tok_rows + GAP)
    return slice(first, first + tok_rows)


def token_shape(tok_rows, tiles):
    return (tiles * (tok_rows + GAP), LANES)


def token_place(t, tok_rows, tiles):
    return (pl.ds(t, tiles, stride=tok_rows + GAP), slice(None))


def spread_tokens(a_ref, b_ref, x_ref):
    tok_rows, width = a_ref.shape
    for tile in range(width // LANES):
        cols = slice(tile * LANES, (tile + 1) * LANES)
        x_ref[tile_rows(tok_rows, tile), :] = product(a_ref[:, cols], b_ref[:, cols]).astype(F32)


def walk_tokens(ref, coef_ref, tok_rows, tiles, start, move):
    modes = coef_ref.shape[1]
    decay = [coef_ref[0, m] for m in range(modes)]
    weight = [coef_ref[2, m] for m in range(modes)]

    def step(t, held):
        place = token_place(start + move * t, tok_rows, tiles)
        x = ref[place]
        held = tuple(decay[m] * held[m] + x for m in range(modes))
        ref[place] = tree_sum([weight[m] * held[m] for m in range(modes)])
        return held

    zero = tuple(jnp.zeros((tiles, LANES), F32) for _ in range(modes))
    return lax.fori_loop(0, tok_rows, step, zero, unroll=8)


def tree_sum(terms):
    while len(terms) > 1:
        terms = [sum(terms[i : i + 2][1:], terms[i]) for i in range(0, len(terms), 2)]
    return terms[0]


def state_kernel(q_ref, k_ref, v_ref, o_ref, coef_ref, own_ref, sent_ref, x_ref, g_ref):
    tok_rows, width = k_ref.shape
    tiles = width // LANES
    modes = coef_ref.shape[1]
    spread_tokens(k_ref, v_ref, x_ref)
    spread_tokens(o_ref, q_ref, g_ref)
    decay = [coef_ref[0, m] for m in range(modes)]

    def step(t, carry):
        x = x_ref[token_place(t, tok_rows, tiles)]
        g = g_ref[token_place(tok_rows - 1 - t, tok_rows, tiles)]
        ahead = tuple(decay[m] * carry[0][m] + x for m in range(modes))
        behind = tuple(decay[m] * carry[1][m] + g for m in range(modes))
        return (ahead, behind)

    zero = tuple(jnp.zeros((tiles, LANES), F32) for _ in range(modes))
    for side, held in enumerate(lax.fori_loop(0, tok_rows, step, (zero, zero), unroll=8)):
        held = jnp.concatenate(held, axis=0)
        own_ref[side] = held
        sent_ref[side] = held.astype(LINK)


def block_states(query_proj, key_proj, value_proj, out_grad, coefs):
    tok_rows, width = key_proj.shape
    modes, tiles = coefs.shape[1:3]
    return pl.pallas_call(
        state_kernel,
        out_shape=[
            jax.ShapeDtypeStruct((2, modes * tiles, LANES), F32),
            jax.ShapeDtypeStruct((2, modes * tiles, LANES), LINK),
        ],
        scratch_shapes=[pltpu.VMEM(token_shape(tok_rows, tiles), F32)] * 2,
        compiler_params=pltpu.CompilerParams(vmem_limit_bytes=VMEM_BYTES),
        name="block_states",
    )(query_proj, key_proj, value_proj, out_grad, coefs)


def pair_kernel(seq_ref, coef_ref, own_ref, near_ref, *state_refs):
    pairs = len(state_refs) + 1
    modes, tiles = coef_ref.shape[1:3]
    pair = seq_ref[0] // 2
    second = seq_ref[0] % 2 == 1
    ahead, behind = [], []
    for m in range(modes):
        rows = slice(m * tiles, (m + 1) * tiles)
        decay = coef_ref[1, m]
        own, near = own_ref[0, rows], near_ref[0].astype(F32)[rows]
        ahead.append(jnp.where(second, own + decay * near, near + decay * own))
        own, near = own_ref[1, rows], near_ref[1].astype(F32)[rows]
        behind.append(jnp.where(second, near + decay * own, own + decay * near))
    ahead = jnp.concatenate(ahead, axis=0)
    behind = jnp.concatenate(behind, axis=0)
    for k in range(1, pairs):
        state_refs[k - 1][...] = jnp.where(pair + k < pairs, ahead, behind).astype(LINK)


def pair_states(seq_index, pairs, coefs, own, near):
    whole = pl.BlockSpec(memory_space=pltpu.VMEM)
    return pl.pallas_call(
        pair_kernel,
        in_specs=[pl.BlockSpec(memory_space=pltpu.SMEM)] + [whole] * 3,
        out_specs=[whole] * (pairs - 1),
        out_shape=[jax.ShapeDtypeStruct(own.shape[1:], LINK)] * (pairs - 1),
        compiler_params=pltpu.CompilerParams(vmem_limit_bytes=VMEM_BYTES),
        name="pair_states",
    )(seq_index, coefs, own, near)


def sum_pairs(side, seq, coef_ref, near_ref, state_refs):
    pairs = len(state_refs) + 1
    modes, tiles = coef_ref.shape[1:3]
    pair, count = seq // 2, (seq // 2, pairs - 1 - seq // 2)[side]
    beside = seq % 2 == 1 - side
    held = []
    for m in range(modes):
        rows = slice(m * tiles, (m + 1) * tiles)
        decay = coef_ref[1, m]
        total = jnp.zeros((tiles, LANES), F32)
        for k in range(pairs - 1, 0, -1):
            state_ref = state_refs[k - 1 if side == 0 else pairs - k - 1]
            block = state_ref[...].astype(F32)[rows]
            total = decay * decay * total + jnp.where(k <= count, block, 0.0)
        near = near_ref[side].astype(F32)[rows]
        held.append(jnp.where(beside, decay * total + near, total))
    return held


def local_kernel(
    q_ref, k_ref, v_ref, o_ref, coef_ref, gain_ref, conv_ref, grad_ref, done_ref, x_ref, g_ref
):
    tok_rows, width = k_ref.shape
    tiles = width // LANES
    spread_tokens(k_ref, v_ref, x_ref)
    spread_tokens(o_ref, q_ref, g_ref)
    walk_tokens(x_ref, coef_ref, tok_rows, tiles, 0, 1)
    walk_tokens(g_ref, coef_ref, tok_rows, tiles, tok_rows - 1, -1)
    for tile in range(tiles):
        cols = slice(tile * LANES, (tile + 1) * LANES)
        rows = tile_rows(tok_rows, tile)
        gain = gain_ref[:, cols]
        conv_in = product(k_ref[:, cols], v_ref[:, cols]).astype(F32)
        conv_ref[:, cols] = x_ref[rows, :] + gain * conv_in
        mid_grad = product(o_ref[:, cols], q_ref[:, cols]).astype(F32)
        grad_ref[:, cols] = g_ref[rows, :] + gain * mid_grad
    done_ref[...] = jnp.zeros(done_ref.shape, F32)


def local_parts(query_proj, key_proj, value_proj, out_grad, coefs, gain):
    tok_rows, width = key_proj.shape
    tiles = coefs.shape[2]
    return pl.pallas_call(
        local_kernel,
        out_shape=[jax.ShapeDtypeStruct((tok_rows, width), F32)] * 2
        + [jax.ShapeDtypeStruct((SUBLANES, LANES), F32)],
        scratch_shapes=[pltpu.VMEM(token_shape(tok_rows, tiles), F32)] * 2,
        compiler_params=pltpu.CompilerParams(vmem_limit_bytes=VMEM_BYTES),
        name="local_parts",
    )(query_proj, key_proj, value_proj, out_grad, coefs, gain)


def along_column(state, pairs, k):
    route = [(2 * p + b, 2 * ((p + k) % pairs) + b) for p in range(pairs) for b in range(2)]
    return lax.ppermute(state, "seq", route)


def inside_pair(state, pairs):
    return lax.ppermute(state, "seq", [(i, i ^ 1) for i in range(2 * pairs)])


def fill_edge(ref, held, coef_ref, tok_rows, tiles, start, move):
    modes = coef_ref.shape[1]
    decay = [coef_ref[0, m] for m in range(modes)]

    def step(t, held):
        held = tuple(decay[m] * held[m] for m in range(modes))
        ref[token_place(start + move * t, tok_rows, tiles)] = tree_sum(list(held))
        return held

    held = tuple(coef_ref[2, m] * held[m] for m in range(modes))
    lax.fori_loop(0, tok_rows, step, held, unroll=8)


def edge_kernel(seq_ref, coef_ref, near_ref, *refs):
    state_refs, edge_ref = refs[:-1], refs[-1]
    fill_side(0, edge_ref, seq_ref, coef_ref, near_ref, state_refs)


def fill_side(side, edge_ref, seq_ref, coef_ref, near_ref, state_refs):
    tiles = coef_ref.shape[2]
    tok_rows = edge_ref.shape[0] // tiles - GAP
    held = sum_pairs(side, seq_ref[0], coef_ref, near_ref, state_refs)
    start, move = ((0, 1), (tok_rows - 1, -1))[side]
    fill_edge(edge_ref, held, coef_ref, tok_rows, tiles, start, move)


def edge_terms(tok_rows, seq_index, coefs, near, states):
    whole = pl.BlockSpec(memory_space=pltpu.VMEM)
    return pl.pallas_call(
        edge_kernel,
        in_specs=[pl.BlockSpec(memory_space=pltpu.SMEM)] + [whole] * (2 + len(states)),
        out_shape=jax.ShapeDtypeStruct(token_shape(tok_rows, coefs.shape[2]), F32),
        compiler_params=pltpu.CompilerParams(vmem_limit_bytes=VMEM_BYTES),
        name="edge_terms",
    )(seq_index, coefs, near, *states)


def multiply_out(part_ref, edge_ref, factor_refs, out_refs, hbm_refs, sems):
    tok_rows, width = part_ref.shape
    copies = []
    for tile in range(width // LANES):
        cols = slice(tile * LANES, (tile + 1) * LANES)
        value = part_ref[:, cols] + edge_ref[tile_rows(tok_rows, tile), :]
        for i, (factor_ref, out_ref, hbm_ref) in enumerate(zip(factor_refs, out_refs, hbm_refs)):
            out_ref[:, cols] = (value * factor_ref[:, cols].astype(F32)).astype(BF16)
            place = (slice(None), pl.ds(tile * LANES, LANES))
            copies.append(
                pltpu.make_async_copy(out_ref.at[place], hbm_ref.at[place], sems.at[i, tile])
            )
            copies[-1].start()
    return copies


def conv_kernel(seq_ref, part_ref, edge_ref, q_ref, coef_ref, near_ref, *refs):
    state_refs, (layer_hbm, next_ref, layer_ref, sems) = refs[:-4], refs[-4:]
    copies = multiply_out(part_ref, edge_ref, [q_ref], [layer_ref], [layer_hbm], sems)
    fill_side(1, next_ref, seq_ref, coef_ref, near_ref, state_refs)
    for copy in copies:
        copy.wait()


def conv_outputs(seq_index, part, edge, query_proj, coefs, near, states):
    tok_rows, width = part.shape
    whole = pl.BlockSpec(memory_space=pltpu.VMEM)
    return pl.pallas_call(
        conv_kernel,
        in_specs=[pl.BlockSpec(memory_space=pltpu.SMEM)] + [whole] * (5 + len(states)),
        out_specs=[pl.BlockSpec(memory_space=pl.ANY), whole],
        out_shape=[
            jax.ShapeDtypeStruct((tok_rows, width), BF16),
            jax.ShapeDtypeStruct(edge.shape, F32),
        ],
        scratch_shapes=[
            pltpu.VMEM((tok_rows, width), BF16),
            pltpu.SemaphoreType.DMA((1, width // LANES)),
        ],
        compiler_params=pltpu.CompilerParams(vmem_limit_bytes=VMEM_BYTES),
        name="conv_outputs",
    )(seq_index, part, edge, query_proj, coefs, near, *states)


def grad_kernel(
    part_ref, edge_ref, v_ref, k_ref, key_hbm, value_hbm, key_ref, value_ref, sems
):
    copies = multiply_out(
        part_ref, edge_ref, [v_ref, k_ref], [key_ref, value_ref], [key_hbm, value_hbm], sems
    )
    for copy in copies:
        copy.wait()


def grad_outputs(part, edge, value_proj, key_proj):
    tok_rows, width = part.shape
    return pl.pallas_call(
        grad_kernel,
        in_specs=[pl.BlockSpec(memory_space=pltpu.VMEM)] * 4,
        out_specs=[pl.BlockSpec(memory_space=pl.ANY)] * 2,
        out_shape=[jax.ShapeDtypeStruct((tok_rows, width), BF16)] * 2,
        scratch_shapes=[pltpu.VMEM((tok_rows, width), BF16)] * 2
        + [pltpu.SemaphoreType.DMA((2, width // LANES))],
        compiler_params=pltpu.CompilerParams(vmem_limit_bytes=VMEM_BYTES),
        name="grad_outputs",
    )(part, edge, value_proj, key_proj)


def lag_kernel(shards, chans, groups, owned, *refs):
    in_refs, (out_ref, lag_sums, u_all, g_all, turned_all) = refs[1:-5], refs[-5:]
    halves = out_ref.shape[1] // owned
    tok_rows = halves * LANES
    blocks = shards * halves
    depth = chans * groups
    full = blocks * depth
    if len(in_refs) == 1:
        take = chans * groups * owned

        def by_filter(row):
            return row % depth * owned + row // depth

        order = one_hot(take, take, by_filter)
        for which, kept in enumerate((u_all, g_all)):
            rows = slice(which * groups * owned, (which + 1) * groups * owned)
            for s in range(shards):
                piece = in_refs[0][s * chans : (s + 1) * chans, rows, :].reshape(take, tok_rows)
                piece = jnp.dot(order, piece, preferred_element_type=F32).astype(BF16)
                piece = piece.reshape(owned, depth, tok_rows)
                for h in range(halves):
                    first = (s * halves + h) * depth
                    kept[:, first : first + depth, :] = piece[:, :, h * LANES : (h + 1) * LANES]
    else:
        u_all[...] = in_refs[0][...]
        g_all[:, :full, :] = in_refs[1][...]
    g_all[:, full:, :] = jnp.zeros((owned, g_all.shape[1] - full, LANES), BF16)
    mirror = one_hot(LANES, LANES, lambda row: LANES - 1 - row)
    row = lax.broadcasted_iota(jnp.int32, (LANES, LANES), 0)
    col = lax.broadcasted_iota(jnp.int32, (LANES, LANES), 1)
    same_block = row + col >= LANES - 1
    filter_row = lax.broadcasted_iota(jnp.int32, (owned, LANES), 0)
    batch = min(blocks, 16)

    def one_filter(f, _):
        turned = turned_all[f]

        def some_lags(first):
            tables = []
            for d in range(0, batch, 2):
                live = full
                if batch == blocks:
                    live = min(full, -(-(blocks - d) * depth // LANES) * LANES)
                pair = jnp.concatenate(
                    [
                        g_all[f, pl.ds(pl.multiple_of((first + d + e) * depth, depth), live), :]
                        for e in range(2)
                    ],
                    axis=1,
                )
                table = jnp.dot(turned[:, :live], pair, preferred_element_type=F32)
                tables += [table[:, :LANES], table[:, LANES:]]
            last = g_all[f, pl.ds(pl.multiple_of((first + batch) * depth, depth), full), :]
            if batch < blocks:
                tables.append(jnp.dot(turned, last, preferred_element_type=F32))
            else:
                tables.append(jnp.zeros((LANES, LANES), F32))
            for d in range(batch):
                joined = jnp.where(same_block, tables[d], tables[d + 1])
                skewed = pltpu.roll(joined, 1, 1, stride=1, stride_axis=0)
                sums = jnp.sum(skewed, axis=0, keepdims=True)
                row = d % halves * owned
                place = ((first + d) // halves, slice(row, row + owned), slice(None))
                lag_sums[place] = jnp.where(filter_row == f, sums, lag_sums[place])

        if batch == blocks:
            some_lags(0)
        else:
            lax.fori_loop(0, blocks // batch, lambda i, c: (some_lags(i * batch), c)[1], 0)
        return 0

    for f in range(owned):
        turned_all[f] = lax.dot_general(
            mirror, u_all[f], (((1,), (1,)), ((), ())), preferred_element_type=F32
        ).astype(BF16)
    lax.fori_loop(0, owned, one_filter, 0, unroll=min(owned, 8))
    out_ref[...] = lag_sums[...].astype(LINK)


def filter_lags(received, done, shards, chans, owned):
    tok_rows = received.shape[2]
    groups = received.shape[1] // (2 * owned)
    halves = tok_rows // LANES
    depth = chans * groups
    full = shards * halves * depth
    args = (received,)
    if owned % SUBLANES:
        split = received.reshape(shards, chans, 2, groups, owned, halves, LANES)
        split = split.transpose(2, 4, 0, 5, 1, 3, 6).reshape(2, owned, full, LANES)
        args = (split[0], split[1])
    whole = pl.BlockSpec(memory_space=pltpu.VMEM)
    return pl.pallas_call(
        functools.partial(lag_kernel, shards, chans, groups, owned),
        in_specs=[pl.BlockSpec(memory_space=pl.ANY)] + [whole] * len(args),
        out_specs=whole,
        out_shape=jax.ShapeDtypeStruct((shards, halves * owned, LANES), LINK),
        scratch_shapes=[
            pltpu.VMEM((shards, halves * owned, LANES), F32),
            pltpu.VMEM((owned, full, LANES), BF16),
            pltpu.VMEM((owned, 2 * full + depth, LANES), BF16),
            pltpu.VMEM((owned, LANES, full), BF16),
        ],
        compiler_params=pltpu.CompilerParams(vmem_limit_bytes=VMEM_BYTES),
        name="filter_lags",
    )(done, *args)


def per_device(query_proj, key_proj, value_proj, out_grad, residues, decay_rate, skip_gain):
    tok_rows, width = key_proj.shape
    shards = lax.axis_size("seq")
    chans = lax.axis_size("chan")
    length = shards * tok_rows
    owned = FILTERS // (shards * chans)
    modes = residues.shape[1]
    signals = (query_proj, key_proj, value_proj, out_grad)

    send = pack_signals(shards, chans, owned, *signals)
    send, *signals, residues, decay_rate = lax.optimization_barrier(
        (send, *signals, residues, decay_rate)
    )
    received = lax.all_to_all(send, ("seq", "chan"), split_axis=0, concat_axis=0, tiled=True)

    coefs = jnp.stack(
        [
            jnp.exp(-decay_rate),
            jnp.exp(-(decay_rate * float(tok_rows))),
            residues * jnp.sqrt(decay_rate),
        ]
    )
    coefs = coefs.transpose(0, 2, 1).reshape(3, modes, 1, FILTERS // LANES, LANES)
    coefs = jnp.broadcast_to(coefs, (3, modes, width // FILTERS, FILTERS // LANES, LANES))
    coefs = coefs.reshape(3, modes, width // LANES, LANES)
    seq_index = lax.axis_index("seq").reshape(1)
    pairs = shards // 2
    own, sent = block_states(*signals, coefs)
    conv_part, grad_part, done = local_parts(*signals, coefs, skip_gain[None, :])
    sent, done = lax.optimization_barrier((sent, done))
    near = inside_pair(sent, pairs)
    states = pair_states(seq_index, pairs, coefs, own, near)
    states = [along_column(state, pairs, 1 + i) for i, state in enumerate(states)]

    scale = 1.0 / math.sqrt(length * (CHANNELS // FILTERS))
    lags = filter_lags(received, done, shards, chans, owned)
    lags, *states = lax.optimization_barrier((lags, *states))
    lags = lax.all_to_all(lags, "seq", split_axis=0, concat_axis=0, tiled=True)
    lags = lags.reshape(shards, tok_rows // LANES, owned, LANES).transpose(0, 2, 1, 3)
    filter_grad = lags.reshape(shards * owned, tok_rows).T.astype(F32) * scale
    query_proj, key_proj, value_proj, _ = signals
    edge = edge_terms(tok_rows, seq_index, coefs, near, states)
    layer_out, edge = conv_outputs(seq_index, conv_part, edge, query_proj, coefs, near, states)
    key_grad, value_grad = grad_outputs(grad_part, edge, value_proj, key_proj)
    return (layer_out, key_grad, value_grad, filter_grad)


def solution(mesh):
    split = P("seq", "chan")
    return jax.shard_map(
        per_device,
        mesh=mesh,
        in_specs=(split, split, split, split, P(), P(), P("chan")),
        out_specs=(split, split, split, split),
        check_vma=False,
    )
```

```python
import functools
import math

import jax
import jax.numpy as jnp
from jax import lax
from jax.experimental import pallas as pl
from jax.experimental.pallas import tpu as pltpu
from jax.sharding import PartitionSpec as P

CHANNELS = 4096
FILTERS = 256
LANES = 128
SUBLANES = 8
GAP = 8
VMEM_BYTES = 16 * 1024 * 1024
FULL_VMEM_BYTES = 62 * 1024 * 1024
F32 = jnp.float32
BF16 = jnp.bfloat16
LINK = jnp.bfloat16


def product(first, second):
    return first * second


def one_hot(rows, cols, column_of):
    row = lax.broadcasted_iota(jnp.int32, (rows, cols), 0)
    col = lax.broadcasted_iota(jnp.int32, (rows, cols), 1)
    return (col == column_of(row)).astype(F32).astype(BF16)


def pack_kernel(shards, chans, owned, *refs):
    hbm_refs, send_ref, held, packed, in_sems, out_sems = refs[:4], *refs[4:]
    tok_rows, width = held.shape[1:]
    groups = width // FILTERS
    per_chan = FILTERS // chans
    units = [(which, first) for which in range(2) for first in range(0, groups, 2)]

    def arrival(i, first):
        place = (slice(None), pl.ds(first * FILTERS, 2 * FILTERS))
        return pltpu.make_async_copy(
            hbm_refs[i].at[place], held.at[(i, *place)], in_sems.at[i, first // 2]
        )

    def departure(which, first):
        if owned % SUBLANES:
            place = (which, pl.ds(first, 2))
        else:
            place = (slice(None), pl.ds((which * groups + first) * owned, 2 * owned))
        return pltpu.make_async_copy(
            packed.at[place], send_ref.at[place], out_sems.at[which, first // 2]
        )

    for which, first in units:
        for i in (2 * which, 2 * which + 1):
            arrival(i, first).start()

    def owned_filter(row):
        seq = row // (chans * owned)
        chan = row // owned % chans
        return chan * per_chan + seq * owned + row % owned

    order = one_hot(FILTERS, FILTERS, owned_filter)
    for which, first in units:
        for i in (2 * which, 2 * which + 1):
            arrival(i, first).wait()
        pieces = []
        for group in (first, first + 1):
            cols = slice(group * FILTERS, (group + 1) * FILTERS)
            piece = lax.dot_general(
                order,
                product(held[2 * which, :, cols], held[2 * which + 1, :, cols]),
                (((1,), (1,)), ((), ())),
                preferred_element_type=F32,
            )
            if owned % SUBLANES:
                packed[which, group] = piece.astype(BF16)
            else:
                pieces.append(piece.reshape(shards * chans, owned, tok_rows))
        if pieces:
            row = (which * groups + first) * owned
            packed[:, row : row + 2 * owned, :] = jnp.concatenate(pieces, axis=1).astype(BF16)
        departure(which, first).start()
    for which, first in units:
        departure(which, first).wait()


def pack_signals(shards, chans, owned, query_proj, key_proj, value_proj, out_grad):
    tok_rows, width = key_proj.shape
    groups = width // FILTERS
    dests = shards * chans
    if owned % SUBLANES:
        shape = (2, groups, FILTERS, tok_rows)
    else:
        shape = (dests, 2 * groups * owned, tok_rows)
    send = pl.pallas_call(
        functools.partial(pack_kernel, shards, chans, owned),
        in_specs=[pl.BlockSpec(memory_space=pl.ANY)] * 4,
        out_specs=pl.BlockSpec(memory_space=pl.ANY),
        out_shape=jax.ShapeDtypeStruct(shape, BF16),
        scratch_shapes=[
            pltpu.VMEM((4, tok_rows, width), BF16),
            pltpu.VMEM(shape, BF16),
            pltpu.SemaphoreType.DMA((4, groups // 2)),
            pltpu.SemaphoreType.DMA((2, groups // 2)),
        ],
        compiler_params=pltpu.CompilerParams(vmem_limit_bytes=FULL_VMEM_BYTES),
        name="pack_signals",
    )(key_proj, value_proj, out_grad, query_proj)
    if owned % SUBLANES:
        send = send.reshape(2, groups, dests, owned, tok_rows)
        send = send.transpose(2, 0, 1, 3, 4).reshape(dests, 2 * groups * owned, tok_rows)
    return send


def tile_rows(tok_rows, tile):
    first = tile * (tok_rows + GAP)
    return slice(first, first + tok_rows)


def token_shape(tok_rows, tiles):
    return (tiles * (tok_rows + GAP), LANES)


def token_place(t, tok_rows, tiles):
    return (pl.ds(t, tiles, stride=tok_rows + GAP), slice(None))


def spread_tokens(a_ref, b_ref, x_ref):
    tok_rows, width = a_ref.shape
    for tile in range(width // LANES):
        cols = slice(tile * LANES, (tile + 1) * LANES)
        x_ref[tile_rows(tok_rows, tile), :] = product(a_ref[:, cols], b_ref[:, cols]).astype(F32)


def walk_tokens(ref, coef_ref, tok_rows, tiles, start, move):
    modes = coef_ref.shape[1]
    decay = [coef_ref[0, m] for m in range(modes)]
    weight = [coef_ref[2, m] for m in range(modes)]

    def step(t, held):
        place = token_place(start + move * t, tok_rows, tiles)
        x = ref[place]
        held = tuple(decay[m] * held[m] + x for m in range(modes))
        ref[place] = tree_sum([weight[m] * held[m] for m in range(modes)])
        return held

    zero = tuple(jnp.zeros((tiles, LANES), F32) for _ in range(modes))
    return lax.fori_loop(0, tok_rows, step, zero, unroll=8)


def tree_sum(terms):
    while len(terms) > 1:
        terms = [sum(terms[i : i + 2][1:], terms[i]) for i in range(0, len(terms), 2)]
    return terms[0]


def state_kernel(q_ref, k_ref, v_ref, o_ref, coef_ref, own_ref, sent_ref, x_ref, g_ref):
    tok_rows, width = k_ref.shape
    tiles = width // LANES
    modes = coef_ref.shape[1]
    spread_tokens(k_ref, v_ref, x_ref)
    spread_tokens(o_ref, q_ref, g_ref)
    decay = [coef_ref[0, m] for m in range(modes)]

    def step(t, carry):
        x = x_ref[token_place(t, tok_rows, tiles)]
        g = g_ref[token_place(tok_rows - 1 - t, tok_rows, tiles)]
        ahead = tuple(decay[m] * carry[0][m] + x for m in range(modes))
        behind = tuple(decay[m] * carry[1][m] + g for m in range(modes))
        return (ahead, behind)

    zero = tuple(jnp.zeros((tiles, LANES), F32) for _ in range(modes))
    for side, held in enumerate(lax.fori_loop(0, tok_rows, step, (zero, zero), unroll=8)):
        held = jnp.concatenate(held, axis=0)
        own_ref[side] = held
        sent_ref[side] = held.astype(LINK)


def block_states(query_proj, key_proj, value_proj, out_grad, coefs):
    tok_rows, width = key_proj.shape
    modes, tiles = coefs.shape[1:3]
    return pl.pallas_call(
        state_kernel,
        out_shape=[
            jax.ShapeDtypeStruct((2, modes * tiles, LANES), F32),
            jax.ShapeDtypeStruct((2, modes * tiles, LANES), LINK),
        ],
        scratch_shapes=[pltpu.VMEM(token_shape(tok_rows, tiles), F32)] * 2,
        compiler_params=pltpu.CompilerParams(vmem_limit_bytes=VMEM_BYTES),
        name="block_states",
    )(query_proj, key_proj, value_proj, out_grad, coefs)


def pair_kernel(seq_ref, coef_ref, own_ref, near_ref, *state_refs):
    pairs = len(state_refs) + 1
    modes, tiles = coef_ref.shape[1:3]
    pair = seq_ref[0] // 2
    second = seq_ref[0] % 2 == 1
    ahead, behind = [], []
    for m in range(modes):
        rows = slice(m * tiles, (m + 1) * tiles)
        decay = coef_ref[1, m]
        own, near = own_ref[0, rows], near_ref[0].astype(F32)[rows]
        ahead.append(jnp.where(second, own + decay * near, near + decay * own))
        own, near = own_ref[1, rows], near_ref[1].astype(F32)[rows]
        behind.append(jnp.where(second, near + decay * own, own + decay * near))
    ahead = jnp.concatenate(ahead, axis=0)
    behind = jnp.concatenate(behind, axis=0)
    for k in range(1, pairs):
        state_refs[k - 1][...] = jnp.where(pair + k < pairs, ahead, behind).astype(LINK)


def pair_states(seq_index, pairs, coefs, own, near):
    whole = pl.BlockSpec(memory_space=pltpu.VMEM)
    return pl.pallas_call(
        pair_kernel,
        in_specs=[pl.BlockSpec(memory_space=pltpu.SMEM)] + [whole] * 3,
        out_specs=[whole] * (pairs - 1),
        out_shape=[jax.ShapeDtypeStruct(own.shape[1:], LINK)] * (pairs - 1),
        compiler_params=pltpu.CompilerParams(vmem_limit_bytes=VMEM_BYTES),
        name="pair_states",
    )(seq_index, coefs, own, near)


def sum_pairs(side, seq, coef_ref, near_ref, state_refs):
    pairs = len(state_refs) + 1
    modes, tiles = coef_ref.shape[1:3]
    pair, count = seq // 2, (seq // 2, pairs - 1 - seq // 2)[side]
    beside = seq % 2 == 1 - side
    held = []
    for m in range(modes):
        rows = slice(m * tiles, (m + 1) * tiles)
        decay = coef_ref[1, m]
        total = jnp.zeros((tiles, LANES), F32)
        for k in range(pairs - 1, 0, -1):
            state_ref = state_refs[k - 1 if side == 0 else pairs - k - 1]
            block = state_ref[...].astype(F32)[rows]
            total = decay * decay * total + jnp.where(k <= count, block, 0.0)
        near = near_ref[side].astype(F32)[rows]
        held.append(jnp.where(beside, decay * total + near, total))
    return held


def local_kernel(
    q_ref, k_ref, v_ref, o_ref, coef_ref, gain_ref, conv_ref, grad_ref, done_ref, x_ref, g_ref
):
    tok_rows, width = k_ref.shape
    tiles = width // LANES
    spread_tokens(k_ref, v_ref, x_ref)
    spread_tokens(o_ref, q_ref, g_ref)
    walk_tokens(x_ref, coef_ref, tok_rows, tiles, 0, 1)
    walk_tokens(g_ref, coef_ref, tok_rows, tiles, tok_rows - 1, -1)
    for tile in range(tiles):
        cols = slice(tile * LANES, (tile + 1) * LANES)
        rows = tile_rows(tok_rows, tile)
        gain = gain_ref[:, cols]
        conv_in = product(k_ref[:, cols], v_ref[:, cols]).astype(F32)
        conv_ref[:, cols] = x_ref[rows, :] + gain * conv_in
        mid_grad = product(o_ref[:, cols], q_ref[:, cols]).astype(F32)
        grad_ref[:, cols] = g_ref[rows, :] + gain * mid_grad
    done_ref[...] = jnp.zeros(done_ref.shape, F32)


def local_parts(query_proj, key_proj, value_proj, out_grad, coefs, gain):
    tok_rows, width = key_proj.shape
    tiles = coefs.shape[2]
    return pl.pallas_call(
        local_kernel,
        out_shape=[jax.ShapeDtypeStruct((tok_rows, width), F32)] * 2
        + [jax.ShapeDtypeStruct((SUBLANES, LANES), F32)],
        scratch_shapes=[pltpu.VMEM(token_shape(tok_rows, tiles), F32)] * 2,
        compiler_params=pltpu.CompilerParams(vmem_limit_bytes=VMEM_BYTES),
        name="local_parts",
    )(query_proj, key_proj, value_proj, out_grad, coefs, gain)


def along_column(state, pairs, k):
    route = [(2 * p + b, 2 * ((p + k) % pairs) + b) for p in range(pairs) for b in range(2)]
    return lax.ppermute(state, "seq", route)


def inside_pair(state, pairs):
    return lax.ppermute(state, "seq", [(i, i ^ 1) for i in range(2 * pairs)])


def fill_edge(ref, held, coef_ref, tok_rows, tiles, start, move):
    modes = coef_ref.shape[1]
    decay = [coef_ref[0, m] for m in range(modes)]

    def step(t, held):
        held = tuple(decay[m] * held[m] for m in range(modes))
        ref[token_place(start + move * t, tok_rows, tiles)] = tree_sum(list(held))
        return held

    held = tuple(coef_ref[2, m] * held[m] for m in range(modes))
    lax.fori_loop(0, tok_rows, step, held, unroll=8)


def edge_kernel(seq_ref, coef_ref, near_ref, *refs):
    state_refs, edge_ref = refs[:-1], refs[-1]
    fill_side(0, edge_ref, seq_ref, coef_ref, near_ref, state_refs)


def fill_side(side, edge_ref, seq_ref, coef_ref, near_ref, state_refs):
    tiles = coef_ref.shape[2]
    tok_rows = edge_ref.shape[0] // tiles - GAP
    held = sum_pairs(side, seq_ref[0], coef_ref, near_ref, state_refs)
    start, move = ((0, 1), (tok_rows - 1, -1))[side]
    fill_edge(edge_ref, held, coef_ref, tok_rows, tiles, start, move)


def edge_terms(tok_rows, seq_index, coefs, near, states):
    whole = pl.BlockSpec(memory_space=pltpu.VMEM)
    return pl.pallas_call(
        edge_kernel,
        in_specs=[pl.BlockSpec(memory_space=pltpu.SMEM)] + [whole] * (2 + len(states)),
        out_shape=jax.ShapeDtypeStruct(token_shape(tok_rows, coefs.shape[2]), F32),
        compiler_params=pltpu.CompilerParams(vmem_limit_bytes=VMEM_BYTES),
        name="edge_terms",
    )(seq_index, coefs, near, *states)


def multiply_out(part_ref, edge_ref, factor_refs, out_refs, hbm_refs, sems):
    tok_rows, width = part_ref.shape
    copies = []
    for tile in range(width // LANES):
        cols = slice(tile * LANES, (tile + 1) * LANES)
        value = part_ref[:, cols] + edge_ref[tile_rows(tok_rows, tile), :]
        for i, (factor_ref, out_ref, hbm_ref) in enumerate(zip(factor_refs, out_refs, hbm_refs)):
            out_ref[:, cols] = (value * factor_ref[:, cols].astype(F32)).astype(BF16)
            place = (slice(None), pl.ds(tile * LANES, LANES))
            copies.append(
                pltpu.make_async_copy(out_ref.at[place], hbm_ref.at[place], sems.at[i, tile])
            )
            copies[-1].start()
    return copies


def conv_kernel(seq_ref, part_ref, edge_ref, q_ref, coef_ref, near_ref, *refs):
    state_refs, (layer_hbm, next_ref, layer_ref, sems) = refs[:-4], refs[-4:]
    copies = multiply_out(part_ref, edge_ref, [q_ref], [layer_ref], [layer_hbm], sems)
    fill_side(1, next_ref, seq_ref, coef_ref, near_ref, state_refs)
    for copy in copies:
        copy.wait()


def conv_outputs(seq_index, part, edge, query_proj, coefs, near, states):
    tok_rows, width = part.shape
    whole = pl.BlockSpec(memory_space=pltpu.VMEM)
    return pl.pallas_call(
        conv_kernel,
        in_specs=[pl.BlockSpec(memory_space=pltpu.SMEM)] + [whole] * (5 + len(states)),
        out_specs=[pl.BlockSpec(memory_space=pl.ANY), whole],
        out_shape=[
            jax.ShapeDtypeStruct((tok_rows, width), BF16),
            jax.ShapeDtypeStruct(edge.shape, F32),
        ],
        scratch_shapes=[
            pltpu.VMEM((tok_rows, width), BF16),
            pltpu.SemaphoreType.DMA((1, width // LANES)),
        ],
        compiler_params=pltpu.CompilerParams(vmem_limit_bytes=VMEM_BYTES),
        name="conv_outputs",
    )(seq_index, part, edge, query_proj, coefs, near, *states)


def grad_kernel(
    part_ref, edge_ref, v_ref, k_ref, key_hbm, value_hbm, key_ref, value_ref, sems
):
    copies = multiply_out(
        part_ref, edge_ref, [v_ref, k_ref], [key_ref, value_ref], [key_hbm, value_hbm], sems
    )
    for copy in copies:
        copy.wait()


def grad_outputs(part, edge, value_proj, key_proj):
    tok_rows, width = part.shape
    return pl.pallas_call(
        grad_kernel,
        in_specs=[pl.BlockSpec(memory_space=pltpu.VMEM)] * 4,
        out_specs=[pl.BlockSpec(memory_space=pl.ANY)] * 2,
        out_shape=[jax.ShapeDtypeStruct((tok_rows, width), BF16)] * 2,
        scratch_shapes=[pltpu.VMEM((tok_rows, width), BF16)] * 2
        + [pltpu.SemaphoreType.DMA((2, width // LANES))],
        compiler_params=pltpu.CompilerParams(vmem_limit_bytes=VMEM_BYTES),
        name="grad_outputs",
    )(part, edge, value_proj, key_proj)


def lag_kernel(shards, chans, groups, owned, *refs):
    in_refs, (out_ref, lag_sums, u_all, g_all, turned_all) = refs[1:-5], refs[-5:]
    halves = out_ref.shape[1] // owned
    tok_rows = halves * LANES
    blocks = shards * halves
    depth = chans * groups
    full = blocks * depth
    if len(in_refs) == 1:
        take = chans * groups * owned

        def by_filter(row):
            return row % depth * owned + row // depth

        order = one_hot(take, take, by_filter)
        for which, kept in enumerate((u_all, g_all)):
            rows = slice(which * groups * owned, (which + 1) * groups * owned)
            for s in range(shards):
                piece = in_refs[0][s * chans : (s + 1) * chans, rows, :].reshape(take, tok_rows)
                piece = jnp.dot(order, piece, preferred_element_type=F32).astype(BF16)
                piece = piece.reshape(owned, depth, tok_rows)
                for h in range(halves):
                    first = (s * halves + h) * depth
                    kept[:, first : first + depth, :] = piece[:, :, h * LANES : (h + 1) * LANES]
    else:
        u_all[...] = in_refs[0][...]
        g_all[:, :full, :] = in_refs[1][...]
    g_all[:, full:, :] = jnp.zeros((owned, g_all.shape[1] - full, LANES), BF16)
    mirror = one_hot(LANES, LANES, lambda row: LANES - 1 - row)
    row = lax.broadcasted_iota(jnp.int32, (LANES, LANES), 0)
    col = lax.broadcasted_iota(jnp.int32, (LANES, LANES), 1)
    same_block = row + col >= LANES - 1
    batch = min(blocks, 16)

    def one_filter(f):
        turned = turned_all[f]

        def some_lags(first):
            tables = []
            for d in range(0, batch, 2):
                live = full
                if batch == blocks:
                    live = min(full, -(-(blocks - d) * depth // LANES) * LANES)
                pair = jnp.concatenate(
                    [
                        g_all[f, pl.ds(pl.multiple_of((first + d + e) * depth, depth), live), :]
                        for e in range(2)
                    ],
                    axis=1,
                )
                table = jnp.dot(turned[:, :live], pair, preferred_element_type=F32)
                tables += [table[:, :LANES], table[:, LANES:]]
            last = g_all[f, pl.ds(pl.multiple_of((first + batch) * depth, depth), full), :]
            if batch < blocks:
                tables.append(jnp.dot(turned, last, preferred_element_type=F32))
            else:
                tables.append(jnp.zeros((LANES, LANES), F32))
            for d in range(batch):
                joined = jnp.where(same_block, tables[d], tables[d + 1])
                skewed = pltpu.roll(joined, 1, 1, stride=1, stride_axis=0)
                sums = jnp.sum(skewed, axis=0, keepdims=True)
                row = d % halves * owned + f
                lag_sums[(first + d) // halves, row : row + 1, :] = sums

        if batch == blocks:
            some_lags(0)
        else:
            lax.fori_loop(0, blocks // batch, lambda i, c: (some_lags(i * batch), c)[1], 0)

    for f in range(owned):
        turned_all[f] = lax.dot_general(
            mirror, u_all[f], (((1,), (1,)), ((), ())), preferred_element_type=F32
        ).astype(BF16)
    for f in range(owned):
        one_filter(f)
    out_ref[...] = lag_sums[...].astype(LINK)


def filter_lags(received, done, shards, chans, owned):
    tok_rows = received.shape[2]
    groups = received.shape[1] // (2 * owned)
    halves = tok_rows // LANES
    depth = chans * groups
    full = shards * halves * depth
    args = (received,)
    if owned % SUBLANES:
        split = received.reshape(shards, chans, 2, groups, owned, halves, LANES)
        split = split.transpose(2, 4, 0, 5, 1, 3, 6).reshape(2, owned, full, LANES)
        args = (split[0], split[1])
    whole = pl.BlockSpec(memory_space=pltpu.VMEM)
    return pl.pallas_call(
        functools.partial(lag_kernel, shards, chans, groups, owned),
        in_specs=[pl.BlockSpec(memory_space=pl.ANY)] + [whole] * len(args),
        out_specs=whole,
        out_shape=jax.ShapeDtypeStruct((shards, halves * owned, LANES), LINK),
        scratch_shapes=[
            pltpu.VMEM((shards, halves * owned, LANES), F32),
            pltpu.VMEM((owned, full, LANES), BF16),
            pltpu.VMEM((owned, 2 * full + depth, LANES), BF16),
            pltpu.VMEM((owned, LANES, full), BF16),
        ],
        compiler_params=pltpu.CompilerParams(vmem_limit_bytes=VMEM_BYTES),
        name="filter_lags",
    )(done, *args)


def per_device(query_proj, key_proj, value_proj, out_grad, residues, decay_rate, skip_gain):
    tok_rows, width = key_proj.shape
    shards = lax.axis_size("seq")
    chans = lax.axis_size("chan")
    length = shards * tok_rows
    owned = FILTERS // (shards * chans)
    modes = residues.shape[1]
    signals = (query_proj, key_proj, value_proj, out_grad)

    send = pack_signals(shards, chans, owned, *signals)
    send, *signals, residues, decay_rate = lax.optimization_barrier(
        (send, *signals, residues, decay_rate)
    )
    received = lax.all_to_all(send, ("seq", "chan"), split_axis=0, concat_axis=0, tiled=True)

    coefs = jnp.stack(
        [
            jnp.exp(-decay_rate),
            jnp.exp(-(decay_rate * float(tok_rows))),
            residues * jnp.sqrt(decay_rate),
        ]
    )
    coefs = coefs.transpose(0, 2, 1).reshape(3, modes, 1, FILTERS // LANES, LANES)
    coefs = jnp.broadcast_to(coefs, (3, modes, width // FILTERS, FILTERS // LANES, LANES))
    coefs = coefs.reshape(3, modes, width // LANES, LANES)
    seq_index = lax.axis_index("seq").reshape(1)
    pairs = shards // 2
    own, sent = block_states(*signals, coefs)
    conv_part, grad_part, done = local_parts(*signals, coefs, skip_gain[None, :])
    sent, done = lax.optimization_barrier((sent, done))
    near = inside_pair(sent, pairs)
    states = pair_states(seq_index, pairs, coefs, own, near)
    states = [along_column(state, pairs, 1 + i) for i, state in enumerate(states)]

    scale = 1.0 / math.sqrt(length * (CHANNELS // FILTERS))
    lags = filter_lags(received, done, shards, chans, owned)
    lags, *states = lax.optimization_barrier((lags, *states))
    lags = lax.all_to_all(lags, "seq", split_axis=0, concat_axis=0, tiled=True)
    lags = lags.reshape(shards, tok_rows // LANES, owned, LANES).transpose(0, 2, 1, 3)
    filter_grad = lags.reshape(shards * owned, tok_rows).T.astype(F32) * scale
    query_proj, key_proj, value_proj, _ = signals
    edge = edge_terms(tok_rows, seq_index, coefs, near, states)
    layer_out, edge = conv_outputs(seq_index, conv_part, edge, query_proj, coefs, near, states)
    key_grad, value_grad = grad_outputs(grad_part, edge, value_proj, key_proj)
    return (layer_out, key_grad, value_grad, filter_grad)


def solution(mesh):
    split = P("seq", "chan")
    return jax.shard_map(
        per_device,
        mesh=mesh,
        in_specs=(split, split, split, split, P(), P(), P("chan")),
        out_specs=(split, split, split, split),
        check_vma=False,
    )
```

```python
import functools
import math

import jax
import jax.numpy as jnp
from jax import lax
from jax.experimental import pallas as pl
from jax.experimental.pallas import tpu as pltpu
from jax.sharding import PartitionSpec as P

CHANNELS = 4096
FILTERS = 256
LANES = 128
SUBLANES = 8
GAP = 8
VMEM_BYTES = 16 * 1024 * 1024
FULL_VMEM_BYTES = 62 * 1024 * 1024
F32 = jnp.float32
BF16 = jnp.bfloat16
LINK = jnp.bfloat16


def product(first, second):
    return first * second


def one_hot(rows, cols, column_of):
    row = lax.broadcasted_iota(jnp.int32, (rows, cols), 0)
    col = lax.broadcasted_iota(jnp.int32, (rows, cols), 1)
    return (col == column_of(row)).astype(F32).astype(BF16)


def pack_kernel(shards, chans, owned, *refs):
    hbm_refs, send_ref, held, packed, in_sems, out_sems = refs[:4], *refs[4:]
    tok_rows, width = held.shape[1:]
    groups = width // FILTERS
    per_chan = FILTERS // chans
    units = [(which, first) for which in range(2) for first in range(0, groups, 2)]

    def arrival(i, group):
        place = (slice(None), pl.ds(group * FILTERS, FILTERS))
        return pltpu.make_async_copy(
            hbm_refs[i].at[place], held.at[(i, *place)], in_sems.at[i, group]
        )

    def departure(which, first):
        if owned % SUBLANES:
            place = (which, pl.ds(first, 2))
        else:
            place = (slice(None), pl.ds((which * groups + first) * owned, 2 * owned))
        return pltpu.make_async_copy(
            packed.at[place], send_ref.at[place], out_sems.at[which, first // 2]
        )

    for which in range(2):
        for group in range(groups):
            for i in (2 * which, 2 * which + 1):
                arrival(i, group).start()

    def owned_filter(row):
        seq = row // (chans * owned)
        chan = row // owned % chans
        return chan * per_chan + seq * owned + row % owned

    order = one_hot(FILTERS, FILTERS, owned_filter)
    for which, first in units:
        pieces = []
        for group in (first, first + 1):
            for i in (2 * which, 2 * which + 1):
                arrival(i, group).wait()
            cols = slice(group * FILTERS, (group + 1) * FILTERS)
            piece = lax.dot_general(
                order,
                product(held[2 * which, :, cols], held[2 * which + 1, :, cols]),
                (((1,), (1,)), ((), ())),
                preferred_element_type=F32,
            )
            if owned % SUBLANES:
                packed[which, group] = piece.astype(BF16)
            else:
                pieces.append(piece.reshape(shards * chans, owned, tok_rows))
        if pieces:
            row = (which * groups + first) * owned
            packed[:, row : row + 2 * owned, :] = jnp.concatenate(pieces, axis=1).astype(BF16)
        departure(which, first).start()
    for which, first in units:
        departure(which, first).wait()


def pack_signals(shards, chans, owned, query_proj, key_proj, value_proj, out_grad):
    tok_rows, width = key_proj.shape
    groups = width // FILTERS
    dests = shards * chans
    if owned % SUBLANES:
        shape = (2, groups, FILTERS, tok_rows)
    else:
        shape = (dests, 2 * groups * owned, tok_rows)
    send = pl.pallas_call(
        functools.partial(pack_kernel, shards, chans, owned),
        in_specs=[pl.BlockSpec(memory_space=pl.ANY)] * 4,
        out_specs=pl.BlockSpec(memory_space=pl.ANY),
        out_shape=jax.ShapeDtypeStruct(shape, BF16),
        scratch_shapes=[
            pltpu.VMEM((4, tok_rows, width), BF16),
            pltpu.VMEM(shape, BF16),
            pltpu.SemaphoreType.DMA((4, groups)),
            pltpu.SemaphoreType.DMA((2, groups // 2)),
        ],
        compiler_params=pltpu.CompilerParams(vmem_limit_bytes=FULL_VMEM_BYTES),
        name="pack_signals",
    )(key_proj, value_proj, out_grad, query_proj)
    if owned % SUBLANES:
        send = send.reshape(2, groups, dests, owned, tok_rows)
        send = send.transpose(2, 0, 1, 3, 4).reshape(dests, 2 * groups * owned, tok_rows)
    return send


def tile_rows(tok_rows, tile):
    first = tile * (tok_rows + GAP)
    return slice(first, first + tok_rows)


def token_shape(tok_rows, tiles):
    return (tiles * (tok_rows + GAP), LANES)


def token_place(t, tok_rows, tiles):
    return (pl.ds(t, tiles, stride=tok_rows + GAP), slice(None))


def spread_tokens(a_ref, b_ref, x_ref):
    tok_rows, width = a_ref.shape
    for tile in range(width // LANES):
        cols = slice(tile * LANES, (tile + 1) * LANES)
        x_ref[tile_rows(tok_rows, tile), :] = product(a_ref[:, cols], b_ref[:, cols]).astype(F32)


def walk_tokens(ref, coef_ref, tok_rows, tiles, start, move):
    modes = coef_ref.shape[1]
    decay = [coef_ref[0, m] for m in range(modes)]
    weight = [coef_ref[2, m] for m in range(modes)]

    def step(t, held):
        place = token_place(start + move * t, tok_rows, tiles)
        x = ref[place]
        held = tuple(decay[m] * held[m] + x for m in range(modes))
        ref[place] = tree_sum([weight[m] * held[m] for m in range(modes)])
        return held

    zero = tuple(jnp.zeros((tiles, LANES), F32) for _ in range(modes))
    return lax.fori_loop(0, tok_rows, step, zero, unroll=8)


def tree_sum(terms):
    while len(terms) > 1:
        terms = [sum(terms[i : i + 2][1:], terms[i]) for i in range(0, len(terms), 2)]
    return terms[0]


def state_kernel(q_ref, k_ref, v_ref, o_ref, coef_ref, own_ref, sent_ref, x_ref, g_ref):
    tok_rows, width = k_ref.shape
    tiles = width // LANES
    modes = coef_ref.shape[1]
    spread_tokens(k_ref, v_ref, x_ref)
    spread_tokens(o_ref, q_ref, g_ref)
    decay = [coef_ref[0, m] for m in range(modes)]

    def step(t, carry):
        x = x_ref[token_place(t, tok_rows, tiles)]
        g = g_ref[token_place(tok_rows - 1 - t, tok_rows, tiles)]
        ahead = tuple(decay[m] * carry[0][m] + x for m in range(modes))
        behind = tuple(decay[m] * carry[1][m] + g for m in range(modes))
        return (ahead, behind)

    zero = tuple(jnp.zeros((tiles, LANES), F32) for _ in range(modes))
    for side, held in enumerate(lax.fori_loop(0, tok_rows, step, (zero, zero), unroll=8)):
        held = jnp.concatenate(held, axis=0)
        own_ref[side] = held
        sent_ref[side] = held.astype(LINK)


def block_states(query_proj, key_proj, value_proj, out_grad, coefs):
    tok_rows, width = key_proj.shape
    modes, tiles = coefs.shape[1:3]
    return pl.pallas_call(
        state_kernel,
        out_shape=[
            jax.ShapeDtypeStruct((2, modes * tiles, LANES), F32),
            jax.ShapeDtypeStruct((2, modes * tiles, LANES), LINK),
        ],
        scratch_shapes=[pltpu.VMEM(token_shape(tok_rows, tiles), F32)] * 2,
        compiler_params=pltpu.CompilerParams(vmem_limit_bytes=VMEM_BYTES),
        name="block_states",
    )(query_proj, key_proj, value_proj, out_grad, coefs)


def pair_kernel(seq_ref, coef_ref, own_ref, near_ref, *state_refs):
    pairs = len(state_refs) + 1
    modes, tiles = coef_ref.shape[1:3]
    pair = seq_ref[0] // 2
    second = seq_ref[0] % 2 == 1
    ahead, behind = [], []
    for m in range(modes):
        rows = slice(m * tiles, (m + 1) * tiles)
        decay = coef_ref[1, m]
        own, near = own_ref[0, rows], near_ref[0].astype(F32)[rows]
        ahead.append(jnp.where(second, own + decay * near, near + decay * own))
        own, near = own_ref[1, rows], near_ref[1].astype(F32)[rows]
        behind.append(jnp.where(second, near + decay * own, own + decay * near))
    ahead = jnp.concatenate(ahead, axis=0)
    behind = jnp.concatenate(behind, axis=0)
    for k in range(1, pairs):
        state_refs[k - 1][...] = jnp.where(pair + k < pairs, ahead, behind).astype(LINK)


def pair_states(seq_index, pairs, coefs, own, near):
    whole = pl.BlockSpec(memory_space=pltpu.VMEM)
    return pl.pallas_call(
        pair_kernel,
        in_specs=[pl.BlockSpec(memory_space=pltpu.SMEM)] + [whole] * 3,
        out_specs=[whole] * (pairs - 1),
        out_shape=[jax.ShapeDtypeStruct(own.shape[1:], LINK)] * (pairs - 1),
        compiler_params=pltpu.CompilerParams(vmem_limit_bytes=VMEM_BYTES),
        name="pair_states",
    )(seq_index, coefs, own, near)


def sum_pairs(side, seq, coef_ref, near_ref, state_refs):
    pairs = len(state_refs) + 1
    modes, tiles = coef_ref.shape[1:3]
    pair, count = seq // 2, (seq // 2, pairs - 1 - seq // 2)[side]
    beside = seq % 2 == 1 - side
    held = []
    for m in range(modes):
        rows = slice(m * tiles, (m + 1) * tiles)
        decay = coef_ref[1, m]
        total = jnp.zeros((tiles, LANES), F32)
        for k in range(pairs - 1, 0, -1):
            state_ref = state_refs[k - 1 if side == 0 else pairs - k - 1]
            block = state_ref[...].astype(F32)[rows]
            total = decay * decay * total + jnp.where(k <= count, block, 0.0)
        near = near_ref[side].astype(F32)[rows]
        held.append(jnp.where(beside, decay * total + near, total))
    return held


def local_kernel(
    q_ref, k_ref, v_ref, o_ref, coef_ref, gain_ref, conv_ref, grad_ref, done_ref, x_ref, g_ref
):
    tok_rows, width = k_ref.shape
    tiles = width // LANES
    spread_tokens(k_ref, v_ref, x_ref)
    spread_tokens(o_ref, q_ref, g_ref)
    walk_tokens(x_ref, coef_ref, tok_rows, tiles, 0, 1)
    walk_tokens(g_ref, coef_ref, tok_rows, tiles, tok_rows - 1, -1)
    for tile in range(tiles):
        cols = slice(tile * LANES, (tile + 1) * LANES)
        rows = tile_rows(tok_rows, tile)
        gain = gain_ref[:, cols]
        conv_in = product(k_ref[:, cols], v_ref[:, cols]).astype(F32)
        conv_ref[:, cols] = x_ref[rows, :] + gain * conv_in
        mid_grad = product(o_ref[:, cols], q_ref[:, cols]).astype(F32)
        grad_ref[:, cols] = g_ref[rows, :] + gain * mid_grad
    done_ref[...] = jnp.zeros(done_ref.shape, F32)


def local_parts(query_proj, key_proj, value_proj, out_grad, coefs, gain):
    tok_rows, width = key_proj.shape
    tiles = coefs.shape[2]
    return pl.pallas_call(
        local_kernel,
        out_shape=[jax.ShapeDtypeStruct((tok_rows, width), F32)] * 2
        + [jax.ShapeDtypeStruct((SUBLANES, LANES), F32)],
        scratch_shapes=[pltpu.VMEM(token_shape(tok_rows, tiles), F32)] * 2,
        compiler_params=pltpu.CompilerParams(vmem_limit_bytes=VMEM_BYTES),
        name="local_parts",
    )(query_proj, key_proj, value_proj, out_grad, coefs, gain)


def along_column(state, pairs, k):
    route = [(2 * p + b, 2 * ((p + k) % pairs) + b) for p in range(pairs) for b in range(2)]
    return lax.ppermute(state, "seq", route)


def inside_pair(state, pairs):
    return lax.ppermute(state, "seq", [(i, i ^ 1) for i in range(2 * pairs)])


def fill_edge(ref, held, coef_ref, tok_rows, tiles, start, move):
    modes = coef_ref.shape[1]
    decay = [coef_ref[0, m] for m in range(modes)]

    def step(t, held):
        held = tuple(decay[m] * held[m] for m in range(modes))
        ref[token_place(start + move * t, tok_rows, tiles)] = tree_sum(list(held))
        return held

    held = tuple(coef_ref[2, m] * held[m] for m in range(modes))
    lax.fori_loop(0, tok_rows, step, held, unroll=8)


def edge_kernel(seq_ref, coef_ref, near_ref, *refs):
    state_refs, edge_ref = refs[:-1], refs[-1]
    fill_side(0, edge_ref, seq_ref, coef_ref, near_ref, state_refs)


def fill_side(side, edge_ref, seq_ref, coef_ref, near_ref, state_refs):
    tiles = coef_ref.shape[2]
    tok_rows = edge_ref.shape[0] // tiles - GAP
    held = sum_pairs(side, seq_ref[0], coef_ref, near_ref, state_refs)
    start, move = ((0, 1), (tok_rows - 1, -1))[side]
    fill_edge(edge_ref, held, coef_ref, tok_rows, tiles, start, move)


def edge_terms(tok_rows, seq_index, coefs, near, states):
    whole = pl.BlockSpec(memory_space=pltpu.VMEM)
    return pl.pallas_call(
        edge_kernel,
        in_specs=[pl.BlockSpec(memory_space=pltpu.SMEM)] + [whole] * (2 + len(states)),
        out_shape=jax.ShapeDtypeStruct(token_shape(tok_rows, coefs.shape[2]), F32),
        compiler_params=pltpu.CompilerParams(vmem_limit_bytes=VMEM_BYTES),
        name="edge_terms",
    )(seq_index, coefs, near, *states)


def multiply_out(part_ref, edge_ref, factor_refs, out_refs, hbm_refs, sems):
    tok_rows, width = part_ref.shape
    copies = []
    for tile in range(width // LANES):
        cols = slice(tile * LANES, (tile + 1) * LANES)
        value = part_ref[:, cols] + edge_ref[tile_rows(tok_rows, tile), :]
        for i, (factor_ref, out_ref, hbm_ref) in enumerate(zip(factor_refs, out_refs, hbm_refs)):
            out_ref[:, cols] = (value * factor_ref[:, cols].astype(F32)).astype(BF16)
            place = (slice(None), pl.ds(tile * LANES, LANES))
            copies.append(
                pltpu.make_async_copy(out_ref.at[place], hbm_ref.at[place], sems.at[i, tile])
            )
            copies[-1].start()
    return copies


def conv_kernel(seq_ref, part_ref, edge_ref, q_ref, coef_ref, near_ref, *refs):
    state_refs, (layer_hbm, next_ref, layer_ref, sems) = refs[:-4], refs[-4:]
    copies = multiply_out(part_ref, edge_ref, [q_ref], [layer_ref], [layer_hbm], sems)
    fill_side(1, next_ref, seq_ref, coef_ref, near_ref, state_refs)
    for copy in copies:
        copy.wait()


def conv_outputs(seq_index, part, edge, query_proj, coefs, near, states):
    tok_rows, width = part.shape
    whole = pl.BlockSpec(memory_space=pltpu.VMEM)
    return pl.pallas_call(
        conv_kernel,
        in_specs=[pl.BlockSpec(memory_space=pltpu.SMEM)] + [whole] * (5 + len(states)),
        out_specs=[pl.BlockSpec(memory_space=pl.ANY), whole],
        out_shape=[
            jax.ShapeDtypeStruct((tok_rows, width), BF16),
            jax.ShapeDtypeStruct(edge.shape, F32),
        ],
        scratch_shapes=[
            pltpu.VMEM((tok_rows, width), BF16),
            pltpu.SemaphoreType.DMA((1, width // LANES)),
        ],
        compiler_params=pltpu.CompilerParams(vmem_limit_bytes=VMEM_BYTES),
        name="conv_outputs",
    )(seq_index, part, edge, query_proj, coefs, near, *states)


def grad_kernel(
    part_ref, edge_ref, v_ref, k_ref, key_hbm, value_hbm, key_ref, value_ref, sems
):
    copies = multiply_out(
        part_ref, edge_ref, [v_ref, k_ref], [key_ref, value_ref], [key_hbm, value_hbm], sems
    )
    for copy in copies:
        copy.wait()


def grad_outputs(part, edge, value_proj, key_proj):
    tok_rows, width = part.shape
    return pl.pallas_call(
        grad_kernel,
        in_specs=[pl.BlockSpec(memory_space=pltpu.VMEM)] * 4,
        out_specs=[pl.BlockSpec(memory_space=pl.ANY)] * 2,
        out_shape=[jax.ShapeDtypeStruct((tok_rows, width), BF16)] * 2,
        scratch_shapes=[pltpu.VMEM((tok_rows, width), BF16)] * 2
        + [pltpu.SemaphoreType.DMA((2, width // LANES))],
        compiler_params=pltpu.CompilerParams(vmem_limit_bytes=VMEM_BYTES),
        name="grad_outputs",
    )(part, edge, value_proj, key_proj)


def lag_kernel(shards, chans, groups, owned, *refs):
    in_refs, (out_ref, lag_sums, u_all, g_all, turned_all) = refs[1:-5], refs[-5:]
    halves = out_ref.shape[1] // owned
    tok_rows = halves * LANES
    blocks = shards * halves
    depth = chans * groups
    full = blocks * depth
    if len(in_refs) == 1:
        take = chans * groups * owned

        def by_filter(row):
            return row % depth * owned + row // depth

        order = one_hot(take, take, by_filter)
        for which, kept in enumerate((u_all, g_all)):
            rows = slice(which * groups * owned, (which + 1) * groups * owned)
            for s in range(shards):
                piece = in_refs[0][s * chans : (s + 1) * chans, rows, :].reshape(take, tok_rows)
                piece = jnp.dot(order, piece, preferred_element_type=F32).astype(BF16)
                piece = piece.reshape(owned, depth, tok_rows)
                for h in range(halves):
                    first = (s * halves + h) * depth
                    kept[:, first : first + depth, :] = piece[:, :, h * LANES : (h + 1) * LANES]
    else:
        u_all[...] = in_refs[0][...]
        g_all[:, :full, :] = in_refs[1][...]
    g_all[:, full:, :] = jnp.zeros((owned, g_all.shape[1] - full, LANES), BF16)
    mirror = one_hot(LANES, LANES, lambda row: LANES - 1 - row)
    row = lax.broadcasted_iota(jnp.int32, (LANES, LANES), 0)
    col = lax.broadcasted_iota(jnp.int32, (LANES, LANES), 1)
    same_block = row + col >= LANES - 1
    filter_row = lax.broadcasted_iota(jnp.int32, (owned, LANES), 0)
    batch = min(blocks, 16)

    def one_filter(f, _):
        turned = turned_all[f]

        def some_lags(first):
            tables = []
            for d in range(0, batch, 2):
                live = full
                if batch == blocks:
                    live = min(full, -(-(blocks - d) * depth // LANES) * LANES)
                pair = jnp.concatenate(
                    [
                        g_all[f, pl.ds(pl.multiple_of((first + d + e) * depth, depth), live), :]
                        for e in range(2)
                    ],
                    axis=1,
                )
                table = jnp.dot(turned[:, :live], pair, preferred_element_type=F32)
                tables += [table[:, :LANES], table[:, LANES:]]
            last = g_all[f, pl.ds(pl.multiple_of((first + batch) * depth, depth), full), :]
            if batch < blocks:
                tables.append(jnp.dot(turned, last, preferred_element_type=F32))
            else:
                tables.append(jnp.zeros((LANES, LANES), F32))
            for d in range(batch):
                joined = jnp.where(same_block, tables[d], tables[d + 1])
                skewed = pltpu.roll(joined, 1, 1, stride=1, stride_axis=0)
                sums = jnp.sum(skewed, axis=0, keepdims=True)
                row = d % halves * owned
                place = ((first + d) // halves, slice(row, row + owned), slice(None))
                lag_sums[place] = jnp.where(filter_row == f, sums, lag_sums[place])

        if batch == blocks:
            some_lags(0)
        else:
            lax.fori_loop(0, blocks // batch, lambda i, c: (some_lags(i * batch), c)[1], 0)
        return 0

    for f in range(owned):
        turned_all[f] = lax.dot_general(
            mirror, u_all[f], (((1,), (1,)), ((), ())), preferred_element_type=F32
        ).astype(BF16)
    lax.fori_loop(0, owned, one_filter, 0, unroll=min(owned, 8))
    out_ref[...] = lag_sums[...].astype(LINK)


def filter_lags(received, done, shards, chans, owned):
    tok_rows = received.shape[2]
    groups = received.shape[1] // (2 * owned)
    halves = tok_rows // LANES
    depth = chans * groups
    full = shards * halves * depth
    args = (received,)
    if owned % SUBLANES:
        split = received.reshape(shards, chans, 2, groups, owned, halves, LANES)
        split = split.transpose(2, 4, 0, 5, 1, 3, 6).reshape(2, owned, full, LANES)
        args = (split[0], split[1])
    whole = pl.BlockSpec(memory_space=pltpu.VMEM)
    return pl.pallas_call(
        functools.partial(lag_kernel, shards, chans, groups, owned),
        in_specs=[pl.BlockSpec(memory_space=pl.ANY)] + [whole] * len(args),
        out_specs=whole,
        out_shape=jax.ShapeDtypeStruct((shards, halves * owned, LANES), LINK),
        scratch_shapes=[
            pltpu.VMEM((shards, halves * owned, LANES), F32),
            pltpu.VMEM((owned, full, LANES), BF16),
            pltpu.VMEM((owned, 2 * full + depth, LANES), BF16),
            pltpu.VMEM((owned, LANES, full), BF16),
        ],
        compiler_params=pltpu.CompilerParams(vmem_limit_bytes=VMEM_BYTES),
        name="filter_lags",
    )(done, *args)


def per_device(query_proj, key_proj, value_proj, out_grad, residues, decay_rate, skip_gain):
    tok_rows, width = key_proj.shape
    shards = lax.axis_size("seq")
    chans = lax.axis_size("chan")
    length = shards * tok_rows
    owned = FILTERS // (shards * chans)
    modes = residues.shape[1]
    signals = (query_proj, key_proj, value_proj, out_grad)

    send = pack_signals(shards, chans, owned, *signals)
    send, *signals, residues, decay_rate = lax.optimization_barrier(
        (send, *signals, residues, decay_rate)
    )
    received = lax.all_to_all(send, ("seq", "chan"), split_axis=0, concat_axis=0, tiled=True)

    coefs = jnp.stack(
        [
            jnp.exp(-decay_rate),
            jnp.exp(-(decay_rate * float(tok_rows))),
            residues * jnp.sqrt(decay_rate),
        ]
    )
    coefs = coefs.transpose(0, 2, 1).reshape(3, modes, 1, FILTERS // LANES, LANES)
    coefs = jnp.broadcast_to(coefs, (3, modes, width // FILTERS, FILTERS // LANES, LANES))
    coefs = coefs.reshape(3, modes, width // LANES, LANES)
    seq_index = lax.axis_index("seq").reshape(1)
    pairs = shards // 2
    own, sent = block_states(*signals, coefs)
    conv_part, grad_part, done = local_parts(*signals, coefs, skip_gain[None, :])
    sent, done = lax.optimization_barrier((sent, done))
    near = inside_pair(sent, pairs)
    states = pair_states(seq_index, pairs, coefs, own, near)
    states = [along_column(state, pairs, 1 + i) for i, state in enumerate(states)]

    scale = 1.0 / math.sqrt(length * (CHANNELS // FILTERS))
    lags = filter_lags(received, done, shards, chans, owned)
    lags, *states = lax.optimization_barrier((lags, *states))
    lags = lax.all_to_all(lags, "seq", split_axis=0, concat_axis=0, tiled=True)
    lags = lags.reshape(shards, tok_rows // LANES, owned, LANES).transpose(0, 2, 1, 3)
    filter_grad = lags.reshape(shards * owned, tok_rows).T.astype(F32) * scale
    query_proj, key_proj, value_proj, _ = signals
    edge = edge_terms(tok_rows, seq_index, coefs, near, states)
    layer_out, edge = conv_outputs(seq_index, conv_part, edge, query_proj, coefs, near, states)
    key_grad, value_grad = grad_outputs(grad_part, edge, value_proj, key_proj)
    return (layer_out, key_grad, value_grad, filter_grad)


def solution(mesh):
    split = P("seq", "chan")
    return jax.shard_map(
        per_device,
        mesh=mesh,
        in_specs=(split, split, split, split, P(), P(), P("chan")),
        out_specs=(split, split, split, split),
        check_vma=False,
    )
```

```python
import functools
import math

import jax
import jax.numpy as jnp
from jax import lax
from jax.experimental import pallas as pl
from jax.experimental.pallas import tpu as pltpu
from jax.sharding import PartitionSpec as P

CHANNELS = 4096
FILTERS = 256
LANES = 128
SUBLANES = 8
GAP = 8
VMEM_BYTES = 16 * 1024 * 1024
FULL_VMEM_BYTES = 62 * 1024 * 1024
F32 = jnp.float32
BF16 = jnp.bfloat16
LINK = jnp.bfloat16


def product(first, second):
    return first * second


def one_hot(rows, cols, column_of):
    row = lax.broadcasted_iota(jnp.int32, (rows, cols), 0)
    col = lax.broadcasted_iota(jnp.int32, (rows, cols), 1)
    return (col == column_of(row)).astype(F32).astype(BF16)


def pack_kernel(shards, chans, owned, *refs):
    hbm_refs, send_ref, held, packed, in_sems, out_sems = refs[:4], *refs[4:]
    tok_rows, width = held.shape[1:]
    groups = width // FILTERS
    per_chan = FILTERS // chans
    half = tok_rows // 2

    def arrival(i, part):
        place = (pl.ds(part * half, half), slice(None))
        return pltpu.make_async_copy(
            hbm_refs[i].at[place], held.at[(i, *place)], in_sems.at[i, part]
        )

    def departure(which):
        if owned % SUBLANES:
            place = (which,)
        else:
            place = (slice(None), pl.ds(which * groups * owned, groups * owned))
        return pltpu.make_async_copy(packed.at[place], send_ref.at[place], out_sems.at[which])

    for i in range(len(hbm_refs)):
        for part in range(2):
            arrival(i, part).start()

    def owned_filter(row):
        seq = row // (chans * owned)
        chan = row // owned % chans
        return chan * per_chan + seq * owned + row % owned

    order = one_hot(FILTERS, FILTERS, owned_filter)
    for which in range(2):
        for i in (2 * which, 2 * which + 1):
            for part in range(2):
                arrival(i, part).wait()
        pieces = []
        for group in range(groups):
            cols = slice(group * FILTERS, (group + 1) * FILTERS)
            piece = lax.dot_general(
                order,
                product(held[2 * which, :, cols], held[2 * which + 1, :, cols]),
                (((1,), (1,)), ((), ())),
                preferred_element_type=F32,
            )
            if owned % SUBLANES:
                packed[which, group] = piece.astype(BF16)
            else:
                pieces.append(piece.reshape(shards * chans, owned, tok_rows))
        if pieces:
            rows = slice(which * groups * owned, (which + 1) * groups * owned)
            packed[:, rows, :] = jnp.concatenate(pieces, axis=1).astype(BF16)
        departure(which).start()
    for which in range(2):
        departure(which).wait()


def pack_signals(shards, chans, owned, query_proj, key_proj, value_proj, out_grad):
    tok_rows, width = key_proj.shape
    groups = width // FILTERS
    dests = shards * chans
    if owned % SUBLANES:
        shape = (2, groups, FILTERS, tok_rows)
    else:
        shape = (dests, 2 * groups * owned, tok_rows)
    send = pl.pallas_call(
        functools.partial(pack_kernel, shards, chans, owned),
        in_specs=[pl.BlockSpec(memory_space=pl.ANY)] * 4,
        out_specs=pl.BlockSpec(memory_space=pl.ANY),
        out_shape=jax.ShapeDtypeStruct(shape, BF16),
        scratch_shapes=[
            pltpu.VMEM((4, tok_rows, width), BF16),
            pltpu.VMEM(shape, BF16),
            pltpu.SemaphoreType.DMA((4, 2)),
            pltpu.SemaphoreType.DMA((2,)),
        ],
        compiler_params=pltpu.CompilerParams(vmem_limit_bytes=FULL_VMEM_BYTES),
        name="pack_signals",
    )(key_proj, value_proj, out_grad, query_proj)
    if owned % SUBLANES:
        send = send.reshape(2, groups, dests, owned, tok_rows)
        send = send.transpose(2, 0, 1, 3, 4).reshape(dests, 2 * groups * owned, tok_rows)
    return send


def tile_rows(tok_rows, tile):
    first = tile * (tok_rows + GAP)
    return slice(first, first + tok_rows)


def token_shape(tok_rows, tiles):
    return (tiles * (tok_rows + GAP), LANES)


def token_place(t, tok_rows, tiles):
    return (pl.ds(t, tiles, stride=tok_rows + GAP), slice(None))


def spread_tokens(a_ref, b_ref, x_ref):
    tok_rows, width = a_ref.shape
    for tile in range(width // LANES):
        cols = slice(tile * LANES, (tile + 1) * LANES)
        x_ref[tile_rows(tok_rows, tile), :] = product(a_ref[:, cols], b_ref[:, cols]).astype(F32)


def walk_tokens(ref, coef_ref, tok_rows, tiles, start, move):
    modes = coef_ref.shape[1]
    decay = [coef_ref[0, m] for m in range(modes)]
    weight = [coef_ref[2, m] for m in range(modes)]

    def step(t, held):
        place = token_place(start + move * t, tok_rows, tiles)
        x = ref[place]
        held = tuple(decay[m] * held[m] + x for m in range(modes))
        ref[place] = tree_sum([weight[m] * held[m] for m in range(modes)])
        return held

    zero = tuple(jnp.zeros((tiles, LANES), F32) for _ in range(modes))
    return lax.fori_loop(0, tok_rows, step, zero, unroll=8)


def tree_sum(terms):
    while len(terms) > 1:
        terms = [sum(terms[i : i + 2][1:], terms[i]) for i in range(0, len(terms), 2)]
    return terms[0]


def state_kernel(q_ref, k_ref, v_ref, o_ref, coef_ref, own_ref, sent_ref, x_ref, g_ref):
    tok_rows, width = k_ref.shape
    tiles = width // LANES
    modes = coef_ref.shape[1]
    spread_tokens(k_ref, v_ref, x_ref)
    spread_tokens(o_ref, q_ref, g_ref)
    decay = [coef_ref[0, m] for m in range(modes)]

    def step(t, carry):
        x = x_ref[token_place(t, tok_rows, tiles)]
        g = g_ref[token_place(tok_rows - 1 - t, tok_rows, tiles)]
        ahead = tuple(decay[m] * carry[0][m] + x for m in range(modes))
        behind = tuple(decay[m] * carry[1][m] + g for m in range(modes))
        return (ahead, behind)

    zero = tuple(jnp.zeros((tiles, LANES), F32) for _ in range(modes))
    for side, held in enumerate(lax.fori_loop(0, tok_rows, step, (zero, zero), unroll=8)):
        held = jnp.concatenate(held, axis=0)
        own_ref[side] = held
        sent_ref[side] = held.astype(LINK)


def block_states(query_proj, key_proj, value_proj, out_grad, coefs):
    tok_rows, width = key_proj.shape
    modes, tiles = coefs.shape[1:3]
    return pl.pallas_call(
        state_kernel,
        out_shape=[
            jax.ShapeDtypeStruct((2, modes * tiles, LANES), F32),
            jax.ShapeDtypeStruct((2, modes * tiles, LANES), LINK),
        ],
        scratch_shapes=[pltpu.VMEM(token_shape(tok_rows, tiles), F32)] * 2,
        compiler_params=pltpu.CompilerParams(vmem_limit_bytes=VMEM_BYTES),
        name="block_states",
    )(query_proj, key_proj, value_proj, out_grad, coefs)


def pair_kernel(seq_ref, coef_ref, own_ref, near_ref, *state_refs):
    pairs = len(state_refs) + 1
    modes, tiles = coef_ref.shape[1:3]
    pair = seq_ref[0] // 2
    second = seq_ref[0] % 2 == 1
    ahead, behind = [], []
    for m in range(modes):
        rows = slice(m * tiles, (m + 1) * tiles)
        decay = coef_ref[1, m]
        own, near = own_ref[0, rows], near_ref[0].astype(F32)[rows]
        ahead.append(jnp.where(second, own + decay * near, near + decay * own))
        own, near = own_ref[1, rows], near_ref[1].astype(F32)[rows]
        behind.append(jnp.where(second, near + decay * own, own + decay * near))
    ahead = jnp.concatenate(ahead, axis=0)
    behind = jnp.concatenate(behind, axis=0)
    for k in range(1, pairs):
        state_refs[k - 1][...] = jnp.where(pair + k < pairs, ahead, behind).astype(LINK)


def pair_states(seq_index, pairs, coefs, own, near):
    whole = pl.BlockSpec(memory_space=pltpu.VMEM)
    return pl.pallas_call(
        pair_kernel,
        in_specs=[pl.BlockSpec(memory_space=pltpu.SMEM)] + [whole] * 3,
        out_specs=[whole] * (pairs - 1),
        out_shape=[jax.ShapeDtypeStruct(own.shape[1:], LINK)] * (pairs - 1),
        compiler_params=pltpu.CompilerParams(vmem_limit_bytes=VMEM_BYTES),
        name="pair_states",
    )(seq_index, coefs, own, near)


def sum_pairs(side, seq, coef_ref, near_ref, state_refs):
    pairs = len(state_refs) + 1
    modes, tiles = coef_ref.shape[1:3]
    pair, count = seq // 2, (seq // 2, pairs - 1 - seq // 2)[side]
    beside = seq % 2 == 1 - side
    held = []
    for m in range(modes):
        rows = slice(m * tiles, (m + 1) * tiles)
        decay = coef_ref[1, m]
        total = jnp.zeros((tiles, LANES), F32)
        for k in range(pairs - 1, 0, -1):
            state_ref = state_refs[k - 1 if side == 0 else pairs - k - 1]
            block = state_ref[...].astype(F32)[rows]
            total = decay * decay * total + jnp.where(k <= count, block, 0.0)
        near = near_ref[side].astype(F32)[rows]
        held.append(jnp.where(beside, decay * total + near, total))
    return held


def local_kernel(
    q_ref, k_ref, v_ref, o_ref, coef_ref, gain_ref, conv_ref, grad_ref, done_ref, x_ref, g_ref
):
    tok_rows, width = k_ref.shape
    tiles = width // LANES
    spread_tokens(k_ref, v_ref, x_ref)
    spread_tokens(o_ref, q_ref, g_ref)
    walk_tokens(x_ref, coef_ref, tok_rows, tiles, 0, 1)
    walk_tokens(g_ref, coef_ref, tok_rows, tiles, tok_rows - 1, -1)
    for tile in range(tiles):
        cols = slice(tile * LANES, (tile + 1) * LANES)
        rows = tile_rows(tok_rows, tile)
        gain = gain_ref[:, cols]
        conv_in = product(k_ref[:, cols], v_ref[:, cols]).astype(F32)
        conv_ref[:, cols] = x_ref[rows, :] + gain * conv_in
        mid_grad = product(o_ref[:, cols], q_ref[:, cols]).astype(F32)
        grad_ref[:, cols] = g_ref[rows, :] + gain * mid_grad
    done_ref[...] = jnp.zeros(done_ref.shape, F32)


def local_parts(query_proj, key_proj, value_proj, out_grad, coefs, gain):
    tok_rows, width = key_proj.shape
    tiles = coefs.shape[2]
    return pl.pallas_call(
        local_kernel,
        out_shape=[jax.ShapeDtypeStruct((tok_rows, width), F32)] * 2
        + [jax.ShapeDtypeStruct((SUBLANES, LANES), F32)],
        scratch_shapes=[pltpu.VMEM(token_shape(tok_rows, tiles), F32)] * 2,
        compiler_params=pltpu.CompilerParams(vmem_limit_bytes=VMEM_BYTES),
        name="local_parts",
    )(query_proj, key_proj, value_proj, out_grad, coefs, gain)


def along_column(state, pairs, k):
    route = [(2 * p + b, 2 * ((p + k) % pairs) + b) for p in range(pairs) for b in range(2)]
    return lax.ppermute(state, "seq", route)


def inside_pair(state, pairs):
    return lax.ppermute(state, "seq", [(i, i ^ 1) for i in range(2 * pairs)])


def fill_edge(ref, held, coef_ref, tok_rows, tiles, start, move):
    modes = coef_ref.shape[1]
    decay = [coef_ref[0, m] for m in range(modes)]

    def step(t, held):
        held = tuple(decay[m] * held[m] for m in range(modes))
        ref[token_place(start + move * t, tok_rows, tiles)] = tree_sum(list(held))
        return held

    held = tuple(coef_ref[2, m] * held[m] for m in range(modes))
    lax.fori_loop(0, tok_rows, step, held, unroll=8)


def edge_kernel(seq_ref, coef_ref, near_ref, *refs):
    state_refs, edge_ref = refs[:-1], refs[-1]
    fill_side(0, edge_ref, seq_ref, coef_ref, near_ref, state_refs)


def fill_side(side, edge_ref, seq_ref, coef_ref, near_ref, state_refs):
    tiles = coef_ref.shape[2]
    tok_rows = edge_ref.shape[0] // tiles - GAP
    held = sum_pairs(side, seq_ref[0], coef_ref, near_ref, state_refs)
    start, move = ((0, 1), (tok_rows - 1, -1))[side]
    fill_edge(edge_ref, held, coef_ref, tok_rows, tiles, start, move)


def edge_terms(tok_rows, seq_index, coefs, near, states):
    whole = pl.BlockSpec(memory_space=pltpu.VMEM)
    return pl.pallas_call(
        edge_kernel,
        in_specs=[pl.BlockSpec(memory_space=pltpu.SMEM)] + [whole] * (2 + len(states)),
        out_shape=jax.ShapeDtypeStruct(token_shape(tok_rows, coefs.shape[2]), F32),
        compiler_params=pltpu.CompilerParams(vmem_limit_bytes=VMEM_BYTES),
        name="edge_terms",
    )(seq_index, coefs, near, *states)


def multiply_out(part_ref, edge_ref, factor_refs, out_refs, hbm_refs, sems):
    tok_rows, width = part_ref.shape
    copies = []
    for tile in range(width // LANES):
        cols = slice(tile * LANES, (tile + 1) * LANES)
        value = part_ref[:, cols] + edge_ref[tile_rows(tok_rows, tile), :]
        for i, (factor_ref, out_ref, hbm_ref) in enumerate(zip(factor_refs, out_refs, hbm_refs)):
            out_ref[:, cols] = (value * factor_ref[:, cols].astype(F32)).astype(BF16)
            place = (slice(None), pl.ds(tile * LANES, LANES))
            copies.append(
                pltpu.make_async_copy(out_ref.at[place], hbm_ref.at[place], sems.at[i, tile])
            )
            copies[-1].start()
    return copies


def conv_kernel(seq_ref, part_ref, edge_ref, q_ref, coef_ref, near_ref, *refs):
    state_refs, (layer_hbm, next_ref, layer_ref, sems) = refs[:-4], refs[-4:]
    copies = multiply_out(part_ref, edge_ref, [q_ref], [layer_ref], [layer_hbm], sems)
    fill_side(1, next_ref, seq_ref, coef_ref, near_ref, state_refs)
    for copy in copies:
        copy.wait()


def conv_outputs(seq_index, part, edge, query_proj, coefs, near, states):
    tok_rows, width = part.shape
    whole = pl.BlockSpec(memory_space=pltpu.VMEM)
    return pl.pallas_call(
        conv_kernel,
        in_specs=[pl.BlockSpec(memory_space=pltpu.SMEM)] + [whole] * (5 + len(states)),
        out_specs=[pl.BlockSpec(memory_space=pl.ANY), whole],
        out_shape=[
            jax.ShapeDtypeStruct((tok_rows, width), BF16),
            jax.ShapeDtypeStruct(edge.shape, F32),
        ],
        scratch_shapes=[
            pltpu.VMEM((tok_rows, width), BF16),
            pltpu.SemaphoreType.DMA((1, width // LANES)),
        ],
        compiler_params=pltpu.CompilerParams(vmem_limit_bytes=VMEM_BYTES),
        name="conv_outputs",
    )(seq_index, part, edge, query_proj, coefs, near, *states)


def grad_kernel(
    part_ref, edge_ref, v_ref, k_ref, key_hbm, value_hbm, key_ref, value_ref, sems
):
    copies = multiply_out(
        part_ref, edge_ref, [v_ref, k_ref], [key_ref, value_ref], [key_hbm, value_hbm], sems
    )
    for copy in copies:
        copy.wait()


def grad_outputs(part, edge, value_proj, key_proj):
    tok_rows, width = part.shape
    return pl.pallas_call(
        grad_kernel,
        in_specs=[pl.BlockSpec(memory_space=pltpu.VMEM)] * 4,
        out_specs=[pl.BlockSpec(memory_space=pl.ANY)] * 2,
        out_shape=[jax.ShapeDtypeStruct((tok_rows, width), BF16)] * 2,
        scratch_shapes=[pltpu.VMEM((tok_rows, width), BF16)] * 2
        + [pltpu.SemaphoreType.DMA((2, width // LANES))],
        compiler_params=pltpu.CompilerParams(vmem_limit_bytes=VMEM_BYTES),
        name="grad_outputs",
    )(part, edge, value_proj, key_proj)


def lag_kernel(shards, chans, groups, owned, *refs):
    in_refs, (out_ref, lag_sums, u_all, g_all, turned_all) = refs[1:-5], refs[-5:]
    halves = out_ref.shape[1] // owned
    tok_rows = halves * LANES
    blocks = shards * halves
    depth = chans * groups
    full = blocks * depth
    if len(in_refs) == 1:
        take = chans * groups * owned

        def by_filter(row):
            return row % depth * owned + row // depth

        order = one_hot(take, take, by_filter)
        for which, kept in enumerate((u_all, g_all)):
            rows = slice(which * groups * owned, (which + 1) * groups * owned)
            for s in range(shards):
                piece = in_refs[0][s * chans : (s + 1) * chans, rows, :].reshape(take, tok_rows)
                piece = jnp.dot(order, piece, preferred_element_type=F32).astype(BF16)
                piece = piece.reshape(owned, depth, tok_rows)
                for h in range(halves):
                    first = (s * halves + h) * depth
                    kept[:, first : first + depth, :] = piece[:, :, h * LANES : (h + 1) * LANES]
    else:
        u_all[...] = in_refs[0][...]
        g_all[:, :full, :] = in_refs[1][...]
    g_all[:, full:, :] = jnp.zeros((owned, g_all.shape[1] - full, LANES), BF16)
    mirror = one_hot(LANES, LANES, lambda row: LANES - 1 - row)
    row = lax.broadcasted_iota(jnp.int32, (LANES, LANES), 0)
    col = lax.broadcasted_iota(jnp.int32, (LANES, LANES), 1)
    same_block = row + col >= LANES - 1
    filter_row = lax.broadcasted_iota(jnp.int32, (owned, LANES), 0)
    batch = min(blocks, 16)

    def one_filter(f, _):
        turned = turned_all[f]

        def some_lags(first):
            tables = []
            for d in range(0, batch, 2):
                live = full
                if batch == blocks:
                    live = min(full, -(-(blocks - d) * depth // LANES) * LANES)
                pair = jnp.concatenate(
                    [
                        g_all[f, pl.ds(pl.multiple_of((first + d + e) * depth, depth), live), :]
                        for e in range(2)
                    ],
                    axis=1,
                )
                table = jnp.dot(turned[:, :live], pair, preferred_element_type=F32)
                tables += [table[:, :LANES], table[:, LANES:]]
            last = g_all[f, pl.ds(pl.multiple_of((first + batch) * depth, depth), full), :]
            if batch < blocks:
                tables.append(jnp.dot(turned, last, preferred_element_type=F32))
            else:
                tables.append(jnp.zeros((LANES, LANES), F32))
            for d in range(batch):
                joined = jnp.where(same_block, tables[d], tables[d + 1])
                skewed = pltpu.roll(joined, 1, 1, stride=1, stride_axis=0)
                sums = jnp.sum(skewed, axis=0, keepdims=True)
                row = d % halves * owned
                place = ((first + d) // halves, slice(row, row + owned), slice(None))
                lag_sums[place] = jnp.where(filter_row == f, sums, lag_sums[place])

        if batch == blocks:
            some_lags(0)
        else:
            lax.fori_loop(0, blocks // batch, lambda i, c: (some_lags(i * batch), c)[1], 0)
        return 0

    for f in range(owned):
        turned_all[f] = lax.dot_general(
            mirror, u_all[f], (((1,), (1,)), ((), ())), preferred_element_type=F32
        ).astype(BF16)
    lax.fori_loop(0, owned, one_filter, 0, unroll=min(owned, 8))
    out_ref[...] = lag_sums[...].astype(LINK)


def filter_lags(received, done, shards, chans, owned):
    tok_rows = received.shape[2]
    groups = received.shape[1] // (2 * owned)
    halves = tok_rows // LANES
    depth = chans * groups
    full = shards * halves * depth
    args = (received,)
    if owned % SUBLANES:
        split = received.reshape(shards, chans, 2, groups, owned, halves, LANES)
        split = split.transpose(2, 4, 0, 5, 1, 3, 6).reshape(2, owned, full, LANES)
        args = (split[0], split[1])
    whole = pl.BlockSpec(memory_space=pltpu.VMEM)
    return pl.pallas_call(
        functools.partial(lag_kernel, shards, chans, groups, owned),
        in_specs=[pl.BlockSpec(memory_space=pl.ANY)] + [whole] * len(args),
        out_specs=whole,
        out_shape=jax.ShapeDtypeStruct((shards, halves * owned, LANES), LINK),
        scratch_shapes=[
            pltpu.VMEM((shards, halves * owned, LANES), F32),
            pltpu.VMEM((owned, full, LANES), BF16),
            pltpu.VMEM((owned, 2 * full + depth, LANES), BF16),
            pltpu.VMEM((owned, LANES, full), BF16),
        ],
        compiler_params=pltpu.CompilerParams(vmem_limit_bytes=VMEM_BYTES),
        name="filter_lags",
    )(done, *args)


def per_device(query_proj, key_proj, value_proj, out_grad, residues, decay_rate, skip_gain):
    tok_rows, width = key_proj.shape
    shards = lax.axis_size("seq")
    chans = lax.axis_size("chan")
    length = shards * tok_rows
    owned = FILTERS // (shards * chans)
    modes = residues.shape[1]
    signals = (query_proj, key_proj, value_proj, out_grad)

    send = pack_signals(shards, chans, owned, *signals)
    send, *signals, residues, decay_rate = lax.optimization_barrier(
        (send, *signals, residues, decay_rate)
    )
    received = lax.all_to_all(send, ("seq", "chan"), split_axis=0, concat_axis=0, tiled=True)

    coefs = jnp.stack(
        [
            jnp.exp(-decay_rate),
            jnp.exp(-(decay_rate * float(tok_rows))),
            residues * jnp.sqrt(decay_rate),
        ]
    )
    coefs = coefs.transpose(0, 2, 1).reshape(3, modes, 1, FILTERS // LANES, LANES)
    coefs = jnp.broadcast_to(coefs, (3, modes, width // FILTERS, FILTERS // LANES, LANES))
    coefs = coefs.reshape(3, modes, width // LANES, LANES)
    seq_index = lax.axis_index("seq").reshape(1)
    pairs = shards // 2
    own, sent = block_states(*signals, coefs)
    conv_part, grad_part, done = local_parts(*signals, coefs, skip_gain[None, :])
    sent, done = lax.optimization_barrier((sent, done))
    near = inside_pair(sent, pairs)
    states = pair_states(seq_index, pairs, coefs, own, near)
    states = [along_column(state, pairs, 1 + i) for i, state in enumerate(states)]

    scale = 1.0 / math.sqrt(length * (CHANNELS // FILTERS))
    lags = filter_lags(received, done, shards, chans, owned)
    lags, *states = lax.optimization_barrier((lags, *states))
    lags = lax.all_to_all(lags, "seq", split_axis=0, concat_axis=0, tiled=True)
    lags = lags.reshape(shards, tok_rows // LANES, owned, LANES).transpose(0, 2, 1, 3)
    filter_grad = lags.reshape(shards * owned, tok_rows).T.astype(F32) * scale
    query_proj, key_proj, value_proj, _ = signals
    edge = edge_terms(tok_rows, seq_index, coefs, near, states)
    layer_out, edge = conv_outputs(seq_index, conv_part, edge, query_proj, coefs, near, states)
    key_grad, value_grad = grad_outputs(grad_part, edge, value_proj, key_proj)
    return (layer_out, key_grad, value_grad, filter_grad)


def solution(mesh):
    split = P("seq", "chan")
    return jax.shard_map(
        per_device,
        mesh=mesh,
        in_specs=(split, split, split, split, P(), P(), P("chan")),
        out_specs=(split, split, split, split),
        check_vma=False,
    )
```

```python
import functools
import math

import jax
import jax.numpy as jnp
from jax import lax
from jax.experimental import pallas as pl
from jax.experimental.pallas import tpu as pltpu
from jax.sharding import PartitionSpec as P

CHANNELS = 4096
FILTERS = 256
LANES = 128
SUBLANES = 8
GAP = 8
VMEM_BYTES = 16 * 1024 * 1024
FULL_VMEM_BYTES = 62 * 1024 * 1024
F32 = jnp.float32
BF16 = jnp.bfloat16
LINK = jnp.bfloat16


def product(first, second):
    return first * second


def one_hot(rows, cols, column_of):
    row = lax.broadcasted_iota(jnp.int32, (rows, cols), 0)
    col = lax.broadcasted_iota(jnp.int32, (rows, cols), 1)
    return (col == column_of(row)).astype(F32).astype(BF16)


def pack_kernel(shards, chans, owned, *refs):
    hbm_refs, send_ref, held, packed, in_sems, out_sems = refs[:4], *refs[4:]
    tok_rows, width = held.shape[1:]
    groups = width // FILTERS
    per_chan = FILTERS // chans
    half = tok_rows // 2

    def arrival(i, part):
        place = (pl.ds(part * half, half), slice(None))
        return pltpu.make_async_copy(
            hbm_refs[i].at[place], held.at[(i, *place)], in_sems.at[i, part]
        )

    def departure(which):
        if owned % SUBLANES:
            place = (which,)
        else:
            place = (slice(None), pl.ds(which * groups * owned, groups * owned))
        return pltpu.make_async_copy(packed.at[place], send_ref.at[place], out_sems.at[which])

    for i in range(len(hbm_refs)):
        for part in range(2):
            arrival(i, part).start()

    def owned_filter(row):
        seq = row // (chans * owned)
        chan = row // owned % chans
        return chan * per_chan + seq * owned + row % owned

    order = one_hot(FILTERS, FILTERS, owned_filter)
    for which in range(2):
        for i in (2 * which, 2 * which + 1):
            for part in range(2):
                arrival(i, part).wait()
        pieces = []
        for group in range(groups):
            cols = slice(group * FILTERS, (group + 1) * FILTERS)
            piece = lax.dot_general(
                order,
                product(held[2 * which, :, cols], held[2 * which + 1, :, cols]),
                (((1,), (1,)), ((), ())),
                preferred_element_type=F32,
            )
            if owned % SUBLANES:
                packed[which, group] = piece.astype(BF16)
            else:
                pieces.append(piece.reshape(shards * chans, owned, tok_rows))
        if pieces:
            rows = slice(which * groups * owned, (which + 1) * groups * owned)
            packed[:, rows, :] = jnp.concatenate(pieces, axis=1).astype(BF16)
        departure(which).start()
    for which in range(2):
        departure(which).wait()


def pack_signals(shards, chans, owned, query_proj, key_proj, value_proj, out_grad):
    tok_rows, width = key_proj.shape
    groups = width // FILTERS
    dests = shards * chans
    if owned % SUBLANES:
        shape = (2, groups, FILTERS, tok_rows)
    else:
        shape = (dests, 2 * groups * owned, tok_rows)
    send = pl.pallas_call(
        functools.partial(pack_kernel, shards, chans, owned),
        in_specs=[pl.BlockSpec(memory_space=pl.ANY)] * 4,
        out_specs=pl.BlockSpec(memory_space=pl.ANY),
        out_shape=jax.ShapeDtypeStruct(shape, BF16),
        scratch_shapes=[
            pltpu.VMEM((4, tok_rows, width), BF16),
            pltpu.VMEM(shape, BF16),
            pltpu.SemaphoreType.DMA((4, 2)),
            pltpu.SemaphoreType.DMA((2,)),
        ],
        compiler_params=pltpu.CompilerParams(vmem_limit_bytes=FULL_VMEM_BYTES),
        name="pack_signals",
    )(key_proj, value_proj, out_grad, query_proj)
    if owned % SUBLANES:
        send = send.reshape(2, groups, dests, owned, tok_rows)
        send = send.transpose(2, 0, 1, 3, 4).reshape(dests, 2 * groups * owned, tok_rows)
    return send


def tile_rows(tok_rows, tile):
    first = tile * (tok_rows + GAP)
    return slice(first, first + tok_rows)


def token_shape(tok_rows, tiles):
    return (tiles * (tok_rows + GAP), LANES)


def token_place(t, tok_rows, tiles):
    return (pl.ds(t, tiles, stride=tok_rows + GAP), slice(None))


def spread_tokens(a_ref, b_ref, x_ref):
    tok_rows, width = a_ref.shape
    for tile in range(width // LANES):
        cols = slice(tile * LANES, (tile + 1) * LANES)
        x_ref[tile_rows(tok_rows, tile), :] = product(a_ref[:, cols], b_ref[:, cols]).astype(F32)


def walk_tokens(ref, coef_ref, tok_rows, tiles, start, move):
    modes = coef_ref.shape[1]
    decay = [coef_ref[0, m] for m in range(modes)]
    weight = [coef_ref[2, m] for m in range(modes)]

    def step(t, held):
        place = token_place(start + move * t, tok_rows, tiles)
        x = ref[place]
        held = tuple(decay[m] * held[m] + x for m in range(modes))
        ref[place] = tree_sum([weight[m] * held[m] for m in range(modes)])
        return held

    zero = tuple(jnp.zeros((tiles, LANES), F32) for _ in range(modes))
    return lax.fori_loop(0, tok_rows, step, zero, unroll=8)


def tree_sum(terms):
    while len(terms) > 1:
        terms = [sum(terms[i : i + 2][1:], terms[i]) for i in range(0, len(terms), 2)]
    return terms[0]


def state_kernel(q_ref, k_ref, v_ref, o_ref, coef_ref, own_ref, sent_ref, x_ref, g_ref):
    tok_rows, width = k_ref.shape
    tiles = width // LANES
    modes = coef_ref.shape[1]
    spread_tokens(k_ref, v_ref, x_ref)
    spread_tokens(o_ref, q_ref, g_ref)
    decay = [coef_ref[0, m] for m in range(modes)]

    def step(t, carry):
        x = x_ref[token_place(t, tok_rows, tiles)]
        g = g_ref[token_place(tok_rows - 1 - t, tok_rows, tiles)]
        ahead = tuple(decay[m] * carry[0][m] + x for m in range(modes))
        behind = tuple(decay[m] * carry[1][m] + g for m in range(modes))
        return (ahead, behind)

    zero = tuple(jnp.zeros((tiles, LANES), F32) for _ in range(modes))
    for side, held in enumerate(lax.fori_loop(0, tok_rows, step, (zero, zero), unroll=8)):
        held = jnp.concatenate(held, axis=0)
        own_ref[side] = held
        sent_ref[side] = held.astype(LINK)


def block_states(query_proj, key_proj, value_proj, out_grad, coefs):
    tok_rows, width = key_proj.shape
    modes, tiles = coefs.shape[1:3]
    return pl.pallas_call(
        state_kernel,
        out_shape=[
            jax.ShapeDtypeStruct((2, modes * tiles, LANES), F32),
            jax.ShapeDtypeStruct((2, modes * tiles, LANES), LINK),
        ],
        scratch_shapes=[pltpu.VMEM(token_shape(tok_rows, tiles), F32)] * 2,
        compiler_params=pltpu.CompilerParams(vmem_limit_bytes=VMEM_BYTES),
        name="block_states",
    )(query_proj, key_proj, value_proj, out_grad, coefs)


def pair_kernel(seq_ref, coef_ref, own_ref, near_ref, *state_refs):
    pairs = len(state_refs) + 1
    modes, tiles = coef_ref.shape[1:3]
    pair = seq_ref[0] // 2
    second = seq_ref[0] % 2 == 1
    ahead, behind = [], []
    for m in range(modes):
        rows = slice(m * tiles, (m + 1) * tiles)
        decay = coef_ref[1, m]
        own, near = own_ref[0, rows], near_ref[0].astype(F32)[rows]
        ahead.append(jnp.where(second, own + decay * near, near + decay * own))
        own, near = own_ref[1, rows], near_ref[1].astype(F32)[rows]
        behind.append(jnp.where(second, near + decay * own, own + decay * near))
    ahead = jnp.concatenate(ahead, axis=0)
    behind = jnp.concatenate(behind, axis=0)
    for k in range(1, pairs):
        state_refs[k - 1][...] = jnp.where(pair + k < pairs, ahead, behind).astype(LINK)


def pair_states(seq_index, pairs, coefs, own, near):
    whole = pl.BlockSpec(memory_space=pltpu.VMEM)
    return pl.pallas_call(
        pair_kernel,
        in_specs=[pl.BlockSpec(memory_space=pltpu.SMEM)] + [whole] * 3,
        out_specs=[whole] * (pairs - 1),
        out_shape=[jax.ShapeDtypeStruct(own.shape[1:], LINK)] * (pairs - 1),
        compiler_params=pltpu.CompilerParams(vmem_limit_bytes=VMEM_BYTES),
        name="pair_states",
    )(seq_index, coefs, own, near)


def sum_pairs(side, seq, coef_ref, near_ref, state_refs):
    pairs = len(state_refs) + 1
    modes, tiles = coef_ref.shape[1:3]
    pair, count = seq // 2, (seq // 2, pairs - 1 - seq // 2)[side]
    beside = seq % 2 == 1 - side
    held = []
    for m in range(modes):
        rows = slice(m * tiles, (m + 1) * tiles)
        decay = coef_ref[1, m]
        total = jnp.zeros((tiles, LANES), F32)
        for k in range(pairs - 1, 0, -1):
            state_ref = state_refs[k - 1 if side == 0 else pairs - k - 1]
            block = state_ref[...].astype(F32)[rows]
            total = decay * decay * total + jnp.where(k <= count, block, 0.0)
        near = near_ref[side].astype(F32)[rows]
        held.append(jnp.where(beside, decay * total + near, total))
    return held


def local_kernel(
    q_ref, k_ref, v_ref, o_ref, coef_ref, gain_ref, conv_ref, grad_ref, done_ref, x_ref, g_ref
):
    tok_rows, width = k_ref.shape
    tiles = width // LANES
    spread_tokens(k_ref, v_ref, x_ref)
    spread_tokens(o_ref, q_ref, g_ref)
    walk_tokens(x_ref, coef_ref, tok_rows, tiles, 0, 1)
    walk_tokens(g_ref, coef_ref, tok_rows, tiles, tok_rows - 1, -1)
    for tile in range(tiles):
        cols = slice(tile * LANES, (tile + 1) * LANES)
        rows = tile_rows(tok_rows, tile)
        gain = gain_ref[:, cols]
        conv_in = product(k_ref[:, cols], v_ref[:, cols]).astype(F32)
        conv_ref[:, cols] = x_ref[rows, :] + gain * conv_in
        mid_grad = product(o_ref[:, cols], q_ref[:, cols]).astype(F32)
        grad_ref[:, cols] = g_ref[rows, :] + gain * mid_grad
    done_ref[...] = jnp.zeros(done_ref.shape, F32)


def local_parts(query_proj, key_proj, value_proj, out_grad, coefs, gain):
    tok_rows, width = key_proj.shape
    tiles = coefs.shape[2]
    return pl.pallas_call(
        local_kernel,
        out_shape=[jax.ShapeDtypeStruct((tok_rows, width), F32)] * 2
        + [jax.ShapeDtypeStruct((SUBLANES, LANES), F32)],
        scratch_shapes=[pltpu.VMEM(token_shape(tok_rows, tiles), F32)] * 2,
        compiler_params=pltpu.CompilerParams(vmem_limit_bytes=VMEM_BYTES),
        name="local_parts",
    )(query_proj, key_proj, value_proj, out_grad, coefs, gain)


def along_column(state, pairs, k):
    route = [(2 * p + b, 2 * ((p + k) % pairs) + b) for p in range(pairs) for b in range(2)]
    return lax.ppermute(state, "seq", route)


def inside_pair(state, pairs):
    return lax.ppermute(state, "seq", [(i, i ^ 1) for i in range(2 * pairs)])


def fill_edge(ref, held, coef_ref, tok_rows, tiles, start, move):
    modes = coef_ref.shape[1]
    decay = [coef_ref[0, m] for m in range(modes)]

    def step(t, held):
        held = tuple(decay[m] * held[m] for m in range(modes))
        ref[token_place(start + move * t, tok_rows, tiles)] = tree_sum(list(held))
        return held

    held = tuple(coef_ref[2, m] * held[m] for m in range(modes))
    lax.fori_loop(0, tok_rows, step, held, unroll=8)


def edge_kernel(seq_ref, coef_ref, near_ref, *refs):
    state_refs, edge_ref = refs[:-1], refs[-1]
    fill_side(0, edge_ref, seq_ref, coef_ref, near_ref, state_refs)


def fill_side(side, edge_ref, seq_ref, coef_ref, near_ref, state_refs):
    tiles = coef_ref.shape[2]
    tok_rows = edge_ref.shape[0] // tiles - GAP
    held = sum_pairs(side, seq_ref[0], coef_ref, near_ref, state_refs)
    start, move = ((0, 1), (tok_rows - 1, -1))[side]
    fill_edge(edge_ref, held, coef_ref, tok_rows, tiles, start, move)


def edge_terms(tok_rows, seq_index, coefs, near, states):
    whole = pl.BlockSpec(memory_space=pltpu.VMEM)
    return pl.pallas_call(
        edge_kernel,
        in_specs=[pl.BlockSpec(memory_space=pltpu.SMEM)] + [whole] * (2 + len(states)),
        out_shape=jax.ShapeDtypeStruct(token_shape(tok_rows, coefs.shape[2]), F32),
        compiler_params=pltpu.CompilerParams(vmem_limit_bytes=VMEM_BYTES),
        name="edge_terms",
    )(seq_index, coefs, near, *states)


def multiply_out(part_ref, edge_ref, factor_refs, out_refs, hbm_refs, sems):
    tok_rows, width = part_ref.shape
    copies = []
    for tile in range(width // LANES):
        cols = slice(tile * LANES, (tile + 1) * LANES)
        value = part_ref[:, cols] + edge_ref[tile_rows(tok_rows, tile), :]
        for i, (factor_ref, out_ref, hbm_ref) in enumerate(zip(factor_refs, out_refs, hbm_refs)):
            out_ref[:, cols] = (value * factor_ref[:, cols].astype(F32)).astype(BF16)
            place = (slice(None), pl.ds(tile * LANES, LANES))
            copies.append(
                pltpu.make_async_copy(out_ref.at[place], hbm_ref.at[place], sems.at[i, tile])
            )
            copies[-1].start()
    return copies


def conv_kernel(seq_ref, part_ref, edge_ref, q_ref, coef_ref, near_ref, *refs):
    state_refs, (layer_hbm, next_ref, layer_ref, sems) = refs[:-4], refs[-4:]
    copies = multiply_out(part_ref, edge_ref, [q_ref], [layer_ref], [layer_hbm], sems)
    fill_side(1, next_ref, seq_ref, coef_ref, near_ref, state_refs)
    for copy in copies:
        copy.wait()


def conv_outputs(seq_index, part, edge, query_proj, coefs, near, states):
    tok_rows, width = part.shape
    whole = pl.BlockSpec(memory_space=pltpu.VMEM)
    return pl.pallas_call(
        conv_kernel,
        in_specs=[pl.BlockSpec(memory_space=pltpu.SMEM)] + [whole] * (5 + len(states)),
        out_specs=[pl.BlockSpec(memory_space=pl.ANY), whole],
        out_shape=[
            jax.ShapeDtypeStruct((tok_rows, width), BF16),
            jax.ShapeDtypeStruct(edge.shape, F32),
        ],
        scratch_shapes=[
            pltpu.VMEM((tok_rows, width), BF16),
            pltpu.SemaphoreType.DMA((1, width // LANES)),
        ],
        compiler_params=pltpu.CompilerParams(vmem_limit_bytes=VMEM_BYTES),
        name="conv_outputs",
    )(seq_index, part, edge, query_proj, coefs, near, *states)


def grad_kernel(
    part_ref, edge_ref, v_ref, k_ref, key_hbm, value_hbm, key_ref, value_ref, sems
):
    copies = multiply_out(
        part_ref, edge_ref, [v_ref, k_ref], [key_ref, value_ref], [key_hbm, value_hbm], sems
    )
    for copy in copies:
        copy.wait()


def grad_outputs(part, edge, value_proj, key_proj):
    tok_rows, width = part.shape
    return pl.pallas_call(
        grad_kernel,
        in_specs=[pl.BlockSpec(memory_space=pltpu.VMEM)] * 4,
        out_specs=[pl.BlockSpec(memory_space=pl.ANY)] * 2,
        out_shape=[jax.ShapeDtypeStruct((tok_rows, width), BF16)] * 2,
        scratch_shapes=[pltpu.VMEM((tok_rows, width), BF16)] * 2
        + [pltpu.SemaphoreType.DMA((2, width // LANES))],
        compiler_params=pltpu.CompilerParams(vmem_limit_bytes=VMEM_BYTES),
        name="grad_outputs",
    )(part, edge, value_proj, key_proj)


def lag_kernel(shards, chans, groups, owned, *refs):
    in_refs, (out_ref, lag_sums, u_all, g_all, turned_all) = refs[1:-5], refs[-5:]
    halves = out_ref.shape[1] // owned
    tok_rows = halves * LANES
    blocks = shards * halves
    depth = chans * groups
    full = blocks * depth
    if len(in_refs) == 1:
        take = 2 * chans * groups * owned

        def by_filter(row):
            return row % (2 * depth) * owned + row // (2 * depth)

        order = one_hot(take, take, by_filter)
        for which, kept in enumerate((u_all, g_all)):
            rows = slice(which * groups * owned, (which + 1) * groups * owned)
            for s in range(0, shards, 2):
                piece = in_refs[0][s * chans : (s + 2) * chans, rows, :].reshape(take, tok_rows)
                piece = jnp.dot(order, piece, preferred_element_type=F32).astype(BF16)
                piece = piece.reshape(owned, 2 * depth, tok_rows)
                for e in range(2):
                    part = piece[:, e * depth : (e + 1) * depth, :]
                    for h in range(halves):
                        first = ((s + e) * halves + h) * depth
                        kept[:, first : first + depth, :] = part[:, :, h * LANES : (h + 1) * LANES]
    else:
        u_all[...] = in_refs[0][...]
        g_all[:, :full, :] = in_refs[1][...]
    g_all[:, full:, :] = jnp.zeros((owned, g_all.shape[1] - full, LANES), BF16)
    mirror = one_hot(LANES, LANES, lambda row: LANES - 1 - row)
    row = lax.broadcasted_iota(jnp.int32, (LANES, LANES), 0)
    col = lax.broadcasted_iota(jnp.int32, (LANES, LANES), 1)
    same_block = row + col >= LANES - 1
    filter_row = lax.broadcasted_iota(jnp.int32, (owned, LANES), 0)
    batch = min(blocks, 16)

    def one_filter(f, _):
        turned = turned_all[f]

        def some_lags(first):
            tables = []
            for d in range(0, batch, 2):
                live = full
                if batch == blocks:
                    live = min(full, -(-(blocks - d) * depth // LANES) * LANES)
                pair = jnp.concatenate(
                    [
                        g_all[f, pl.ds(pl.multiple_of((first + d + e) * depth, depth), live), :]
                        for e in range(2)
                    ],
                    axis=1,
                )
                table = jnp.dot(turned[:, :live], pair, preferred_element_type=F32)
                tables += [table[:, :LANES], table[:, LANES:]]
            last = g_all[f, pl.ds(pl.multiple_of((first + batch) * depth, depth), full), :]
            if batch < blocks:
                tables.append(jnp.dot(turned, last, preferred_element_type=F32))
            else:
                tables.append(jnp.zeros((LANES, LANES), F32))
            for d in range(batch):
                joined = jnp.where(same_block, tables[d], tables[d + 1])
                skewed = pltpu.roll(joined, 1, 1, stride=1, stride_axis=0)
                sums = jnp.sum(skewed, axis=0, keepdims=True)
                row = d % halves * owned
                place = ((first + d) // halves, slice(row, row + owned), slice(None))
                lag_sums[place] = jnp.where(filter_row == f, sums, lag_sums[place])

        if batch == blocks:
            some_lags(0)
        else:
            lax.fori_loop(0, blocks // batch, lambda i, c: (some_lags(i * batch), c)[1], 0)
        return 0

    for f in range(owned):
        turned_all[f] = lax.dot_general(
            mirror, u_all[f], (((1,), (1,)), ((), ())), preferred_element_type=F32
        ).astype(BF16)
    lax.fori_loop(0, owned, one_filter, 0, unroll=min(owned, 8))
    out_ref[...] = lag_sums[...].astype(LINK)


def filter_lags(received, done, shards, chans, owned):
    tok_rows = received.shape[2]
    groups = received.shape[1] // (2 * owned)
    halves = tok_rows // LANES
    depth = chans * groups
    full = shards * halves * depth
    args = (received,)
    if owned % SUBLANES:
        split = received.reshape(shards, chans, 2, groups, owned, halves, LANES)
        split = split.transpose(2, 4, 0, 5, 1, 3, 6).reshape(2, owned, full, LANES)
        args = (split[0], split[1])
    whole = pl.BlockSpec(memory_space=pltpu.VMEM)
    return pl.pallas_call(
        functools.partial(lag_kernel, shards, chans, groups, owned),
        in_specs=[pl.BlockSpec(memory_space=pl.ANY)] + [whole] * len(args),
        out_specs=whole,
        out_shape=jax.ShapeDtypeStruct((shards, halves * owned, LANES), LINK),
        scratch_shapes=[
            pltpu.VMEM((shards, halves * owned, LANES), F32),
            pltpu.VMEM((owned, full, LANES), BF16),
            pltpu.VMEM((owned, 2 * full + depth, LANES), BF16),
            pltpu.VMEM((owned, LANES, full), BF16),
        ],
        compiler_params=pltpu.CompilerParams(vmem_limit_bytes=VMEM_BYTES),
        name="filter_lags",
    )(done, *args)


def per_device(query_proj, key_proj, value_proj, out_grad, residues, decay_rate, skip_gain):
    tok_rows, width = key_proj.shape
    shards = lax.axis_size("seq")
    chans = lax.axis_size("chan")
    length = shards * tok_rows
    owned = FILTERS // (shards * chans)
    modes = residues.shape[1]
    signals = (query_proj, key_proj, value_proj, out_grad)

    send = pack_signals(shards, chans, owned, *signals)
    send, *signals, residues, decay_rate = lax.optimization_barrier(
        (send, *signals, residues, decay_rate)
    )
    received = lax.all_to_all(send, ("seq", "chan"), split_axis=0, concat_axis=0, tiled=True)

    coefs = jnp.stack(
        [
            jnp.exp(-decay_rate),
            jnp.exp(-(decay_rate * float(tok_rows))),
            residues * jnp.sqrt(decay_rate),
        ]
    )
    coefs = coefs.transpose(0, 2, 1).reshape(3, modes, 1, FILTERS // LANES, LANES)
    coefs = jnp.broadcast_to(coefs, (3, modes, width // FILTERS, FILTERS // LANES, LANES))
    coefs = coefs.reshape(3, modes, width // LANES, LANES)
    seq_index = lax.axis_index("seq").reshape(1)
    pairs = shards // 2
    own, sent = block_states(*signals, coefs)
    conv_part, grad_part, done = local_parts(*signals, coefs, skip_gain[None, :])
    sent, done = lax.optimization_barrier((sent, done))
    near = inside_pair(sent, pairs)
    states = pair_states(seq_index, pairs, coefs, own, near)
    states = [along_column(state, pairs, 1 + i) for i, state in enumerate(states)]

    scale = 1.0 / math.sqrt(length * (CHANNELS // FILTERS))
    lags = filter_lags(received, done, shards, chans, owned)
    lags, *states = lax.optimization_barrier((lags, *states))
    lags = lax.all_to_all(lags, "seq", split_axis=0, concat_axis=0, tiled=True)
    lags = lags.reshape(shards, tok_rows // LANES, owned, LANES).transpose(0, 2, 1, 3)
    filter_grad = lags.reshape(shards * owned, tok_rows).T.astype(F32) * scale
    query_proj, key_proj, value_proj, _ = signals
    edge = edge_terms(tok_rows, seq_index, coefs, near, states)
    layer_out, edge = conv_outputs(seq_index, conv_part, edge, query_proj, coefs, near, states)
    key_grad, value_grad = grad_outputs(grad_part, edge, value_proj, key_proj)
    return (layer_out, key_grad, value_grad, filter_grad)


def solution(mesh):
    split = P("seq", "chan")
    return jax.shard_map(
        per_device,
        mesh=mesh,
        in_specs=(split, split, split, split, P(), P(), P("chan")),
        out_specs=(split, split, split, split),
        check_vma=False,
    )
```
